32 devices in a mesh: tm: 4 (over z), height: 4 (over y, x), width: 2 (over core).
Axes of the slice: x: 2, y: 2, z: 4, core: 2. Of those that a mesh axis runs over, the one named last changes fastest.
Arguments:
- latent: bfloat16 [128, 8, 16, 512], P(None, 'tm', 'height', 'width'), may hold values from -64 to 64
- exponents: int32 [32], replicated, may hold values from -1 to 1
- cotangent: bfloat16 [128, 8, 16, 512], P(None, 'tm', 'height', 'width'), may hold values from -6 to 6
- conv_first: bfloat16 [128, 3456], replicated, may hold values from -0.109375 to 0.109375
- conv_second: bfloat16 [128, 3456], replicated, may hold values from -0.109375 to 0.109375
- gain_first: float32 [128], replicated, may hold values from 0.1 to 1.9
- shift_first: float32 [128], replicated, may hold values from -2.5 to 2.5
- gain_second: float32 [128], replicated, may hold values from 0.1 to 1.9
- shift_second: float32 [128], replicated, may hold values from -2.5 to 2.5
Outputs:
- decoded_grad: float32 [128, 8, 16, 512], P(None, 'tm', 'height', 'width')
- conv_first_grad: float32 [128, 3456], replicated
- conv_second_grad: float32 [128, 3456], replicated
The draws below stay inside these ranges and needn't reach their ends.
All inputs are finite; a program needn't handle non-finite values.
Results may differ from the reference program's by a relative error of at most 0.005.
Values may be sent and summed in bfloat16 or wider, within the bound.
No kernel may reach another device: no remote copies, remote signals or barrier semaphores. Data moves between devices by JAX's collectives and lax.ppermute only.
A program may use at most 128 MiB of HBM per device.

```python
import jax
import jax.numpy as jnp
from jax import lax

CH = 128
GROUPS = 32
ROWS_DEV = 4
NT = 8
NR = 16
NC = 512


def draw_latent(key, part):
    key = jax.random.fold_in(key, 11)
    row_key, col_key, noise_key = jax.random.split(key, 3)
    frame_place = (jnp.arange(NT, dtype=jnp.float32) / (NT - 1))[None, :, None, None]
    row_scale = jnp.power(10.0, jax.random.uniform(row_key, (1, 1, NR, 1), dtype=jnp.float32))
    col_scale = jnp.power(10.0, jax.random.uniform(col_key, (1, 1, 1, NC), dtype=jnp.float32))
    noise_draw = jnp.clip(jax.random.normal(noise_key, (CH, NT, NR, NC), dtype=jnp.float32), -4.0, 4.0)
    frame_ramp = jnp.sqrt(1.0 + 2.0 * frame_place)
    offset = 5.0 + 10.0 * frame_place
    values = 0.1 * (noise_draw * frame_ramp * row_scale * col_scale + offset)
    return jnp.clip(values, -64.0, 64.0).astype(jnp.bfloat16)


def draw_cotangent(key, part):
    key = jax.random.fold_in(key, 23)
    noise_key, chan_key, frame_key, band_key = jax.random.split(key, 4)
    bands = NR // ROWS_DEV
    noise_draw = jnp.clip(jax.random.normal(noise_key, (CH, NT, NR, NC), dtype=jnp.float32), -4.0, 4.0)
    chan_offset = jax.random.uniform(chan_key, (CH, 1, 1, 1), dtype=jnp.float32, minval=-1.0, maxval=1.0)
    frame_offset = jax.random.uniform(frame_key, (CH, NT, 1, 1), dtype=jnp.float32, minval=-0.7, maxval=0.7)
    band_draw = jax.random.uniform(band_key, (CH, 1, bands, 1), dtype=jnp.float32, minval=-0.7, maxval=0.7)
    band_offset = jnp.repeat(band_draw, ROWS_DEV, axis=2)
    values = noise_draw + (chan_offset + frame_offset + band_offset)
    return jnp.clip(values, -6.0, 6.0).astype(jnp.bfloat16)


def place_ends(array, rng, smallest, top_value):
    place = [jax.random.randint(jax.random.fold_in(rng, axis), (), 0, length) for axis, length in enumerate(array.shape)]
    longest = array.shape.index(max(array.shape))
    beside = place[:longest] + [(place[longest] + 1) % array.shape[longest]] + place[longest + 1:]
    return array.at[tuple(place)].set(smallest).at[tuple(beside)].set(top_value)


def bell_draw(own_key, extent, scale, bound, kind=jnp.bfloat16):
    entries = jax.random.normal(own_key, extent, jnp.float32) * scale
    return jnp.minimum(jnp.maximum(entries, -bound), bound).astype(kind)


def setup_inputs(seed: int = 0) -> dict:
    streams_of = jax.random.split(jax.random.key(seed), 10)
    latent = draw_latent(jax.random.fold_in(streams_of[9], 71), 0)
    exponents = place_ends(jax.random.randint(streams_of[1], (GROUPS,), -1, 2), jax.random.fold_in(streams_of[1], 1), -1, 1).astype(jnp.int32)
    cotangent = draw_cotangent(jax.random.fold_in(streams_of[9], 71), 0)
    conv_first = bell_draw(streams_of[3], (CH, 27 * CH), (27 * CH) ** -0.5, 0.109375)
    conv_second = bell_draw(streams_of[4], (CH, 27 * CH), (27 * CH) ** -0.5, 0.109375)
    gain_first = jnp.clip(1.0 + 0.18 * jax.random.normal(streams_of[5], (CH,), jnp.float32), 0.1, 1.9)
    shift_first = bell_draw(streams_of[6], (CH,), 0.5, 2.5, jnp.float32)
    gain_second = jnp.clip(1.0 + 0.18 * jax.random.normal(streams_of[7], (CH,), jnp.float32), 0.1, 1.9)
    shift_second = bell_draw(streams_of[8], (CH,), 0.5, 2.5, jnp.float32)
    return dict(latent=latent, exponents=exponents, cotangent=cotangent, conv_first=conv_first, conv_second=conv_second, gain_first=gain_first, shift_first=shift_first, gain_second=gain_second, shift_second=shift_second)


epsilon = 1e-05

def convolve(values, weight):
    channels = values.shape[0]
    kernel = weight.reshape(channels, 3, 3, 3, channels).transpose(0, 4, 1, 2, 3)
    result = lax.conv_general_dilated(values[None], kernel, (1, 1, 1), [(2, 0), (1, 1), (1, 1)], dimension_numbers=('NCDHW', 'OIDHW', 'NCDHW'), precision=lax.Precision.HIGHEST)
    return result[0]

def per_channel(stat):
    return jnp.repeat(stat, CH // GROUPS)[:, None, None, None]

def channel(vector):
    return vector[:, None, None, None]

def group_mean(values):
    return lax.optimization_barrier(jnp.mean(values.reshape(GROUPS, -1), axis=1))

def normalize(values):
    mean_value = group_mean(values)
    centered = values - per_channel(mean_value)
    variance = group_mean(centered * centered)
    inverse = 1.0 / jnp.sqrt(variance + epsilon)
    return (centered * per_channel(inverse), inverse)

def silu_slope(pre):
    sigmoid_value = jax.nn.sigmoid(pre)
    return sigmoid_value * (1.0 + pre * (1.0 - sigmoid_value))

def norm_backward(grad, pre, normed, gain, inverse):
    scaled = grad * silu_slope(pre) * channel(gain)
    first_mean = group_mean(scaled)
    second_mean = group_mean(scaled * normed)
    return per_channel(inverse) * (scaled - per_channel(first_mean) - normed * per_channel(second_mean))

def reference(latent, exponents, cotangent, conv_first, conv_second, gain_first, shift_first, gain_second, shift_second):
    scaling = jnp.exp2(exponents.astype(jnp.float32))
    decoded = latent.astype(jnp.float32) * per_channel(scaling)
    normed_first, inverse_first = normalize(decoded)
    pre_first = normed_first * channel(gain_first) + channel(shift_first)
    act_first = jax.nn.silu(pre_first).astype(jnp.bfloat16)
    hidden, pull_first = jax.vjp(convolve, act_first.astype(jnp.float32), conv_first.astype(jnp.float32))
    normed_second, inverse_second = normalize(hidden)
    pre_second = normed_second * channel(gain_second) + channel(shift_second)
    act_second = jax.nn.silu(pre_second).astype(jnp.bfloat16)
    output_value, pull_second = jax.vjp(convolve, act_second.astype(jnp.float32), conv_second.astype(jnp.float32))
    grad_second, conv_second_grad = pull_second(cotangent.astype(jnp.float32))
    hidden_grad = norm_backward(grad_second, pre_second, normed_second, gain_second, inverse_second).astype(jnp.bfloat16)
    grad_first, conv_first_grad = pull_first(hidden_grad.astype(jnp.float32))
    decoded_grad = cotangent.astype(jnp.float32) + norm_backward(grad_first, pre_first, normed_first, gain_first, inverse_first)
    return (decoded_grad, conv_first_grad, conv_second_grad)
```

```python
import functools

import jax
import jax.numpy as jnp
from jax import lax
from jax.experimental import pallas as pl
from jax.experimental.pallas import tpu as pltpu
from jax.sharding import PartitionSpec as P

epsilon = 1e-05
F32 = jnp.float32
BF16 = jnp.bfloat16
GROUP = 4
VMEM = pl.BlockSpec(memory_space=pltpu.VMEM)
SMEM = pl.BlockSpec(memory_space=pltpu.SMEM)


def call(body, outs, specs, args, scratch=(), flops=0, transcendentals=0, limit=48):
    moved = sum(a.size * a.dtype.itemsize for a in args)
    moved += sum(o.size * o.dtype.itemsize for o in outs)
    return pl.pallas_call(
        body,
        out_shape=tuple(outs),
        in_specs=specs,
        out_specs=tuple(VMEM for _ in outs),
        scratch_shapes=scratch,
        compiler_params=pltpu.CompilerParams(vmem_limit_bytes=limit << 20),
        cost_estimate=pl.CostEstimate(
            flops=flops, bytes_accessed=moved, transcendentals=transcendentals
        ),
    )(*args)


def shape(dims, dtype):
    return jax.ShapeDtypeStruct(dims, dtype)


def group_sums(acc):
    rows = acc.shape[0]
    row = lax.broadcasted_iota(jnp.int32, acc.shape, 0)
    step = 1
    while step < GROUP:
        up = pltpu.roll(acc, rows - step, axis=0)
        down = pltpu.roll(acc, step, axis=0)
        acc = acc + jnp.where((row & step) == 0, up, down)
        step *= 2
    return jnp.sum(acc, axis=1, keepdims=True)


def lanes_of(plane):
    total = plane[:, :128]
    for start in range(128, plane.shape[1], 128):
        total = total + plane[:, start : start + 128]
    return total


def as_rows(first, second):
    channels = first.shape[0]
    lane = lax.broadcasted_iota(jnp.int32, (channels, 128), 1)
    both = jnp.where(lane == 0, first, jnp.where(lane == 1, second, 0.0))
    return jnp.transpose(both)[:8]


def local_stats(planes, count):
    acc = None
    for plane in planes:
        part = lanes_of(plane())
        acc = part if acc is None else acc + part
    mean = group_sums(acc) / count
    acc = None
    for plane in planes:
        off = plane() - mean
        part = lanes_of(off * off)
        acc = part if acc is None else acc + part
    return as_rows(mean, group_sums(acc))


def columns_of(rows):
    return jnp.transpose(rows)


def sigmoid(value):
    return 0.5 + 0.5 * jnp.tanh(0.5 * value)


def stats_kernel(planes_ref, par_ref, out_ref):
    rows, frames, _, cols = planes_ref.shape
    scale = columns_of(par_ref[...])[:, 0:1]
    planes = [
        functools.partial(lambda r, t: planes_ref[r, t].astype(F32) * scale, r, t)
        for r in range(rows)
        for t in range(frames)
    ]
    out_ref[...] = local_stats(planes, float(GROUP * rows * frames * cols))


def source(own, other, top, bottom, other_first):
    def at(row, frame):
        if row == 0:
            return top, (frame,)
        if row == own.shape[0] + 1:
            return bottom, (frame,)
        if (frame < 2) == other_first:
            return other, (row - 1, frame % 2)
        return own, (row - 1, frame % 2)

    return at


def edges_kernel(flag_ref, own, other, top, bottom, out_ref, *, other_first):
    at = source(own, other, top, bottom, other_first)
    is_first = flag_ref[3] == 0
    channels = own.shape[2]
    lane = lax.broadcasted_iota(jnp.int32, (channels, 128), 1)
    acc = jnp.zeros((channels, 128), F32)
    for row in range(own.shape[0] + 2):
        for frame in range(4):
            ref, index = at(row, frame)
            plane = ref[index]
            last = pltpu.roll(plane[:, -128:].astype(F32), 1, axis=1)
            edge = jnp.where(is_first, last, plane[:, :128].astype(F32))
            number = 4 * row + frame
            moved = pltpu.roll(edge, number, axis=1) if number else edge
            acc = jnp.where(lane == number, moved, acc)
    out_ref[...] = acc.astype(BF16)


def fill_stack(stack, row, frame, plane, edge, on_left, on_right):
    channels, cols = plane.shape
    lane = lax.broadcasted_iota(jnp.int32, (channels, cols), 1)
    number = 4 * row + frame
    column = edge[:, number : number + 1]
    left = jnp.where(lane == 0, column * on_left, pltpu.roll(plane, 1, axis=1))
    right = jnp.where(lane == cols - 1, column * on_right, pltpu.roll(plane, cols - 1, axis=1))
    stack[row, frame, 0:channels] = left.astype(BF16)
    stack[row, frame, channels : 2 * channels] = plane.astype(BF16)
    stack[row, frame, 2 * channels : 3 * channels] = right.astype(BF16)


def sides(flag_ref):
    on_left = (flag_ref[3] != 0).astype(F32)
    on_right = (flag_ref[3] == 0).astype(F32)
    return on_left, on_right


def conv_rows(stack, weight, row):
    three = stack[row : row + 3].reshape(weight.shape[1], stack.shape[3])
    return jnp.dot(weight[...], three, preferred_element_type=F32)


def norm_columns(par_ref, st_ref, count, gain_row):
    par = par_ref[...]
    stats = st_ref[...]
    mean = stats[0:1]
    inverse = 1.0 / jnp.sqrt(stats[1:2] / count + epsilon)
    gain = par[gain_row : gain_row + 1]
    shift = par[gain_row + 1 : gain_row + 2]
    rows = jnp.concatenate([mean, inverse, gain, shift, par[0:1], stats[2:5]], axis=0)
    cols = columns_of(rows)
    return [cols[:, i : i + 1] for i in range(5)]


def conv_first_kernel(
    flag_ref, own, past, top, bottom, edge_ref, par_ref, st_ref, weight, hidden_ref, st_out, stack_ref, *, count
):
    rows, frames, channels, cols = own.shape
    at = source(own, past, top, bottom, True)
    mean, inverse, gain, shift, scale = norm_columns(par_ref, st_ref, count, 1)

    def act(latent):
        pre = (latent.astype(F32) * scale - mean) * inverse * gain + shift
        return pre * sigmoid(pre)

    has_past = flag_ref[0].astype(F32)
    has_top = flag_ref[1].astype(F32)
    has_bottom = flag_ref[2].astype(F32)
    on_left, on_right = sides(flag_ref)
    lane = lax.broadcasted_iota(jnp.int32, (channels, 128), 1)
    edge = act(edge_ref[...])
    edge = edge * jnp.where((lane & 3) < 2, has_past, 1.0)
    edge = edge * jnp.where(lane < 4, has_top, 1.0)
    edge = edge * jnp.where(lane >= 4 * (rows + 1), has_bottom, 1.0)
    for row in range(rows + 2):
        for frame in range(4):
            ref, index = at(row, frame)
            plane = act(ref[index])
            factor = None
            if frame < 2:
                factor = has_past
            if row in (0, rows + 1):
                beside = has_top if row == 0 else has_bottom
                factor = beside if factor is None else factor * beside
            if factor is not None:
                plane = plane * factor
            fill_stack(stack_ref, row, frame, plane, edge, on_left, on_right)
    for row in range(rows):
        out = conv_rows(stack_ref, weight, row)
        for frame in range(frames):
            hidden_ref[row, frame] = out[frame * channels : (frame + 1) * channels]
    planes = [
        functools.partial(lambda r, t: hidden_ref[r, t], r, t) for r in range(rows) for t in range(frames)
    ]
    st_out[...] = local_stats(planes, float(GROUP * rows * frames * cols))


def conv_back_kernel(flag_ref, own, future, top, bottom, edge_ref, weight, grad_ref, stack_ref):
    rows, frames, channels, cols = own.shape
    at = source(own, future, top, bottom, False)
    on_left, on_right = sides(flag_ref)
    edge = edge_ref[...].astype(F32)
    for row in range(rows + 2):
        for frame in range(4):
            ref, index = at(row, frame)
            fill_stack(stack_ref, row, frame, ref[index].astype(F32), edge, on_left, on_right)
    for row in range(rows):
        out = conv_rows(stack_ref, weight, row)
        for frame in range(frames):
            grad_ref[row, frame] = out[frame * channels : (frame + 1) * channels]


def norm_second_kernel(hidden, grad, par_ref, st_ref, act_ref, scaled_ref, sums_ref, *, count):
    rows, frames, channels, cols = hidden.shape
    mean, inverse, gain, shift, _ = norm_columns(par_ref, st_ref, count, 3)
    first = jnp.zeros((channels, 128), F32)
    second = jnp.zeros((channels, 128), F32)
    for row in range(rows):
        for frame in range(frames):
            normed = (hidden[row, frame] - mean) * inverse
            pre = normed * gain + shift
            sig = sigmoid(pre)
            act = pre * sig
            act_ref[row, frame] = act.astype(BF16)
            scaled = grad[row, frame] * (sig + act * (1.0 - sig)) * gain
            scaled_ref[row, frame] = scaled
            first = first + lanes_of(scaled)
            second = second + lanes_of(scaled * normed)
    sums_ref[...] = as_rows(group_sums(first), group_sums(second))


def hidden_grad_kernel(hidden, scaled, par_ref, st_ref, sums_ref, out_ref, *, count):
    rows, frames, channels, cols = hidden.shape
    mean, inverse, _, _, _ = norm_columns(par_ref, st_ref, count, 3)
    means = columns_of(sums_ref[...] / count)
    first, second = means[:, 0:1], means[:, 1:2]
    for row in range(rows):
        for frame in range(frames):
            normed = (hidden[row, frame] - mean) * inverse
            out_ref[row, frame] = (inverse * (scaled[row, frame] - first - normed * second)).astype(BF16)


def weight_second_kernel(stack_ref, act_ref, out_ref, right_ref):
    rows, frames, channels, cols = act_ref.shape
    for row in range(rows):
        right_ref[row * cols : (row + 1) * cols] = jnp.transpose(
            act_ref[row].reshape(frames * channels, cols)
        )
    right = right_ref[...]
    for down in range(3):
        parts = []
        for frame in range(4):
            left = jnp.concatenate([stack_ref[down + row, frame] for row in range(rows)], axis=1)
            parts.append(jnp.dot(left, right, preferred_element_type=F32))
        for kt in range(3):
            term = parts[2 - kt][:, :channels] + parts[3 - kt][:, channels:]
            for across in range(3):
                tap = 9 * kt + 3 * (2 - down) + (2 - across)
                out_ref[:, tap * channels : (tap + 1) * channels] = term[
                    across * channels : (across + 1) * channels
                ]


def weight_first_kernel(stack_ref, grad_ref, out_ref, right_ref):
    rows, frames, channels, cols = grad_ref.shape
    for row in range(rows):
        right_ref[row * cols : (row + 1) * cols] = jnp.transpose(
            grad_ref[row].reshape(frames * channels, cols)
        )
    right = right_ref[...]
    for down in range(3):
        parts = []
        for frame in range(4):
            left = jnp.concatenate([stack_ref[down + row, frame] for row in range(rows)], axis=1)
            parts.append(jnp.dot(left, right, preferred_element_type=F32))
        for kt in range(3):
            term = parts[kt][:, :channels] + parts[kt + 1][:, channels:]
            for across in range(3):
                tap = 9 * kt + 3 * down + across
                out_ref[:, tap * channels : (tap + 1) * channels] = jnp.transpose(
                    term[across * channels : (across + 1) * channels]
                )


def first_grad_kernel(
    flag_ref, own, future, top, bottom, edge_ref, weight, latent, par_ref, st_ref, scaled_ref, sums_ref, stack_ref,
    *, count
):
    rows, frames, channels, cols = own.shape
    at = source(own, future, top, bottom, False)
    on_left, on_right = sides(flag_ref)
    edge = edge_ref[...].astype(F32)
    mean, inverse, gain, shift, scale = norm_columns(par_ref, st_ref, count, 1)
    for row in range(rows + 2):
        for frame in range(4):
            ref, index = at(row, frame)
            fill_stack(stack_ref, row, frame, ref[index].astype(F32), edge, on_left, on_right)
    first = jnp.zeros((channels, 128), F32)
    second = jnp.zeros((channels, 128), F32)
    for row in range(rows):
        out = conv_rows(stack_ref, weight, row)
        for frame in range(frames):
            grad = out[frame * channels : (frame + 1) * channels]
            normed = (latent[row, frame].astype(F32) * scale - mean) * inverse
            pre = normed * gain + shift
            sig = sigmoid(pre)
            scaled = grad * (sig + pre * sig * (1.0 - sig)) * gain
            scaled_ref[row, frame] = scaled
            first = first + lanes_of(scaled)
            second = second + lanes_of(scaled * normed)
    sums_ref[...] = as_rows(group_sums(first), group_sums(second))


def decoded_grad_kernel(scaled, latent, cotangent, par_ref, st_ref, sums_ref, out_ref, *, count):
    rows, frames, channels, cols = latent.shape
    mean, inverse, _, _, scale = norm_columns(par_ref, st_ref, count, 1)
    means = columns_of(sums_ref[...] / count)
    first, second = means[:, 0:1], means[:, 1:2]
    for row in range(rows):
        for frame in range(frames):
            normed = (latent[row, frame].astype(F32) * scale - mean) * inverse
            out_ref[row, frame] = cotangent[row, frame].astype(F32) + inverse * (
                scaled[row, frame] - first - normed * second
            )


def weight_forward_kernel(weight, out_ref):
    channels = weight.shape[0]
    wide = 3 * channels
    for t in range(2):
        for kr in range(3):
            for f in range(4):
                kt = f - t
                here = slice((kr * 4 + f) * wide, (kr * 4 + f + 1) * wide)
                if 0 <= kt < 3:
                    tap = 3 * kt + kr
                    block = weight[:, tap * wide : (tap + 1) * wide]
                else:
                    block = jnp.zeros((channels, wide), BF16)
                out_ref[t * channels : (t + 1) * channels, here] = block


def weight_back_kernel(weight, out_ref):
    channels = weight.shape[0]
    for down in range(3):
        for across in range(3):
            blocks = [
                jnp.transpose(
                    weight[
                        :,
                        (9 * kt + 3 * (2 - down) + 2 - across) * channels : (9 * kt + 3 * (2 - down) + 3 - across)
                        * channels,
                    ]
                )
                for kt in range(3)
            ]
            for t in range(2):
                for f in range(4):
                    kt = t + 2 - f
                    start = ((down * 4 + f) * 3 + across) * channels
                    block = blocks[kt] if 0 <= kt < 3 else jnp.zeros((channels, channels), BF16)
                    out_ref[t * channels : (t + 1) * channels, start : start + channels] = block


def shifted(value, axis, steps):
    count = lax.axis_size(axis)
    initial, last = max(0, -steps), min(count, count - steps)
    return lax.ppermute(value, axis, [(source, source + steps) for source in range(initial, last)])


def rounds():
    for axis in ("width", "height", "tm"):
        step = 1
        while step < lax.axis_size(axis):
            yield axis, [(i, i ^ step) for i in range(lax.axis_size(axis))]
            step *= 2


def all_sum(value):
    for axis, pairs in rounds():
        value = value + lax.ppermute(value, axis, pairs)
    return value


def all_stats(value, count):
    for axis, pairs in rounds():
        other = lax.ppermute(value, axis, pairs)
        gap = value[0:1] - other[0:1]
        value = jnp.concatenate(
            [
                0.5 * (value[0:1] + other[0:1]),
                value[1:2] + other[1:2] + gap * gap * (0.5 * count),
                jnp.zeros_like(value[2:]),
            ],
            axis=0,
        )
        count = 2.0 * count
    return value


def reduce_weights(term, after):
    stages = (
        lambda v: lax.psum_scatter(v, "width", scatter_dimension=0, tiled=True),
        lambda v: lax.psum_scatter(v, "tm", scatter_dimension=0, tiled=True),
        lambda v: lax.psum(v, "height"),
        lambda v: lax.all_gather(v, "tm", axis=0, tiled=True),
        lambda v: lax.all_gather(v, "width", axis=0, tiled=True),
    )
    results = []
    for number, stage in enumerate(stages):
        if after:
            term, _ = lax.optimization_barrier((term, after[number]))
        term = stage(term)
        results.append(term)
    return term, results


def extended(flags, own, steps):
    other = shifted(own, "tm", steps)
    pair = (other, own) if steps > 0 else (own, other)
    top = shifted(jnp.concatenate([part[-1] for part in pair], axis=0), "height", 1)
    bottom = shifted(jnp.concatenate([part[0] for part in pair], axis=0), "height", -1)
    channels = own.shape[2]
    (edge,) = call(
        functools.partial(edges_kernel, other_first=steps > 0),
        [shape((channels, 128), BF16)],
        [SMEM] + [VMEM] * 4,
        (flags, own, other, top, bottom),
    )
    edge = lax.ppermute(edge, "width", [(0, 1), (1, 0)])
    return other, top, bottom, edge


def shards(
    latent,
    exponents,
    cotangent,
    conv_first,
    conv_second,
    gain_first,
    shift_first,
    gain_second,
    shift_second,
):
    channels, frames, rows, cols = latent.shape
    groups = exponents.shape[0]
    devices = lax.axis_size("tm") * lax.axis_size("height") * lax.axis_size("width")
    here = channels // groups * frames * rows * cols
    count = float(here * devices)
    tm, height, width = (lax.axis_index(axis) for axis in ("tm", "height", "width"))
    flags = jnp.stack(
        [
            (tm > 0).astype(jnp.int32),
            (height > 0).astype(jnp.int32),
            (height < lax.axis_size("height") - 1).astype(jnp.int32),
            width.astype(jnp.int32),
        ]
    )
    scale = jnp.repeat(jnp.exp2(exponents.astype(F32)), channels // groups)
    zeros = jnp.zeros_like(scale)
    par = jnp.stack([scale, gain_first, shift_first, gain_second, shift_second, zeros, zeros, zeros])
    latent = latent.transpose(2, 1, 0, 3)
    cotangent = cotangent.transpose(2, 1, 0, 3)
    block = (rows, frames, channels, cols)
    stack = (rows + 2, 4, 3 * channels, cols)
    taps = (2 * channels, 36 * channels)
    conv_flops = 2 * 4 * 256 * 36 * channels * 2 * channels
    small = shape((8, channels), F32)

    (stats_first,) = call(stats_kernel, [small], [VMEM] * 2, (latent, par))
    past, top, bottom, edge = extended(flags, latent, 1)
    future_c, top_c, bottom_c, edge_c = extended(flags, cotangent, -1)
    stats_first = all_stats(stats_first, float(here))
    (weight_first,) = call(weight_forward_kernel, [shape(taps, BF16)], [VMEM], (conv_first,))
    (weight_second_t,) = call(weight_back_kernel, [shape(taps, BF16)], [VMEM], (conv_second,))
    (weight_first_t,) = call(weight_back_kernel, [shape(taps, BF16)], [VMEM], (conv_first,))

    hidden, stats_second, stack_first = call(
        functools.partial(conv_first_kernel, count=count),
        [shape(block, F32), small, shape(stack, BF16)],
        [SMEM] + [VMEM] * 8,
        (flags, latent, past, top, bottom, edge, par, stats_first, weight_first),
        flops=conv_flops,
        transcendentals=3 * latent.size,
    )
    stats_second = all_stats(stats_second, float(here))
    grad_second, stack_c = call(
        conv_back_kernel,
        [shape(block, F32), shape(stack, BF16)],
        [SMEM] + [VMEM] * 6,
        (flags, cotangent, future_c, top_c, bottom_c, edge_c, weight_second_t),
        flops=conv_flops,
    )
    act_second, scaled, sums = call(
        functools.partial(norm_second_kernel, count=count),
        [shape(block, BF16), shape(block, F32), small],
        [VMEM] * 4,
        (hidden, grad_second, par, stats_second),
        transcendentals=latent.size,
    )
    sums = all_sum(sums)
    (conv_second_grad,) = call(
        weight_second_kernel,
        [shape((channels, 27 * channels), F32)],
        [VMEM] * 2,
        (stack_c, act_second),
        scratch=[pltpu.VMEM((rows * cols, frames * channels), BF16)],
        flops=conv_flops,
    )
    conv_second_grad, stages = reduce_weights(conv_second_grad, None)
    (hidden_grad,) = call(
        functools.partial(hidden_grad_kernel, count=count),
        [shape(block, BF16)],
        [VMEM] * 5,
        (hidden, scaled, par, stats_second, sums),
    )
    future, top, bottom, edge = extended(flags, hidden_grad, -1)
    (conv_first_grad,) = call(
        weight_first_kernel,
        [shape((channels, 27 * channels), F32)],
        [VMEM] * 2,
        (stack_first, hidden_grad),
        scratch=[pltpu.VMEM((rows * cols, frames * channels), BF16)],
        flops=conv_flops,
    )
    conv_first_grad, _ = reduce_weights(conv_first_grad, stages)
    scaled, sums = call(
        functools.partial(first_grad_kernel, count=count),
        [shape(block, F32), small],
        [SMEM] + [VMEM] * 9,
        (flags, hidden_grad, future, top, bottom, edge, weight_first_t, latent, par, stats_first),
        scratch=[pltpu.VMEM(stack, BF16)],
        flops=conv_flops,
        transcendentals=latent.size,
    )
    sums = all_sum(sums)
    (decoded_grad,) = call(
        functools.partial(decoded_grad_kernel, count=count),
        [shape(block, F32)],
        [VMEM] * 6,
        (scaled, latent, cotangent, par, stats_first, sums),
    )
    return decoded_grad.transpose(2, 1, 0, 3), conv_first_grad, conv_second_grad


def solution(mesh):
    block = P(None, "tm", "height", "width")
    return jax.shard_map(
        shards,
        mesh=mesh,
        in_specs=(block, P(), block, P(), P(), P(), P(), P(), P()),
        out_specs=(block, P(), P()),
        check_vma=False,
    )
```

```python
import functools

import jax
import jax.numpy as jnp
from jax import lax
from jax.experimental import pallas as pl
from jax.experimental.pallas import tpu as pltpu
from jax.sharding import PartitionSpec as P

epsilon = 1e-05
F32 = jnp.float32
BF16 = jnp.bfloat16
GROUP = 4
VMEM = pl.BlockSpec(memory_space=pltpu.VMEM)
SMEM = pl.BlockSpec(memory_space=pltpu.SMEM)
ANY = pl.BlockSpec(memory_space=pl.ANY)


def call(body, outs, specs, args, scratch=(), flops=0, transcendentals=0, limit=48):
    moved = sum(a.size * a.dtype.itemsize for a in args)
    moved += sum(o.size * o.dtype.itemsize for o in outs)
    return pl.pallas_call(
        body,
        out_shape=tuple(outs),
        in_specs=specs,
        out_specs=tuple(VMEM for _ in outs),
        scratch_shapes=scratch,
        compiler_params=pltpu.CompilerParams(vmem_limit_bytes=limit << 20),
        cost_estimate=pl.CostEstimate(
            flops=flops, bytes_accessed=moved, transcendentals=transcendentals
        ),
    )(*args)


def shape(dims, dtype):
    return jax.ShapeDtypeStruct(dims, dtype)


def group_sums(acc):
    rows = acc.shape[0]
    row = lax.broadcasted_iota(jnp.int32, acc.shape, 0)
    step = 1
    while step < GROUP:
        up = pltpu.roll(acc, rows - step, axis=0)
        down = pltpu.roll(acc, step, axis=0)
        acc = acc + jnp.where((row & step) == 0, up, down)
        step *= 2
    return jnp.sum(acc, axis=1, keepdims=True)


def lanes_of(plane):
    total = plane[:, :128]
    for start in range(128, plane.shape[1], 128):
        total = total + plane[:, start : start + 128]
    return total


def as_rows(first, second):
    channels = first.shape[0]
    lane = lax.broadcasted_iota(jnp.int32, (channels, 128), 1)
    both = jnp.where(lane == 0, first, jnp.where(lane == 1, second, 0.0))
    return jnp.transpose(both)[:2]


def local_stats(planes, count):
    acc = None
    for plane in planes:
        part = lanes_of(plane())
        acc = part if acc is None else acc + part
    mean = group_sums(acc) / count
    acc = None
    for plane in planes:
        off = plane() - mean
        part = lanes_of(off * off)
        acc = part if acc is None else acc + part
    return as_rows(mean, group_sums(acc))


def columns_of(*rows):
    rows = list(rows) + [jnp.zeros_like(rows[0])] * (8 - len(rows))
    cols = jnp.transpose(jnp.concatenate(rows, axis=0))
    return [cols[:, i : i + 1] for i in range(8)]


def sigmoid(value):
    return 0.5 + 0.5 * jnp.tanh(0.5 * value)


def stats_kernel(planes_ref, par_ref, out_ref):
    rows, frames, _, cols = planes_ref.shape
    scale = columns_of(par_ref[0:1])[0]
    planes = [
        functools.partial(lambda r, t: planes_ref[r, t].astype(F32) * scale, r, t)
        for r in range(rows)
        for t in range(frames)
    ]
    out_ref[...] = local_stats(planes, float(GROUP * rows * frames * cols))


def source(own, other, near, far, other_first):
    def at(row, frame):
        is_other = (frame < 2) == other_first
        if row == 0 or row == own.shape[0] + 1:
            return (far if is_other else near), (0 if row == 0 else 1, frame % 2)
        return (other if is_other else own), (row - 1, frame % 2)

    return at


def edges_kernel(flag_ref, *refs):
    planes, out_ref = refs[:-1], refs[-1]
    is_first = flag_ref[3] == 0
    channels = planes[0].shape[2]
    lane = lax.broadcasted_iota(jnp.int32, (channels, 128), 1)
    acc = jnp.zeros((channels, 128), F32)
    number = 0
    for ref in planes:
        for row in range(ref.shape[0]):
            for frame in range(ref.shape[1]):
                last = pltpu.roll(ref[row, frame, :, -128:].astype(F32), 1, axis=1)
                edge = jnp.where(is_first, last, ref[row, frame, :, :128].astype(F32))
                moved = pltpu.roll(edge, number, axis=1) if number else edge
                acc = jnp.where(lane == number, moved, acc)
                number += 1
    out_ref[...] = acc.astype(BF16)


def edge_lane(row, frame, rows, other_first):
    is_other = int((frame < 2) == other_first)
    if row == 0 or row == rows + 1:
        return 1, 4 * is_other + 2 * int(row > 0) + frame % 2
    return 0, 2 * rows * is_other + 2 * (row - 1) + frame % 2


def fill_stack(stack, row, frame, plane, column, on_left, on_right):
    channels, cols = plane.shape
    lane = lax.broadcasted_iota(jnp.int32, (channels, cols), 1)
    column = column.astype(F32)
    left = jnp.where(lane == 0, (column * on_left).astype(BF16), pltpu.roll(plane, 1, axis=1))
    right = jnp.where(lane == cols - 1, (column * on_right).astype(BF16), pltpu.roll(plane, cols - 1, axis=1))
    stack[row, frame, 0:channels] = left
    stack[row, frame, channels : 2 * channels] = plane
    stack[row, frame, 2 * channels : 3 * channels] = right


def sides(flag_ref):
    on_left = (flag_ref[3] != 0).astype(F32)
    on_right = (flag_ref[3] == 0).astype(F32)
    return on_left, on_right


def conv_rows(stack, weight, row):
    three = stack[row : row + 3].reshape(weight.shape[1], stack.shape[3])
    return jnp.dot(weight[...], three, preferred_element_type=F32)


def norm_columns(par_ref, st_ref, count, gain_row):
    par = par_ref[...]
    stats = st_ref[...]
    mean = stats[0:1]
    inverse = 1.0 / jnp.sqrt(stats[1:2] / count + epsilon)
    gain = par[gain_row : gain_row + 1]
    shift = par[gain_row + 1 : gain_row + 2]
    return columns_of(mean, inverse, gain, shift, par[0:1])[:5]


def conv_first_kernel(
    flag_ref, own, past, near, far, edge_ref, rim_ref, par_ref, st_ref, weight, after, hidden_ref, st_out, stack_ref,
    *, count
):
    rows, frames, channels, cols = own.shape
    at = source(own, past, near, far, True)
    mean, inverse, gain, shift, scale = norm_columns(par_ref, st_ref, count, 1)

    def act(latent):
        pre = (latent.astype(F32) * scale - mean) * inverse * gain + shift
        return pre * sigmoid(pre)

    has_past = flag_ref[0].astype(F32)
    has_top = flag_ref[1].astype(F32)
    has_bottom = flag_ref[2].astype(F32)
    on_left, on_right = sides(flag_ref)
    edges = (act(edge_ref[...]), act(rim_ref[...]))
    for row in range(rows + 2):
        for frame in range(4):
            ref, index = at(row, frame)
            which, number = edge_lane(row, frame, rows, True)
            plane = act(ref[index])
            column = edges[which][:, number : number + 1]
            factor = None
            if frame < 2:
                factor = has_past
            if row in (0, rows + 1):
                beside = has_top if row == 0 else has_bottom
                factor = beside if factor is None else factor * beside
            if factor is not None:
                plane = plane * factor
                column = column * factor
            fill_stack(stack_ref, row, frame, plane.astype(BF16), column, on_left, on_right)
    for row in range(rows):
        out = conv_rows(stack_ref, weight, row)
        for frame in range(frames):
            hidden_ref[row, frame] = out[frame * channels : (frame + 1) * channels]
    planes = [
        functools.partial(lambda r, t: hidden_ref[r, t], r, t) for r in range(rows) for t in range(frames)
    ]
    st_out[...] = local_stats(planes, float(GROUP * rows * frames * cols))


def fill_future(stack, flag_ref, own, future, near, far, edge_ref, rim_ref):
    rows = own.shape[0]
    at = source(own, future, near, far, False)
    on_left, on_right = sides(flag_ref)
    edges = (edge_ref[...], rim_ref[...])
    for row in range(rows + 2):
        for frame in range(4):
            ref, index = at(row, frame)
            which, number = edge_lane(row, frame, rows, False)
            fill_stack(stack, row, frame, ref[index], edges[which][:, number : number + 1], on_left, on_right)


def conv_back_kernel(flag_ref, own, future, near, far, edge_ref, rim_ref, weight, grad_ref, stack_ref):
    rows, frames, channels, cols = own.shape
    fill_future(stack_ref, flag_ref, own, future, near, far, edge_ref, rim_ref)
    for row in range(rows):
        out = conv_rows(stack_ref, weight, row)
        for frame in range(frames):
            grad_ref[row, frame] = out[frame * channels : (frame + 1) * channels]


def norm_second_kernel(hidden, grad, par_ref, st_ref, act_ref, scaled_ref, sums_ref, *, count):
    rows, frames, channels, cols = hidden.shape
    mean, inverse, gain, shift, _ = norm_columns(par_ref, st_ref, count, 3)
    first = jnp.zeros((channels, 128), F32)
    second = jnp.zeros((channels, 128), F32)
    for row in range(rows):
        for frame in range(frames):
            normed = (hidden[row, frame] - mean) * inverse
            pre = normed * gain + shift
            sig = sigmoid(pre)
            act = pre * sig
            act_ref[row, frame] = act.astype(BF16)
            scaled = grad[row, frame] * (sig + act * (1.0 - sig)) * gain
            scaled_ref[row, frame] = scaled
            first = first + lanes_of(scaled)
            second = second + lanes_of(scaled * normed)
    sums_ref[...] = as_rows(group_sums(first), group_sums(second))


def hidden_grad_kernel(hidden, scaled, par_ref, st_ref, sums_ref, out_ref, *, count):
    rows, frames, channels, cols = hidden.shape
    mean, inverse, _, _, _ = norm_columns(par_ref, st_ref, count, 3)
    means = sums_ref[...] / count
    first, second = columns_of(means[0:1], means[1:2])[:2]
    for row in range(rows):
        for frame in range(frames):
            normed = (hidden[row, frame] - mean) * inverse
            out_ref[row, frame] = (inverse * (scaled[row, frame] - first - normed * second)).astype(BF16)


def put_halves(flag_ref, mine_ref, theirs_ref, tap, block):
    channels = block.shape[0]
    here = slice(tap * channels, (tap + 1) * channels)
    upper, lower = block[: channels // 2], block[channels // 2 :]
    is_first = flag_ref[3] == 0
    mine_ref[:, here] = jnp.where(is_first, upper, lower)
    theirs_ref[:, here] = jnp.where(is_first, lower, upper)


def add_kernel(mine_ref, other_ref, after, *outs):
    start = 0
    for out in outs:
        end = start + out.shape[0]
        out[...] = mine_ref[start:end] + other_ref[start:end]
        start = end


def join_kernel(flag_ref, *refs):
    out_ref = refs[-1]
    pieces = len(refs[:-1]) // 2
    mine, theirs = refs[:pieces], refs[pieces : 2 * pieces]
    is_first = flag_ref[3] == 0
    half = out_ref.shape[0] // 2
    start = 0
    for a, b in zip(mine, theirs):
        end = start + a.shape[0]
        out_ref[start:end] = jnp.where(is_first, a[...], b[...])
        out_ref[half + start : half + end] = jnp.where(is_first, b[...], a[...])
        start = end


def weight_second_kernel(flag_ref, stack_ref, act_ref, mine_ref, theirs_ref, right_ref):
    rows, frames, channels, cols = act_ref.shape
    for row in range(rows):
        right_ref[row * cols : (row + 1) * cols] = jnp.transpose(
            act_ref[row].reshape(frames * channels, cols)
        )
    right = right_ref[...]
    for down in range(3):
        parts = []
        for frame in range(4):
            left = jnp.concatenate([stack_ref[down + row, frame] for row in range(rows)], axis=1)
            parts.append(jnp.dot(left, right, preferred_element_type=F32))
        for kt in range(3):
            term = parts[2 - kt][:, :channels] + parts[3 - kt][:, channels:]
            for across in range(3):
                tap = 9 * kt + 3 * (2 - down) + (2 - across)
                put_halves(flag_ref, mine_ref, theirs_ref, tap, term[across * channels : (across + 1) * channels])


def weight_first_kernel(flag_ref, stack_ref, grad_ref, mine_ref, theirs_ref, right_ref):
    rows, frames, channels, cols = grad_ref.shape
    for row in range(rows):
        right_ref[row * cols : (row + 1) * cols] = jnp.transpose(
            grad_ref[row].reshape(frames * channels, cols)
        )
    right = right_ref[...]
    for down in range(3):
        parts = []
        for frame in range(4):
            left = jnp.concatenate([stack_ref[down + row, frame] for row in range(rows)], axis=1)
            parts.append(jnp.dot(left, right, preferred_element_type=F32))
        for kt in range(3):
            term = parts[kt][:, :channels] + parts[kt + 1][:, channels:]
            for across in range(3):
                tap = 9 * kt + 3 * down + across
                block = jnp.transpose(term[across * channels : (across + 1) * channels])
                put_halves(flag_ref, mine_ref, theirs_ref, tap, block)


def first_grad_kernel(
    flag_ref, own, future, near, far, edge_ref, rim_ref, weight, latent, par_ref, st_ref, scaled_ref, sums_ref,
    stack_ref, *, count
):
    rows, frames, channels, cols = own.shape
    mean, inverse, gain, shift, scale = norm_columns(par_ref, st_ref, count, 1)
    fill_future(stack_ref, flag_ref, own, future, near, far, edge_ref, rim_ref)
    first = jnp.zeros((channels, 128), F32)
    second = jnp.zeros((channels, 128), F32)
    for row in range(rows):
        out = conv_rows(stack_ref, weight, row)
        for frame in range(frames):
            grad = out[frame * channels : (frame + 1) * channels]
            normed = (latent[row, frame].astype(F32) * scale - mean) * inverse
            pre = normed * gain + shift
            sig = sigmoid(pre)
            scaled = grad * (sig + pre * sig * (1.0 - sig)) * gain
            scaled_ref[row, frame] = scaled
            first = first + lanes_of(scaled)
            second = second + lanes_of(scaled * normed)
    sums_ref[...] = as_rows(group_sums(first), group_sums(second))


def decoded_grad_kernel(scaled, latent, cotangent, par_ref, st_ref, sums_ref, out_ref, *, count):
    rows, frames, channels, cols = latent.shape
    mean, inverse, _, _, scale = norm_columns(par_ref, st_ref, count, 1)
    means = sums_ref[...] / count
    first, second = columns_of(means[0:1], means[1:2])[:2]
    for row in range(rows):
        for frame in range(frames):
            normed = (latent[row, frame].astype(F32) * scale - mean) * inverse
            out_ref[row, frame] = cotangent[row, frame].astype(F32) + inverse * (
                scaled[row, frame] - first - normed * second
            )


def weight_forward_kernel(weight, out_ref):
    channels = weight.shape[0]
    wide = 3 * channels
    for t in range(2):
        for kr in range(3):
            for f in range(4):
                kt = f - t
                here = slice((kr * 4 + f) * wide, (kr * 4 + f + 1) * wide)
                if 0 <= kt < 3:
                    tap = 3 * kt + kr
                    block = weight[:, tap * wide : (tap + 1) * wide]
                else:
                    block = jnp.zeros((channels, wide), BF16)
                out_ref[t * channels : (t + 1) * channels, here] = block


def weight_back_kernel(weight, out_ref):
    channels = weight.shape[0]
    for down in range(3):
        for across in range(3):
            blocks = [
                jnp.transpose(
                    weight[
                        :,
                        (9 * kt + 3 * (2 - down) + 2 - across) * channels : (9 * kt + 3 * (2 - down) + 3 - across)
                        * channels,
                    ]
                )
                for kt in range(3)
            ]
            for t in range(2):
                for f in range(4):
                    kt = t + 2 - f
                    start = ((down * 4 + f) * 3 + across) * channels
                    block = blocks[kt] if 0 <= kt < 3 else jnp.zeros((channels, channels), BF16)
                    out_ref[t * channels : (t + 1) * channels, start : start + channels] = block


def shifted(value, axis, steps):
    count = lax.axis_size(axis)
    initial, last = max(0, -steps), min(count, count - steps)
    return lax.ppermute(value, axis, [(source, source + steps) for source in range(initial, last)])


def rounds(radix=2):
    for axis in ("width", "height", "tm"):
        count = lax.axis_size(axis)
        step = 1
        while step < count:
            wide = radix if step * radix <= count else 2
            yield axis, [[(i, i ^ (step * k)) for i in range(count)] for k in range(1, wide)]
            step *= wide


def all_sum(value, radix=2):
    for axis, exchanges in rounds(radix):
        parts = [value] + [lax.ppermute(value, axis, pairs) for pairs in exchanges]
        while len(parts) > 1:
            parts = [a + b for a, b in zip(parts[::2], parts[1::2])]
        (value,) = parts
    return value


def gathered_sum(value):
    return jnp.sum(lax.all_gather(value, ("tm", "height", "width")), axis=0)


def all_stats(value, count, radix=2):
    for axis, exchanges in rounds(radix):
        parts = [value] + [lax.ppermute(value, axis, pairs) for pairs in exchanges]
        while len(parts) > 1:
            joined = []
            for a, b in zip(parts[::2], parts[1::2]):
                gap = a[0:1] - b[0:1]
                mean = 0.5 * (a[0:1] + b[0:1])
                joined.append(jnp.concatenate([mean, a[1:2] + b[1:2] + gap * gap * (0.5 * count)], axis=0))
            parts = joined
            count = 2.0 * count
        (value,) = parts
    return value


def swapped(value):
    return lax.ppermute(value, "width", [(0, 1), (1, 0)])


def reduce_weights(flags, mine, theirs, pieces, axes, after_first, after_sum):
    other = swapped(theirs)
    half, cols = mine.shape
    parts = call(
        add_kernel,
        [shape((half // pieces, cols), F32)] * pieces,
        [VMEM, VMEM, ANY],
        (mine, other, after_first),
    )
    parts = lax.psum(tuple(parts), axes)
    parts, _ = lax.optimization_barrier((parts, after_sum))
    others = [swapped(part) for part in parts]
    (total,) = call(
        join_kernel, [shape((2 * half, cols), F32)], [SMEM] + [VMEM] * (2 * pieces), (flags, *parts, *others)
    )
    return total


def row_exchange(block):
    return jnp.stack([shifted(block[-1], "height", 1), shifted(block[0], "height", -1)])


def edges(flags, first, second):
    channels = first.shape[2]
    (columns,) = call(edges_kernel, [shape((channels, 128), BF16)], [SMEM, VMEM, VMEM], (flags, first, second))
    return columns


def extended(flags, own, steps):
    other = shifted(own, "tm", steps)
    near = row_exchange(own)
    far = row_exchange(other)
    edge = swapped(edges(flags, own, other))
    rim = edges(flags, near, far)
    return (other, near, far, edge, swapped(rim)), rim


def shards(
    latent,
    exponents,
    cotangent,
    conv_first,
    conv_second,
    gain_first,
    shift_first,
    gain_second,
    shift_second,
):
    channels, frames, rows, cols = latent.shape
    groups = exponents.shape[0]
    devices = lax.axis_size("tm") * lax.axis_size("height") * lax.axis_size("width")
    here = channels // groups * frames * rows * cols
    count = float(here * devices)
    tm, height, width = (lax.axis_index(axis) for axis in ("tm", "height", "width"))
    flags = jnp.stack(
        [
            (tm > 0).astype(jnp.int32),
            (height > 0).astype(jnp.int32),
            (height < lax.axis_size("height") - 1).astype(jnp.int32),
            width.astype(jnp.int32),
        ]
    )
    scale = jnp.repeat(jnp.exp2(exponents.astype(F32)), channels // groups)
    zeros = jnp.zeros_like(scale)
    par = jnp.stack([scale, gain_first, shift_first, gain_second, shift_second, zeros, zeros, zeros])
    latent = latent.transpose(2, 1, 0, 3)
    cotangent = cotangent.transpose(2, 1, 0, 3)
    block = (rows, frames, channels, cols)
    stack = (rows + 2, 4, 3 * channels, cols)
    taps = (2 * channels, 36 * channels)
    halves = [shape((channels // 2, 27 * channels), F32)] * 2
    conv_flops = 2 * 4 * 256 * 36 * channels * 2 * channels
    small = shape((2, channels), F32)

    (stats_first,) = call(stats_kernel, [small], [VMEM] * 2, (latent, par))
    around, _ = extended(flags, latent, 1)
    around_c, ready_c = extended(flags, cotangent, -1)
    stats_first = all_stats(stats_first, float(here))
    (weight_first,) = call(weight_forward_kernel, [shape(taps, BF16)], [VMEM], (conv_first,))
    (weight_second_t,) = call(weight_back_kernel, [shape(taps, BF16)], [VMEM], (conv_second,))
    (weight_first_t,) = call(weight_back_kernel, [shape(taps, BF16)], [VMEM], (conv_first,))

    hidden, stats_second, stack_first = call(
        functools.partial(conv_first_kernel, count=count),
        [shape(block, F32), small, shape(stack, BF16)],
        [SMEM] + [VMEM] * 9 + [ANY],
        (flags, latent, *around, par, stats_first, weight_first, ready_c),
        flops=conv_flops,
        transcendentals=3 * latent.size,
    )
    stats_second = all_stats(stats_second, float(here), 4)
    grad_second, stack_c = call(
        conv_back_kernel,
        [shape(block, F32), shape(stack, BF16)],
        [SMEM] + [VMEM] * 7,
        (flags, cotangent, *around_c, weight_second_t),
        flops=conv_flops,
    )
    act_second, scaled, sums = call(
        functools.partial(norm_second_kernel, count=count),
        [shape(block, BF16), shape(block, F32), small],
        [VMEM] * 4,
        (hidden, grad_second, par, stats_second),
        transcendentals=latent.size,
    )
    sums = gathered_sum(sums)
    halves_second = call(
        weight_second_kernel,
        halves,
        [SMEM] + [VMEM] * 2,
        (flags, stack_c, act_second),
        scratch=[pltpu.VMEM((rows * cols, frames * channels), BF16)],
        flops=conv_flops,
    )
    (hidden_grad,) = call(
        functools.partial(hidden_grad_kernel, count=count),
        [shape(block, BF16)],
        [VMEM] * 5,
        (hidden, scaled, par, stats_second, sums),
    )
    around, _ = extended(flags, hidden_grad, -1)
    halves_first = call(
        weight_first_kernel,
        halves,
        [SMEM] + [VMEM] * 2,
        (flags, stack_first, hidden_grad),
        scratch=[pltpu.VMEM((rows * cols, frames * channels), BF16)],
        flops=conv_flops,
    )
    scaled, sums_first = call(
        functools.partial(first_grad_kernel, count=count),
        [shape(block, F32), small],
        [SMEM] + [VMEM] * 10,
        (flags, hidden_grad, *around, weight_first_t, latent, par, stats_first),
        scratch=[pltpu.VMEM(stack, BF16)],
        flops=conv_flops,
        transcendentals=latent.size,
    )
    sums_first = all_sum(sums_first)
    conv_second_grad = reduce_weights(flags, *halves_second, 2, ("height", "tm"), sums, sums_first)
    conv_first_grad = reduce_weights(flags, *halves_first, 4, ("tm", "height"), hidden_grad, sums_first)
    (decoded_grad,) = call(
        functools.partial(decoded_grad_kernel, count=count),
        [shape(block, F32)],
        [VMEM] * 6,
        (scaled, latent, cotangent, par, stats_first, sums_first),
    )
    return decoded_grad.transpose(2, 1, 0, 3), conv_first_grad, conv_second_grad


def solution(mesh):
    block = P(None, "tm", "height", "width")
    return jax.shard_map(
        shards,
        mesh=mesh,
        in_specs=(block, P(), block, P(), P(), P(), P(), P(), P()),
        out_specs=(block, P(), P()),
        check_vma=False,
    )
```

```python
import functools

import jax
import jax.numpy as jnp
from jax import lax
from jax.experimental import pallas as pl
from jax.experimental.pallas import tpu as pltpu
from jax.sharding import PartitionSpec as P

epsilon = 1e-05
F32 = jnp.float32
BF16 = jnp.bfloat16
GROUP = 4
TAPS, SLOTS = 27, 32
FULL = 32760.0
LN2 = 0.6931471805599453
VMEM = pl.BlockSpec(memory_space=pltpu.VMEM)
SMEM = pl.BlockSpec(memory_space=pltpu.SMEM)
ANY = pl.BlockSpec(memory_space=pl.ANY)


def call(body, outs, specs, args, scratch=(), flops=0, transcendentals=0, limit=48):
    moved = sum(a.size * a.dtype.itemsize for a in args)
    moved += sum(o.size * o.dtype.itemsize for o in outs)
    return pl.pallas_call(
        body,
        out_shape=tuple(outs),
        in_specs=specs,
        out_specs=tuple(VMEM for _ in outs),
        scratch_shapes=scratch,
        compiler_params=pltpu.CompilerParams(vmem_limit_bytes=limit << 20),
        cost_estimate=pl.CostEstimate(
            flops=flops, bytes_accessed=moved, transcendentals=transcendentals
        ),
    )(*args)


def shape(dims, dtype):
    return jax.ShapeDtypeStruct(dims, dtype)


def group_sums(acc):
    rows = acc.shape[0]
    row = lax.broadcasted_iota(jnp.int32, acc.shape, 0)
    step = 1
    while step < GROUP:
        up = pltpu.roll(acc, rows - step, axis=0)
        down = pltpu.roll(acc, step, axis=0)
        acc = acc + jnp.where((row & step) == 0, up, down)
        step *= 2
    return jnp.sum(acc, axis=1, keepdims=True)


def lanes_of(plane):
    total = plane[:, :128]
    for start in range(128, plane.shape[1], 128):
        total = total + plane[:, start : start + 128]
    return total


def as_rows(first, second):
    channels = first.shape[0]
    lane = lax.broadcasted_iota(jnp.int32, (channels, 128), 1)
    both = jnp.where(lane == 0, first, jnp.where(lane == 1, second, 0.0))
    return jnp.transpose(both)[:2]


def local_stats(planes, count):
    acc = None
    for plane in planes:
        part = lanes_of(plane())
        acc = part if acc is None else acc + part
    mean = group_sums(acc) / count
    acc = None
    for plane in planes:
        off = plane() - mean
        part = lanes_of(off * off)
        acc = part if acc is None else acc + part
    return as_rows(mean, group_sums(acc))


def columns_of(*rows):
    rows = list(rows) + [jnp.zeros_like(rows[0])] * (8 - len(rows))
    cols = jnp.transpose(jnp.concatenate(rows, axis=0))
    return [cols[:, i : i + 1] for i in range(8)]


def sigmoid(value):
    return 0.5 + 0.5 * jnp.tanh(0.5 * value)


def planes_kernel(natural_ref, *refs):
    out_ref = refs[-1] if len(refs) == 2 else refs[-2]
    _, frames, rows, cols = natural_ref.shape
    for row in range(rows):
        for frame in range(frames):
            out_ref[row, frame] = natural_ref[:, frame, row, :]
    if len(refs) == 2:
        return
    scale = columns_of(refs[0][0:1])[0]
    planes = [
        functools.partial(lambda r, t: out_ref[r, t].astype(F32) * scale, r, t)
        for r in range(rows)
        for t in range(frames)
    ]
    refs[-1][...] = local_stats(planes, float(GROUP * rows * frames * cols))


def source(own, other, near, far, other_first):
    def at(row, frame):
        is_other = (frame < 2) == other_first
        if row == 0 or row == own.shape[0] + 1:
            return (far if is_other else near)[0 if row == 0 else 1], (0, frame % 2)
        return (other if is_other else own), (row - 1, frame % 2)

    return at


def edges_kernel(flag_ref, *refs):
    planes, out_ref = refs[:-1], refs[-1]
    is_first = flag_ref[3] == 0
    channels = planes[0].shape[2]
    lane = lax.broadcasted_iota(jnp.int32, (channels, 128), 1)
    acc = jnp.zeros((channels, 128), F32)
    number = 0
    for ref in planes:
        for row in range(ref.shape[0]):
            for frame in range(ref.shape[1]):
                last = pltpu.roll(ref[row, frame, :, -128:].astype(F32), 1, axis=1)
                edge = jnp.where(is_first, last, ref[row, frame, :, :128].astype(F32))
                moved = pltpu.roll(edge, number, axis=1) if number else edge
                acc = jnp.where(lane == number, moved, acc)
                number += 1
    out_ref[...] = acc.astype(BF16)


def edge_lane(row, frame, rows, other_first):
    is_other = int((frame < 2) == other_first)
    if row == 0 or row == rows + 1:
        return 1, 4 * is_other + 2 * int(row > 0) + frame % 2
    return 0, 2 * rows * is_other + 2 * (row - 1) + frame % 2


def fill_stack(stack, row, frame, plane, column, on_left, on_right):
    channels, cols = plane.shape
    lane = lax.broadcasted_iota(jnp.int32, (channels, cols), 1)
    column = column.astype(F32)
    left = jnp.where(lane == 0, (column * on_left).astype(BF16), pltpu.roll(plane, 1, axis=1))
    right = jnp.where(lane == cols - 1, (column * on_right).astype(BF16), pltpu.roll(plane, cols - 1, axis=1))
    stack[row, frame, 0:channels] = left
    stack[row, frame, channels : 2 * channels] = plane
    stack[row, frame, 2 * channels : 3 * channels] = right


def sides(flag_ref):
    on_left = (flag_ref[3] != 0).astype(F32)
    on_right = (flag_ref[3] == 0).astype(F32)
    return on_left, on_right


def conv_rows(stack, weight, row):
    three = stack[row : row + 3].reshape(weight.shape[1], stack.shape[3])
    return jnp.dot(weight[...], three, preferred_element_type=F32)


def norm_columns(par_ref, st_ref, count, gain_row):
    par = par_ref[...]
    stats = st_ref[...]
    mean = stats[0:1]
    inverse = 1.0 / jnp.sqrt(stats[1:2] / count + epsilon)
    gain = par[gain_row : gain_row + 1]
    shift = par[gain_row + 1 : gain_row + 2]
    return columns_of(mean, inverse, gain, shift, par[0:1])[:5]


def conv_first_kernel(
    flag_ref, own, past, above, below, far_above, far_below, edge_ref, rim_ref, par_ref, st_ref, weight, hidden_ref, st_out, stack_ref,
    *, count
):
    rows, frames, channels, cols = own.shape
    at = source(own, past, (above, below), (far_above, far_below), True)
    mean, inverse, gain, shift, scale = norm_columns(par_ref, st_ref, count, 1)

    def act(latent):
        pre = (latent.astype(F32) * scale - mean) * inverse * gain + shift
        return pre * sigmoid(pre)

    has_past = flag_ref[0].astype(F32)
    has_top = flag_ref[1].astype(F32)
    has_bottom = flag_ref[2].astype(F32)
    on_left, on_right = sides(flag_ref)
    edges = (act(edge_ref[...]), act(rim_ref[...]))
    for row in range(rows + 2):
        for frame in range(4):
            ref, index = at(row, frame)
            which, number = edge_lane(row, frame, rows, True)
            plane = act(ref[index])
            column = edges[which][:, number : number + 1]
            factor = None
            if frame < 2:
                factor = has_past
            if row in (0, rows + 1):
                beside = has_top if row == 0 else has_bottom
                factor = beside if factor is None else factor * beside
            if factor is not None:
                plane = plane * factor
                column = column * factor
            fill_stack(stack_ref, row, frame, plane.astype(BF16), column, on_left, on_right)
    for row in range(rows):
        out = conv_rows(stack_ref, weight, row)
        for frame in range(frames):
            hidden_ref[row, frame] = out[frame * channels : (frame + 1) * channels]
    planes = [
        functools.partial(lambda r, t: hidden_ref[r, t], r, t) for r in range(rows) for t in range(frames)
    ]
    st_out[...] = local_stats(planes, float(GROUP * rows * frames * cols))


def fill_future(stack, flag_ref, own, future, above, below, far_above, far_below, edge_ref, rim_ref):
    rows = own.shape[0]
    at = source(own, future, (above, below), (far_above, far_below), False)
    on_left, on_right = sides(flag_ref)
    edges = (edge_ref[...], rim_ref[...])
    for row in range(rows + 2):
        for frame in range(4):
            ref, index = at(row, frame)
            which, number = edge_lane(row, frame, rows, False)
            fill_stack(stack, row, frame, ref[index], edges[which][:, number : number + 1], on_left, on_right)


def conv_back_kernel(flag_ref, *refs):
    weight, grad_ref, stack_ref = refs[-3:]
    rows, frames, channels, _ = grad_ref.shape
    fill_future(stack_ref, flag_ref, *refs[:-3])
    for row in range(rows):
        out = conv_rows(stack_ref, weight, row)
        for frame in range(frames):
            grad_ref[row, frame] = out[frame * channels : (frame + 1) * channels]


def norm_second_kernel(hidden, grad, par_ref, st_ref, act_ref, scaled_ref, sums_ref, *, count):
    rows, frames, channels, cols = hidden.shape
    mean, inverse, gain, shift, _ = norm_columns(par_ref, st_ref, count, 3)
    first = jnp.zeros((channels, 128), F32)
    second = jnp.zeros((channels, 128), F32)
    for row in range(rows):
        for frame in range(frames):
            normed = (hidden[row, frame] - mean) * inverse
            pre = normed * gain + shift
            sig = sigmoid(pre)
            act = pre * sig
            act_ref[row, frame] = act.astype(BF16)
            scaled = grad[row, frame] * (sig + act * (1.0 - sig)) * gain
            scaled_ref[row, frame] = scaled
            first = first + lanes_of(scaled)
            second = second + lanes_of(scaled * normed)
    sums_ref[...] = as_rows(group_sums(first), group_sums(second))


def hidden_grad_kernel(hidden, scaled, par_ref, st_ref, sums_ref, out_ref, *, count):
    rows, frames, channels, cols = hidden.shape
    mean, inverse, _, _, _ = norm_columns(par_ref, st_ref, count, 3)
    means = sums_ref[...] / count
    first, second = columns_of(means[0:1], means[1:2])[:2]
    for row in range(rows):
        for frame in range(frames):
            normed = (hidden[row, frame] - mean) * inverse
            out_ref[row, frame] = (inverse * (scaled[row, frame] - first - normed * second)).astype(BF16)


def put_halves(flag_ref, mine_ref, theirs_ref, tap, block):
    half = block.shape[0] // 2
    here = pl.ds(tap, half, stride=SLOTS)
    upper, lower = block[:half], block[half:]
    is_first = flag_ref[3] == 0
    mine_ref[here, :] = jnp.where(is_first, upper, lower)
    theirs_ref[here, :] = jnp.where(is_first, lower, upper)


def encoded(value):
    slot = lax.broadcasted_iota(jnp.int32, value.shape, 1)
    value = jnp.where(slot < TAPS, value, 0.0)
    top = jnp.max(jnp.abs(value), axis=1, keepdims=True)
    power = jnp.ceil(jnp.log(jnp.maximum(top, 1e-30)) * (1.0 / LN2))
    number = jnp.round(value * (FULL * jnp.exp(power * -LN2)))
    return jnp.where(slot < TAPS, number, power).astype(jnp.int32).astype(jnp.int16)


def decoded_value(number):
    number = number.astype(jnp.int32).astype(F32)
    return number * (jnp.exp(number[:, SLOTS - 1 : SLOTS] * LN2) * (1.0 / FULL))


def first_scatter_kernel(mine_ref, other_ref, out_ref):
    out_ref[...] = encoded(mine_ref[...] + other_ref[...])


def scatter_kernel(received, out_ref, *, copies):
    total = decoded_value(received[0])
    for number in range(1, received.shape[0]):
        total = total + decoded_value(received[number])
    total = encoded(total)
    if copies:
        for number in range(copies):
            out_ref[number] = total
    else:
        out_ref[...] = total


def join_kernel(flag_ref, mine_ref, theirs_ref, after, out_ref, first_ref, second_ref):
    half, _, channels = mine_ref.shape
    is_first = flag_ref[3] == 0
    first_ref[...] = decoded_value(jnp.where(is_first, mine_ref[...], theirs_ref[...])).reshape(first_ref.shape)
    second_ref[...] = decoded_value(jnp.where(is_first, theirs_ref[...], mine_ref[...])).reshape(second_ref.shape)
    for tap in range(TAPS):
        here = slice(tap * channels, (tap + 1) * channels)
        out_ref[:half, here] = first_ref[pl.ds(tap, half, stride=SLOTS), :]
        out_ref[half:, here] = second_ref[pl.ds(tap, half, stride=SLOTS), :]


def weight_second_kernel(flag_ref, stack_ref, act_ref, after, mine_ref, theirs_ref, right_ref):
    rows, frames, channels, cols = act_ref.shape
    for row in range(rows):
        right_ref[row * cols : (row + 1) * cols] = jnp.transpose(
            act_ref[row].reshape(frames * channels, cols)
        )
    right = right_ref[...]
    for down in range(3):
        parts = []
        for frame in range(4):
            left = jnp.concatenate([stack_ref[down + row, frame] for row in range(rows)], axis=1)
            parts.append(jnp.dot(left, right, preferred_element_type=F32))
        for kt in range(3):
            term = parts[2 - kt][:, :channels] + parts[3 - kt][:, channels:]
            for across in range(3):
                tap = 9 * kt + 3 * (2 - down) + (2 - across)
                put_halves(flag_ref, mine_ref, theirs_ref, tap, term[across * channels : (across + 1) * channels])


def weight_first_kernel(flag_ref, stack_ref, grad_ref, after, mine_ref, theirs_ref, right_ref):
    rows, frames, channels, cols = grad_ref.shape
    for row in range(rows):
        right_ref[row * cols : (row + 1) * cols] = jnp.transpose(
            grad_ref[row].reshape(frames * channels, cols)
        )
    right = right_ref[...]
    for down in range(3):
        parts = []
        for frame in range(4):
            left = jnp.concatenate([stack_ref[down + row, frame] for row in range(rows)], axis=1)
            parts.append(jnp.dot(left, right, preferred_element_type=F32))
        for kt in range(3):
            term = parts[kt][:, :channels] + parts[kt + 1][:, channels:]
            for across in range(3):
                tap = 9 * kt + 3 * down + across
                block = jnp.transpose(term[across * channels : (across + 1) * channels])
                put_halves(flag_ref, mine_ref, theirs_ref, tap, block)


def first_grad_kernel(flag_ref, *refs, count):
    weight, latent, par_ref, st_ref, scaled_ref, sums_ref, stack_ref = refs[-7:]
    rows, frames, channels, cols = latent.shape
    mean, inverse, gain, shift, scale = norm_columns(par_ref, st_ref, count, 1)
    fill_future(stack_ref, flag_ref, *refs[:-7])
    first = jnp.zeros((channels, 128), F32)
    second = jnp.zeros((channels, 128), F32)
    for row in range(rows):
        out = conv_rows(stack_ref, weight, row)
        for frame in range(frames):
            grad = out[frame * channels : (frame + 1) * channels]
            normed = (latent[row, frame].astype(F32) * scale - mean) * inverse
            pre = normed * gain + shift
            sig = sigmoid(pre)
            scaled = grad * (sig + pre * sig * (1.0 - sig)) * gain
            scaled_ref[row, frame] = scaled
            first = first + lanes_of(scaled)
            second = second + lanes_of(scaled * normed)
    sums_ref[...] = as_rows(group_sums(first), group_sums(second))


def decoded_grad_kernel(scaled, latent, cotangent, par_ref, st_ref, sums_ref, out_ref, *, count):
    rows, frames, channels, cols = latent.shape
    mean, inverse, _, _, scale = norm_columns(par_ref, st_ref, count, 1)
    means = sums_ref[...] / count
    first, second = columns_of(means[0:1], means[1:2])[:2]
    for row in range(rows):
        for frame in range(frames):
            normed = (latent[row, frame].astype(F32) * scale - mean) * inverse
            out_ref[:, frame, row, :] = cotangent[row, frame].astype(F32) + inverse * (
                scaled[row, frame] - first - normed * second
            )


def weight_forward_kernel(weight, out_ref):
    channels = weight.shape[0]
    wide = 3 * channels
    for t in range(2):
        for kr in range(3):
            for f in range(4):
                kt = f - t
                here = slice((kr * 4 + f) * wide, (kr * 4 + f + 1) * wide)
                if 0 <= kt < 3:
                    tap = 3 * kt + kr
                    block = weight[:, tap * wide : (tap + 1) * wide]
                else:
                    block = jnp.zeros((channels, wide), BF16)
                out_ref[t * channels : (t + 1) * channels, here] = block


def weight_back_kernel(weight, out_ref):
    channels = weight.shape[0]
    for down in range(3):
        for across in range(3):
            blocks = [
                jnp.transpose(
                    weight[
                        :,
                        (9 * kt + 3 * (2 - down) + 2 - across) * channels : (9 * kt + 3 * (2 - down) + 3 - across)
                        * channels,
                    ]
                )
                for kt in range(3)
            ]
            for t in range(2):
                for f in range(4):
                    kt = t + 2 - f
                    start = ((down * 4 + f) * 3 + across) * channels
                    block = blocks[kt] if 0 <= kt < 3 else jnp.zeros((channels, channels), BF16)
                    out_ref[t * channels : (t + 1) * channels, start : start + channels] = block


def shifted(value, axis, steps):
    count = lax.axis_size(axis)
    initial, last = max(0, -steps), min(count, count - steps)
    return lax.ppermute(value, axis, [(source, source + steps) for source in range(initial, last)])


def rounds():
    for axis in ("tm", "height", "width"):
        count = lax.axis_size(axis)
        step = 1
        while step < count:
            wide = 4 if 4 * step <= count else 2
            yield axis, step, [[(i, i ^ (step * k)) for i in range(count)] for k in range(1, wide)]
            step *= wide


def all_sum(value):
    for axis, _, exchanges in rounds():
        parts = [value] + [lax.ppermute(value, axis, pairs) for pairs in exchanges]
        while len(parts) > 1:
            parts = [a + b for a, b in zip(parts[::2], parts[1::2])]
        (value,) = parts
    return value


def exchanged_sum(value):
    axes = ("tm", "height", "width")
    devices = lax.axis_size(axes)
    value = jnp.broadcast_to(value[None], (devices, *value.shape))
    return jnp.sum(lax.all_to_all(value, axes, 0, 0, tiled=True), axis=0)


def all_stats(value, count):
    for axis, _, exchanges in rounds():
        parts = [value] + [lax.ppermute(value, axis, pairs) for pairs in exchanges]
        while len(parts) > 1:
            joined = []
            for a, b in zip(parts[::2], parts[1::2]):
                gap = a[0:1] - b[0:1]
                mean = 0.5 * (a[0:1] + b[0:1])
                joined.append(jnp.concatenate([mean, a[1:2] + b[1:2] + gap * gap * (0.5 * count)], axis=0))
            parts = joined
            count = 2.0 * count
        (value,) = parts
    return value


def swapped(value):
    return lax.ppermute(value, "width", [(0, 1), (1, 0)])


def exchanged(value, axis):
    return lax.all_to_all(value, axis, 0, 0, tiled=True)


def reduce_weights(flags, mine, theirs, after):
    half, _, channels = mine.shape
    by_height, by_tm = lax.axis_size("height"), lax.axis_size("tm")
    coded = functools.partial(lambda *dims: shape((*dims, SLOTS, channels), jnp.int16))
    (value,) = call(first_scatter_kernel, [coded(half)], [VMEM] * 2, (mine, swapped(theirs)))
    value = exchanged(value, "height")
    rows = half // by_height
    (value,) = call(
        functools.partial(scatter_kernel, copies=0),
        [coded(rows)],
        [VMEM],
        (value.reshape(by_height, rows, SLOTS, channels),),
    )
    value = exchanged(value, "tm")
    rows = rows // by_tm
    (value,) = call(
        functools.partial(scatter_kernel, copies=by_tm),
        [coded(by_tm, rows)],
        [VMEM],
        (value.reshape(by_tm, rows, SLOTS, channels),),
    )
    value = exchanged(value, "tm").reshape(1, by_tm * rows, SLOTS, channels)
    value = exchanged(jnp.broadcast_to(value, (by_height, *value.shape[1:])), "height")
    value = value.reshape(half, SLOTS, channels)
    (total,) = call(
        join_kernel,
        [shape((2 * half, TAPS * channels), F32)],
        [SMEM] + [VMEM] * 2 + [ANY],
        (flags, value, swapped(value), after),
        scratch=[pltpu.VMEM((half * SLOTS, channels), F32)] * 2,
    )
    return total


def row_exchange(block):
    return shifted(block[-1:], "height", 1), shifted(block[:1], "height", -1)


def edges(flags, *planes):
    channels = planes[0].shape[2]
    (columns,) = call(
        edges_kernel, [shape((channels, 128), BF16)], [SMEM] + [VMEM] * len(planes), (flags, *planes)
    )
    return columns


def extended(flags, own, steps):
    other = shifted(own, "tm", steps)
    near = row_exchange(own)
    far = [shifted(row, "tm", steps) for row in near]
    edge = swapped(edges(flags, own, other))
    rim = swapped(edges(flags, *near, *far))
    return other, *near, *far, edge, rim


def shards(
    latent,
    exponents,
    cotangent,
    conv_first,
    conv_second,
    gain_first,
    shift_first,
    gain_second,
    shift_second,
):
    channels, frames, rows, cols = latent.shape
    groups = exponents.shape[0]
    devices = lax.axis_size("tm") * lax.axis_size("height") * lax.axis_size("width")
    here = channels // groups * frames * rows * cols
    count = float(here * devices)
    tm, height, width = (lax.axis_index(axis) for axis in ("tm", "height", "width"))
    flags = jnp.stack(
        [
            (tm > 0).astype(jnp.int32),
            (height > 0).astype(jnp.int32),
            (height < lax.axis_size("height") - 1).astype(jnp.int32),
            width.astype(jnp.int32),
        ]
    )
    scale = jnp.repeat(jnp.exp2(exponents.astype(F32)), channels // groups)
    zeros = jnp.zeros_like(scale)
    par = jnp.stack([scale, gain_first, shift_first, gain_second, shift_second, zeros, zeros, zeros])
    block = (rows, frames, channels, cols)
    stack = (rows + 2, 4, 3 * channels, cols)
    taps = (2 * channels, 36 * channels)
    halves = [shape((channels // 2 * SLOTS, channels), F32)] * 2
    conv_flops = 2 * 4 * 256 * 36 * channels * 2 * channels
    small = shape((2, channels), F32)

    latent, stats_first = call(
        planes_kernel, [shape(block, BF16), small], [VMEM] * 2, (latent, par)
    )
    around = extended(flags, latent, 1)
    (cotangent,) = call(planes_kernel, [shape(block, BF16)], [VMEM, ANY], (cotangent, around[0]))
    around_c = extended(flags, cotangent, -1)
    stats_first = all_stats(stats_first, float(here))
    (weight_first,) = call(weight_forward_kernel, [shape(taps, BF16)], [VMEM], (conv_first,))
    (weight_second_t,) = call(weight_back_kernel, [shape(taps, BF16)], [VMEM], (conv_second,))
    (weight_first_t,) = call(weight_back_kernel, [shape(taps, BF16)], [VMEM], (conv_first,))

    hidden, stats_second, stack_first = call(
        functools.partial(conv_first_kernel, count=count),
        [shape(block, F32), small, shape(stack, BF16)],
        [SMEM] + [VMEM] * 11,
        (flags, latent, *around, par, stats_first, weight_first),
        flops=conv_flops,
        transcendentals=3 * latent.size,
    )
    stats_second = all_stats(stats_second, float(here))
    grad_second, stack_c = call(
        conv_back_kernel,
        [shape(block, F32), shape(stack, BF16)],
        [SMEM] + [VMEM] * 9,
        (flags, cotangent, *around_c, weight_second_t),
        flops=conv_flops,
    )
    act_second, scaled, sums = call(
        functools.partial(norm_second_kernel, count=count),
        [shape(block, BF16), shape(block, F32), small],
        [VMEM] * 4,
        (hidden, grad_second, par, stats_second),
        transcendentals=latent.size,
    )
    sums = all_sum(sums)
    halves_second = call(
        weight_second_kernel,
        halves,
        [SMEM] + [VMEM] * 2 + [ANY],
        (flags, stack_c, act_second, act_second),
        scratch=[pltpu.VMEM((rows * cols, frames * channels), BF16)],
        flops=conv_flops,
    )
    (hidden_grad,) = call(
        functools.partial(hidden_grad_kernel, count=count),
        [shape(block, BF16)],
        [VMEM] * 5,
        (hidden, scaled, par, stats_second, sums),
    )
    around = extended(flags, hidden_grad, -1)
    halves_first = call(
        weight_first_kernel,
        halves,
        [SMEM] + [VMEM] * 2 + [ANY],
        (flags, stack_first, hidden_grad, around[1]),
        scratch=[pltpu.VMEM((rows * cols, frames * channels), BF16)],
        flops=conv_flops,
    )
    scaled, sums_first = call(
        functools.partial(first_grad_kernel, count=count),
        [shape(block, F32), small],
        [SMEM] + [VMEM] * 12,
        (flags, hidden_grad, *around, weight_first_t, latent, par, stats_first),
        scratch=[pltpu.VMEM(stack, BF16)],
        flops=conv_flops,
        transcendentals=latent.size,
    )
    sums_first = exchanged_sum(sums_first)
    halves_second, halves_first = (
        [v.reshape(channels // 2, SLOTS, channels) for v in halves] for halves in (halves_second, halves_first)
    )
    conv_second_grad = reduce_weights(flags, *halves_second, sums_first)
    conv_first_grad = reduce_weights(flags, *halves_first, sums_first)
    (decoded_grad,) = call(
        functools.partial(decoded_grad_kernel, count=count),
        [shape((channels, frames, rows, cols), F32)],
        [VMEM] * 6,
        (scaled, latent, cotangent, par, stats_first, sums_first),
    )
    return decoded_grad, conv_first_grad, conv_second_grad


def solution(mesh):
    block = P(None, "tm", "height", "width")
    return jax.shard_map(
        shards,
        mesh=mesh,
        in_specs=(block, P(), block, P(), P(), P(), P(), P(), P()),
        out_specs=(block, P(), P()),
        check_vma=False,
    )
```

```python
import functools

import jax
import jax.numpy as jnp
from jax import lax
from jax.experimental import pallas as pl
from jax.experimental.pallas import tpu as pltpu
from jax.sharding import PartitionSpec as P

epsilon = 1e-05
F32 = jnp.float32
BF16 = jnp.bfloat16
GROUP = 4
TAPS, SLOTS = 27, 32
FULL = 32760.0
LN2 = 0.6931471805599453
VMEM = pl.BlockSpec(memory_space=pltpu.VMEM)
SMEM = pl.BlockSpec(memory_space=pltpu.SMEM)
ANY = pl.BlockSpec(memory_space=pl.ANY)


def call(body, outs, specs, args, scratch=(), flops=0, transcendentals=0, limit=48):
    moved = sum(a.size * a.dtype.itemsize for a in args)
    moved += sum(o.size * o.dtype.itemsize for o in outs)
    return pl.pallas_call(
        body,
        out_shape=tuple(outs),
        in_specs=specs,
        out_specs=tuple(VMEM for _ in outs),
        scratch_shapes=scratch,
        compiler_params=pltpu.CompilerParams(vmem_limit_bytes=limit << 20),
        cost_estimate=pl.CostEstimate(
            flops=flops, bytes_accessed=moved, transcendentals=transcendentals
        ),
    )(*args)


def shape(dims, dtype):
    return jax.ShapeDtypeStruct(dims, dtype)


def group_sums(acc):
    rows = acc.shape[0]
    row = lax.broadcasted_iota(jnp.int32, acc.shape, 0)
    step = 1
    while step < GROUP:
        up = pltpu.roll(acc, rows - step, axis=0)
        down = pltpu.roll(acc, step, axis=0)
        acc = acc + jnp.where((row & step) == 0, up, down)
        step *= 2
    return jnp.sum(acc, axis=1, keepdims=True)


def lanes_of(plane):
    total = plane[:, :128]
    for start in range(128, plane.shape[1], 128):
        total = total + plane[:, start : start + 128]
    return total


def as_rows(first, second):
    channels = first.shape[0]
    lane = lax.broadcasted_iota(jnp.int32, (channels, 128), 1)
    both = jnp.where(lane == 0, first, jnp.where(lane == 1, second, 0.0))
    return jnp.transpose(both)[:2]


def local_stats(planes, count):
    acc = None
    for plane in planes:
        part = lanes_of(plane())
        acc = part if acc is None else acc + part
    mean = group_sums(acc) / count
    acc = None
    for plane in planes:
        off = plane() - mean
        part = lanes_of(off * off)
        acc = part if acc is None else acc + part
    return mean, group_sums(acc)


def put_rows(out_ref, first, second):
    out_ref[...] = jnp.broadcast_to(as_rows(first, second)[None], out_ref.shape)


def combined(st_ref, count):
    devices = st_ref.shape[0]
    mean = jnp.mean(st_ref[:, 0:1], axis=0)
    off = st_ref[:, 0:1] - mean[None]
    squares = jnp.sum(st_ref[:, 1:2] + off * off * (count / devices), axis=0)
    return mean, squares / count


def columns_of(*rows):
    rows = list(rows) + [jnp.zeros_like(rows[0])] * (8 - len(rows))
    cols = jnp.transpose(jnp.concatenate(rows, axis=0))
    return [cols[:, i : i + 1] for i in range(8)]


def sigmoid(value):
    return 0.5 + 0.5 * jnp.tanh(0.5 * value)


def planes_kernel(natural_ref, *refs):
    out_ref = refs[-1] if len(refs) == 1 else refs[-2]
    _, frames, rows, cols = natural_ref.shape
    for row in range(rows):
        for frame in range(frames):
            out_ref[row, frame] = natural_ref[:, frame, row, :]
    if len(refs) == 1:
        return
    scale = columns_of(refs[0][0:1])[0]
    planes = [
        functools.partial(lambda r, t: out_ref[r, t].astype(F32) * scale, r, t)
        for r in range(rows)
        for t in range(frames)
    ]
    put_rows(refs[-1], *local_stats(planes, float(GROUP * rows * frames * cols)))


def source(own, other, near, far, other_first):
    def at(row, frame):
        is_other = (frame < 2) == other_first
        if row == 0 or row == own.shape[0] + 1:
            return (far if is_other else near)[0 if row == 0 else 1], (0, frame % 2)
        return (other if is_other else own), (row - 1, frame % 2)

    return at


def edges_kernel(flag_ref, *refs):
    planes, out_ref = refs[:-1], refs[-1]
    is_first = flag_ref[3] == 0
    channels = planes[0].shape[2]
    lane = lax.broadcasted_iota(jnp.int32, (channels, 128), 1)
    acc = jnp.zeros((channels, 128), F32)
    number = 0
    for ref in planes:
        for row in range(ref.shape[0]):
            for frame in range(ref.shape[1]):
                last = pltpu.roll(ref[row, frame, :, -128:].astype(F32), 1, axis=1)
                edge = jnp.where(is_first, last, ref[row, frame, :, :128].astype(F32))
                moved = pltpu.roll(edge, number, axis=1) if number else edge
                acc = jnp.where(lane == number, moved, acc)
                number += 1
    out_ref[...] = acc.astype(BF16)


def edge_lane(row, frame, rows, other_first):
    is_other = int((frame < 2) == other_first)
    if row == 0 or row == rows + 1:
        return 1, 4 * is_other + 2 * int(row > 0) + frame % 2
    return 0, 2 * rows * is_other + 2 * (row - 1) + frame % 2


def fill_stack(stack, row, frame, plane, column, on_left, on_right):
    channels, cols = plane.shape
    lane = lax.broadcasted_iota(jnp.int32, (channels, cols), 1)
    column = column.astype(F32)
    left = jnp.where(lane == 0, (column * on_left).astype(BF16), pltpu.roll(plane, 1, axis=1))
    right = jnp.where(lane == cols - 1, (column * on_right).astype(BF16), pltpu.roll(plane, cols - 1, axis=1))
    stack[row, frame, 0:channels] = left
    stack[row, frame, channels : 2 * channels] = plane
    stack[row, frame, 2 * channels : 3 * channels] = right


def sides(flag_ref):
    on_left = (flag_ref[3] != 0).astype(F32)
    on_right = (flag_ref[3] == 0).astype(F32)
    return on_left, on_right


def conv_rows(stack, weight, row):
    three = stack[row : row + 3].reshape(weight.shape[1], stack.shape[3])
    return jnp.dot(weight[...], three, preferred_element_type=F32)


def norm_columns(par_ref, st_ref, count, gain_row):
    par = par_ref[...]
    mean, variance = combined(st_ref, count)
    inverse = 1.0 / jnp.sqrt(variance + epsilon)
    gain = par[gain_row : gain_row + 1]
    shift = par[gain_row + 1 : gain_row + 2]
    return columns_of(mean, inverse, gain, shift, par[0:1])[:5]


def conv_first_kernel(
    flag_ref, own, past, above, below, far_above, far_below, edge_ref, rim_ref, par_ref, st_ref, weight, after, hidden_ref, st_out, stack_ref,
    *, count
):
    rows, frames, channels, cols = own.shape
    at = source(own, past, (above, below), (far_above, far_below), True)
    mean, inverse, gain, shift, scale = norm_columns(par_ref, st_ref, count, 1)

    def act(latent):
        pre = (latent.astype(F32) * scale - mean) * inverse * gain + shift
        return pre * sigmoid(pre)

    has_past = flag_ref[0].astype(F32)
    has_top = flag_ref[1].astype(F32)
    has_bottom = flag_ref[2].astype(F32)
    on_left, on_right = sides(flag_ref)
    edges = (act(edge_ref[...]), act(rim_ref[...]))
    for row in range(rows + 2):
        for frame in range(4):
            ref, index = at(row, frame)
            which, number = edge_lane(row, frame, rows, True)
            plane = act(ref[index])
            column = edges[which][:, number : number + 1]
            factor = None
            if frame < 2:
                factor = has_past
            if row in (0, rows + 1):
                beside = has_top if row == 0 else has_bottom
                factor = beside if factor is None else factor * beside
            if factor is not None:
                plane = plane * factor
                column = column * factor
            fill_stack(stack_ref, row, frame, plane.astype(BF16), column, on_left, on_right)
    for row in range(rows):
        out = conv_rows(stack_ref, weight, row)
        for frame in range(frames):
            hidden_ref[row, frame] = out[frame * channels : (frame + 1) * channels]
    planes = [
        functools.partial(lambda r, t: hidden_ref[r, t], r, t) for r in range(rows) for t in range(frames)
    ]
    put_rows(st_out, *local_stats(planes, float(GROUP * rows * frames * cols)))


def fill_future(stack, flag_ref, own, future, above, below, far_above, far_below, edge_ref, rim_ref):
    rows = own.shape[0]
    at = source(own, future, (above, below), (far_above, far_below), False)
    on_left, on_right = sides(flag_ref)
    edges = (edge_ref[...], rim_ref[...])
    for row in range(rows + 2):
        for frame in range(4):
            ref, index = at(row, frame)
            which, number = edge_lane(row, frame, rows, False)
            fill_stack(stack, row, frame, ref[index], edges[which][:, number : number + 1], on_left, on_right)


def conv_back_kernel(flag_ref, *refs):
    weight, grad_ref, stack_ref = refs[-3:]
    rows, frames, channels, _ = grad_ref.shape
    fill_future(stack_ref, flag_ref, *refs[:-3])
    for row in range(rows):
        out = conv_rows(stack_ref, weight, row)
        for frame in range(frames):
            grad_ref[row, frame] = out[frame * channels : (frame + 1) * channels]


def norm_second_kernel(hidden, grad, par_ref, st_ref, act_ref, scaled_ref, sums_ref, *, count):
    rows, frames, channels, cols = hidden.shape
    mean, inverse, gain, shift, _ = norm_columns(par_ref, st_ref, count, 3)
    first = jnp.zeros((channels, 128), F32)
    second = jnp.zeros((channels, 128), F32)
    for row in range(rows):
        for frame in range(frames):
            normed = (hidden[row, frame] - mean) * inverse
            pre = normed * gain + shift
            sig = sigmoid(pre)
            act = pre * sig
            act_ref[row, frame] = act.astype(BF16)
            scaled = grad[row, frame] * (sig + act * (1.0 - sig)) * gain
            scaled_ref[row, frame] = scaled
            first = first + lanes_of(scaled)
            second = second + lanes_of(scaled * normed)
    put_rows(sums_ref, group_sums(first), group_sums(second))


def hidden_grad_kernel(hidden, scaled, par_ref, st_ref, sums_ref, out_ref, *, count):
    rows, frames, channels, cols = hidden.shape
    mean, inverse, _, _, _ = norm_columns(par_ref, st_ref, count, 3)
    means = jnp.sum(sums_ref[...], axis=0) / count
    first, second = columns_of(means[0:1], means[1:2])[:2]
    for row in range(rows):
        for frame in range(frames):
            normed = (hidden[row, frame] - mean) * inverse
            out_ref[row, frame] = (inverse * (scaled[row, frame] - first - normed * second)).astype(BF16)


def put_halves(flag_ref, mine_ref, theirs_ref, tap, block):
    half = block.shape[0] // 2
    here = pl.ds(tap, half, stride=SLOTS)
    upper, lower = block[:half], block[half:]
    is_first = flag_ref[3] == 0
    mine_ref[here, :] = jnp.where(is_first, upper, lower)
    theirs_ref[here, :] = jnp.where(is_first, lower, upper)


def encoded(value):
    slot = lax.broadcasted_iota(jnp.int32, value.shape, 1)
    value = jnp.where(slot < TAPS, value, 0.0)
    top = jnp.max(jnp.abs(value), axis=1, keepdims=True)
    power = jnp.ceil(jnp.log(jnp.maximum(top, 1e-30)) * (1.0 / LN2))
    number = jnp.round(value * (FULL * jnp.exp(power * -LN2)))
    return jnp.where(slot < TAPS, number, power).astype(jnp.int32).astype(jnp.int16)


def decoded_value(number):
    number = number.astype(jnp.int32).astype(F32)
    return number * (jnp.exp(number[:, SLOTS - 1 : SLOTS] * LN2) * (1.0 / FULL))


def first_scatter_kernel(*refs):
    out_ref = refs[-1]
    chunks, _, rows = out_ref.shape[:3]
    for which in range(2):
        mine_ref, other_ref = refs[2 * which], refs[2 * which + 1]
        for chunk in range(chunks):
            here = slice(chunk * rows, (chunk + 1) * rows)
            out_ref[chunk, which] = encoded(mine_ref[here] + other_ref[here])


def second_scatter_kernel(received, after, out_ref):
    chunks, _, rows = out_ref.shape[:3]
    for which in range(2):
        for chunk in range(chunks):
            here = slice(chunk * rows, (chunk + 1) * rows)
            total = decoded_value(received[0, which, here])
            for number in range(1, received.shape[0]):
                total = total + decoded_value(received[number, which, here])
            out_ref[chunk, which] = encoded(total)


def total_kernel(received, out_ref):
    for which in range(2):
        total = decoded_value(received[0, which])
        for number in range(1, received.shape[0]):
            total = total + decoded_value(received[number, which])
        total = encoded(total)
        for copy in range(out_ref.shape[0]):
            out_ref[copy, which] = total


def copies_kernel(value, after, *outs):
    for which, out_ref in enumerate(outs):
        for copy in range(out_ref.shape[0]):
            out_ref[copy] = value[:, which]


def join_kernel(flag_ref, mine_ref, theirs_ref, out_ref, first_ref, second_ref):
    half, _, channels = mine_ref.shape
    is_first = flag_ref[3] == 0
    first_ref[...] = decoded_value(jnp.where(is_first, mine_ref[...], theirs_ref[...])).reshape(first_ref.shape)
    second_ref[...] = decoded_value(jnp.where(is_first, theirs_ref[...], mine_ref[...])).reshape(second_ref.shape)
    for tap in range(TAPS):
        here = slice(tap * channels, (tap + 1) * channels)
        out_ref[:half, here] = first_ref[pl.ds(tap, half, stride=SLOTS), :]
        out_ref[half:, here] = second_ref[pl.ds(tap, half, stride=SLOTS), :]


def weight_second_kernel(flag_ref, stack_ref, act_ref, after, after_too, mine_ref, theirs_ref, right_ref):
    rows, frames, channels, cols = act_ref.shape
    for row in range(rows):
        right_ref[row * cols : (row + 1) * cols] = jnp.transpose(
            act_ref[row].reshape(frames * channels, cols)
        )
    right = right_ref[...]
    for down in range(3):
        parts = []
        for frame in range(4):
            left = jnp.concatenate([stack_ref[down + row, frame] for row in range(rows)], axis=1)
            parts.append(jnp.dot(left, right, preferred_element_type=F32))
        for kt in range(3):
            term = parts[2 - kt][:, :channels] + parts[3 - kt][:, channels:]
            for across in range(3):
                tap = 9 * kt + 3 * (2 - down) + (2 - across)
                put_halves(flag_ref, mine_ref, theirs_ref, tap, term[across * channels : (across + 1) * channels])


def weight_first_kernel(flag_ref, stack_ref, grad_ref, after, mine_ref, theirs_ref, right_ref):
    rows, frames, channels, cols = grad_ref.shape
    for row in range(rows):
        right_ref[row * cols : (row + 1) * cols] = jnp.transpose(
            grad_ref[row].reshape(frames * channels, cols)
        )
    right = right_ref[...]
    for down in range(3):
        parts = []
        for frame in range(4):
            left = jnp.concatenate([stack_ref[down + row, frame] for row in range(rows)], axis=1)
            parts.append(jnp.dot(left, right, preferred_element_type=F32))
        for kt in range(3):
            term = parts[kt][:, :channels] + parts[kt + 1][:, channels:]
            for across in range(3):
                tap = 9 * kt + 3 * down + across
                block = jnp.transpose(term[across * channels : (across + 1) * channels])
                put_halves(flag_ref, mine_ref, theirs_ref, tap, block)


def first_grad_kernel(flag_ref, *refs, count):
    weight, latent, par_ref, st_ref, _, scaled_ref, sums_ref, stack_ref = refs[-8:]
    rows, frames, channels, cols = latent.shape
    mean, inverse, gain, shift, scale = norm_columns(par_ref, st_ref, count, 1)
    fill_future(stack_ref, flag_ref, *refs[:-8])
    first = jnp.zeros((channels, 128), F32)
    second = jnp.zeros((channels, 128), F32)
    for row in range(rows):
        out = conv_rows(stack_ref, weight, row)
        for frame in range(frames):
            grad = out[frame * channels : (frame + 1) * channels]
            normed = (latent[row, frame].astype(F32) * scale - mean) * inverse
            pre = normed * gain + shift
            sig = sigmoid(pre)
            scaled = grad * (sig + pre * sig * (1.0 - sig)) * gain
            scaled_ref[row, frame] = scaled
            first = first + lanes_of(scaled)
            second = second + lanes_of(scaled * normed)
    put_rows(sums_ref, group_sums(first), group_sums(second))


def decoded_grad_kernel(scaled, latent, cotangent, par_ref, st_ref, sums_ref, after, out_ref, *, count):
    rows, frames, channels, cols = latent.shape
    mean, inverse, _, _, scale = norm_columns(par_ref, st_ref, count, 1)
    means = jnp.sum(sums_ref[...], axis=0) / count
    first, second = columns_of(means[0:1], means[1:2])[:2]
    for row in range(rows):
        for frame in range(frames):
            normed = (latent[row, frame].astype(F32) * scale - mean) * inverse
            out_ref[:, frame, row, :] = cotangent[row, frame].astype(F32) + inverse * (
                scaled[row, frame] - first - normed * second
            )


def weight_forward_kernel(weight, out_ref):
    channels = weight.shape[0]
    wide = 3 * channels
    for t in range(2):
        for kr in range(3):
            for f in range(4):
                kt = f - t
                here = slice((kr * 4 + f) * wide, (kr * 4 + f + 1) * wide)
                if 0 <= kt < 3:
                    tap = 3 * kt + kr
                    block = weight[:, tap * wide : (tap + 1) * wide]
                else:
                    block = jnp.zeros((channels, wide), BF16)
                out_ref[t * channels : (t + 1) * channels, here] = block


def weight_back_kernel(weight, out_ref):
    channels = weight.shape[0]
    for down in range(3):
        for across in range(3):
            blocks = [
                jnp.transpose(
                    weight[
                        :,
                        (9 * kt + 3 * (2 - down) + 2 - across) * channels : (9 * kt + 3 * (2 - down) + 3 - across)
                        * channels,
                    ]
                )
                for kt in range(3)
            ]
            for t in range(2):
                for f in range(4):
                    kt = t + 2 - f
                    start = ((down * 4 + f) * 3 + across) * channels
                    block = blocks[kt] if 0 <= kt < 3 else jnp.zeros((channels, channels), BF16)
                    out_ref[t * channels : (t + 1) * channels, start : start + channels] = block


def shifted(value, axis, steps):
    count = lax.axis_size(axis)
    initial, last = max(0, -steps), min(count, count - steps)
    return lax.ppermute(value, axis, [(source, source + steps) for source in range(initial, last)])


def exchanged(value, axis):
    return lax.all_to_all(value, axis, 0, 0, tiled=True)


def shared(value):
    return exchanged(value, ("tm", "height", "width"))


def swapped(value):
    return lax.ppermute(value, "width", [(0, 1), (1, 0)])


def scattered(second, first, after):
    half, _, channels = second[0].shape
    by_height = lax.axis_size("height")
    terms = [part for mine, theirs in (second, first) for part in (mine, swapped(theirs))]
    (value,) = call(
        first_scatter_kernel,
        [shape((by_height, 2, half // by_height, SLOTS, channels), jnp.int16)],
        [VMEM] * 4 + [ANY] * len(after),
        (*terms, *after),
    )
    return exchanged(value, "height"), value


def summed(value, after):
    by_tm = lax.axis_size("tm")
    _, _, rows, _, channels = value.shape
    (value,) = call(
        second_scatter_kernel,
        [shape((by_tm, 2, rows // by_tm, SLOTS, channels), jnp.int16)],
        [VMEM, ANY],
        (value, after),
    )
    return exchanged(value, "tm"), value


def gathered(value, after_last):
    (value,) = call(total_kernel, [shape(value.shape, jnp.int16)], [VMEM], (value,))
    value = exchanged(value, "tm")
    by_height = lax.axis_size("height")
    by_tm, _, rows, _, channels = value.shape
    copies = call(
        copies_kernel,
        [shape((by_height, by_tm, rows, SLOTS, channels), jnp.int16)] * 2,
        [VMEM, ANY],
        (value, after_last),
    )
    return [exchanged(copy, "height").reshape(-1, SLOTS, channels) for copy in copies]


def joined(flags, mine, theirs):
    half, _, channels = mine.shape
    (total,) = call(
        join_kernel,
        [shape((2 * half, TAPS * channels), F32)],
        [SMEM] + [VMEM] * 2,
        (flags, mine, theirs),
        scratch=[pltpu.VMEM((half * SLOTS, channels), F32)] * 2,
    )
    return total


def row_exchange(block):
    return shifted(block[-1:], "height", 1), shifted(block[:1], "height", -1)


def edges(flags, *planes):
    channels = planes[0].shape[2]
    (columns,) = call(
        edges_kernel, [shape((channels, 128), BF16)], [SMEM] + [VMEM] * len(planes), (flags, *planes)
    )
    return columns


def extended(flags, own, steps):
    other = shifted(own, "tm", steps)
    near = row_exchange(own)
    far = [shifted(row, "tm", steps) for row in near]
    edge = swapped(edges(flags, own, other))
    rim = swapped(edges(flags, *near, *far))
    return other, *near, *far, edge, rim


def shards(
    latent,
    exponents,
    cotangent,
    conv_first,
    conv_second,
    gain_first,
    shift_first,
    gain_second,
    shift_second,
):
    channels, frames, rows, cols = latent.shape
    groups = exponents.shape[0]
    devices = lax.axis_size("tm") * lax.axis_size("height") * lax.axis_size("width")
    count = float(channels // groups * frames * rows * cols * devices)
    tm, height, width = (lax.axis_index(axis) for axis in ("tm", "height", "width"))
    flags = jnp.stack(
        [
            (tm > 0).astype(jnp.int32),
            (height > 0).astype(jnp.int32),
            (height < lax.axis_size("height") - 1).astype(jnp.int32),
            width.astype(jnp.int32),
        ]
    )
    scale = jnp.repeat(jnp.exp2(exponents.astype(F32)), channels // groups)
    zeros = jnp.zeros_like(scale)
    par = jnp.stack([scale, gain_first, shift_first, gain_second, shift_second, zeros, zeros, zeros])
    block = (rows, frames, channels, cols)
    stack = (rows + 2, 4, 3 * channels, cols)
    taps = (2 * channels, 36 * channels)
    halves = [shape((channels // 2 * SLOTS, channels), F32)] * 2
    conv_flops = 2 * 4 * 256 * 36 * channels * 2 * channels
    small = shape((devices, 2, channels), F32)

    latent, stats_first = call(
        planes_kernel, [shape(block, BF16), small], [VMEM] * 2, (latent, par)
    )
    around = extended(flags, latent, 1)
    (cotangent,) = call(planes_kernel, [shape(block, BF16)], [VMEM], (cotangent,))
    around_c = extended(flags, cotangent, -1)
    stats_first = shared(stats_first)
    (weight_first,) = call(weight_forward_kernel, [shape(taps, BF16)], [VMEM], (conv_first,))
    (weight_second_t,) = call(weight_back_kernel, [shape(taps, BF16)], [VMEM], (conv_second,))
    (weight_first_t,) = call(weight_back_kernel, [shape(taps, BF16)], [VMEM], (conv_first,))

    hidden, stats_second, stack_first = call(
        functools.partial(conv_first_kernel, count=count),
        [shape(block, F32), small, shape(stack, BF16)],
        [SMEM] + [VMEM] * 11 + [ANY],
        (flags, latent, *around, par, stats_first, weight_first, around_c[0]),
        flops=conv_flops,
        transcendentals=3 * latent.size,
    )
    stats_second = shared(stats_second)
    grad_second, stack_c = call(
        conv_back_kernel,
        [shape(block, F32), shape(stack, BF16)],
        [SMEM] + [VMEM] * 9,
        (flags, cotangent, *around_c, weight_second_t),
        flops=conv_flops,
    )
    act_second, scaled, sums = call(
        functools.partial(norm_second_kernel, count=count),
        [shape(block, BF16), shape(block, F32), small],
        [VMEM] * 4,
        (hidden, grad_second, par, stats_second),
        transcendentals=latent.size,
    )
    sums = shared(sums)
    (hidden_grad,) = call(
        functools.partial(hidden_grad_kernel, count=count),
        [shape(block, BF16)],
        [VMEM] * 5,
        (hidden, scaled, par, stats_second, sums),
    )
    around = extended(flags, hidden_grad, -1)
    halves_second = call(
        weight_second_kernel,
        halves,
        [SMEM] + [VMEM] * 2 + [ANY] * 2,
        (flags, stack_c, act_second, around[1], around[2]),
        scratch=[pltpu.VMEM((rows * cols, frames * channels), BF16)],
        flops=conv_flops,
    )
    halves_first = call(
        weight_first_kernel,
        halves,
        [SMEM] + [VMEM] * 2 + [ANY],
        (flags, stack_first, hidden_grad, around[0]),
        scratch=[pltpu.VMEM((rows * cols, frames * channels), BF16)],
        flops=conv_flops,
    )
    halves_second, halves_first = (
        [v.reshape(channels // 2, SLOTS, channels) for v in halves] for halves in (halves_second, halves_first)
    )
    weights, sent = scattered(halves_second, halves_first, (around[3], around[4]))
    scaled, sums_first = call(
        functools.partial(first_grad_kernel, count=count),
        [shape(block, F32), small],
        [SMEM] + [VMEM] * 12 + [ANY],
        (flags, hidden_grad, *around, weight_first_t, latent, par, stats_first, sent),
        scratch=[pltpu.VMEM(stack, BF16)],
        flops=conv_flops,
        transcendentals=latent.size,
    )
    weights, sent = summed(weights, sums_first)
    sums_first = shared(sums_first)
    (decoded_grad,) = call(
        functools.partial(decoded_grad_kernel, count=count),
        [shape((channels, frames, rows, cols), F32)],
        [VMEM] * 6 + [ANY],
        (scaled, latent, cotangent, par, stats_first, sums_first, sent),
    )
    second, first = gathered(weights, decoded_grad)
    conv_second_grad = joined(flags, second, swapped(second))
    conv_first_grad = joined(flags, first, swapped(first))
    return decoded_grad, conv_first_grad, conv_second_grad


def solution(mesh):
    block = P(None, "tm", "height", "width")
    return jax.shard_map(
        shards,
        mesh=mesh,
        in_specs=(block, P(), block, P(), P(), P(), P(), P(), P()),
        out_specs=(block, P(), P()),
        check_vma=False,
    )
```

```python
import functools

import jax
import jax.numpy as jnp
from jax import lax
from jax.experimental import pallas as pl
from jax.experimental.pallas import tpu as pltpu
from jax.sharding import PartitionSpec as P

epsilon = 1e-05
F32 = jnp.float32
BF16 = jnp.bfloat16
GROUP = 4
TAPS, SLOTS = 27, 32
FULL = 32760.0
LN2 = 0.6931471805599453
VMEM = pl.BlockSpec(memory_space=pltpu.VMEM)
SMEM = pl.BlockSpec(memory_space=pltpu.SMEM)


def call(body, outs, specs, args, scratch=(), flops=0, transcendentals=0, limit=48):
    moved = sum(a.size * a.dtype.itemsize for a in args)
    moved += sum(o.size * o.dtype.itemsize for o in outs)
    return pl.pallas_call(
        body,
        out_shape=tuple(outs),
        in_specs=specs,
        out_specs=tuple(VMEM for _ in outs),
        scratch_shapes=scratch,
        compiler_params=pltpu.CompilerParams(vmem_limit_bytes=limit << 20),
        cost_estimate=pl.CostEstimate(
            flops=flops, bytes_accessed=moved, transcendentals=transcendentals
        ),
    )(*args)


def shape(dims, dtype):
    return jax.ShapeDtypeStruct(dims, dtype)


def group_sums(acc):
    rows = acc.shape[0]
    row = lax.broadcasted_iota(jnp.int32, acc.shape, 0)
    step = 1
    while step < GROUP:
        up = pltpu.roll(acc, rows - step, axis=0)
        down = pltpu.roll(acc, step, axis=0)
        acc = acc + jnp.where((row & step) == 0, up, down)
        step *= 2
    return jnp.sum(acc, axis=1, keepdims=True)


def lanes_of(plane):
    total = plane[:, :128]
    for start in range(128, plane.shape[1], 128):
        total = total + plane[:, start : start + 128]
    return total


def as_rows(first, second):
    channels = first.shape[0]
    lane = lax.broadcasted_iota(jnp.int32, (channels, 128), 1)
    both = jnp.where(lane == 0, first, jnp.where(lane == 1, second, 0.0))
    return jnp.transpose(both)[:2]


def local_stats(planes, count):
    acc = None
    for plane in planes:
        part = lanes_of(plane())
        acc = part if acc is None else acc + part
    mean = group_sums(acc) / count
    acc = None
    for plane in planes:
        off = plane() - mean
        part = lanes_of(off * off)
        acc = part if acc is None else acc + part
    return mean, group_sums(acc)


def put_rows(out_ref, first, second):
    out_ref[...] = jnp.broadcast_to(as_rows(first, second)[None], out_ref.shape)


def combined(st_ref, count):
    devices = st_ref.shape[0]
    mean = jnp.mean(st_ref[:, 0:1], axis=0)
    off = st_ref[:, 0:1] - mean[None]
    squares = jnp.sum(st_ref[:, 1:2] + off * off * (count / devices), axis=0)
    return mean, squares / count


def columns_of(*rows):
    rows = list(rows) + [jnp.zeros_like(rows[0])] * (8 - len(rows))
    cols = jnp.transpose(jnp.concatenate(rows, axis=0))
    return [cols[:, i : i + 1] for i in range(8)]


def sigmoid(value):
    return 0.5 + 0.5 * jnp.tanh(0.5 * value)


def planes_kernel(natural_ref, *refs):
    out_ref = refs[-1] if len(refs) == 1 else refs[-2]
    _, frames, rows, cols = natural_ref.shape
    for row in range(rows):
        for frame in range(frames):
            out_ref[row, frame] = natural_ref[:, frame, row, :]
    if len(refs) == 1:
        return
    scale = columns_of(refs[0][0:1])[0]
    planes = [
        functools.partial(lambda r, t: out_ref[r, t].astype(F32) * scale, r, t)
        for r in range(rows)
        for t in range(frames)
    ]
    put_rows(refs[-1], *local_stats(planes, float(GROUP * rows * frames * cols)))


def source(own, other, near, far, other_first):
    def at(row, frame):
        is_other = (frame < 2) == other_first
        if row == 0 or row == own.shape[0] + 1:
            return (far if is_other else near)[0 if row == 0 else 1], (0, frame % 2)
        return (other if is_other else own), (row - 1, frame % 2)

    return at


def edges_kernel(flag_ref, *refs):
    planes, out_ref = [ref for ref in refs[:-1] if len(ref.shape) == 4], refs[-1]
    is_first = flag_ref[3] == 0
    channels = planes[0].shape[2]
    lane = lax.broadcasted_iota(jnp.int32, (channels, 128), 1)
    acc = jnp.zeros((channels, 128), F32)
    number = 0
    for ref in planes:
        for row in range(ref.shape[0]):
            for frame in range(ref.shape[1]):
                last = pltpu.roll(ref[row, frame, :, -128:].astype(F32), 1, axis=1)
                edge = jnp.where(is_first, last, ref[row, frame, :, :128].astype(F32))
                moved = pltpu.roll(edge, number, axis=1) if number else edge
                acc = jnp.where(lane == number, moved, acc)
                number += 1
    out_ref[...] = acc.astype(BF16)


def edge_lane(row, frame, rows, other_first):
    is_other = int((frame < 2) == other_first)
    if row == 0 or row == rows + 1:
        return 1, 4 * is_other + 2 * int(row > 0) + frame % 2
    return 0, 2 * rows * is_other + 2 * (row - 1) + frame % 2


def fill_stack(stack, row, frame, plane, column, on_left, on_right):
    channels, cols = plane.shape
    lane = lax.broadcasted_iota(jnp.int32, (channels, cols), 1)
    column = column.astype(F32)
    left = jnp.where(lane == 0, (column * on_left).astype(BF16), pltpu.roll(plane, 1, axis=1))
    right = jnp.where(lane == cols - 1, (column * on_right).astype(BF16), pltpu.roll(plane, cols - 1, axis=1))
    stack[row, frame, 0:channels] = left
    stack[row, frame, channels : 2 * channels] = plane
    stack[row, frame, 2 * channels : 3 * channels] = right


def sides(flag_ref):
    on_left = (flag_ref[3] != 0).astype(F32)
    on_right = (flag_ref[3] == 0).astype(F32)
    return on_left, on_right


def conv_rows(stack, weight, row):
    three = stack[row : row + 3].reshape(weight.shape[1], stack.shape[3])
    return jnp.dot(weight[...], three, preferred_element_type=F32)


def norm_columns(par_ref, st_ref, count, gain_row):
    par = par_ref[...]
    mean, variance = combined(st_ref, count)
    inverse = 1.0 / jnp.sqrt(variance + epsilon)
    gain = par[gain_row : gain_row + 1]
    shift = par[gain_row + 1 : gain_row + 2]
    return columns_of(mean, inverse, gain, shift, par[0:1])[:5]


def conv_first_kernel(
    flag_ref, own, past, above, below, far_above, far_below, edge_ref, rim_ref, par_ref, st_ref, weight, after, hidden_ref, st_out, stack_ref,
    *, count
):
    rows, frames, channels, cols = own.shape
    at = source(own, past, (above, below), (far_above, far_below), True)
    mean, inverse, gain, shift, scale = norm_columns(par_ref, st_ref, count, 1)

    def act(latent):
        pre = (latent.astype(F32) * scale - mean) * inverse * gain + shift
        return pre * sigmoid(pre)

    has_past = flag_ref[0].astype(F32)
    has_top = flag_ref[1].astype(F32)
    has_bottom = flag_ref[2].astype(F32)
    on_left, on_right = sides(flag_ref)
    edges = (act(edge_ref[...]), act(rim_ref[...]))
    for row in range(rows + 2):
        for frame in range(4):
            ref, index = at(row, frame)
            which, number = edge_lane(row, frame, rows, True)
            plane = act(ref[index])
            column = edges[which][:, number : number + 1]
            factor = None
            if frame < 2:
                factor = has_past
            if row in (0, rows + 1):
                beside = has_top if row == 0 else has_bottom
                factor = beside if factor is None else factor * beside
            if factor is not None:
                plane = plane * factor
                column = column * factor
            fill_stack(stack_ref, row, frame, plane.astype(BF16), column, on_left, on_right)
    for row in range(rows):
        out = conv_rows(stack_ref, weight, row)
        for frame in range(frames):
            hidden_ref[row, frame] = out[frame * channels : (frame + 1) * channels]
    planes = [
        functools.partial(lambda r, t: hidden_ref[r, t], r, t) for r in range(rows) for t in range(frames)
    ]
    put_rows(st_out, *local_stats(planes, float(GROUP * rows * frames * cols)))


def fill_future(stack, flag_ref, own, future, above, below, far_above, far_below, edge_ref, rim_ref):
    rows = own.shape[0]
    at = source(own, future, (above, below), (far_above, far_below), False)
    on_left, on_right = sides(flag_ref)
    edges = (edge_ref[...], rim_ref[...])
    for row in range(rows + 2):
        for frame in range(4):
            ref, index = at(row, frame)
            which, number = edge_lane(row, frame, rows, False)
            fill_stack(stack, row, frame, ref[index], edges[which][:, number : number + 1], on_left, on_right)


def conv_back_kernel(flag_ref, *refs):
    weight, grad_ref, stack_ref = refs[-3:]
    rows, frames, channels, _ = grad_ref.shape
    fill_future(stack_ref, flag_ref, *refs[:-3])
    for row in range(rows):
        out = conv_rows(stack_ref, weight, row)
        for frame in range(frames):
            grad_ref[row, frame] = out[frame * channels : (frame + 1) * channels]


def norm_second_kernel(hidden, grad, par_ref, st_ref, act_ref, scaled_ref, sums_ref, *, count):
    rows, frames, channels, cols = hidden.shape
    mean, inverse, gain, shift, _ = norm_columns(par_ref, st_ref, count, 3)
    first = jnp.zeros((channels, 128), F32)
    second = jnp.zeros((channels, 128), F32)
    for row in range(rows):
        for frame in range(frames):
            normed = (hidden[row, frame] - mean) * inverse
            pre = normed * gain + shift
            sig = sigmoid(pre)
            act = pre * sig
            act_ref[row, frame] = act.astype(BF16)
            scaled = grad[row, frame] * (sig + act * (1.0 - sig)) * gain
            scaled_ref[row, frame] = scaled
            first = first + lanes_of(scaled)
            second = second + lanes_of(scaled * normed)
    put_rows(sums_ref, group_sums(first), group_sums(second))


def hidden_grad_kernel(hidden, scaled, par_ref, st_ref, sums_ref, after, out_ref, *, count):
    rows, frames, channels, cols = hidden.shape
    mean, inverse, _, _, _ = norm_columns(par_ref, st_ref, count, 3)
    means = jnp.sum(sums_ref[...], axis=0) / count
    first, second = columns_of(means[0:1], means[1:2])[:2]
    for row in range(rows):
        for frame in range(frames):
            normed = (hidden[row, frame] - mean) * inverse
            out_ref[row, frame] = (inverse * (scaled[row, frame] - first - normed * second)).astype(BF16)


def put_halves(flag_ref, mine_ref, theirs_ref, tap, block):
    half = block.shape[0] // 2
    here = pl.ds(tap, half, stride=SLOTS)
    upper, lower = block[:half], block[half:]
    is_first = flag_ref[3] == 0
    mine_ref[here, :] = jnp.where(is_first, upper, lower)
    theirs_ref[here, :] = jnp.where(is_first, lower, upper)


def encoded(value):
    slot = lax.broadcasted_iota(jnp.int32, value.shape, 1)
    value = jnp.where(slot < TAPS, value, 0.0)
    top = jnp.max(jnp.abs(value), axis=1, keepdims=True)
    power = jnp.ceil(jnp.log(jnp.maximum(top, 1e-30)) * (1.0 / LN2))
    number = jnp.round(value * (FULL * jnp.exp(power * -LN2)))
    return jnp.where(slot < TAPS, number, power).astype(jnp.int32).astype(jnp.int16)


def decoded_value(number):
    number = number.astype(jnp.int32).astype(F32)
    return number * (jnp.exp(number[:, SLOTS - 1 : SLOTS] * LN2) * (1.0 / FULL))


def first_scatter_kernel(*refs):
    out_ref = refs[-1]
    chunks, _, rows = out_ref.shape[:3]
    for which in range(2):
        mine_ref, other_ref = refs[2 * which], refs[2 * which + 1]
        for chunk in range(chunks):
            here = slice(chunk * rows, (chunk + 1) * rows)
            out_ref[chunk, which] = encoded(mine_ref[here] + other_ref[here])


def second_scatter_kernel(received, *refs):
    out_ref = refs[-1]
    chunks, _, rows = out_ref.shape[:3]
    for which in range(2):
        for chunk in range(chunks):
            here = slice(chunk * rows, (chunk + 1) * rows)
            total = decoded_value(received[0, which, here])
            for number in range(1, received.shape[0]):
                total = total + decoded_value(received[number, which, here])
            out_ref[chunk, which] = encoded(total)


def total_kernel(received, *refs):
    out_ref = refs[-1]
    for which in range(2):
        total = decoded_value(received[0, which])
        for number in range(1, received.shape[0]):
            total = total + decoded_value(received[number, which])
        total = encoded(total)
        for copy in range(out_ref.shape[0]):
            out_ref[copy, which] = total


def copies_kernel(value, after, *outs):
    for which, out_ref in enumerate(outs):
        for copy in range(out_ref.shape[0]):
            out_ref[copy] = value[:, which]


def join_kernel(flag_ref, mine_ref, theirs_ref, after, out_ref, first_ref, second_ref):
    half, _, channels = mine_ref.shape
    is_first = flag_ref[3] == 0
    first_ref[...] = decoded_value(jnp.where(is_first, mine_ref[...], theirs_ref[...])).reshape(first_ref.shape)
    second_ref[...] = decoded_value(jnp.where(is_first, theirs_ref[...], mine_ref[...])).reshape(second_ref.shape)
    for tap in range(TAPS):
        here = slice(tap * channels, (tap + 1) * channels)
        out_ref[:half, here] = first_ref[pl.ds(tap, half, stride=SLOTS), :]
        out_ref[half:, here] = second_ref[pl.ds(tap, half, stride=SLOTS), :]


def weight_second_kernel(flag_ref, stack_ref, act_ref, mine_ref, theirs_ref, right_ref):
    rows, frames, channels, cols = act_ref.shape
    for row in range(rows):
        right_ref[row * cols : (row + 1) * cols] = jnp.transpose(
            act_ref[row].reshape(frames * channels, cols)
        )
    right = right_ref[...]
    for down in range(3):
        parts = []
        for frame in range(4):
            left = jnp.concatenate([stack_ref[down + row, frame] for row in range(rows)], axis=1)
            parts.append(jnp.dot(left, right, preferred_element_type=F32))
        for kt in range(3):
            term = parts[2 - kt][:, :channels] + parts[3 - kt][:, channels:]
            for across in range(3):
                tap = 9 * kt + 3 * (2 - down) + (2 - across)
                put_halves(flag_ref, mine_ref, theirs_ref, tap, term[across * channels : (across + 1) * channels])


def weight_first_kernel(flag_ref, stack_ref, grad_ref, mine_ref, theirs_ref, right_ref):
    rows, frames, channels, cols = grad_ref.shape
    for row in range(rows):
        right_ref[row * cols : (row + 1) * cols] = jnp.transpose(
            grad_ref[row].reshape(frames * channels, cols)
        )
    right = right_ref[...]
    for down in range(3):
        parts = []
        for frame in range(4):
            left = jnp.concatenate([stack_ref[down + row, frame] for row in range(rows)], axis=1)
            parts.append(jnp.dot(left, right, preferred_element_type=F32))
        for kt in range(3):
            term = parts[kt][:, :channels] + parts[kt + 1][:, channels:]
            for across in range(3):
                tap = 9 * kt + 3 * down + across
                block = jnp.transpose(term[across * channels : (across + 1) * channels])
                put_halves(flag_ref, mine_ref, theirs_ref, tap, block)


def first_grad_kernel(flag_ref, *refs, count):
    weight, latent, par_ref, st_ref, scaled_ref, sums_ref, stack_ref = refs[-7:]
    rows, frames, channels, cols = latent.shape
    mean, inverse, gain, shift, scale = norm_columns(par_ref, st_ref, count, 1)
    fill_future(stack_ref, flag_ref, *refs[:-7])
    first = jnp.zeros((channels, 128), F32)
    second = jnp.zeros((channels, 128), F32)
    for row in range(rows):
        out = conv_rows(stack_ref, weight, row)
        for frame in range(frames):
            grad = out[frame * channels : (frame + 1) * channels]
            normed = (latent[row, frame].astype(F32) * scale - mean) * inverse
            pre = normed * gain + shift
            sig = sigmoid(pre)
            scaled = grad * (sig + pre * sig * (1.0 - sig)) * gain
            scaled_ref[row, frame] = scaled
            first = first + lanes_of(scaled)
            second = second + lanes_of(scaled * normed)
    put_rows(sums_ref, group_sums(first), group_sums(second))


def decoded_grad_kernel(scaled, latent, cotangent, par_ref, st_ref, sums_ref, out_ref, *, count):
    rows, frames, channels, cols = latent.shape
    mean, inverse, _, _, scale = norm_columns(par_ref, st_ref, count, 1)
    means = jnp.sum(sums_ref[...], axis=0) / count
    first, second = columns_of(means[0:1], means[1:2])[:2]
    for row in range(rows):
        for frame in range(frames):
            normed = (latent[row, frame].astype(F32) * scale - mean) * inverse
            out_ref[:, frame, row, :] = cotangent[row, frame].astype(F32) + inverse * (
                scaled[row, frame] - first - normed * second
            )


def weight_forward_kernel(weight, out_ref):
    channels = weight.shape[0]
    wide = 3 * channels
    for t in range(2):
        for kr in range(3):
            for f in range(4):
                kt = f - t
                here = slice((kr * 4 + f) * wide, (kr * 4 + f + 1) * wide)
                if 0 <= kt < 3:
                    tap = 3 * kt + kr
                    block = weight[:, tap * wide : (tap + 1) * wide]
                else:
                    block = jnp.zeros((channels, wide), BF16)
                out_ref[t * channels : (t + 1) * channels, here] = block


def weight_back_kernel(weight, out_ref):
    channels = weight.shape[0]
    for down in range(3):
        for across in range(3):
            blocks = [
                jnp.transpose(
                    weight[
                        :,
                        (9 * kt + 3 * (2 - down) + 2 - across) * channels : (9 * kt + 3 * (2 - down) + 3 - across)
                        * channels,
                    ]
                )
                for kt in range(3)
            ]
            for t in range(2):
                for f in range(4):
                    kt = t + 2 - f
                    start = ((down * 4 + f) * 3 + across) * channels
                    block = blocks[kt] if 0 <= kt < 3 else jnp.zeros((channels, channels), BF16)
                    out_ref[t * channels : (t + 1) * channels, start : start + channels] = block


def shifted(value, axis, steps):
    count = lax.axis_size(axis)
    initial, last = max(0, -steps), min(count, count - steps)
    return lax.ppermute(value, axis, [(source, source + steps) for source in range(initial, last)])


def exchanged(value, axis):
    return lax.all_to_all(value, axis, 0, 0, tiled=True)


def all_stats(value, count):
    value = value[0]
    for axis in ("tm", "height", "width"):
        size = lax.axis_size(axis)
        step = 1
        while step < size:
            wide = 4 if 4 * step <= size else 2
            parts = [value] + [
                lax.ppermute(value, axis, [(i, i ^ (step * k)) for i in range(size)]) for k in range(1, wide)
            ]
            while len(parts) > 1:
                joined = []
                for a, b in zip(parts[::2], parts[1::2]):
                    gap = a[0:1] - b[0:1]
                    mean = 0.5 * (a[0:1] + b[0:1])
                    joined.append(jnp.concatenate([mean, a[1:2] + b[1:2] + gap * gap * (0.5 * count)], axis=0))
                parts = joined
                count = 2.0 * count
            (value,) = parts
            step *= wide
    return value[None]


def token(value):
    if value.ndim > 2:
        value = value[(0,) * (value.ndim - 2)]
    return value[:16, :128]


def shared(value):
    return exchanged(value, ("tm", "height", "width"))


def swapped(value):
    return lax.ppermute(value, "width", [(0, 1), (1, 0)])


def scattered(second, first):
    half, _, channels = second[0].shape
    by_height = lax.axis_size("height")
    terms = [part for mine, theirs in (second, first) for part in (mine, swapped(theirs))]
    (value,) = call(
        first_scatter_kernel,
        [shape((by_height, 2, half // by_height, SLOTS, channels), jnp.int16)],
        [VMEM] * 4,
        terms,
    )
    return exchanged(value, "height"), value


def summed(value, after):
    by_tm = lax.axis_size("tm")
    _, _, rows, _, channels = value.shape
    (value,) = call(
        second_scatter_kernel,
        [shape((by_tm, 2, rows // by_tm, SLOTS, channels), jnp.int16)],
        [VMEM] * (1 + len(after)),
        (value, *map(token, after)),
    )
    return exchanged(value, "tm")


def gathered(value, after, after_last):
    (value,) = call(total_kernel, [shape(value.shape, jnp.int16)], [VMEM] * (1 + len(after)), (value, *map(token, after)))
    value = exchanged(value, "tm")
    by_height = lax.axis_size("height")
    by_tm, _, rows, _, channels = value.shape
    copies = call(
        copies_kernel,
        [shape((by_height, by_tm, rows, SLOTS, channels), jnp.int16)] * 2,
        [VMEM] * 2,
        (value, token(after_last)),
    )
    return [exchanged(copy, "height").reshape(-1, SLOTS, channels) for copy in copies]


def joined(flags, mine, theirs, after):
    half, _, channels = mine.shape
    (total,) = call(
        join_kernel,
        [shape((2 * half, TAPS * channels), F32)],
        [SMEM] + [VMEM] * 3,
        (flags, mine, theirs, token(after)),
        scratch=[pltpu.VMEM((half * SLOTS, channels), F32)] * 2,
    )
    return total


def row_exchange(block):
    return shifted(block[-1:], "height", 1), shifted(block[:1], "height", -1)


def edges(flags, planes, after):
    channels = planes[0].shape[2]
    args = (*planes, *map(token, after))
    (columns,) = call(edges_kernel, [shape((channels, 128), BF16)], [SMEM] + [VMEM] * len(args), (flags, *args))
    return columns


def halo(own, steps):
    other = shifted(own, "tm", steps)
    near = row_exchange(own)
    far = [shifted(row, "tm", steps) for row in near]
    return other, *near, *far


def with_columns(flags, own, around, after=()):
    edge = swapped(edges(flags, (own, around[0]), after))
    rim = swapped(edges(flags, around[1:], after))
    return *around, edge, rim


def shards(
    latent,
    exponents,
    cotangent,
    conv_first,
    conv_second,
    gain_first,
    shift_first,
    gain_second,
    shift_second,
):
    channels, frames, rows, cols = latent.shape
    groups = exponents.shape[0]
    devices = lax.axis_size("tm") * lax.axis_size("height") * lax.axis_size("width")
    count = float(channels // groups * frames * rows * cols * devices)
    tm, height, width = (lax.axis_index(axis) for axis in ("tm", "height", "width"))
    flags = jnp.stack(
        [
            (tm > 0).astype(jnp.int32),
            (height > 0).astype(jnp.int32),
            (height < lax.axis_size("height") - 1).astype(jnp.int32),
            width.astype(jnp.int32),
        ]
    )
    scale = jnp.repeat(jnp.exp2(exponents.astype(F32)), channels // groups)
    zeros = jnp.zeros_like(scale)
    par = jnp.stack([scale, gain_first, shift_first, gain_second, shift_second, zeros, zeros, zeros])
    block = (rows, frames, channels, cols)
    stack = (rows + 2, 4, 3 * channels, cols)
    taps = (2 * channels, 36 * channels)
    halves = [shape((channels // 2 * SLOTS, channels), F32)] * 2
    conv_flops = 3 * 2 * 4 * 256 * 36 * channels * 2 * channels
    small = shape((devices, 2, channels), F32)

    latent, stats_first = call(
        planes_kernel, [shape(block, BF16), small], [VMEM] * 2, (latent, par)
    )
    around = with_columns(flags, latent, halo(latent, 1))
    (cotangent,) = call(planes_kernel, [shape(block, BF16)], [VMEM], (cotangent,))
    around_c = with_columns(flags, cotangent, halo(cotangent, -1))
    stats_first = all_stats(stats_first, count / devices)
    (weight_first,) = call(weight_forward_kernel, [shape(taps, BF16)], [VMEM], (conv_first,))
    (weight_second_t,) = call(weight_back_kernel, [shape(taps, BF16)], [VMEM], (conv_second,))
    (weight_first_t,) = call(weight_back_kernel, [shape(taps, BF16)], [VMEM], (conv_first,))

    hidden, stats_second, stack_first = call(
        functools.partial(conv_first_kernel, count=count),
        [shape(block, F32), small, shape(stack, BF16)],
        [SMEM] + [VMEM] * 12,
        (flags, latent, *around, par, stats_first, weight_first, token(around_c[0])),
        flops=conv_flops,
        transcendentals=3 * latent.size,
    )
    stats_second = shared(stats_second)
    grad_second, stack_c = call(
        conv_back_kernel,
        [shape(block, F32), shape(stack, BF16)],
        [SMEM] + [VMEM] * 9,
        (flags, cotangent, *around_c, weight_second_t),
        flops=conv_flops,
    )
    act_second, scaled, sums = call(
        functools.partial(norm_second_kernel, count=count),
        [shape(block, BF16), shape(block, F32), small],
        [VMEM] * 4,
        (hidden, grad_second, par, stats_second),
        transcendentals=latent.size,
    )
    sums = shared(sums)
    halves_second = call(
        weight_second_kernel,
        halves,
        [SMEM] + [VMEM] * 2,
        (flags, stack_c, act_second),
        scratch=[pltpu.VMEM((rows * cols, frames * channels), BF16)],
        flops=conv_flops,
    )
    (hidden_grad,) = call(
        functools.partial(hidden_grad_kernel, count=count),
        [shape(block, BF16)],
        [VMEM] * 6,
        (hidden, scaled, par, stats_second, sums, token(halves_second[0])),
    )
    around = halo(hidden_grad, -1)
    halves_first = call(
        weight_first_kernel,
        halves,
        [SMEM] + [VMEM] * 2,
        (flags, stack_first, hidden_grad),
        scratch=[pltpu.VMEM((rows * cols, frames * channels), BF16)],
        flops=conv_flops,
    )
    halves_second, halves_first = (
        [v.reshape(channels // 2, SLOTS, channels) for v in halves] for halves in (halves_second, halves_first)
    )
    weights, sent = scattered(halves_second, halves_first)
    around = with_columns(flags, hidden_grad, around, (sent,))
    scaled, sums_first = call(
        functools.partial(first_grad_kernel, count=count),
        [shape(block, F32), small],
        [SMEM] + [VMEM] * 12,
        (flags, hidden_grad, *around, weight_first_t, latent, par, stats_first),
        scratch=[pltpu.VMEM(stack, BF16)],
        flops=conv_flops,
        transcendentals=latent.size,
    )
    weights = summed(weights, around[:3])
    second, first = gathered(weights, around[3:5], sums_first)
    sums_first = shared(sums_first)
    (decoded_grad,) = call(
        functools.partial(decoded_grad_kernel, count=count),
        [shape((channels, frames, rows, cols), F32)],
        [VMEM] * 6,
        (scaled, latent, cotangent, par, stats_first, sums_first),
    )
    conv_second_grad = joined(flags, second, swapped(second), sums_first)
    conv_first_grad = joined(flags, first, swapped(first), sums_first)
    return decoded_grad, conv_first_grad, conv_second_grad


def solution(mesh):
    block = P(None, "tm", "height", "width")
    return jax.shard_map(
        shards,
        mesh=mesh,
        in_specs=(block, P(), block, P(), P(), P(), P(), P(), P()),
        out_specs=(block, P(), P()),
        check_vma=False,
    )
```

```python
import functools

import jax
import jax.numpy as jnp
from jax import lax
from jax.experimental import pallas as pl
from jax.experimental.pallas import tpu as pltpu
from jax.sharding import PartitionSpec as P

epsilon = 1e-05
F32 = jnp.float32
BF16 = jnp.bfloat16
GROUP = 4
TAPS, SLOTS = 27, 32
FULL = 32760.0
LN2 = 0.6931471805599453
VMEM = pl.BlockSpec(memory_space=pltpu.VMEM)
SMEM = pl.BlockSpec(memory_space=pltpu.SMEM)


def call(body, outs, specs, args, scratch=(), flops=0, transcendentals=0, limit=20):
    moved = sum(a.size * a.dtype.itemsize for a in args)
    moved += sum(o.size * o.dtype.itemsize for o in outs)
    return pl.pallas_call(
        body,
        out_shape=tuple(outs),
        in_specs=specs,
        out_specs=tuple(VMEM for _ in outs),
        scratch_shapes=scratch,
        compiler_params=pltpu.CompilerParams(vmem_limit_bytes=limit << 20),
        cost_estimate=pl.CostEstimate(
            flops=flops, bytes_accessed=moved, transcendentals=transcendentals
        ),
    )(*args)


def shape(dims, dtype):
    return jax.ShapeDtypeStruct(dims, dtype)


def group_sums(acc):
    rows = acc.shape[0]
    row = lax.broadcasted_iota(jnp.int32, acc.shape, 0)
    step = 1
    while step < GROUP:
        up = pltpu.roll(acc, rows - step, axis=0)
        down = pltpu.roll(acc, step, axis=0)
        acc = acc + jnp.where((row & step) == 0, up, down)
        step *= 2
    return jnp.sum(acc, axis=1, keepdims=True)


def lanes_of(plane):
    total = plane[:, :128]
    for start in range(128, plane.shape[1], 128):
        total = total + plane[:, start : start + 128]
    return total


def as_rows(first, second):
    channels = first.shape[0]
    lane = lax.broadcasted_iota(jnp.int32, (channels, 128), 1)
    both = jnp.where(lane == 0, first, jnp.where(lane == 1, second, 0.0))
    return jnp.transpose(both)[:2]


def local_stats(planes, count):
    acc = None
    for plane in planes:
        part = lanes_of(plane())
        acc = part if acc is None else acc + part
    mean = group_sums(acc) / count
    acc = None
    for plane in planes:
        off = plane() - mean
        part = lanes_of(off * off)
        acc = part if acc is None else acc + part
    return mean, group_sums(acc)


def put_rows(out_ref, first, second):
    out_ref[...] = jnp.broadcast_to(as_rows(first, second)[None], out_ref.shape)


def combined(st_ref, count):
    devices = st_ref.shape[0]
    mean = jnp.mean(st_ref[:, 0:1], axis=0)
    off = st_ref[:, 0:1] - mean[None]
    squares = jnp.sum(st_ref[:, 1:2] + off * off * (count / devices), axis=0)
    return mean, squares / count


def columns_of(*rows):
    rows = list(rows) + [jnp.zeros_like(rows[0])] * (8 - len(rows))
    cols = jnp.transpose(jnp.concatenate(rows, axis=0))
    return [cols[:, i : i + 1] for i in range(8)]


def sigmoid(value):
    return 0.5 + 0.5 * jnp.tanh(0.5 * value)


def planes_kernel(latent_ref, cotangent_ref, par_ref, latent_out, cotangent_out, down_ref, up_ref, st_ref):
    _, frames, rows, cols = latent_ref.shape
    for which, (natural, out) in enumerate(((latent_ref, latent_out), (cotangent_ref, cotangent_out))):
        for row in range(rows):
            for frame in range(frames):
                plane = natural[:, frame, row, :]
                out[row, frame] = plane
                if row == rows - 1:
                    down_ref[which, frame] = plane
                if row == 0:
                    up_ref[which, frame] = plane
    scale = columns_of(par_ref[0:1])[0]
    planes = [
        functools.partial(lambda r, t: latent_out[r, t].astype(F32) * scale, r, t)
        for r in range(rows)
        for t in range(frames)
    ]
    put_rows(st_ref, *local_stats(planes, float(GROUP * rows * frames * cols)))


def rows_kernel(above_ref, below_ref, *outs):
    for which, out in enumerate(outs):
        out[0] = above_ref[which]
        out[1] = below_ref[which]


def source(own, other, near, far, other_first):
    def at(row, frame):
        is_other = (frame < 2) == other_first
        if row == 0 or row == own.shape[0] + 1:
            return (far if is_other else near), (0 if row == 0 else 1, frame % 2)
        return (other if is_other else own), (row - 1, frame % 2)

    return at


def edges_kernel(flag_ref, first_ref, second_ref, *refs):
    planes, out_ref = (first_ref, second_ref), refs[-1]
    is_first = flag_ref[3] == 0
    channels = planes[0].shape[2]
    lane = lax.broadcasted_iota(jnp.int32, (channels, 128), 1)
    acc = jnp.zeros((channels, 128), F32)
    number = 0
    for ref in planes:
        for row in range(ref.shape[0]):
            for frame in range(ref.shape[1]):
                last = pltpu.roll(ref[row, frame, :, -128:].astype(F32), 1, axis=1)
                edge = jnp.where(is_first, last, ref[row, frame, :, :128].astype(F32))
                moved = pltpu.roll(edge, number, axis=1) if number else edge
                acc = jnp.where(lane == number, moved, acc)
                number += 1
    out_ref[...] = acc.astype(BF16)


def edge_lane(row, frame, rows, other_first):
    is_other = int((frame < 2) == other_first)
    if row == 0 or row == rows + 1:
        return 1, 4 * is_other + 2 * int(row > 0) + frame % 2
    return 0, 2 * rows * is_other + 2 * (row - 1) + frame % 2


def fill_stack(stack, row, frame, plane, column, on_left, on_right):
    channels, cols = plane.shape
    lane = lax.broadcasted_iota(jnp.int32, (channels, cols), 1)
    column = column.astype(F32)
    left = jnp.where(lane == 0, (column * on_left).astype(BF16), pltpu.roll(plane, 1, axis=1))
    right = jnp.where(lane == cols - 1, (column * on_right).astype(BF16), pltpu.roll(plane, cols - 1, axis=1))
    stack[row, frame, 0:channels] = left
    stack[row, frame, channels : 2 * channels] = plane
    stack[row, frame, 2 * channels : 3 * channels] = right


def sides(flag_ref):
    on_left = (flag_ref[3] != 0).astype(F32)
    on_right = (flag_ref[3] == 0).astype(F32)
    return on_left, on_right


def conv_rows(stack, weight, row):
    three = stack[row : row + 3].reshape(weight.shape[1], stack.shape[3])
    return jnp.dot(weight[...], three, preferred_element_type=F32)


def norm_columns(par_ref, st_ref, count, gain_row):
    par = par_ref[...]
    mean, variance = combined(st_ref, count)
    inverse = 1.0 / jnp.sqrt(variance + epsilon)
    gain = par[gain_row : gain_row + 1]
    shift = par[gain_row + 1 : gain_row + 2]
    return columns_of(mean, inverse, gain, shift, par[0:1])[:5]


def conv_first_kernel(
    flag_ref, own, past, near, far, edge_ref, rim_ref, par_ref, st_ref, weight, after, hidden_ref, st_out, stack_ref,
    *, count
):
    rows, frames, channels, cols = own.shape
    at = source(own, past, near, far, True)
    mean, inverse, gain, shift, scale = norm_columns(par_ref, st_ref, count, 1)

    def act(latent):
        pre = (latent.astype(F32) * scale - mean) * inverse * gain + shift
        return pre * sigmoid(pre)

    has_past = flag_ref[0].astype(F32)
    has_top = flag_ref[1].astype(F32)
    has_bottom = flag_ref[2].astype(F32)
    on_left, on_right = sides(flag_ref)
    edges = (act(edge_ref[...]), act(rim_ref[...]))
    for row in range(rows + 2):
        for frame in range(4):
            ref, index = at(row, frame)
            which, number = edge_lane(row, frame, rows, True)
            plane = act(ref[index])
            column = edges[which][:, number : number + 1]
            factor = None
            if frame < 2:
                factor = has_past
            if row in (0, rows + 1):
                beside = has_top if row == 0 else has_bottom
                factor = beside if factor is None else factor * beside
            if factor is not None:
                plane = plane * factor
                column = column * factor
            fill_stack(stack_ref, row, frame, plane.astype(BF16), column, on_left, on_right)
    for row in range(rows):
        out = conv_rows(stack_ref, weight, row)
        for frame in range(frames):
            hidden_ref[row, frame] = out[frame * channels : (frame + 1) * channels]
    planes = [
        functools.partial(lambda r, t: hidden_ref[r, t], r, t) for r in range(rows) for t in range(frames)
    ]
    put_rows(st_out, *local_stats(planes, float(GROUP * rows * frames * cols)))


def fill_future(stack, flag_ref, own, future, near, far, edge_ref, rim_ref):
    rows = own.shape[0]
    at = source(own, future, near, far, False)
    on_left, on_right = sides(flag_ref)
    edges = (edge_ref[...], rim_ref[...])
    for row in range(rows + 2):
        for frame in range(4):
            ref, index = at(row, frame)
            which, number = edge_lane(row, frame, rows, False)
            fill_stack(stack, row, frame, ref[index], edges[which][:, number : number + 1], on_left, on_right)


def conv_back_kernel(flag_ref, *refs):
    weight, grad_ref, stack_ref = refs[-3:]
    rows, frames, channels, _ = grad_ref.shape
    fill_future(stack_ref, flag_ref, *refs[:-3])
    for row in range(rows):
        out = conv_rows(stack_ref, weight, row)
        for frame in range(frames):
            grad_ref[row, frame] = out[frame * channels : (frame + 1) * channels]


def norm_second_kernel(hidden, grad, par_ref, st_ref, act_ref, scaled_ref, sums_ref, *, count):
    rows, frames, channels, cols = hidden.shape
    mean, inverse, gain, shift, _ = norm_columns(par_ref, st_ref, count, 3)
    first = jnp.zeros((channels, 128), F32)
    second = jnp.zeros((channels, 128), F32)
    for row in range(rows):
        for frame in range(frames):
            normed = (hidden[row, frame] - mean) * inverse
            pre = normed * gain + shift
            sig = sigmoid(pre)
            act = pre * sig
            act_ref[row, frame] = act.astype(BF16)
            scaled = grad[row, frame] * (sig + act * (1.0 - sig)) * gain
            scaled_ref[row, frame] = scaled
            first = first + lanes_of(scaled)
            second = second + lanes_of(scaled * normed)
    put_rows(sums_ref, group_sums(first), group_sums(second))


def hidden_grad_kernel(
    hidden, scaled, par_ref, st_ref, sums_ref, after, out_ref, down_ref, up_ref, *, count
):
    rows, frames, channels, cols = hidden.shape
    mean, inverse, _, _, _ = norm_columns(par_ref, st_ref, count, 3)
    means = jnp.sum(sums_ref[...], axis=0) / count
    first, second = columns_of(means[0:1], means[1:2])[:2]
    for row in range(rows):
        for frame in range(frames):
            normed = (hidden[row, frame] - mean) * inverse
            plane = (inverse * (scaled[row, frame] - first - normed * second)).astype(BF16)
            out_ref[row, frame] = plane
            if row == rows - 1:
                down_ref[0, frame] = plane
            if row == 0:
                up_ref[0, frame] = plane


def put_halves(flag_ref, mine_ref, theirs_ref, tap, block):
    half = block.shape[0] // 2
    here = pl.ds(tap, half, stride=SLOTS)
    upper, lower = block[:half], block[half:]
    is_first = flag_ref[3] == 0
    mine_ref[here, :] = jnp.where(is_first, upper, lower)
    theirs_ref[here, :] = jnp.where(is_first, lower, upper)


def encoded(value):
    slot = lax.broadcasted_iota(jnp.int32, value.shape, 1)
    value = jnp.where(slot < TAPS, value, 0.0)
    top = jnp.max(jnp.abs(value), axis=1, keepdims=True)
    power = jnp.ceil(jnp.log(jnp.maximum(top, 1e-30)) * (1.0 / LN2))
    number = jnp.round(value * (FULL * jnp.exp(power * -LN2)))
    return jnp.where(slot < TAPS, number, power).astype(jnp.int32).astype(jnp.int16)


def decoded_value(number):
    number = number.astype(jnp.int32).astype(F32)
    return number * (jnp.exp(number[:, SLOTS - 1 : SLOTS] * LN2) * (1.0 / FULL))


def first_scatter_kernel(*refs):
    out_ref = refs[-1]
    chunks, _, rows = out_ref.shape[:3]
    for which in range(2):
        mine_ref, other_ref = refs[2 * which], refs[2 * which + 1]
        for chunk in range(chunks):
            here = slice(chunk * rows, (chunk + 1) * rows)
            out_ref[chunk, which] = encoded(mine_ref[here] + other_ref[here])


def second_scatter_kernel(received, *refs):
    out_ref = refs[-1]
    chunks, _, rows = out_ref.shape[:3]
    for which in range(2):
        for chunk in range(chunks):
            here = slice(chunk * rows, (chunk + 1) * rows)
            total = decoded_value(received[0, which, here])
            for number in range(1, received.shape[0]):
                total = total + decoded_value(received[number, which, here])
            out_ref[chunk, which] = encoded(total)


def total_kernel(received, *refs):
    out_ref = refs[-1]
    for which in range(2):
        total = decoded_value(received[0, which])
        for number in range(1, received.shape[0]):
            total = total + decoded_value(received[number, which])
        total = encoded(total)
        for copy in range(out_ref.shape[0]):
            out_ref[copy, which] = total


def copies_kernel(value, after, *outs):
    for which, out_ref in enumerate(outs):
        for copy in range(out_ref.shape[0]):
            out_ref[copy] = value[:, which]


def join_kernel(flag_ref, mine_ref, theirs_ref, out_ref, first_ref, second_ref):
    half, _, channels = mine_ref.shape
    is_first = flag_ref[3] == 0
    first_ref[...] = decoded_value(jnp.where(is_first, mine_ref[...], theirs_ref[...])).reshape(first_ref.shape)
    second_ref[...] = decoded_value(jnp.where(is_first, theirs_ref[...], mine_ref[...])).reshape(second_ref.shape)
    for tap in range(TAPS):
        here = slice(tap * channels, (tap + 1) * channels)
        out_ref[:half, here] = first_ref[pl.ds(tap, half, stride=SLOTS), :]
        out_ref[half:, here] = second_ref[pl.ds(tap, half, stride=SLOTS), :]


def weight_second_kernel(flag_ref, stack_ref, act_ref, mine_ref, theirs_ref, right_ref):
    rows, frames, channels, cols = act_ref.shape
    for row in range(rows):
        right_ref[row * cols : (row + 1) * cols] = jnp.transpose(
            act_ref[row].reshape(frames * channels, cols)
        )
    right = right_ref[...]
    for down in range(3):
        parts = []
        for frame in range(4):
            left = jnp.concatenate([stack_ref[down + row, frame] for row in range(rows)], axis=1)
            parts.append(jnp.dot(left, right, preferred_element_type=F32))
        for kt in range(3):
            term = parts[2 - kt][:, :channels] + parts[3 - kt][:, channels:]
            for across in range(3):
                tap = 9 * kt + 3 * (2 - down) + (2 - across)
                put_halves(flag_ref, mine_ref, theirs_ref, tap, term[across * channels : (across + 1) * channels])


def weight_first_kernel(flag_ref, stack_ref, grad_ref, mine_ref, theirs_ref, right_ref):
    rows, frames, channels, cols = grad_ref.shape
    for row in range(rows):
        right_ref[row * cols : (row + 1) * cols] = jnp.transpose(
            grad_ref[row].reshape(frames * channels, cols)
        )
    right = right_ref[...]
    for down in range(3):
        parts = []
        for frame in range(4):
            left = jnp.concatenate([stack_ref[down + row, frame] for row in range(rows)], axis=1)
            parts.append(jnp.dot(left, right, preferred_element_type=F32))
        for kt in range(3):
            term = parts[kt][:, :channels] + parts[kt + 1][:, channels:]
            for across in range(3):
                tap = 9 * kt + 3 * down + across
                block = jnp.transpose(term[across * channels : (across + 1) * channels])
                put_halves(flag_ref, mine_ref, theirs_ref, tap, block)


def first_grad_kernel(flag_ref, *refs, count):
    weight, latent, par_ref, st_ref, scaled_ref, sums_ref, stack_ref = refs[-7:]
    rows, frames, channels, cols = latent.shape
    mean, inverse, gain, shift, scale = norm_columns(par_ref, st_ref, count, 1)
    fill_future(stack_ref, flag_ref, *refs[:-7])
    first = jnp.zeros((channels, 128), F32)
    second = jnp.zeros((channels, 128), F32)
    for row in range(rows):
        out = conv_rows(stack_ref, weight, row)
        for frame in range(frames):
            grad = out[frame * channels : (frame + 1) * channels]
            normed = (latent[row, frame].astype(F32) * scale - mean) * inverse
            pre = normed * gain + shift
            sig = sigmoid(pre)
            scaled = grad * (sig + pre * sig * (1.0 - sig)) * gain
            scaled_ref[row, frame] = scaled
            first = first + lanes_of(scaled)
            second = second + lanes_of(scaled * normed)
    put_rows(sums_ref, group_sums(first), group_sums(second))


def decoded_grad_kernel(scaled, latent, cotangent, par_ref, st_ref, sums_ref, out_ref, token_ref, *, count):
    token_ref[...] = jnp.zeros(token_ref.shape, F32)
    rows, frames, channels, cols = latent.shape
    mean, inverse, _, _, scale = norm_columns(par_ref, st_ref, count, 1)
    means = jnp.sum(sums_ref[...], axis=0) / count
    first, second = columns_of(means[0:1], means[1:2])[:2]
    for row in range(rows):
        for frame in range(frames):
            normed = (latent[row, frame].astype(F32) * scale - mean) * inverse
            out_ref[:, frame, row, :] = cotangent[row, frame].astype(F32) + inverse * (
                scaled[row, frame] - first - normed * second
            )


def weight_forward_kernel(weight, out_ref):
    channels = weight.shape[0]
    wide = 3 * channels
    for t in range(2):
        for kr in range(3):
            for f in range(4):
                kt = f - t
                here = slice((kr * 4 + f) * wide, (kr * 4 + f + 1) * wide)
                if 0 <= kt < 3:
                    tap = 3 * kt + kr
                    block = weight[:, tap * wide : (tap + 1) * wide]
                else:
                    block = jnp.zeros((channels, wide), BF16)
                out_ref[t * channels : (t + 1) * channels, here] = block


def weight_back_kernel(weight, out_ref):
    channels = weight.shape[0]
    for down in range(3):
        for across in range(3):
            blocks = [
                jnp.transpose(
                    weight[
                        :,
                        (9 * kt + 3 * (2 - down) + 2 - across) * channels : (9 * kt + 3 * (2 - down) + 3 - across)
                        * channels,
                    ]
                )
                for kt in range(3)
            ]
            for t in range(2):
                for f in range(4):
                    kt = t + 2 - f
                    start = ((down * 4 + f) * 3 + across) * channels
                    block = blocks[kt] if 0 <= kt < 3 else jnp.zeros((channels, channels), BF16)
                    out_ref[t * channels : (t + 1) * channels, start : start + channels] = block


def shifted(value, axis, steps):
    count = lax.axis_size(axis)
    initial, last = max(0, -steps), min(count, count - steps)
    return lax.ppermute(value, axis, [(source, source + steps) for source in range(initial, last)])


def exchanged(value, axis):
    return lax.all_to_all(value, axis, 0, 0, tiled=True)


def all_stats(value, count):
    value = value[0]
    for axis in ("tm", "height", "width"):
        size = lax.axis_size(axis)
        step = 1
        while step < size:
            wide = 4 if 4 * step <= size else 2
            parts = [value] + [
                lax.ppermute(value, axis, [(i, i ^ (step * k)) for i in range(size)]) for k in range(1, wide)
            ]
            while len(parts) > 1:
                joined = []
                for a, b in zip(parts[::2], parts[1::2]):
                    gap = a[0:1] - b[0:1]
                    mean = 0.5 * (a[0:1] + b[0:1])
                    joined.append(jnp.concatenate([mean, a[1:2] + b[1:2] + gap * gap * (0.5 * count)], axis=0))
                parts = joined
                count = 2.0 * count
            (value,) = parts
            step *= wide
    return value[None]


def shared(value):
    return exchanged(value, ("tm", "height", "width"))


def swapped(value):
    return lax.ppermute(value, "width", [(0, 1), (1, 0)])


def scattered(second, first):
    half, _, channels = second[0].shape
    by_height = lax.axis_size("height")
    terms = [part for mine, theirs in (second, first) for part in (mine, swapped(theirs))]
    (value,) = call(
        first_scatter_kernel,
        [shape((by_height, 2, half // by_height, SLOTS, channels), jnp.int16)],
        [VMEM] * 4,
        terms,
    )
    return exchanged(value, "height"), value


def summed(value, after):
    by_tm = lax.axis_size("tm")
    _, _, rows, _, channels = value.shape
    (value,) = call(
        second_scatter_kernel,
        [shape((by_tm, 2, rows // by_tm, SLOTS, channels), jnp.int16)],
        [VMEM] * (1 + len(after)),
        (value, *after),
    )
    return exchanged(value, "tm")


def gathered(value, after, after_last):
    (value,) = call(total_kernel, [shape(value.shape, jnp.int16)], [VMEM] * (1 + len(after)), (value, *after))
    value = exchanged(value, "tm")
    by_height = lax.axis_size("height")
    by_tm, _, rows, _, channels = value.shape
    copies = call(
        copies_kernel,
        [shape((by_height, by_tm, rows, SLOTS, channels), jnp.int16)] * 2,
        [VMEM] * 2,
        (value, after_last),
    )
    return [exchanged(copy, "height").reshape(-1, SLOTS, channels) for copy in copies]


def joined(flags, mine, theirs):
    half, _, channels = mine.shape
    (total,) = call(
        join_kernel,
        [shape((2 * half, TAPS * channels), F32)],
        [SMEM] + [VMEM] * 2,
        (flags, mine, theirs),
        scratch=[pltpu.VMEM((half * SLOTS, channels), F32)] * 2,
    )
    return total


def edges(flags, planes, after):
    channels = planes[0].shape[2]
    args = (*planes, *after)
    (columns,) = call(edges_kernel, [shape((channels, 128), BF16)], [SMEM] + [VMEM] * len(args), (flags, *args))
    return columns


def row_halos(down, up):
    above, below = shifted(down, "height", 1), shifted(up, "height", -1)
    return call(rows_kernel, [shape((2, *down.shape[1:]), BF16)] * down.shape[0], [VMEM] * 2, (above, below))


def halo(own, near, steps):
    return shifted(own, "tm", steps), near, shifted(near, "tm", steps)


def with_columns(flags, own, around, after=()):
    edge = swapped(edges(flags, (own, around[0]), after))
    rim = swapped(edges(flags, around[1:], after))
    return *around, edge, rim


def shards(
    latent,
    exponents,
    cotangent,
    conv_first,
    conv_second,
    gain_first,
    shift_first,
    gain_second,
    shift_second,
):
    channels, frames, rows, cols = latent.shape
    groups = exponents.shape[0]
    devices = lax.axis_size("tm") * lax.axis_size("height") * lax.axis_size("width")
    count = float(channels // groups * frames * rows * cols * devices)
    tm, height, width = (lax.axis_index(axis) for axis in ("tm", "height", "width"))
    flags = jnp.stack(
        [
            (tm > 0).astype(jnp.int32),
            (height > 0).astype(jnp.int32),
            (height < lax.axis_size("height") - 1).astype(jnp.int32),
            width.astype(jnp.int32),
        ]
    )
    scale = jnp.repeat(jnp.exp2(exponents.astype(F32)), channels // groups)
    zeros = jnp.zeros_like(scale)
    par = jnp.stack([scale, gain_first, shift_first, gain_second, shift_second, zeros, zeros, zeros])
    block = (rows, frames, channels, cols)
    stack = (rows + 2, 4, 3 * channels, cols)
    taps = (2 * channels, 36 * channels)
    halves = [shape((channels // 2 * SLOTS, channels), F32)] * 2
    conv_flops = 3 * 2 * 4 * 256 * 36 * channels * 2 * channels
    small = shape((devices, 2, channels), F32)

    message = shape((2, frames, channels, cols), BF16)
    latent, cotangent, down, up, stats_first = call(
        planes_kernel,
        [shape(block, BF16), shape(block, BF16), message, message, small],
        [VMEM] * 3,
        (latent, cotangent, par),
    )
    near, near_c = row_halos(down, up)
    around = with_columns(flags, latent, halo(latent, near, 1))
    around_c = halo(cotangent, near_c, -1)
    stats_first = all_stats(stats_first, count / devices)
    (weight_first,) = call(weight_forward_kernel, [shape(taps, BF16)], [VMEM], (conv_first,))
    (weight_second_t,) = call(weight_back_kernel, [shape(taps, BF16)], [VMEM], (conv_second,))
    (weight_first_t,) = call(weight_back_kernel, [shape(taps, BF16)], [VMEM], (conv_first,))

    hidden, stats_second, stack_first = call(
        functools.partial(conv_first_kernel, count=count),
        [shape(block, F32), small, shape(stack, BF16)],
        [SMEM] + [VMEM] * 10,
        (flags, latent, *around, par, stats_first, weight_first, around_c[0]),
        flops=conv_flops,
        transcendentals=3 * latent.size,
    )
    around_c = with_columns(flags, cotangent, around_c, (stats_second,))
    stats_second = shared(stats_second)
    grad_second, stack_c = call(
        conv_back_kernel,
        [shape(block, F32), shape(stack, BF16)],
        [SMEM] + [VMEM] * 7,
        (flags, cotangent, *around_c, weight_second_t),
        flops=conv_flops,
    )
    act_second, scaled, sums = call(
        functools.partial(norm_second_kernel, count=count),
        [shape(block, BF16), shape(block, F32), small],
        [VMEM] * 4,
        (hidden, grad_second, par, stats_second),
        transcendentals=latent.size,
    )
    sums = shared(sums)
    halves_second = call(
        weight_second_kernel,
        halves,
        [SMEM] + [VMEM] * 2,
        (flags, stack_c, act_second),
        scratch=[pltpu.VMEM((rows * cols, frames * channels), BF16)],
        flops=conv_flops,
    )
    message = shape((1, frames, channels, cols), BF16)
    hidden_grad, down, up = call(
        functools.partial(hidden_grad_kernel, count=count),
        [shape(block, BF16), message, message],
        [VMEM] * 6,
        (hidden, scaled, par, stats_second, sums, halves_second[0]),
    )
    (near,) = row_halos(down, up)
    around = halo(hidden_grad, near, -1)
    halves_first = call(
        weight_first_kernel,
        halves,
        [SMEM] + [VMEM] * 2,
        (flags, stack_first, hidden_grad),
        scratch=[pltpu.VMEM((rows * cols, frames * channels), BF16)],
        flops=conv_flops,
    )
    halves_second, halves_first = (
        [v.reshape(channels // 2, SLOTS, channels) for v in halves] for halves in (halves_second, halves_first)
    )
    weights, sent = scattered(halves_second, halves_first)
    around = with_columns(flags, hidden_grad, around, (sent,))
    scaled, sums_first = call(
        functools.partial(first_grad_kernel, count=count),
        [shape(block, F32), small],
        [SMEM] + [VMEM] * 10,
        (flags, hidden_grad, *around, weight_first_t, latent, par, stats_first),
        scratch=[pltpu.VMEM(stack, BF16)],
        flops=conv_flops,
        transcendentals=latent.size,
    )
    weights = summed(weights, around[:2])
    sums_first = shared(sums_first)
    decoded_grad, token = call(
        functools.partial(decoded_grad_kernel, count=count),
        [shape((channels, frames, rows, cols), F32), shape((8, 128), F32)],
        [VMEM] * 6,
        (scaled, latent, cotangent, par, stats_first, sums_first),
    )
    second, first = gathered(weights, (sums_first,), token)
    conv_second_grad = joined(flags, second, swapped(second))
    conv_first_grad = joined(flags, first, swapped(first))
    return decoded_grad, conv_first_grad, conv_second_grad


def solution(mesh):
    block = P(None, "tm", "height", "width")
    return jax.shard_map(
        shards,
        mesh=mesh,
        in_specs=(block, P(), block, P(), P(), P(), P(), P(), P()),
        out_specs=(block, P(), P()),
        check_vma=False,
    )
```

```python
import functools

import jax
import jax.numpy as jnp
from jax import lax
from jax.experimental import pallas as pl
from jax.experimental.pallas import tpu as pltpu
from jax.sharding import PartitionSpec as P

epsilon = 1e-05
F32 = jnp.float32
BF16 = jnp.bfloat16
GROUP = 4
TAPS, SLOTS = 27, 32
FULL = 32760.0
LN2 = 0.6931471805599453
VMEM = pl.BlockSpec(memory_space=pltpu.VMEM)
SMEM = pl.BlockSpec(memory_space=pltpu.SMEM)


def call(body, outs, specs, args, scratch=(), flops=0, transcendentals=0, limit=20):
    moved = sum(a.size * a.dtype.itemsize for a in args)
    moved += sum(o.size * o.dtype.itemsize for o in outs)
    return pl.pallas_call(
        body,
        out_shape=tuple(outs),
        in_specs=specs,
        out_specs=tuple(VMEM for _ in outs),
        scratch_shapes=scratch,
        compiler_params=pltpu.CompilerParams(vmem_limit_bytes=limit << 20),
        cost_estimate=pl.CostEstimate(
            flops=flops, bytes_accessed=moved, transcendentals=transcendentals
        ),
    )(*args)


def shape(dims, dtype):
    return jax.ShapeDtypeStruct(dims, dtype)


def group_sums(acc):
    rows = acc.shape[0]
    row = lax.broadcasted_iota(jnp.int32, acc.shape, 0)
    step = 1
    while step < GROUP:
        up = pltpu.roll(acc, rows - step, axis=0)
        down = pltpu.roll(acc, step, axis=0)
        acc = acc + jnp.where((row & step) == 0, up, down)
        step *= 2
    return jnp.sum(acc, axis=1, keepdims=True)


def lanes_of(plane):
    total = plane[:, :128]
    for start in range(128, plane.shape[1], 128):
        total = total + plane[:, start : start + 128]
    return total


def as_rows(first, second):
    channels = first.shape[0]
    lane = lax.broadcasted_iota(jnp.int32, (channels, 128), 1)
    both = jnp.where(lane == 0, first, jnp.where(lane == 1, second, 0.0))
    return jnp.transpose(both)[:2]


def local_stats(planes, count):
    acc = None
    for plane in planes:
        part = lanes_of(plane())
        acc = part if acc is None else acc + part
    mean = group_sums(acc) / count
    acc = None
    for plane in planes:
        off = plane() - mean
        part = lanes_of(off * off)
        acc = part if acc is None else acc + part
    return mean, group_sums(acc)


def put_rows(out_ref, first, second):
    out_ref[0] = as_rows(first, second)


def combined(st_ref, count):
    return st_ref[0, 0:1], st_ref[0, 1:2] / count


def columns_of(*rows):
    rows = list(rows) + [jnp.zeros_like(rows[0])] * (8 - len(rows))
    cols = jnp.transpose(jnp.concatenate(rows, axis=0))
    return [cols[:, i : i + 1] for i in range(8)]


def sigmoid(value):
    return 0.5 + 0.5 * jnp.tanh(0.5 * value)


def planes_kernel(latent_ref, cotangent_ref, par_ref, latent_out, cotangent_out, down_ref, up_ref, st_ref):
    _, frames, rows, cols = latent_ref.shape
    for which, (natural, out) in enumerate(((latent_ref, latent_out), (cotangent_ref, cotangent_out))):
        for row in range(rows):
            for frame in range(frames):
                plane = natural[:, frame, row, :]
                out[row, frame] = plane
                if row == rows - 1:
                    down_ref[which, frame] = plane
                if row == 0:
                    up_ref[which, frame] = plane
    scale = columns_of(par_ref[0:1])[0]
    planes = [
        functools.partial(lambda r, t: latent_out[r, t].astype(F32) * scale, r, t)
        for r in range(rows)
        for t in range(frames)
    ]
    put_rows(st_ref, *local_stats(planes, float(GROUP * rows * frames * cols)))


def rows_kernel(above_ref, below_ref, *outs):
    for which, out in enumerate(outs):
        out[0] = above_ref[which]
        out[1] = below_ref[which]


def source(own, other, near, far, other_first):
    def at(row, frame):
        is_other = (frame < 2) == other_first
        if row == 0 or row == own.shape[0] + 1:
            return (far if is_other else near), (0 if row == 0 else 1, frame % 2)
        return (other if is_other else own), (row - 1, frame % 2)

    return at


def edges_kernel(flag_ref, first_ref, second_ref, *refs):
    planes, out_ref = (first_ref, second_ref), refs[-1]
    is_first = flag_ref[3] == 0
    channels = planes[0].shape[2]
    lane = lax.broadcasted_iota(jnp.int32, (channels, 128), 1)
    acc = jnp.zeros((channels, 128), F32)
    number = 0
    for ref in planes:
        for row in range(ref.shape[0]):
            for frame in range(ref.shape[1]):
                last = pltpu.roll(ref[row, frame, :, -128:].astype(F32), 1, axis=1)
                edge = jnp.where(is_first, last, ref[row, frame, :, :128].astype(F32))
                moved = pltpu.roll(edge, number, axis=1) if number else edge
                acc = jnp.where(lane == number, moved, acc)
                number += 1
    out_ref[...] = acc.astype(BF16)


def edge_lane(row, frame, rows, other_first):
    is_other = int((frame < 2) == other_first)
    if row == 0 or row == rows + 1:
        return 1, 4 * is_other + 2 * int(row > 0) + frame % 2
    return 0, 2 * rows * is_other + 2 * (row - 1) + frame % 2


def fill_stack(stack, row, frame, plane, column, on_left, on_right):
    channels, cols = plane.shape
    lane = lax.broadcasted_iota(jnp.int32, (channels, cols), 1)
    column = column.astype(F32)
    left = jnp.where(lane == 0, (column * on_left).astype(BF16), pltpu.roll(plane, 1, axis=1))
    right = jnp.where(lane == cols - 1, (column * on_right).astype(BF16), pltpu.roll(plane, cols - 1, axis=1))
    stack[row, frame, 0:channels] = left
    stack[row, frame, channels : 2 * channels] = plane
    stack[row, frame, 2 * channels : 3 * channels] = right


def sides(flag_ref):
    on_left = (flag_ref[3] != 0).astype(F32)
    on_right = (flag_ref[3] == 0).astype(F32)
    return on_left, on_right


def conv_rows(stack, weight, row):
    three = stack[row : row + 3].reshape(weight.shape[1], stack.shape[3])
    return jnp.dot(weight[...], three, preferred_element_type=F32)


def norm_columns(par_ref, st_ref, count, gain_row):
    par = par_ref[...]
    mean, variance = combined(st_ref, count)
    inverse = 1.0 / jnp.sqrt(variance + epsilon)
    gain = par[gain_row : gain_row + 1]
    shift = par[gain_row + 1 : gain_row + 2]
    return columns_of(mean, inverse, gain, shift, par[0:1])[:5]


def conv_first_kernel(
    flag_ref, own, past, near, far, edge_ref, rim_ref, par_ref, st_ref, weight, after, hidden_ref, st_out, stack_ref,
    *, count
):
    rows, frames, channels, cols = own.shape
    at = source(own, past, near, far, True)
    mean, inverse, gain, shift, scale = norm_columns(par_ref, st_ref, count, 1)

    def act(latent):
        pre = (latent.astype(F32) * scale - mean) * inverse * gain + shift
        return pre * sigmoid(pre)

    has_past = flag_ref[0].astype(F32)
    has_top = flag_ref[1].astype(F32)
    has_bottom = flag_ref[2].astype(F32)
    on_left, on_right = sides(flag_ref)
    edges = (act(edge_ref[...]), act(rim_ref[...]))
    for row in range(rows + 2):
        for frame in range(4):
            ref, index = at(row, frame)
            which, number = edge_lane(row, frame, rows, True)
            plane = act(ref[index])
            column = edges[which][:, number : number + 1]
            factor = None
            if frame < 2:
                factor = has_past
            if row in (0, rows + 1):
                beside = has_top if row == 0 else has_bottom
                factor = beside if factor is None else factor * beside
            if factor is not None:
                plane = plane * factor
                column = column * factor
            fill_stack(stack_ref, row, frame, plane.astype(BF16), column, on_left, on_right)
    for row in range(rows):
        out = conv_rows(stack_ref, weight, row)
        for frame in range(frames):
            hidden_ref[row, frame] = out[frame * channels : (frame + 1) * channels]
    planes = [
        functools.partial(lambda r, t: hidden_ref[r, t], r, t) for r in range(rows) for t in range(frames)
    ]
    put_rows(st_out, *local_stats(planes, float(GROUP * rows * frames * cols)))


def fill_future(stack, flag_ref, own, future, near, far, edge_ref, rim_ref):
    rows = own.shape[0]
    at = source(own, future, near, far, False)
    on_left, on_right = sides(flag_ref)
    edges = (edge_ref[...], rim_ref[...])
    for row in range(rows + 2):
        for frame in range(4):
            ref, index = at(row, frame)
            which, number = edge_lane(row, frame, rows, False)
            fill_stack(stack, row, frame, ref[index], edges[which][:, number : number + 1], on_left, on_right)


def conv_back_kernel(flag_ref, *refs):
    weight, grad_ref, stack_ref = refs[-3:]
    rows, frames, channels, _ = grad_ref.shape
    fill_future(stack_ref, flag_ref, *refs[:-3])
    for row in range(rows):
        out = conv_rows(stack_ref, weight, row)
        for frame in range(frames):
            grad_ref[row, frame] = out[frame * channels : (frame + 1) * channels]


def norm_second_kernel(hidden, grad, par_ref, st_ref, act_ref, scaled_ref, sums_ref, *, count):
    rows, frames, channels, cols = hidden.shape
    mean, inverse, gain, shift, _ = norm_columns(par_ref, st_ref, count, 3)
    first = jnp.zeros((channels, 128), F32)
    second = jnp.zeros((channels, 128), F32)
    for row in range(rows):
        for frame in range(frames):
            normed = (hidden[row, frame] - mean) * inverse
            pre = normed * gain + shift
            sig = sigmoid(pre)
            act = pre * sig
            act_ref[row, frame] = act.astype(BF16)
            scaled = grad[row, frame] * (sig + act * (1.0 - sig)) * gain
            scaled_ref[row, frame] = scaled
            first = first + lanes_of(scaled)
            second = second + lanes_of(scaled * normed)
    put_rows(sums_ref, group_sums(first), group_sums(second))


def hidden_grad_kernel(
    hidden, scaled, par_ref, st_ref, sums_ref, after, out_ref, down_ref, up_ref, *, count
):
    rows, frames, channels, cols = hidden.shape
    mean, inverse, _, _, _ = norm_columns(par_ref, st_ref, count, 3)
    means = sums_ref[0] / count
    first, second = columns_of(means[0:1], means[1:2])[:2]
    for row in range(rows):
        for frame in range(frames):
            normed = (hidden[row, frame] - mean) * inverse
            plane = (inverse * (scaled[row, frame] - first - normed * second)).astype(BF16)
            out_ref[row, frame] = plane
            if row == rows - 1:
                down_ref[0, frame] = plane
            if row == 0:
                up_ref[0, frame] = plane


def put_halves(flag_ref, mine_ref, theirs_ref, tap, block):
    half = block.shape[0] // 2
    here = pl.ds(tap, half, stride=SLOTS)
    upper, lower = block[:half], block[half:]
    is_first = flag_ref[3] == 0
    mine_ref[here, :] = jnp.where(is_first, upper, lower)
    theirs_ref[here, :] = jnp.where(is_first, lower, upper)


def encoded(value):
    slot = lax.broadcasted_iota(jnp.int32, value.shape, 1)
    value = jnp.where(slot < TAPS, value, 0.0)
    top = jnp.max(jnp.abs(value), axis=1, keepdims=True)
    power = jnp.ceil(jnp.log(jnp.maximum(top, 1e-30)) * (1.0 / LN2))
    number = jnp.round(value * (FULL * jnp.exp(power * -LN2)))
    return jnp.where(slot < TAPS, number, power).astype(jnp.int32).astype(jnp.int16)


def decoded_value(number):
    number = number.astype(jnp.int32).astype(F32)
    return number * (jnp.exp(number[:, SLOTS - 1 : SLOTS] * LN2) * (1.0 / FULL))


def first_scatter_kernel(flag_ref, *refs, slot):
    me = flag_ref[slot]
    for which in range(2):
        mine, other = refs[2 * which], refs[2 * which + 1]
        for k, out in enumerate(refs[4:]):
            total = mine[me ^ k] + other[me ^ k]
            out[which] = total if k == 0 else encoded(total)


def scatter_kernel(flag_ref, *refs, received, sent, slot):
    me = flag_ref[slot]
    for which in range(2):
        for k, out in enumerate(refs[-sent:]):
            total = refs[0][which, me ^ k]
            for ref in refs[1:received]:
                total = total + decoded_value(ref[which, me ^ k])
            out[which] = total if k == 0 else encoded(total)


def total_kernel(*refs, received):
    for which in range(2):
        total = refs[0][which]
        for ref in refs[1:received]:
            total = total + decoded_value(ref[which])
        refs[-1][which] = encoded(total)


def split_kernel(flag_ref, *refs, received, slot):
    me = flag_ref[slot]
    for which in range(2):
        for k, ref in enumerate(refs[:received]):
            refs[which - 2][me ^ k] = ref[which]


def gather_kernel(flag_ref, *refs, slot):
    me = flag_ref[slot]
    for k, ref in enumerate(refs[:-1]):
        refs[-1][me ^ k] = ref[...]


def join_kernel(flag_ref, mine_ref, theirs_ref, out_ref, first_ref, second_ref):
    half, _, channels = mine_ref.shape
    is_first = flag_ref[3] == 0
    first_ref[...] = decoded_value(jnp.where(is_first, mine_ref[...], theirs_ref[...])).reshape(first_ref.shape)
    second_ref[...] = decoded_value(jnp.where(is_first, theirs_ref[...], mine_ref[...])).reshape(second_ref.shape)
    for tap in range(TAPS):
        here = slice(tap * channels, (tap + 1) * channels)
        out_ref[:half, here] = first_ref[pl.ds(tap, half, stride=SLOTS), :]
        out_ref[half:, here] = second_ref[pl.ds(tap, half, stride=SLOTS), :]


def weight_second_kernel(flag_ref, stack_ref, act_ref, mine_ref, theirs_ref, right_ref):
    rows, frames, channels, cols = act_ref.shape
    for row in range(rows):
        right_ref[row * cols : (row + 1) * cols] = jnp.transpose(
            act_ref[row].reshape(frames * channels, cols)
        )
    right = right_ref[...]
    for down in range(3):
        parts = []
        for frame in range(4):
            left = jnp.concatenate([stack_ref[down + row, frame] for row in range(rows)], axis=1)
            parts.append(jnp.dot(left, right, preferred_element_type=F32))
        for kt in range(3):
            term = parts[2 - kt][:, :channels] + parts[3 - kt][:, channels:]
            for across in range(3):
                tap = 9 * kt + 3 * (2 - down) + (2 - across)
                put_halves(flag_ref, mine_ref, theirs_ref, tap, term[across * channels : (across + 1) * channels])


def weight_first_kernel(flag_ref, stack_ref, grad_ref, mine_ref, theirs_ref, right_ref):
    rows, frames, channels, cols = grad_ref.shape
    for row in range(rows):
        right_ref[row * cols : (row + 1) * cols] = jnp.transpose(
            grad_ref[row].reshape(frames * channels, cols)
        )
    right = right_ref[...]
    for down in range(3):
        parts = []
        for frame in range(4):
            left = jnp.concatenate([stack_ref[down + row, frame] for row in range(rows)], axis=1)
            parts.append(jnp.dot(left, right, preferred_element_type=F32))
        for kt in range(3):
            term = parts[kt][:, :channels] + parts[kt + 1][:, channels:]
            for across in range(3):
                tap = 9 * kt + 3 * down + across
                block = jnp.transpose(term[across * channels : (across + 1) * channels])
                put_halves(flag_ref, mine_ref, theirs_ref, tap, block)


def first_grad_kernel(flag_ref, *refs, count):
    weight, latent, par_ref, st_ref, scaled_ref, sums_ref, stack_ref = refs[-7:]
    rows, frames, channels, cols = latent.shape
    mean, inverse, gain, shift, scale = norm_columns(par_ref, st_ref, count, 1)
    fill_future(stack_ref, flag_ref, *refs[:-7])
    first = jnp.zeros((channels, 128), F32)
    second = jnp.zeros((channels, 128), F32)
    for row in range(rows):
        out = conv_rows(stack_ref, weight, row)
        for frame in range(frames):
            grad = out[frame * channels : (frame + 1) * channels]
            normed = (latent[row, frame].astype(F32) * scale - mean) * inverse
            pre = normed * gain + shift
            sig = sigmoid(pre)
            scaled = grad * (sig + pre * sig * (1.0 - sig)) * gain
            scaled_ref[row, frame] = scaled
            first = first + lanes_of(scaled)
            second = second + lanes_of(scaled * normed)
    put_rows(sums_ref, group_sums(first), group_sums(second))


def decoded_grad_kernel(scaled, latent, cotangent, par_ref, st_ref, sums_ref, out_ref, token_ref, *, count):
    token_ref[...] = jnp.zeros(token_ref.shape, F32)
    rows, frames, channels, cols = latent.shape
    mean, inverse, _, _, scale = norm_columns(par_ref, st_ref, count, 1)
    means = sums_ref[0] / count
    first, second = columns_of(means[0:1], means[1:2])[:2]
    for row in range(rows):
        for frame in range(frames):
            normed = (latent[row, frame].astype(F32) * scale - mean) * inverse
            out_ref[:, frame, row, :] = cotangent[row, frame].astype(F32) + inverse * (
                scaled[row, frame] - first - normed * second
            )


def weight_forward_kernel(weight, out_ref):
    channels = weight.shape[0]
    wide = 3 * channels
    for t in range(2):
        for kr in range(3):
            for f in range(4):
                kt = f - t
                here = slice((kr * 4 + f) * wide, (kr * 4 + f + 1) * wide)
                if 0 <= kt < 3:
                    tap = 3 * kt + kr
                    block = weight[:, tap * wide : (tap + 1) * wide]
                else:
                    block = jnp.zeros((channels, wide), BF16)
                out_ref[t * channels : (t + 1) * channels, here] = block


def weight_back_kernel(weight, out_ref):
    channels = weight.shape[0]
    for down in range(3):
        for across in range(3):
            blocks = [
                jnp.transpose(
                    weight[
                        :,
                        (9 * kt + 3 * (2 - down) + 2 - across) * channels : (9 * kt + 3 * (2 - down) + 3 - across)
                        * channels,
                    ]
                )
                for kt in range(3)
            ]
            for t in range(2):
                for f in range(4):
                    kt = t + 2 - f
                    start = ((down * 4 + f) * 3 + across) * channels
                    block = blocks[kt] if 0 <= kt < 3 else jnp.zeros((channels, channels), BF16)
                    out_ref[t * channels : (t + 1) * channels, start : start + channels] = block


def shifted(value, axis, steps):
    count = lax.axis_size(axis)
    initial, last = max(0, -steps), min(count, count - steps)
    return lax.ppermute(value, axis, [(source, source + steps) for source in range(initial, last)])


def rounds(axes):
    for axis in axes:
        count = lax.axis_size(axis)
        step = 1
        while step < count:
            wide = 4 if 4 * step <= count else 2
            yield axis, step, [[(i, i ^ (step * k)) for i in range(count)] for k in range(1, wide)]
            step *= wide


def pairwise(parts, join):
    while len(parts) > 1:
        parts = [join(a, b) for a, b in zip(parts[::2], parts[1::2])]
    return parts[0]


def all_sum(value):
    for axis, _, exchanges in rounds(("tm", "height", "width")):
        parts = [value] + [lax.ppermute(value, axis, pairs) for pairs in exchanges]
        value = pairwise(parts, lambda a, b: a + b)
    return value


def all_stats(value, count):
    for axis, _, exchanges in rounds(("tm", "height", "width")):
        parts = [(value, count)] + [(lax.ppermute(value, axis, pairs), count) for pairs in exchanges]
        value, count = pairwise(parts, joined_stats)
    return value


def joined_stats(first, second):
    (a, count), (b, _) = first, second
    gap = a[:, 0:1] - b[:, 0:1]
    squares = a[:, 1:2] + b[:, 1:2] + gap * gap * (0.5 * count)
    return jnp.concatenate([0.5 * (a[:, 0:1] + b[:, 0:1]), squares], axis=1), 2.0 * count


def swapped(value):
    return lax.ppermute(value, "width", [(0, 1), (1, 0)])


def weight_rounds():
    return list(rounds(("height", "tm")))


def scattered(flags, second, first):
    half, _, channels = second[0].shape
    axis, _, exchanges = weight_rounds()[0]
    parts = len(exchanges) + 1
    rows = half // parts
    terms = [part for mine, theirs in (second, first) for part in (mine, swapped(theirs))]
    part = (2, rows, SLOTS, channels)
    kept, *sent = call(
        functools.partial(first_scatter_kernel, slot=4),
        [shape(part, F32)] + [shape(part, jnp.int16)] * (parts - 1),
        [SMEM] + [VMEM] * 4,
        (flags, *[term.reshape(parts, rows, SLOTS, channels) for term in terms]),
    )
    return [kept] + [lax.ppermute(v, axis, pairs) for v, pairs in zip(sent, exchanges)], sent[0]


def summed(flags, received, after):
    for number, (axis, _, exchanges) in enumerate(weight_rounds()[1:], 5):
        parts = len(exchanges) + 1
        _, rows, _, channels = received[0].shape
        part = (2, rows // parts, SLOTS, channels)
        views = [v.reshape(2, parts, *part[1:]) for v in received]
        kept, *sent = call(
            functools.partial(scatter_kernel, received=len(views), sent=parts, slot=number),
            [shape(part, F32)] + [shape(part, jnp.int16)] * (parts - 1),
            [SMEM] + [VMEM] * (len(views) + len(after)),
            (flags, *views, *after),
        )
        after = ()
        received = [kept] + [lax.ppermute(v, axis, pairs) for v, pairs in zip(sent, exchanges)]
    return received


def gathered(flags, received, after, after_last):
    (total,) = call(
        functools.partial(total_kernel, received=len(received)),
        [shape(received[0].shape, jnp.int16)],
        [VMEM] * (len(received) + len(after)),
        (*received, *after),
    )
    _, rows, _, channels = total.shape
    back = list(enumerate(weight_rounds(), 4))[::-1]
    number, (axis, _, exchanges) = back[0]
    pieces = [total] + [lax.ppermute(total, axis, pairs) for pairs in exchanges]
    values = call(
        functools.partial(split_kernel, received=len(pieces), slot=number),
        [shape((len(pieces), rows, SLOTS, channels), jnp.int16)] * 2,
        [SMEM] + [VMEM] * (len(pieces) + 1),
        (flags, *pieces, after_last),
    )
    results = []
    for value in values:
        for number, (axis, _, exchanges) in back[1:]:
            value = value.reshape(-1, SLOTS, channels)
            pieces = [value] + [lax.ppermute(value, axis, pairs) for pairs in exchanges]
            (value,) = call(
                functools.partial(gather_kernel, slot=number),
                [shape((len(pieces), *value.shape), jnp.int16)],
                [SMEM] + [VMEM] * len(pieces),
                (flags, *pieces),
            )
        results.append(value.reshape(-1, SLOTS, channels))
    return results


def joined(flags, mine, theirs):
    half, _, channels = mine.shape
    (total,) = call(
        join_kernel,
        [shape((2 * half, TAPS * channels), F32)],
        [SMEM] + [VMEM] * 2,
        (flags, mine, theirs),
        scratch=[pltpu.VMEM((half * SLOTS, channels), F32)] * 2,
    )
    return total


def edges(flags, planes, after):
    channels = planes[0].shape[2]
    args = (*planes, *after)
    (columns,) = call(edges_kernel, [shape((channels, 128), BF16)], [SMEM] + [VMEM] * len(args), (flags, *args))
    return columns


def row_halos(down, up):
    above, below = shifted(down, "height", 1), shifted(up, "height", -1)
    return call(rows_kernel, [shape((2, *down.shape[1:]), BF16)] * down.shape[0], [VMEM] * 2, (above, below))


def halo(own, near, steps):
    return shifted(own, "tm", steps), near, shifted(near, "tm", steps)


def with_columns(flags, own, around, after=()):
    edge = swapped(edges(flags, (own, around[0]), after))
    rim = swapped(edges(flags, around[1:], after))
    return *around, edge, rim


def shards(
    latent,
    exponents,
    cotangent,
    conv_first,
    conv_second,
    gain_first,
    shift_first,
    gain_second,
    shift_second,
):
    channels, frames, rows, cols = latent.shape
    groups = exponents.shape[0]
    devices = lax.axis_size("tm") * lax.axis_size("height") * lax.axis_size("width")
    count = float(channels // groups * frames * rows * cols * devices)
    tm, height, width = (lax.axis_index(axis) for axis in ("tm", "height", "width"))
    flags = jnp.stack(
        [
            (tm > 0).astype(jnp.int32),
            (height > 0).astype(jnp.int32),
            (height < lax.axis_size("height") - 1).astype(jnp.int32),
            width.astype(jnp.int32),
        ]
        + [
            (lax.axis_index(axis) // step % (len(exchanges) + 1)).astype(jnp.int32)
            for axis, step, exchanges in weight_rounds()
        ]
    )
    scale = jnp.repeat(jnp.exp2(exponents.astype(F32)), channels // groups)
    zeros = jnp.zeros_like(scale)
    par = jnp.stack([scale, gain_first, shift_first, gain_second, shift_second, zeros, zeros, zeros])
    block = (rows, frames, channels, cols)
    stack = (rows + 2, 4, 3 * channels, cols)
    taps = (2 * channels, 36 * channels)
    halves = [shape((channels // 2 * SLOTS, channels), F32)] * 2
    conv_flops = 3 * 2 * 4 * 256 * 36 * channels * 2 * channels
    small = shape((1, 2, channels), F32)

    message = shape((2, frames, channels, cols), BF16)
    latent, cotangent, down, up, stats_first = call(
        planes_kernel,
        [shape(block, BF16), shape(block, BF16), message, message, small],
        [VMEM] * 3,
        (latent, cotangent, par),
    )
    near, near_c = row_halos(down, up)
    around = with_columns(flags, latent, halo(latent, near, 1))
    around_c = halo(cotangent, near_c, -1)
    stats_first = all_stats(stats_first, count / devices)
    (weight_first,) = call(weight_forward_kernel, [shape(taps, BF16)], [VMEM], (conv_first,))
    (weight_second_t,) = call(weight_back_kernel, [shape(taps, BF16)], [VMEM], (conv_second,))
    (weight_first_t,) = call(weight_back_kernel, [shape(taps, BF16)], [VMEM], (conv_first,))

    hidden, stats_second, stack_first = call(
        functools.partial(conv_first_kernel, count=count),
        [shape(block, F32), small, shape(stack, BF16)],
        [SMEM] + [VMEM] * 10,
        (flags, latent, *around, par, stats_first, weight_first, around_c[0]),
        flops=conv_flops,
        transcendentals=3 * latent.size,
    )
    around_c = with_columns(flags, cotangent, around_c, (stats_second,))
    stats_second = all_stats(stats_second, count / devices)
    grad_second, stack_c = call(
        conv_back_kernel,
        [shape(block, F32), shape(stack, BF16)],
        [SMEM] + [VMEM] * 7,
        (flags, cotangent, *around_c, weight_second_t),
        flops=conv_flops,
    )
    act_second, scaled, sums = call(
        functools.partial(norm_second_kernel, count=count),
        [shape(block, BF16), shape(block, F32), small],
        [VMEM] * 4,
        (hidden, grad_second, par, stats_second),
        transcendentals=latent.size,
    )
    sums = all_sum(sums)
    halves_second = call(
        weight_second_kernel,
        halves,
        [SMEM] + [VMEM] * 2,
        (flags, stack_c, act_second),
        scratch=[pltpu.VMEM((rows * cols, frames * channels), BF16)],
        flops=conv_flops,
    )
    message = shape((1, frames, channels, cols), BF16)
    hidden_grad, down, up = call(
        functools.partial(hidden_grad_kernel, count=count),
        [shape(block, BF16), message, message],
        [VMEM] * 6,
        (hidden, scaled, par, stats_second, sums, halves_second[0]),
    )
    (near,) = row_halos(down, up)
    around = halo(hidden_grad, near, -1)
    halves_first = call(
        weight_first_kernel,
        halves,
        [SMEM] + [VMEM] * 2,
        (flags, stack_first, hidden_grad),
        scratch=[pltpu.VMEM((rows * cols, frames * channels), BF16)],
        flops=conv_flops,
    )
    halves_second, halves_first = (
        [v.reshape(channels // 2, SLOTS, channels) for v in halves] for halves in (halves_second, halves_first)
    )
    weights, sent = scattered(flags, halves_second, halves_first)
    around = with_columns(flags, hidden_grad, around, (sent,))
    scaled, sums_first = call(
        functools.partial(first_grad_kernel, count=count),
        [shape(block, F32), small],
        [SMEM] + [VMEM] * 10,
        (flags, hidden_grad, *around, weight_first_t, latent, par, stats_first),
        scratch=[pltpu.VMEM(stack, BF16)],
        flops=conv_flops,
        transcendentals=latent.size,
    )
    weights = summed(flags, weights, around[:2])
    sums_first = all_sum(sums_first)
    decoded_grad, token = call(
        functools.partial(decoded_grad_kernel, count=count),
        [shape((channels, frames, rows, cols), F32), shape((8, 128), F32)],
        [VMEM] * 6,
        (scaled, latent, cotangent, par, stats_first, sums_first),
    )
    second, first = gathered(flags, weights, (sums_first,), token)
    conv_second_grad = joined(flags, second, swapped(second))
    conv_first_grad = joined(flags, first, swapped(first))
    return decoded_grad, conv_first_grad, conv_second_grad


def solution(mesh):
    block = P(None, "tm", "height", "width")
    return jax.shard_map(
        shards,
        mesh=mesh,
        in_specs=(block, P(), block, P(), P(), P(), P(), P(), P()),
        out_specs=(block, P(), P()),
        check_vma=False,
    )
```

```python
import functools

import jax
import jax.numpy as jnp
from jax import lax
from jax.experimental import pallas as pl
from jax.experimental.pallas import tpu as pltpu
from jax.sharding import PartitionSpec as P

epsilon = 1e-05
F32 = jnp.float32
BF16 = jnp.bfloat16
GROUP = 4
TAPS, SLOTS = 27, 32
FULL = 32760.0
LN2 = 0.6931471805599453
VMEM = pl.BlockSpec(memory_space=pltpu.VMEM)
SMEM = pl.BlockSpec(memory_space=pltpu.SMEM)


def call(body, outs, specs, args, scratch=(), flops=0, transcendentals=0, limit=20):
    moved = sum(a.size * a.dtype.itemsize for a in args)
    moved += sum(o.size * o.dtype.itemsize for o in outs)
    return pl.pallas_call(
        body,
        out_shape=tuple(outs),
        in_specs=specs,
        out_specs=tuple(VMEM for _ in outs),
        scratch_shapes=scratch,
        compiler_params=pltpu.CompilerParams(vmem_limit_bytes=limit << 20),
        cost_estimate=pl.CostEstimate(
            flops=flops, bytes_accessed=moved, transcendentals=transcendentals
        ),
    )(*args)


def shape(dims, dtype):
    return jax.ShapeDtypeStruct(dims, dtype)


def group_sums(acc):
    rows = acc.shape[0]
    row = lax.broadcasted_iota(jnp.int32, acc.shape, 0)
    step = 1
    while step < GROUP:
        up = pltpu.roll(acc, rows - step, axis=0)
        down = pltpu.roll(acc, step, axis=0)
        acc = acc + jnp.where((row & step) == 0, up, down)
        step *= 2
    return jnp.sum(acc, axis=1, keepdims=True)


def lanes_of(plane):
    total = plane[:, :128]
    for start in range(128, plane.shape[1], 128):
        total = total + plane[:, start : start + 128]
    return total


def as_rows(first, second):
    channels = first.shape[0]
    lane = lax.broadcasted_iota(jnp.int32, (channels, 128), 1)
    both = jnp.where(lane == 0, first, jnp.where(lane == 1, second, 0.0))
    return jnp.transpose(both)[:2]


def local_stats(planes, count):
    acc = None
    for plane in planes:
        part = lanes_of(plane())
        acc = part if acc is None else acc + part
    mean = group_sums(acc) / count
    acc = None
    for plane in planes:
        off = plane() - mean
        part = lanes_of(off * off)
        acc = part if acc is None else acc + part
    return mean, group_sums(acc)


def put_rows(out_ref, first, second):
    out_ref[0] = as_rows(first, second)


def combined(st_ref, count):
    return st_ref[0, 0:1], st_ref[0, 1:2] / count


def columns_of(*rows):
    rows = list(rows) + [jnp.zeros_like(rows[0])] * (8 - len(rows))
    cols = jnp.transpose(jnp.concatenate(rows, axis=0))
    return [cols[:, i : i + 1] for i in range(8)]


def sigmoid(value):
    return 0.5 + 0.5 * jnp.tanh(0.5 * value)


def planes_kernel(latent_ref, cotangent_ref, par_ref, latent_out, cotangent_out, down_ref, up_ref, st_ref):
    _, frames, rows, cols = latent_ref.shape
    for which, (natural, out) in enumerate(((latent_ref, latent_out), (cotangent_ref, cotangent_out))):
        for row in range(rows):
            for frame in range(frames):
                plane = natural[:, frame, row, :]
                out[row, frame] = plane
                if row == rows - 1:
                    down_ref[which, frame] = plane
                if row == 0:
                    up_ref[which, frame] = plane
    scale = columns_of(par_ref[0:1])[0]
    planes = [
        functools.partial(lambda r, t: latent_out[r, t].astype(F32) * scale, r, t)
        for r in range(rows)
        for t in range(frames)
    ]
    put_rows(st_ref, *local_stats(planes, float(GROUP * rows * frames * cols)))


def rows_kernel(above_ref, below_ref, *refs):
    for which, out in enumerate(refs[-above_ref.shape[0] :]):
        out[0] = above_ref[which]
        out[1] = below_ref[which]


def source(own, other, near, far, other_first):
    def at(row, frame):
        is_other = (frame < 2) == other_first
        if row == 0 or row == own.shape[0] + 1:
            return (far if is_other else near), (0 if row == 0 else 1, frame % 2)
        return (other if is_other else own), (row - 1, frame % 2)

    return at


def edges_kernel(flag_ref, first_ref, second_ref, *refs):
    planes, out_ref = (first_ref, second_ref), refs[-1]
    is_first = flag_ref[3] == 0
    channels = planes[0].shape[2]
    lane = lax.broadcasted_iota(jnp.int32, (channels, 128), 1)
    acc = jnp.zeros((channels, 128), F32)
    number = 0
    for ref in planes:
        for row in range(ref.shape[0]):
            for frame in range(ref.shape[1]):
                last = pltpu.roll(ref[row, frame, :, -128:].astype(F32), 1, axis=1)
                edge = jnp.where(is_first, last, ref[row, frame, :, :128].astype(F32))
                moved = pltpu.roll(edge, number, axis=1) if number else edge
                acc = jnp.where(lane == number, moved, acc)
                number += 1
    out_ref[...] = acc.astype(BF16)


def edge_lane(row, frame, rows, other_first):
    is_other = int((frame < 2) == other_first)
    if row == 0 or row == rows + 1:
        return 1, 4 * is_other + 2 * int(row > 0) + frame % 2
    return 0, 2 * rows * is_other + 2 * (row - 1) + frame % 2


def fill_stack(stack, row, frame, plane, column, on_left, on_right):
    channels, cols = plane.shape
    lane = lax.broadcasted_iota(jnp.int32, (channels, cols), 1)
    column = column.astype(F32)
    left = jnp.where(lane == 0, (column * on_left).astype(BF16), pltpu.roll(plane, 1, axis=1))
    right = jnp.where(lane == cols - 1, (column * on_right).astype(BF16), pltpu.roll(plane, cols - 1, axis=1))
    stack[row, frame, 0:channels] = left
    stack[row, frame, channels : 2 * channels] = plane
    stack[row, frame, 2 * channels : 3 * channels] = right


def sides(flag_ref):
    on_left = (flag_ref[3] != 0).astype(F32)
    on_right = (flag_ref[3] == 0).astype(F32)
    return on_left, on_right


def conv_rows(stack, weight, row):
    three = stack[row : row + 3].reshape(weight.shape[1], stack.shape[3])
    return jnp.dot(weight[...], three, preferred_element_type=F32)


def norm_columns(par_ref, st_ref, count, gain_row):
    par = par_ref[...]
    mean, variance = combined(st_ref, count)
    inverse = 1.0 / jnp.sqrt(variance + epsilon)
    gain = par[gain_row : gain_row + 1]
    shift = par[gain_row + 1 : gain_row + 2]
    return columns_of(mean, inverse, gain, shift, par[0:1])[:5]


def conv_first_kernel(
    flag_ref, own, past, near, far, edge_ref, rim_ref, par_ref, st_ref, weight, after, hidden_ref, st_out, stack_ref,
    *, count
):
    rows, frames, channels, cols = own.shape
    at = source(own, past, near, far, True)
    mean, inverse, gain, shift, scale = norm_columns(par_ref, st_ref, count, 1)

    def act(latent):
        pre = (latent.astype(F32) * scale - mean) * inverse * gain + shift
        return pre * sigmoid(pre)

    has_past = flag_ref[0].astype(F32)
    has_top = flag_ref[1].astype(F32)
    has_bottom = flag_ref[2].astype(F32)
    on_left, on_right = sides(flag_ref)
    edges = (act(edge_ref[...]), act(rim_ref[...]))
    for row in range(rows + 2):
        for frame in range(4):
            ref, index = at(row, frame)
            which, number = edge_lane(row, frame, rows, True)
            plane = act(ref[index])
            column = edges[which][:, number : number + 1]
            factor = None
            if frame < 2:
                factor = has_past
            if row in (0, rows + 1):
                beside = has_top if row == 0 else has_bottom
                factor = beside if factor is None else factor * beside
            if factor is not None:
                plane = plane * factor
                column = column * factor
            fill_stack(stack_ref, row, frame, plane.astype(BF16), column, on_left, on_right)
    for row in range(rows):
        out = conv_rows(stack_ref, weight, row)
        for frame in range(frames):
            hidden_ref[row, frame] = out[frame * channels : (frame + 1) * channels]
    planes = [
        functools.partial(lambda r, t: hidden_ref[r, t], r, t) for r in range(rows) for t in range(frames)
    ]
    put_rows(st_out, *local_stats(planes, float(GROUP * rows * frames * cols)))


def fill_future(stack, flag_ref, own, future, near, far, edge_ref, rim_ref):
    rows = own.shape[0]
    at = source(own, future, near, far, False)
    on_left, on_right = sides(flag_ref)
    edges = (edge_ref[...], rim_ref[...])
    for row in range(rows + 2):
        for frame in range(4):
            ref, index = at(row, frame)
            which, number = edge_lane(row, frame, rows, False)
            fill_stack(stack, row, frame, ref[index], edges[which][:, number : number + 1], on_left, on_right)


def conv_back_kernel(flag_ref, *refs):
    weight, grad_ref, stack_ref = refs[-3:]
    rows, frames, channels, _ = grad_ref.shape
    fill_future(stack_ref, flag_ref, *refs[:-3])
    for row in range(rows):
        out = conv_rows(stack_ref, weight, row)
        for frame in range(frames):
            grad_ref[row, frame] = out[frame * channels : (frame + 1) * channels]


def norm_second_kernel(hidden, grad, par_ref, st_ref, act_ref, scaled_ref, sums_ref, *, count):
    rows, frames, channels, cols = hidden.shape
    mean, inverse, gain, shift, _ = norm_columns(par_ref, st_ref, count, 3)
    first = jnp.zeros((channels, 128), F32)
    second = jnp.zeros((channels, 128), F32)
    for row in range(rows):
        for frame in range(frames):
            normed = (hidden[row, frame] - mean) * inverse
            pre = normed * gain + shift
            sig = sigmoid(pre)
            act = pre * sig
            act_ref[row, frame] = act.astype(BF16)
            scaled = grad[row, frame] * (sig + act * (1.0 - sig)) * gain
            scaled_ref[row, frame] = scaled
            first = first + lanes_of(scaled)
            second = second + lanes_of(scaled * normed)
    put_rows(sums_ref, group_sums(first), group_sums(second))


def hidden_grad_kernel(
    hidden, scaled, par_ref, st_ref, sums_ref, out_ref, down_ref, up_ref, *, count
):
    rows, frames, channels, cols = hidden.shape
    mean, inverse, _, _, _ = norm_columns(par_ref, st_ref, count, 3)
    means = sums_ref[0] / count
    first, second = columns_of(means[0:1], means[1:2])[:2]
    for row in range(rows):
        for frame in range(frames):
            normed = (hidden[row, frame] - mean) * inverse
            plane = (inverse * (scaled[row, frame] - first - normed * second)).astype(BF16)
            out_ref[row, frame] = plane
            if row == rows - 1:
                down_ref[0, frame] = plane
            if row == 0:
                up_ref[0, frame] = plane


def put_halves(flag_ref, mine_ref, theirs_ref, tap, block):
    half = block.shape[0] // 2
    here = pl.ds(tap, half, stride=SLOTS)
    upper, lower = block[:half], block[half:]
    is_first = flag_ref[3] == 0
    mine_ref[here, :] = jnp.where(is_first, upper, lower)
    theirs_ref[here, :] = jnp.where(is_first, lower, upper)


def encoded(value):
    slot = lax.broadcasted_iota(jnp.int32, value.shape, 1)
    value = jnp.where(slot < TAPS, value, 0.0)
    top = jnp.max(jnp.abs(value), axis=1, keepdims=True)
    power = jnp.ceil(jnp.log(jnp.maximum(top, 1e-30)) * (1.0 / LN2))
    number = jnp.round(value * (FULL * jnp.exp(power * -LN2)))
    return jnp.where(slot < TAPS, number, power).astype(jnp.int32).astype(jnp.int16)


def decoded_value(number):
    number = number.astype(jnp.int32).astype(F32)
    return number * (jnp.exp(number[:, SLOTS - 1 : SLOTS] * LN2) * (1.0 / FULL))


def first_scatter_kernel(flag_ref, *refs, slot):
    me = flag_ref[slot]
    for which in range(2):
        mine, other = refs[2 * which], refs[2 * which + 1]
        for k, out in enumerate(refs[4:]):
            total = mine[me ^ k] + other[me ^ k]
            out[which] = total if k == 0 else encoded(total)


def scatter_kernel(flag_ref, *refs, received, sent, slot):
    me = flag_ref[slot]
    for which in range(2):
        for k, out in enumerate(refs[-sent:]):
            total = refs[0][which, me ^ k]
            for ref in refs[1:received]:
                total = total + decoded_value(ref[which, me ^ k])
            out[which] = total if k == 0 else encoded(total)


def total_kernel(*refs, received):
    for which in range(2):
        total = refs[0][which]
        for ref in refs[1:received]:
            total = total + decoded_value(ref[which])
        refs[-1][which] = encoded(total)


def split_kernel(flag_ref, *refs, received, slot):
    me = flag_ref[slot]
    for which in range(2):
        for k, ref in enumerate(refs[:received]):
            refs[which - 2][me ^ k] = ref[which]


def gather_kernel(flag_ref, *refs, slot):
    me = flag_ref[slot]
    for k, ref in enumerate(refs[:-1]):
        refs[-1][me ^ k] = ref[...]


def join_kernel(flag_ref, mine_ref, theirs_ref, out_ref, first_ref, second_ref):
    half, _, channels = mine_ref.shape
    is_first = flag_ref[3] == 0
    first_ref[...] = decoded_value(jnp.where(is_first, mine_ref[...], theirs_ref[...])).reshape(first_ref.shape)
    second_ref[...] = decoded_value(jnp.where(is_first, theirs_ref[...], mine_ref[...])).reshape(second_ref.shape)
    for tap in range(TAPS):
        here = slice(tap * channels, (tap + 1) * channels)
        out_ref[:half, here] = first_ref[pl.ds(tap, half, stride=SLOTS), :]
        out_ref[half:, here] = second_ref[pl.ds(tap, half, stride=SLOTS), :]


def weight_second_kernel(flag_ref, stack_ref, act_ref, after, mine_ref, theirs_ref, right_ref):
    rows, frames, channels, cols = act_ref.shape
    for row in range(rows):
        right_ref[row * cols : (row + 1) * cols] = jnp.transpose(
            act_ref[row].reshape(frames * channels, cols)
        )
    right = right_ref[...]
    for down in range(3):
        parts = []
        for frame in range(4):
            left = jnp.concatenate([stack_ref[down + row, frame] for row in range(rows)], axis=1)
            parts.append(jnp.dot(left, right, preferred_element_type=F32))
        for kt in range(3):
            term = parts[2 - kt][:, :channels] + parts[3 - kt][:, channels:]
            for across in range(3):
                tap = 9 * kt + 3 * (2 - down) + (2 - across)
                put_halves(flag_ref, mine_ref, theirs_ref, tap, term[across * channels : (across + 1) * channels])


def weight_first_kernel(flag_ref, stack_ref, grad_ref, mine_ref, theirs_ref, right_ref):
    rows, frames, channels, cols = grad_ref.shape
    for row in range(rows):
        right_ref[row * cols : (row + 1) * cols] = jnp.transpose(
            grad_ref[row].reshape(frames * channels, cols)
        )
    right = right_ref[...]
    for down in range(3):
        parts = []
        for frame in range(4):
            left = jnp.concatenate([stack_ref[down + row, frame] for row in range(rows)], axis=1)
            parts.append(jnp.dot(left, right, preferred_element_type=F32))
        for kt in range(3):
            term = parts[kt][:, :channels] + parts[kt + 1][:, channels:]
            for across in range(3):
                tap = 9 * kt + 3 * down + across
                block = jnp.transpose(term[across * channels : (across + 1) * channels])
                put_halves(flag_ref, mine_ref, theirs_ref, tap, block)


def first_grad_kernel(flag_ref, *refs, count):
    weight, latent, par_ref, st_ref, scaled_ref, sums_ref, stack_ref = refs[-7:]
    rows, frames, channels, cols = latent.shape
    mean, inverse, gain, shift, scale = norm_columns(par_ref, st_ref, count, 1)
    fill_future(stack_ref, flag_ref, *refs[:-7])
    first = jnp.zeros((channels, 128), F32)
    second = jnp.zeros((channels, 128), F32)
    for row in range(rows):
        out = conv_rows(stack_ref, weight, row)
        for frame in range(frames):
            grad = out[frame * channels : (frame + 1) * channels]
            normed = (latent[row, frame].astype(F32) * scale - mean) * inverse
            pre = normed * gain + shift
            sig = sigmoid(pre)
            scaled = grad * (sig + pre * sig * (1.0 - sig)) * gain
            scaled_ref[row, frame] = scaled
            first = first + lanes_of(scaled)
            second = second + lanes_of(scaled * normed)
    put_rows(sums_ref, group_sums(first), group_sums(second))


def decoded_grad_kernel(scaled, latent, cotangent, par_ref, st_ref, sums_ref, out_ref, token_ref, *, count):
    token_ref[...] = jnp.zeros(token_ref.shape, F32)
    rows, frames, channels, cols = latent.shape
    mean, inverse, _, _, scale = norm_columns(par_ref, st_ref, count, 1)
    means = sums_ref[0] / count
    first, second = columns_of(means[0:1], means[1:2])[:2]
    for row in range(rows):
        for frame in range(frames):
            normed = (latent[row, frame].astype(F32) * scale - mean) * inverse
            out_ref[:, frame, row, :] = cotangent[row, frame].astype(F32) + inverse * (
                scaled[row, frame] - first - normed * second
            )


def weight_forward_kernel(weight, out_ref):
    channels = weight.shape[0]
    wide = 3 * channels
    for t in range(2):
        for kr in range(3):
            for f in range(4):
                kt = f - t
                here = slice((kr * 4 + f) * wide, (kr * 4 + f + 1) * wide)
                if 0 <= kt < 3:
                    tap = 3 * kt + kr
                    block = weight[:, tap * wide : (tap + 1) * wide]
                else:
                    block = jnp.zeros((channels, wide), BF16)
                out_ref[t * channels : (t + 1) * channels, here] = block


def weight_back_kernel(weight, out_ref):
    channels = weight.shape[0]
    for down in range(3):
        for across in range(3):
            blocks = [
                jnp.transpose(
                    weight[
                        :,
                        (9 * kt + 3 * (2 - down) + 2 - across) * channels : (9 * kt + 3 * (2 - down) + 3 - across)
                        * channels,
                    ]
                )
                for kt in range(3)
            ]
            for t in range(2):
                for f in range(4):
                    kt = t + 2 - f
                    start = ((down * 4 + f) * 3 + across) * channels
                    block = blocks[kt] if 0 <= kt < 3 else jnp.zeros((channels, channels), BF16)
                    out_ref[t * channels : (t + 1) * channels, start : start + channels] = block


def shifted(value, axis, steps):
    count = lax.axis_size(axis)
    initial, last = max(0, -steps), min(count, count - steps)
    return lax.ppermute(value, axis, [(source, source + steps) for source in range(initial, last)])


def rounds(axes):
    for axis in axes:
        count = lax.axis_size(axis)
        step = 1
        while step < count:
            wide = 4 if 4 * step <= count else 2
            yield axis, step, [[(i, i ^ (step * k)) for i in range(count)] for k in range(1, wide)]
            step *= wide


def pairwise(parts, join):
    while len(parts) > 1:
        parts = [join(a, b) for a, b in zip(parts[::2], parts[1::2])]
    return parts[0]


def all_sum(value):
    for axis, _, exchanges in rounds(("tm", "height", "width")):
        parts = [value] + [lax.ppermute(value, axis, pairs) for pairs in exchanges]
        value = pairwise(parts, lambda a, b: a + b)
    return value


def all_stats(value, count):
    for axis, _, exchanges in rounds(("tm", "height", "width")):
        parts = [(value, count)] + [(lax.ppermute(value, axis, pairs), count) for pairs in exchanges]
        value, count = pairwise(parts, joined_stats)
    return value


def joined_stats(first, second):
    (a, count), (b, _) = first, second
    gap = a[:, 0:1] - b[:, 0:1]
    squares = a[:, 1:2] + b[:, 1:2] + gap * gap * (0.5 * count)
    return jnp.concatenate([0.5 * (a[:, 0:1] + b[:, 0:1]), squares], axis=1), 2.0 * count


def swapped(value):
    return lax.ppermute(value, "width", [(0, 1), (1, 0)])


def weight_rounds():
    return list(rounds(("height", "tm")))


def scattered(flags, second, first):
    half, _, channels = second[0].shape
    axis, _, exchanges = weight_rounds()[0]
    parts = len(exchanges) + 1
    rows = half // parts
    terms = [part for mine, theirs in (second, first) for part in (mine, swapped(theirs))]
    part = (2, rows, SLOTS, channels)
    kept, *sent = call(
        functools.partial(first_scatter_kernel, slot=4),
        [shape(part, F32)] + [shape(part, jnp.int16)] * (parts - 1),
        [SMEM] + [VMEM] * 4,
        (flags, *[term.reshape(parts, rows, SLOTS, channels) for term in terms]),
    )
    return [kept] + [lax.ppermute(v, axis, pairs) for v, pairs in zip(sent, exchanges)], sent[0]


def summed(flags, received, after):
    for number, (axis, _, exchanges) in enumerate(weight_rounds()[1:], 5):
        parts = len(exchanges) + 1
        _, rows, _, channels = received[0].shape
        part = (2, rows // parts, SLOTS, channels)
        views = [v.reshape(2, parts, *part[1:]) for v in received]
        kept, *sent = call(
            functools.partial(scatter_kernel, received=len(views), sent=parts, slot=number),
            [shape(part, F32)] + [shape(part, jnp.int16)] * (parts - 1),
            [SMEM] + [VMEM] * (len(views) + len(after)),
            (flags, *views, *after),
        )
        after = ()
        received = [kept] + [lax.ppermute(v, axis, pairs) for v, pairs in zip(sent, exchanges)]
    return received


def gathered(flags, received, after, after_last):
    (total,) = call(
        functools.partial(total_kernel, received=len(received)),
        [shape(received[0].shape, jnp.int16)],
        [VMEM] * (len(received) + len(after)),
        (*received, *after),
    )
    _, rows, _, channels = total.shape
    back = list(enumerate(weight_rounds(), 4))[::-1]
    number, (axis, _, exchanges) = back[0]
    pieces = [total] + [lax.ppermute(total, axis, pairs) for pairs in exchanges]
    values = call(
        functools.partial(split_kernel, received=len(pieces), slot=number),
        [shape((len(pieces), rows, SLOTS, channels), jnp.int16)] * 2,
        [SMEM] + [VMEM] * (len(pieces) + 1),
        (flags, *pieces, after_last),
    )
    results = []
    for value in values:
        for number, (axis, _, exchanges) in back[1:]:
            value = value.reshape(-1, SLOTS, channels)
            pieces = [value] + [lax.ppermute(value, axis, pairs) for pairs in exchanges]
            (value,) = call(
                functools.partial(gather_kernel, slot=number),
                [shape((len(pieces), *value.shape), jnp.int16)],
                [SMEM] + [VMEM] * len(pieces),
                (flags, *pieces),
            )
        results.append(value.reshape(-1, SLOTS, channels))
    return results


def joined(flags, mine, theirs):
    half, _, channels = mine.shape
    (total,) = call(
        join_kernel,
        [shape((2 * half, TAPS * channels), F32)],
        [SMEM] + [VMEM] * 2,
        (flags, mine, theirs),
        scratch=[pltpu.VMEM((half * SLOTS, channels), F32)] * 2,
    )
    return total


def edges(flags, planes, after):
    channels = planes[0].shape[2]
    args = (*planes, *after)
    (columns,) = call(edges_kernel, [shape((channels, 128), BF16)], [SMEM] + [VMEM] * len(args), (flags, *args))
    return columns


def row_halos(down, up, after=()):
    above, below = shifted(down, "height", 1), shifted(up, "height", -1)
    return call(
        rows_kernel, [shape((2, *down.shape[1:]), BF16)] * down.shape[0], [VMEM] * (2 + len(after)), (above, below, *after)
    )


def with_columns(flags, own, around, after=()):
    edge = swapped(edges(flags, (own, around[0]), after))
    rim = swapped(edges(flags, around[1:], after))
    return *around, edge, rim


def shards(
    latent,
    exponents,
    cotangent,
    conv_first,
    conv_second,
    gain_first,
    shift_first,
    gain_second,
    shift_second,
):
    channels, frames, rows, cols = latent.shape
    groups = exponents.shape[0]
    devices = lax.axis_size("tm") * lax.axis_size("height") * lax.axis_size("width")
    count = float(channels // groups * frames * rows * cols * devices)
    tm, height, width = (lax.axis_index(axis) for axis in ("tm", "height", "width"))
    flags = jnp.stack(
        [
            (tm > 0).astype(jnp.int32),
            (height > 0).astype(jnp.int32),
            (height < lax.axis_size("height") - 1).astype(jnp.int32),
            width.astype(jnp.int32),
        ]
        + [
            (lax.axis_index(axis) // step % (len(exchanges) + 1)).astype(jnp.int32)
            for axis, step, exchanges in weight_rounds()
        ]
    )
    scale = jnp.repeat(jnp.exp2(exponents.astype(F32)), channels // groups)
    zeros = jnp.zeros_like(scale)
    par = jnp.stack([scale, gain_first, shift_first, gain_second, shift_second, zeros, zeros, zeros])
    block = (rows, frames, channels, cols)
    stack = (rows + 2, 4, 3 * channels, cols)
    taps = (2 * channels, 36 * channels)
    halves = [shape((channels // 2 * SLOTS, channels), F32)] * 2
    conv_flops = 3 * 2 * 4 * 256 * 36 * channels * 2 * channels
    small = shape((1, 2, channels), F32)

    message = shape((2, frames, channels, cols), BF16)
    latent, cotangent, down, up, stats_first = call(
        planes_kernel,
        [shape(block, BF16), shape(block, BF16), message, message, small],
        [VMEM] * 3,
        (latent, cotangent, par),
    )
    past, future_c = shifted(latent, "tm", 1), shifted(cotangent, "tm", -1)
    near, near_c = row_halos(down, up, (past, future_c))
    around = with_columns(flags, latent, (past, near, shifted(near, "tm", 1)))
    around_c = (future_c, near_c, shifted(near_c, "tm", -1))
    stats_first = all_stats(stats_first, count / devices)
    (weight_first,) = call(weight_forward_kernel, [shape(taps, BF16)], [VMEM], (conv_first,))
    (weight_second_t,) = call(weight_back_kernel, [shape(taps, BF16)], [VMEM], (conv_second,))
    (weight_first_t,) = call(weight_back_kernel, [shape(taps, BF16)], [VMEM], (conv_first,))

    hidden, stats_second, stack_first = call(
        functools.partial(conv_first_kernel, count=count),
        [shape(block, F32), small, shape(stack, BF16)],
        [SMEM] + [VMEM] * 10,
        (flags, latent, *around, par, stats_first, weight_first, around_c[2]),
        flops=conv_flops,
        transcendentals=3 * latent.size,
    )
    around_c = with_columns(flags, cotangent, around_c, (stats_second,))
    stats_second = all_stats(stats_second, count / devices)
    grad_second, stack_c = call(
        conv_back_kernel,
        [shape(block, F32), shape(stack, BF16)],
        [SMEM] + [VMEM] * 7,
        (flags, cotangent, *around_c, weight_second_t),
        flops=conv_flops,
    )
    act_second, scaled, sums = call(
        functools.partial(norm_second_kernel, count=count),
        [shape(block, BF16), shape(block, F32), small],
        [VMEM] * 4,
        (hidden, grad_second, par, stats_second),
        transcendentals=latent.size,
    )
    sums = all_sum(sums)
    message = shape((1, frames, channels, cols), BF16)
    hidden_grad, down, up = call(
        functools.partial(hidden_grad_kernel, count=count),
        [shape(block, BF16), message, message],
        [VMEM] * 5,
        (hidden, scaled, par, stats_second, sums),
    )
    (near,) = row_halos(down, up)
    around = (shifted(hidden_grad, "tm", -1), near, shifted(near, "tm", -1))
    halves_second = call(
        weight_second_kernel,
        halves,
        [SMEM] + [VMEM] * 3,
        (flags, stack_c, act_second, near),
        scratch=[pltpu.VMEM((rows * cols, frames * channels), BF16)],
        flops=conv_flops,
    )
    halves_first = call(
        weight_first_kernel,
        halves,
        [SMEM] + [VMEM] * 2,
        (flags, stack_first, hidden_grad),
        scratch=[pltpu.VMEM((rows * cols, frames * channels), BF16)],
        flops=conv_flops,
    )
    halves_second, halves_first = (
        [v.reshape(channels // 2, SLOTS, channels) for v in halves] for halves in (halves_second, halves_first)
    )
    weights, sent = scattered(flags, halves_second, halves_first)
    around = with_columns(flags, hidden_grad, around, (sent,))
    scaled, sums_first = call(
        functools.partial(first_grad_kernel, count=count),
        [shape(block, F32), small],
        [SMEM] + [VMEM] * 10,
        (flags, hidden_grad, *around, weight_first_t, latent, par, stats_first),
        scratch=[pltpu.VMEM(stack, BF16)],
        flops=conv_flops,
        transcendentals=latent.size,
    )
    weights = summed(flags, weights, around[:2])
    sums_first = all_sum(sums_first)
    decoded_grad, token = call(
        functools.partial(decoded_grad_kernel, count=count),
        [shape((channels, frames, rows, cols), F32), shape((8, 128), F32)],
        [VMEM] * 6,
        (scaled, latent, cotangent, par, stats_first, sums_first),
    )
    second, first = gathered(flags, weights, (sums_first,), token)
    conv_second_grad = joined(flags, second, swapped(second))
    conv_first_grad = joined(flags, first, swapped(first))
    return decoded_grad, conv_first_grad, conv_second_grad


def solution(mesh):
    block = P(None, "tm", "height", "width")
    return jax.shard_map(
        shards,
        mesh=mesh,
        in_specs=(block, P(), block, P(), P(), P(), P(), P(), P()),
        out_specs=(block, P(), P()),
        check_vma=False,
    )
```

```python
import functools

import jax
import jax.numpy as jnp
from jax import lax
from jax.experimental import pallas as pl
from jax.experimental.pallas import tpu as pltpu
from jax.sharding import PartitionSpec as P

epsilon = 1e-05
F32 = jnp.float32
BF16 = jnp.bfloat16
GROUP = 4
TAPS, SLOTS = 27, 32
FULL = 32760.0
LN2 = 0.6931471805599453
VMEM = pl.BlockSpec(memory_space=pltpu.VMEM)
SMEM = pl.BlockSpec(memory_space=pltpu.SMEM)


def call(body, outs, specs, args, scratch=(), flops=0, transcendentals=0, limit=20):
    moved = sum(a.size * a.dtype.itemsize for a in args)
    moved += sum(o.size * o.dtype.itemsize for o in outs)
    return pl.pallas_call(
        body,
        out_shape=tuple(outs),
        in_specs=specs,
        out_specs=tuple(VMEM for _ in outs),
        scratch_shapes=scratch,
        compiler_params=pltpu.CompilerParams(vmem_limit_bytes=limit << 20),
        cost_estimate=pl.CostEstimate(
            flops=flops, bytes_accessed=moved, transcendentals=transcendentals
        ),
    )(*args)


def shape(dims, dtype):
    return jax.ShapeDtypeStruct(dims, dtype)


def group_sums(acc):
    rows = acc.shape[0]
    row = lax.broadcasted_iota(jnp.int32, acc.shape, 0)
    step = 1
    while step < GROUP:
        up = pltpu.roll(acc, rows - step, axis=0)
        down = pltpu.roll(acc, step, axis=0)
        acc = acc + jnp.where((row & step) == 0, up, down)
        step *= 2
    return jnp.sum(acc, axis=1, keepdims=True)


def lanes_of(plane):
    total = plane[:, :128]
    for start in range(128, plane.shape[1], 128):
        total = total + plane[:, start : start + 128]
    return total


def as_rows(first, second):
    channels = first.shape[0]
    lane = lax.broadcasted_iota(jnp.int32, (channels, 128), 1)
    both = jnp.where(lane == 0, first, jnp.where(lane == 1, second, 0.0))
    return jnp.transpose(both)[:2]


def local_stats(planes, count):
    acc = None
    for plane in planes:
        part = lanes_of(plane())
        acc = part if acc is None else acc + part
    mean = group_sums(acc) / count
    acc = None
    for plane in planes:
        off = plane() - mean
        part = lanes_of(off * off)
        acc = part if acc is None else acc + part
    return mean, group_sums(acc)


def put_rows(out_ref, first, second):
    out_ref[0] = as_rows(first, second)


def combined(st_ref, count):
    return st_ref[0, 0:1], st_ref[0, 1:2] / count


def columns_of(*rows):
    rows = list(rows) + [jnp.zeros_like(rows[0])] * (8 - len(rows))
    cols = jnp.transpose(jnp.concatenate(rows, axis=0))
    return [cols[:, i : i + 1] for i in range(8)]


def sigmoid(value):
    return 0.5 + 0.5 * jnp.tanh(0.5 * value)


def planes_kernel(natural_ref, *refs):
    out_ref, down_ref, up_ref = refs[:3] if len(refs) == 3 else refs[1:4]
    _, frames, rows, cols = natural_ref.shape
    for row in range(rows):
        for frame in range(frames):
            plane = natural_ref[:, frame, row, :]
            out_ref[row, frame] = plane
            if row == rows - 1:
                down_ref[0, frame] = plane
            if row == 0:
                up_ref[0, frame] = plane
    if len(refs) == 3:
        return
    scale = columns_of(refs[0][0:1])[0]
    planes = [
        functools.partial(lambda r, t: out_ref[r, t].astype(F32) * scale, r, t)
        for r in range(rows)
        for t in range(frames)
    ]
    put_rows(refs[-1], *local_stats(planes, float(GROUP * rows * frames * cols)))


def rows_kernel(above_ref, below_ref, *refs):
    refs[-1][0] = above_ref[0]
    refs[-1][1] = below_ref[0]


def source(own, other, near, far, other_first):
    def at(row, frame):
        is_other = (frame < 2) == other_first
        if row == 0 or row == own.shape[0] + 1:
            return (far if is_other else near), (0 if row == 0 else 1, frame % 2)
        return (other if is_other else own), (row - 1, frame % 2)

    return at


def edges_kernel(flag_ref, first_ref, second_ref, *refs):
    planes, out_ref = (first_ref, second_ref), refs[-1]
    is_first = flag_ref[3] == 0
    channels = planes[0].shape[2]
    lane = lax.broadcasted_iota(jnp.int32, (channels, 128), 1)
    acc = jnp.zeros((channels, 128), F32)
    number = 0
    for ref in planes:
        for row in range(ref.shape[0]):
            for frame in range(ref.shape[1]):
                last = pltpu.roll(ref[row, frame, :, -128:].astype(F32), 1, axis=1)
                edge = jnp.where(is_first, last, ref[row, frame, :, :128].astype(F32))
                moved = pltpu.roll(edge, number, axis=1) if number else edge
                acc = jnp.where(lane == number, moved, acc)
                number += 1
    out_ref[...] = acc.astype(BF16)


def edge_lane(row, frame, rows, other_first):
    is_other = int((frame < 2) == other_first)
    if row == 0 or row == rows + 1:
        return 1, 4 * is_other + 2 * int(row > 0) + frame % 2
    return 0, 2 * rows * is_other + 2 * (row - 1) + frame % 2


def fill_stack(stack, row, frame, plane, column, on_left, on_right):
    channels, cols = plane.shape
    lane = lax.broadcasted_iota(jnp.int32, (channels, cols), 1)
    column = column.astype(F32)
    left = jnp.where(lane == 0, (column * on_left).astype(BF16), pltpu.roll(plane, 1, axis=1))
    right = jnp.where(lane == cols - 1, (column * on_right).astype(BF16), pltpu.roll(plane, cols - 1, axis=1))
    stack[row, frame, 0:channels] = left
    stack[row, frame, channels : 2 * channels] = plane
    stack[row, frame, 2 * channels : 3 * channels] = right


def sides(flag_ref):
    on_left = (flag_ref[3] != 0).astype(F32)
    on_right = (flag_ref[3] == 0).astype(F32)
    return on_left, on_right


def conv_rows(stack, weight, row):
    three = stack[row : row + 3].reshape(weight.shape[1], stack.shape[3])
    return jnp.dot(weight[...], three, preferred_element_type=F32)


def norm_columns(par_ref, st_ref, count, gain_row):
    par = par_ref[...]
    mean, variance = combined(st_ref, count)
    inverse = 1.0 / jnp.sqrt(variance + epsilon)
    gain = par[gain_row : gain_row + 1]
    shift = par[gain_row + 1 : gain_row + 2]
    return columns_of(mean, inverse, gain, shift, par[0:1])[:5]


def conv_first_kernel(
    flag_ref, own, past, near, far, edge_ref, rim_ref, par_ref, st_ref, weight, after, hidden_ref, st_out, stack_ref,
    *, count
):
    rows, frames, channels, cols = own.shape
    at = source(own, past, near, far, True)
    mean, inverse, gain, shift, scale = norm_columns(par_ref, st_ref, count, 1)

    def act(latent):
        pre = (latent.astype(F32) * scale - mean) * inverse * gain + shift
        return pre * sigmoid(pre)

    has_past = flag_ref[0].astype(F32)
    has_top = flag_ref[1].astype(F32)
    has_bottom = flag_ref[2].astype(F32)
    on_left, on_right = sides(flag_ref)
    edges = (act(edge_ref[...]), act(rim_ref[...]))
    for row in range(rows + 2):
        for frame in range(4):
            ref, index = at(row, frame)
            which, number = edge_lane(row, frame, rows, True)
            plane = act(ref[index])
            column = edges[which][:, number : number + 1]
            factor = None
            if frame < 2:
                factor = has_past
            if row in (0, rows + 1):
                beside = has_top if row == 0 else has_bottom
                factor = beside if factor is None else factor * beside
            if factor is not None:
                plane = plane * factor
                column = column * factor
            fill_stack(stack_ref, row, frame, plane.astype(BF16), column, on_left, on_right)
    for row in range(rows):
        out = conv_rows(stack_ref, weight, row)
        for frame in range(frames):
            hidden_ref[row, frame] = out[frame * channels : (frame + 1) * channels]
    planes = [
        functools.partial(lambda r, t: hidden_ref[r, t], r, t) for r in range(rows) for t in range(frames)
    ]
    put_rows(st_out, *local_stats(planes, float(GROUP * rows * frames * cols)))


def fill_future(stack, flag_ref, own, future, near, far, edge_ref, rim_ref):
    rows = own.shape[0]
    at = source(own, future, near, far, False)
    on_left, on_right = sides(flag_ref)
    edges = (edge_ref[...], rim_ref[...])
    for row in range(rows + 2):
        for frame in range(4):
            ref, index = at(row, frame)
            which, number = edge_lane(row, frame, rows, False)
            fill_stack(stack, row, frame, ref[index], edges[which][:, number : number + 1], on_left, on_right)


def conv_back_kernel(flag_ref, *refs):
    weight, grad_ref, stack_ref = refs[-3:]
    rows, frames, channels, _ = grad_ref.shape
    fill_future(stack_ref, flag_ref, *refs[:-3])
    for row in range(rows):
        out = conv_rows(stack_ref, weight, row)
        for frame in range(frames):
            grad_ref[row, frame] = out[frame * channels : (frame + 1) * channels]


def norm_second_kernel(hidden, grad, par_ref, st_ref, act_ref, scaled_ref, sums_ref, *, count):
    rows, frames, channels, cols = hidden.shape
    mean, inverse, gain, shift, _ = norm_columns(par_ref, st_ref, count, 3)
    first = jnp.zeros((channels, 128), F32)
    second = jnp.zeros((channels, 128), F32)
    for row in range(rows):
        for frame in range(frames):
            normed = (hidden[row, frame] - mean) * inverse
            pre = normed * gain + shift
            sig = sigmoid(pre)
            act = pre * sig
            act_ref[row, frame] = act.astype(BF16)
            scaled = grad[row, frame] * (sig + act * (1.0 - sig)) * gain
            scaled_ref[row, frame] = scaled
            first = first + lanes_of(scaled)
            second = second + lanes_of(scaled * normed)
    put_rows(sums_ref, group_sums(first), group_sums(second))


def hidden_grad_kernel(
    hidden, scaled, par_ref, st_ref, sums_ref, after, out_ref, down_ref, up_ref, *, count
):
    rows, frames, channels, cols = hidden.shape
    mean, inverse, _, _, _ = norm_columns(par_ref, st_ref, count, 3)
    means = sums_ref[0] / count
    first, second = columns_of(means[0:1], means[1:2])[:2]
    for row in range(rows):
        for frame in range(frames):
            normed = (hidden[row, frame] - mean) * inverse
            plane = (inverse * (scaled[row, frame] - first - normed * second)).astype(BF16)
            out_ref[row, frame] = plane
            if row == rows - 1:
                down_ref[0, frame] = plane
            if row == 0:
                up_ref[0, frame] = plane


def put_halves(flag_ref, mine_ref, theirs_ref, tap, block):
    half = block.shape[0] // 2
    here = pl.ds(tap, half, stride=SLOTS)
    upper, lower = block[:half], block[half:]
    is_first = flag_ref[3] == 0
    mine_ref[here, :] = jnp.where(is_first, upper, lower)
    theirs_ref[here, :] = jnp.where(is_first, lower, upper)


def encoded(value):
    slot = lax.broadcasted_iota(jnp.int32, value.shape, 1)
    value = jnp.where(slot < TAPS, value, 0.0)
    top = jnp.max(jnp.abs(value), axis=1, keepdims=True)
    power = jnp.ceil(jnp.log(jnp.maximum(top, 1e-30)) * (1.0 / LN2))
    number = jnp.round(value * (FULL * jnp.exp(power * -LN2)))
    return jnp.where(slot < TAPS, number, power).astype(jnp.int32).astype(jnp.int16)


def decoded_value(number):
    number = number.astype(jnp.int32).astype(F32)
    return number * (jnp.exp(number[:, SLOTS - 1 : SLOTS] * LN2) * (1.0 / FULL))


def first_scatter_kernel(flag_ref, *refs, slot):
    me = flag_ref[slot]
    for which in range(2):
        mine, other = refs[2 * which], refs[2 * which + 1]
        for k, out in enumerate(refs[4:]):
            total = mine[me ^ k] + other[me ^ k]
            out[which] = total if k == 0 else encoded(total)


def scatter_kernel(flag_ref, *refs, received, sent, slot):
    me = flag_ref[slot]
    for which in range(2):
        for k, out in enumerate(refs[-sent:]):
            total = refs[0][which, me ^ k]
            for ref in refs[1:received]:
                total = total + decoded_value(ref[which, me ^ k])
            out[which] = total if k == 0 else encoded(total)


def total_kernel(*refs, received):
    for which in range(2):
        total = refs[0][which]
        for ref in refs[1:received]:
            total = total + decoded_value(ref[which])
        refs[-1][which] = encoded(total)


def split_kernel(flag_ref, *refs, received, slot):
    me = flag_ref[slot]
    for which in range(2):
        for k, ref in enumerate(refs[:received]):
            refs[which - 2][me ^ k] = ref[which]


def gather_kernel(flag_ref, *refs, slot):
    me = flag_ref[slot]
    for k, ref in enumerate(refs[:-1]):
        refs[-1][me ^ k] = ref[...]


def join_kernel(flag_ref, mine_ref, theirs_ref, out_ref, first_ref, second_ref):
    half, _, channels = mine_ref.shape
    is_first = flag_ref[3] == 0
    first_ref[...] = decoded_value(jnp.where(is_first, mine_ref[...], theirs_ref[...])).reshape(first_ref.shape)
    second_ref[...] = decoded_value(jnp.where(is_first, theirs_ref[...], mine_ref[...])).reshape(second_ref.shape)
    for tap in range(TAPS):
        here = slice(tap * channels, (tap + 1) * channels)
        out_ref[:half, here] = first_ref[pl.ds(tap, half, stride=SLOTS), :]
        out_ref[half:, here] = second_ref[pl.ds(tap, half, stride=SLOTS), :]


def weight_second_kernel(flag_ref, stack_ref, act_ref, mine_ref, theirs_ref, right_ref):
    rows, frames, channels, cols = act_ref.shape
    for row in range(rows):
        right_ref[row * cols : (row + 1) * cols] = jnp.transpose(
            act_ref[row].reshape(frames * channels, cols)
        )
    right = right_ref[...]
    for down in range(3):
        parts = []
        for frame in range(4):
            left = jnp.concatenate([stack_ref[down + row, frame] for row in range(rows)], axis=1)
            parts.append(jnp.dot(left, right, preferred_element_type=F32))
        for kt in range(3):
            term = parts[2 - kt][:, :channels] + parts[3 - kt][:, channels:]
            for across in range(3):
                tap = 9 * kt + 3 * (2 - down) + (2 - across)
                put_halves(flag_ref, mine_ref, theirs_ref, tap, term[across * channels : (across + 1) * channels])


def weight_first_kernel(flag_ref, stack_ref, grad_ref, mine_ref, theirs_ref, right_ref):
    rows, frames, channels, cols = grad_ref.shape
    for row in range(rows):
        right_ref[row * cols : (row + 1) * cols] = jnp.transpose(
            grad_ref[row].reshape(frames * channels, cols)
        )
    right = right_ref[...]
    for down in range(3):
        parts = []
        for frame in range(4):
            left = jnp.concatenate([stack_ref[down + row, frame] for row in range(rows)], axis=1)
            parts.append(jnp.dot(left, right, preferred_element_type=F32))
        for kt in range(3):
            term = parts[kt][:, :channels] + parts[kt + 1][:, channels:]
            for across in range(3):
                tap = 9 * kt + 3 * down + across
                block = jnp.transpose(term[across * channels : (across + 1) * channels])
                put_halves(flag_ref, mine_ref, theirs_ref, tap, block)


def first_grad_kernel(flag_ref, *refs, count):
    weight, latent, par_ref, st_ref, scaled_ref, sums_ref, stack_ref = refs[-7:]
    rows, frames, channels, cols = latent.shape
    mean, inverse, gain, shift, scale = norm_columns(par_ref, st_ref, count, 1)
    fill_future(stack_ref, flag_ref, *refs[:-7])
    first = jnp.zeros((channels, 128), F32)
    second = jnp.zeros((channels, 128), F32)
    for row in range(rows):
        out = conv_rows(stack_ref, weight, row)
        for frame in range(frames):
            grad = out[frame * channels : (frame + 1) * channels]
            normed = (latent[row, frame].astype(F32) * scale - mean) * inverse
            pre = normed * gain + shift
            sig = sigmoid(pre)
            scaled = grad * (sig + pre * sig * (1.0 - sig)) * gain
            scaled_ref[row, frame] = scaled
            first = first + lanes_of(scaled)
            second = second + lanes_of(scaled * normed)
    put_rows(sums_ref, group_sums(first), group_sums(second))


def decoded_grad_kernel(scaled, latent, cotangent, par_ref, st_ref, sums_ref, out_ref, token_ref, *, count):
    token_ref[...] = jnp.zeros(token_ref.shape, F32)
    rows, frames, channels, cols = latent.shape
    mean, inverse, _, _, scale = norm_columns(par_ref, st_ref, count, 1)
    means = sums_ref[0] / count
    first, second = columns_of(means[0:1], means[1:2])[:2]
    for row in range(rows):
        for frame in range(frames):
            normed = (latent[row, frame].astype(F32) * scale - mean) * inverse
            out_ref[:, frame, row, :] = cotangent[row, frame].astype(F32) + inverse * (
                scaled[row, frame] - first - normed * second
            )


def weight_forward_kernel(weight, out_ref):
    channels = weight.shape[0]
    wide = 3 * channels
    for t in range(2):
        for kr in range(3):
            for f in range(4):
                kt = f - t
                here = slice((kr * 4 + f) * wide, (kr * 4 + f + 1) * wide)
                if 0 <= kt < 3:
                    tap = 3 * kt + kr
                    block = weight[:, tap * wide : (tap + 1) * wide]
                else:
                    block = jnp.zeros((channels, wide), BF16)
                out_ref[t * channels : (t + 1) * channels, here] = block


def weight_back_kernel(weight, out_ref):
    channels = weight.shape[0]
    for down in range(3):
        for across in range(3):
            blocks = [
                jnp.transpose(
                    weight[
                        :,
                        (9 * kt + 3 * (2 - down) + 2 - across) * channels : (9 * kt + 3 * (2 - down) + 3 - across)
                        * channels,
                    ]
                )
                for kt in range(3)
            ]
            for t in range(2):
                for f in range(4):
                    kt = t + 2 - f
                    start = ((down * 4 + f) * 3 + across) * channels
                    block = blocks[kt] if 0 <= kt < 3 else jnp.zeros((channels, channels), BF16)
                    out_ref[t * channels : (t + 1) * channels, start : start + channels] = block


def shifted(value, axis, steps):
    count = lax.axis_size(axis)
    initial, last = max(0, -steps), min(count, count - steps)
    return lax.ppermute(value, axis, [(source, source + steps) for source in range(initial, last)])


def rounds(axes):
    for axis in axes:
        count = lax.axis_size(axis)
        step = 1
        while step < count:
            wide = 4 if 4 * step <= count else 2
            yield axis, step, [[(i, i ^ (step * k)) for i in range(count)] for k in range(1, wide)]
            step *= wide


def pairwise(parts, join):
    while len(parts) > 1:
        parts = [join(a, b) for a, b in zip(parts[::2], parts[1::2])]
    return parts[0]


def all_sum(value):
    for axis, _, exchanges in rounds(("tm", "height", "width")):
        parts = [value] + [lax.ppermute(value, axis, pairs) for pairs in exchanges]
        value = pairwise(parts, lambda a, b: a + b)
    return value


def all_stats(value, count, axes=("tm", "height", "width")):
    for axis, _, exchanges in rounds(axes):
        parts = [(value, count)] + [(lax.ppermute(value, axis, pairs), count) for pairs in exchanges]
        value, count = pairwise(parts, joined_stats)
    return value


def joined_stats(first, second):
    (a, count), (b, _) = first, second
    gap = a[:, 0:1] - b[:, 0:1]
    squares = a[:, 1:2] + b[:, 1:2] + gap * gap * (0.5 * count)
    return jnp.concatenate([0.5 * (a[:, 0:1] + b[:, 0:1]), squares], axis=1), 2.0 * count


def swapped(value):
    return lax.ppermute(value, "width", [(0, 1), (1, 0)])


def weight_rounds():
    return list(rounds(("height", "tm")))


def scattered(flags, second, first):
    half, _, channels = second[0].shape
    axis, _, exchanges = weight_rounds()[0]
    parts = len(exchanges) + 1
    rows = half // parts
    terms = [part for mine, theirs in (second, first) for part in (mine, swapped(theirs))]
    part = (2, rows, SLOTS, channels)
    kept, *sent = call(
        functools.partial(first_scatter_kernel, slot=4),
        [shape(part, F32)] + [shape(part, jnp.int16)] * (parts - 1),
        [SMEM] + [VMEM] * 4,
        (flags, *[term.reshape(parts, rows, SLOTS, channels) for term in terms]),
    )
    return [kept] + [lax.ppermute(v, axis, pairs) for v, pairs in zip(sent, exchanges)], sent[0]


def summed(flags, received, after):
    for number, (axis, _, exchanges) in enumerate(weight_rounds()[1:], 5):
        parts = len(exchanges) + 1
        _, rows, _, channels = received[0].shape
        part = (2, rows // parts, SLOTS, channels)
        views = [v.reshape(2, parts, *part[1:]) for v in received]
        kept, *sent = call(
            functools.partial(scatter_kernel, received=len(views), sent=parts, slot=number),
            [shape(part, F32)] + [shape(part, jnp.int16)] * (parts - 1),
            [SMEM] + [VMEM] * (len(views) + len(after)),
            (flags, *views, *after),
        )
        after = ()
        received = [kept] + [lax.ppermute(v, axis, pairs) for v, pairs in zip(sent, exchanges)]
    return received


def gathered(flags, received, after, after_last):
    (total,) = call(
        functools.partial(total_kernel, received=len(received)),
        [shape(received[0].shape, jnp.int16)],
        [VMEM] * (len(received) + len(after)),
        (*received, *after),
    )
    _, rows, _, channels = total.shape
    back = list(enumerate(weight_rounds(), 4))[::-1]
    number, (axis, _, exchanges) = back[0]
    pieces = [total] + [lax.ppermute(total, axis, pairs) for pairs in exchanges]
    values = call(
        functools.partial(split_kernel, received=len(pieces), slot=number),
        [shape((len(pieces), rows, SLOTS, channels), jnp.int16)] * 2,
        [SMEM] + [VMEM] * (len(pieces) + 1),
        (flags, *pieces, after_last),
    )
    results = []
    for value in values:
        for number, (axis, _, exchanges) in back[1:]:
            value = value.reshape(-1, SLOTS, channels)
            pieces = [value] + [lax.ppermute(value, axis, pairs) for pairs in exchanges]
            (value,) = call(
                functools.partial(gather_kernel, slot=number),
                [shape((len(pieces), *value.shape), jnp.int16)],
                [SMEM] + [VMEM] * len(pieces),
                (flags, *pieces),
            )
        results.append(value.reshape(-1, SLOTS, channels))
    return results


def joined(flags, mine, theirs):
    half, _, channels = mine.shape
    (total,) = call(
        join_kernel,
        [shape((2 * half, TAPS * channels), F32)],
        [SMEM] + [VMEM] * 2,
        (flags, mine, theirs),
        scratch=[pltpu.VMEM((half * SLOTS, channels), F32)] * 2,
    )
    return total


def edges(flags, planes, after):
    channels = planes[0].shape[2]
    args = (*planes, *after)
    (columns,) = call(edges_kernel, [shape((channels, 128), BF16)], [SMEM] + [VMEM] * len(args), (flags, *args))
    return columns


def row_halos(down, up, after=()):
    above, below = shifted(down, "height", 1), shifted(up, "height", -1)
    (near,) = call(
        rows_kernel, [shape((2, *down.shape[1:]), BF16)], [VMEM] * (2 + len(after)), (above, below, *after)
    )
    return near


def with_columns(flags, own, around, after=()):
    edge = swapped(edges(flags, (own, around[0]), after))
    rim = swapped(edges(flags, around[1:], after))
    return *around, edge, rim


def shards(
    latent,
    exponents,
    cotangent,
    conv_first,
    conv_second,
    gain_first,
    shift_first,
    gain_second,
    shift_second,
):
    channels, frames, rows, cols = latent.shape
    groups = exponents.shape[0]
    devices = lax.axis_size("tm") * lax.axis_size("height") * lax.axis_size("width")
    count = float(channels // groups * frames * rows * cols * devices)
    tm, height, width = (lax.axis_index(axis) for axis in ("tm", "height", "width"))
    flags = jnp.stack(
        [
            (tm > 0).astype(jnp.int32),
            (height > 0).astype(jnp.int32),
            (height < lax.axis_size("height") - 1).astype(jnp.int32),
            width.astype(jnp.int32),
        ]
        + [
            (lax.axis_index(axis) // step % (len(exchanges) + 1)).astype(jnp.int32)
            for axis, step, exchanges in weight_rounds()
        ]
    )
    scale = jnp.repeat(jnp.exp2(exponents.astype(F32)), channels // groups)
    zeros = jnp.zeros_like(scale)
    par = jnp.stack([scale, gain_first, shift_first, gain_second, shift_second, zeros, zeros, zeros])
    block = (rows, frames, channels, cols)
    stack = (rows + 2, 4, 3 * channels, cols)
    taps = (2 * channels, 36 * channels)
    halves = [shape((channels // 2 * SLOTS, channels), F32)] * 2
    conv_flops = 3 * 2 * 4 * 256 * 36 * channels * 2 * channels
    small = shape((1, 2, channels), F32)

    message = shape((1, frames, channels, cols), BF16)
    latent, down, up, stats_first = call(
        planes_kernel, [shape(block, BF16), message, message, small], [VMEM] * 2, (latent, par)
    )
    cotangent, down_c, up_c = call(planes_kernel, [shape(block, BF16), message, message], [VMEM], (cotangent,))
    past, future_c = shifted(latent, "tm", 1), shifted(cotangent, "tm", -1)
    near = row_halos(down, up, (past,))
    near_c = row_halos(down_c, up_c, (future_c,))
    around = with_columns(flags, latent, (past, near, shifted(near, "tm", 1)))
    around_c = (future_c, near_c, shifted(near_c, "tm", -1))
    stats_first = all_stats(stats_first, count / devices, ("height", "width", "tm"))
    (weight_first,) = call(weight_forward_kernel, [shape(taps, BF16)], [VMEM], (conv_first,))
    (weight_second_t,) = call(weight_back_kernel, [shape(taps, BF16)], [VMEM], (conv_second,))
    (weight_first_t,) = call(weight_back_kernel, [shape(taps, BF16)], [VMEM], (conv_first,))

    hidden, stats_second, stack_first = call(
        functools.partial(conv_first_kernel, count=count),
        [shape(block, F32), small, shape(stack, BF16)],
        [SMEM] + [VMEM] * 10,
        (flags, latent, *around, par, stats_first, weight_first, near_c),
        flops=conv_flops,
        transcendentals=3 * latent.size,
    )
    around_c = with_columns(flags, cotangent, around_c, (stats_second,))
    stats_second = all_stats(stats_second, count / devices)
    grad_second, stack_c = call(
        conv_back_kernel,
        [shape(block, F32), shape(stack, BF16)],
        [SMEM] + [VMEM] * 7,
        (flags, cotangent, *around_c, weight_second_t),
        flops=conv_flops,
    )
    act_second, scaled, sums = call(
        functools.partial(norm_second_kernel, count=count),
        [shape(block, BF16), shape(block, F32), small],
        [VMEM] * 4,
        (hidden, grad_second, par, stats_second),
        transcendentals=latent.size,
    )
    sums = all_sum(sums)
    halves_second = call(
        weight_second_kernel,
        halves,
        [SMEM] + [VMEM] * 2,
        (flags, stack_c, act_second),
        scratch=[pltpu.VMEM((rows * cols, frames * channels), BF16)],
        flops=conv_flops,
    )
    hidden_grad, down, up = call(
        functools.partial(hidden_grad_kernel, count=count),
        [shape(block, BF16), message, message],
        [VMEM] * 6,
        (hidden, scaled, par, stats_second, sums, halves_second[0]),
    )
    near = row_halos(down, up)
    around = (shifted(hidden_grad, "tm", -1), near, shifted(near, "tm", -1))
    halves_first = call(
        weight_first_kernel,
        halves,
        [SMEM] + [VMEM] * 2,
        (flags, stack_first, hidden_grad),
        scratch=[pltpu.VMEM((rows * cols, frames * channels), BF16)],
        flops=conv_flops,
    )
    halves_second, halves_first = (
        [v.reshape(channels // 2, SLOTS, channels) for v in halves] for halves in (halves_second, halves_first)
    )
    weights, sent = scattered(flags, halves_second, halves_first)
    around = with_columns(flags, hidden_grad, around, (sent,))
    scaled, sums_first = call(
        functools.partial(first_grad_kernel, count=count),
        [shape(block, F32), small],
        [SMEM] + [VMEM] * 10,
        (flags, hidden_grad, *around, weight_first_t, latent, par, stats_first),
        scratch=[pltpu.VMEM(stack, BF16)],
        flops=conv_flops,
        transcendentals=latent.size,
    )
    weights = summed(flags, weights, around[:2])
    sums_first = all_sum(sums_first)
    decoded_grad, token = call(
        functools.partial(decoded_grad_kernel, count=count),
        [shape((channels, frames, rows, cols), F32), shape((8, 128), F32)],
        [VMEM] * 6,
        (scaled, latent, cotangent, par, stats_first, sums_first),
    )
    second, first = gathered(flags, weights, (sums_first,), token)
    conv_second_grad = joined(flags, second, swapped(second))
    conv_first_grad = joined(flags, first, swapped(first))
    return decoded_grad, conv_first_grad, conv_second_grad


def solution(mesh):
    block = P(None, "tm", "height", "width")
    return jax.shard_map(
        shards,
        mesh=mesh,
        in_specs=(block, P(), block, P(), P(), P(), P(), P(), P()),
        out_specs=(block, P(), P()),
        check_vma=False,
    )
```

```python
import functools

import jax
import jax.numpy as jnp
from jax import lax
from jax.experimental import pallas as pl
from jax.experimental.pallas import tpu as pltpu
from jax.sharding import PartitionSpec as P

epsilon = 1e-05
F32 = jnp.float32
BF16 = jnp.bfloat16
GROUP = 4
TAPS, SLOTS = 27, 32
FULL = 32760.0
LN2 = 0.6931471805599453
VMEM = pl.BlockSpec(memory_space=pltpu.VMEM)
SMEM = pl.BlockSpec(memory_space=pltpu.SMEM)


def call(body, outs, specs, args, scratch=(), flops=0, transcendentals=0, limit=20):
    moved = sum(a.size * a.dtype.itemsize for a in args)
    moved += sum(o.size * o.dtype.itemsize for o in outs)
    return pl.pallas_call(
        body,
        out_shape=tuple(outs),
        in_specs=specs,
        out_specs=tuple(VMEM for _ in outs),
        scratch_shapes=scratch,
        compiler_params=pltpu.CompilerParams(vmem_limit_bytes=limit << 20),
        cost_estimate=pl.CostEstimate(
            flops=flops, bytes_accessed=moved, transcendentals=transcendentals
        ),
    )(*args)


def shape(dims, dtype):
    return jax.ShapeDtypeStruct(dims, dtype)


def group_sums(acc):
    rows = acc.shape[0]
    row = lax.broadcasted_iota(jnp.int32, acc.shape, 0)
    step = 1
    while step < GROUP:
        up = pltpu.roll(acc, rows - step, axis=0)
        down = pltpu.roll(acc, step, axis=0)
        acc = acc + jnp.where((row & step) == 0, up, down)
        step *= 2
    return jnp.sum(acc, axis=1, keepdims=True)


def lanes_of(plane):
    total = plane[:, :128]
    for start in range(128, plane.shape[1], 128):
        total = total + plane[:, start : start + 128]
    return total


def as_rows(first, second):
    channels = first.shape[0]
    lane = lax.broadcasted_iota(jnp.int32, (channels, 128), 1)
    both = jnp.where(lane == 0, first, jnp.where(lane == 1, second, 0.0))
    return jnp.transpose(both)[:2]


def local_stats(planes, count):
    acc = None
    for plane in planes:
        part = lanes_of(plane())
        acc = part if acc is None else acc + part
    mean = group_sums(acc) / count
    acc = None
    for plane in planes:
        off = plane() - mean
        part = lanes_of(off * off)
        acc = part if acc is None else acc + part
    return mean, group_sums(acc)


def put_rows(out_ref, first, second):
    out_ref[0] = as_rows(first, second)


def combined(st_ref, count):
    return st_ref[0, 0:1], st_ref[0, 1:2] / count


def columns_of(*rows):
    rows = list(rows) + [jnp.zeros_like(rows[0])] * (8 - len(rows))
    cols = jnp.transpose(jnp.concatenate(rows, axis=0))
    return [cols[:, i : i + 1] for i in range(8)]


def sigmoid(value):
    return 0.5 + 0.5 * jnp.tanh(0.5 * value)


def planes_kernel(latent_ref, cotangent_ref, par_ref, latent_out, cotangent_out, down_ref, up_ref, st_ref):
    _, frames, rows, cols = latent_ref.shape
    for which, (natural, out) in enumerate(((latent_ref, latent_out), (cotangent_ref, cotangent_out))):
        for row in range(rows):
            for frame in range(frames):
                plane = natural[:, frame, row, :]
                out[row, frame] = plane
                if row == rows - 1:
                    down_ref[which, frame] = plane
                if row == 0:
                    up_ref[which, frame] = plane
    scale = columns_of(par_ref[0:1])[0]
    planes = [
        functools.partial(lambda r, t: latent_out[r, t].astype(F32) * scale, r, t)
        for r in range(rows)
        for t in range(frames)
    ]
    put_rows(st_ref, *local_stats(planes, float(GROUP * rows * frames * cols)))


def rows_kernel(above_ref, below_ref, *refs):
    for which, out in enumerate(refs[-above_ref.shape[0] :]):
        out[0] = above_ref[which]
        out[1] = below_ref[which]


def source(own, other, near, far, other_first):
    def at(row, frame):
        is_other = (frame < 2) == other_first
        if row == 0 or row == own.shape[0] + 1:
            return (far if is_other else near), (0 if row == 0 else 1, frame % 2)
        return (other if is_other else own), (row - 1, frame % 2)

    return at


def edges_kernel(flag_ref, first_ref, second_ref, *refs):
    planes, out_ref = (first_ref, second_ref), refs[-1]
    is_first = flag_ref[3] == 0
    channels = planes[0].shape[2]
    lane = lax.broadcasted_iota(jnp.int32, (channels, 128), 1)
    acc = jnp.zeros((channels, 128), F32)
    number = 0
    for ref in planes:
        for row in range(ref.shape[0]):
            for frame in range(ref.shape[1]):
                last = pltpu.roll(ref[row, frame, :, -128:].astype(F32), 1, axis=1)
                edge = jnp.where(is_first, last, ref[row, frame, :, :128].astype(F32))
                moved = pltpu.roll(edge, number, axis=1) if number else edge
                acc = jnp.where(lane == number, moved, acc)
                number += 1
    out_ref[...] = acc.astype(BF16)


def edge_lane(row, frame, rows, other_first):
    is_other = int((frame < 2) == other_first)
    if row == 0 or row == rows + 1:
        return 1, 4 * is_other + 2 * int(row > 0) + frame % 2
    return 0, 2 * rows * is_other + 2 * (row - 1) + frame % 2


def fill_stack(stack, row, frame, plane, column, on_left, on_right):
    channels, cols = plane.shape
    lane = lax.broadcasted_iota(jnp.int32, (channels, cols), 1)
    column = column.astype(F32)
    left = jnp.where(lane == 0, (column * on_left).astype(BF16), pltpu.roll(plane, 1, axis=1))
    right = jnp.where(lane == cols - 1, (column * on_right).astype(BF16), pltpu.roll(plane, cols - 1, axis=1))
    stack[row, frame, 0:channels] = left
    stack[row, frame, channels : 2 * channels] = plane
    stack[row, frame, 2 * channels : 3 * channels] = right


def sides(flag_ref):
    on_left = (flag_ref[3] != 0).astype(F32)
    on_right = (flag_ref[3] == 0).astype(F32)
    return on_left, on_right


def conv_rows(stack, weight, row):
    three = stack[row : row + 3].reshape(weight.shape[1], stack.shape[3])
    return jnp.dot(weight[...], three, preferred_element_type=F32)


def norm_columns(par_ref, st_ref, count, gain_row):
    par = par_ref[...]
    mean, variance = combined(st_ref, count)
    inverse = 1.0 / jnp.sqrt(variance + epsilon)
    gain = par[gain_row : gain_row + 1]
    shift = par[gain_row + 1 : gain_row + 2]
    return columns_of(mean, inverse, gain, shift, par[0:1])[:5]


def conv_first_kernel(
    flag_ref, own, past, near, far, edge_ref, rim_ref, par_ref, st_ref, weight, after, hidden_ref, st_out, stack_ref,
    *, count
):
    rows, frames, channels, cols = own.shape
    at = source(own, past, near, far, True)
    mean, inverse, gain, shift, scale = norm_columns(par_ref, st_ref, count, 1)

    def act(latent):
        pre = (latent.astype(F32) * scale - mean) * inverse * gain + shift
        return pre * sigmoid(pre)

    has_past = flag_ref[0].astype(F32)
    has_top = flag_ref[1].astype(F32)
    has_bottom = flag_ref[2].astype(F32)
    on_left, on_right = sides(flag_ref)
    edges = (act(edge_ref[...]), act(rim_ref[...]))
    for row in range(rows + 2):
        for frame in range(4):
            ref, index = at(row, frame)
            which, number = edge_lane(row, frame, rows, True)
            plane = act(ref[index])
            column = edges[which][:, number : number + 1]
            factor = None
            if frame < 2:
                factor = has_past
            if row in (0, rows + 1):
                beside = has_top if row == 0 else has_bottom
                factor = beside if factor is None else factor * beside
            if factor is not None:
                plane = plane * factor
                column = column * factor
            fill_stack(stack_ref, row, frame, plane.astype(BF16), column, on_left, on_right)
    for row in range(rows):
        out = conv_rows(stack_ref, weight, row)
        for frame in range(frames):
            hidden_ref[row, frame] = out[frame * channels : (frame + 1) * channels]
    planes = [
        functools.partial(lambda r, t: hidden_ref[r, t], r, t) for r in range(rows) for t in range(frames)
    ]
    put_rows(st_out, *local_stats(planes, float(GROUP * rows * frames * cols)))


def fill_future(stack, flag_ref, own, future, near, far, edge_ref, rim_ref):
    rows = own.shape[0]
    at = source(own, future, near, far, False)
    on_left, on_right = sides(flag_ref)
    edges = (edge_ref[...], rim_ref[...])
    for row in range(rows + 2):
        for frame in range(4):
            ref, index = at(row, frame)
            which, number = edge_lane(row, frame, rows, False)
            fill_stack(stack, row, frame, ref[index], edges[which][:, number : number + 1], on_left, on_right)


def conv_back_kernel(flag_ref, *refs):
    weight, grad_ref, stack_ref = refs[-3:]
    rows, frames, channels, _ = grad_ref.shape
    fill_future(stack_ref, flag_ref, *refs[:-3])
    for row in range(rows):
        out = conv_rows(stack_ref, weight, row)
        for frame in range(frames):
            grad_ref[row, frame] = out[frame * channels : (frame + 1) * channels]


def norm_second_kernel(hidden, grad, par_ref, st_ref, act_ref, scaled_ref, sums_ref, *, count):
    rows, frames, channels, cols = hidden.shape
    mean, inverse, gain, shift, _ = norm_columns(par_ref, st_ref, count, 3)
    first = jnp.zeros((channels, 128), F32)
    second = jnp.zeros((channels, 128), F32)
    for row in range(rows):
        for frame in range(frames):
            normed = (hidden[row, frame] - mean) * inverse
            pre = normed * gain + shift
            sig = sigmoid(pre)
            act = pre * sig
            act_ref[row, frame] = act.astype(BF16)
            scaled = grad[row, frame] * (sig + act * (1.0 - sig)) * gain
            scaled_ref[row, frame] = scaled
            first = first + lanes_of(scaled)
            second = second + lanes_of(scaled * normed)
    put_rows(sums_ref, group_sums(first), group_sums(second))


def hidden_grad_kernel(
    hidden, scaled, par_ref, st_ref, sums_ref, out_ref, down_ref, up_ref, *, count
):
    rows, frames, channels, cols = hidden.shape
    mean, inverse, _, _, _ = norm_columns(par_ref, st_ref, count, 3)
    means = sums_ref[0] / count
    first, second = columns_of(means[0:1], means[1:2])[:2]
    for row in range(rows):
        for frame in range(frames):
            normed = (hidden[row, frame] - mean) * inverse
            plane = (inverse * (scaled[row, frame] - first - normed * second)).astype(BF16)
            out_ref[row, frame] = plane
            if row == rows - 1:
                down_ref[0, frame] = plane
            if row == 0:
                up_ref[0, frame] = plane


def put_halves(flag_ref, mine_ref, theirs_ref, tap, block):
    half = block.shape[0] // 2
    here = pl.ds(tap, half, stride=SLOTS)
    upper, lower = block[:half], block[half:]
    is_first = flag_ref[3] == 0
    mine_ref[here, :] = jnp.where(is_first, upper, lower)
    theirs_ref[here, :] = jnp.where(is_first, lower, upper)


def encoded(value):
    slot = lax.broadcasted_iota(jnp.int32, value.shape, 1)
    value = jnp.where(slot < TAPS, value, 0.0)
    top = jnp.max(jnp.abs(value), axis=1, keepdims=True)
    power = jnp.ceil(jnp.log(jnp.maximum(top, 1e-30)) * (1.0 / LN2))
    number = jnp.round(value * (FULL * jnp.exp(power * -LN2)))
    return jnp.where(slot < TAPS, number, power).astype(jnp.int32).astype(jnp.int16)


def decoded_value(number):
    number = number.astype(jnp.int32).astype(F32)
    return number * (jnp.exp(number[:, SLOTS - 1 : SLOTS] * LN2) * (1.0 / FULL))


def first_scatter_kernel(flag_ref, *refs, slot):
    me = flag_ref[slot]
    for which in range(2):
        mine, other = refs[2 * which], refs[2 * which + 1]
        for k, out in enumerate(refs[4:]):
            total = mine[me ^ k] + other[me ^ k]
            out[which] = total if k == 0 else encoded(total)


def scatter_kernel(flag_ref, *refs, received, sent, slot):
    me = flag_ref[slot]
    for which in range(2):
        for k, out in enumerate(refs[-sent:]):
            total = refs[0][which, me ^ k]
            for ref in refs[1:received]:
                total = total + decoded_value(ref[which, me ^ k])
            out[which] = total if k == 0 else encoded(total)


def total_kernel(*refs, received):
    for which in range(2):
        total = refs[0][which]
        for ref in refs[1:received]:
            total = total + decoded_value(ref[which])
        refs[-1][which] = encoded(total)


def split_kernel(flag_ref, *refs, received, slot):
    me = flag_ref[slot]
    for which in range(2):
        for k, ref in enumerate(refs[:received]):
            refs[which - 2][me ^ k] = ref[which]


def gather_kernel(flag_ref, *refs, slot):
    me = flag_ref[slot]
    for k, ref in enumerate(refs[:-1]):
        refs[-1][me ^ k] = ref[...]


def join_kernel(flag_ref, mine_ref, theirs_ref, out_ref, first_ref, second_ref):
    half, _, channels = mine_ref.shape

    @pl.when(pl.program_id(0) == 0)
    def _():
        is_first = flag_ref[3] == 0
        mine, theirs = mine_ref[...], theirs_ref[...]
        first_ref[...] = decoded_value(jnp.where(is_first, mine, theirs)).reshape(first_ref.shape)
        second_ref[...] = decoded_value(jnp.where(is_first, theirs, mine)).reshape(second_ref.shape)

    for number in range(3):
        here = pl.ds(3 * pl.program_id(0) + number, half, stride=SLOTS)
        there = slice(number * channels, (number + 1) * channels)
        out_ref[:half, there] = first_ref[here, :]
        out_ref[half:, there] = second_ref[here, :]


def weight_second_kernel(flag_ref, stack_ref, act_ref, mine_ref, theirs_ref, right_ref):
    rows, frames, channels, cols = act_ref.shape
    for row in range(rows):
        right_ref[row * cols : (row + 1) * cols] = jnp.transpose(
            act_ref[row].reshape(frames * channels, cols)
        )
    right = right_ref[...]
    for down in range(3):
        parts = []
        for frame in range(4):
            left = jnp.concatenate([stack_ref[down + row, frame] for row in range(rows)], axis=1)
            parts.append(jnp.dot(left, right, preferred_element_type=F32))
        for kt in range(3):
            term = parts[2 - kt][:, :channels] + parts[3 - kt][:, channels:]
            for across in range(3):
                tap = 9 * kt + 3 * (2 - down) + (2 - across)
                put_halves(flag_ref, mine_ref, theirs_ref, tap, term[across * channels : (across + 1) * channels])


def weight_first_kernel(flag_ref, stack_ref, grad_ref, mine_ref, theirs_ref, right_ref):
    rows, frames, channels, cols = grad_ref.shape
    for row in range(rows):
        right_ref[row * cols : (row + 1) * cols] = jnp.transpose(
            grad_ref[row].reshape(frames * channels, cols)
        )
    right = right_ref[...]
    for down in range(3):
        parts = []
        for frame in range(4):
            left = jnp.concatenate([stack_ref[down + row, frame] for row in range(rows)], axis=1)
            parts.append(jnp.dot(left, right, preferred_element_type=F32))
        for kt in range(3):
            term = parts[kt][:, :channels] + parts[kt + 1][:, channels:]
            for across in range(3):
                tap = 9 * kt + 3 * down + across
                block = jnp.transpose(term[across * channels : (across + 1) * channels])
                put_halves(flag_ref, mine_ref, theirs_ref, tap, block)


def first_grad_kernel(flag_ref, *refs, count):
    weight, latent, par_ref, st_ref, scaled_ref, sums_ref, stack_ref = refs[-7:]
    rows, frames, channels, cols = latent.shape
    mean, inverse, gain, shift, scale = norm_columns(par_ref, st_ref, count, 1)
    fill_future(stack_ref, flag_ref, *refs[:-7])
    first = jnp.zeros((channels, 128), F32)
    second = jnp.zeros((channels, 128), F32)
    for row in range(rows):
        out = conv_rows(stack_ref, weight, row)
        for frame in range(frames):
            grad = out[frame * channels : (frame + 1) * channels]
            normed = (latent[row, frame].astype(F32) * scale - mean) * inverse
            pre = normed * gain + shift
            sig = sigmoid(pre)
            scaled = grad * (sig + pre * sig * (1.0 - sig)) * gain
            scaled_ref[row, frame] = scaled
            first = first + lanes_of(scaled)
            second = second + lanes_of(scaled * normed)
    put_rows(sums_ref, group_sums(first), group_sums(second))


def decoded_grad_kernel(scaled, latent, cotangent, par_ref, st_ref, sums_ref, out_ref, token_ref, *, count):
    token_ref[...] = jnp.zeros(token_ref.shape, F32)
    rows, frames, channels, cols = latent.shape
    mean, inverse, _, _, scale = norm_columns(par_ref, st_ref, count, 1)
    means = sums_ref[0] / count
    first, second = columns_of(means[0:1], means[1:2])[:2]
    for row in range(rows):
        for frame in range(frames):
            normed = (latent[row, frame].astype(F32) * scale - mean) * inverse
            out_ref[:, frame, row, :] = cotangent[row, frame].astype(F32) + inverse * (
                scaled[row, frame] - first - normed * second
            )


def weight_forward_kernel(weight, out_ref):
    channels = weight.shape[0]
    wide = 3 * channels
    for t in range(2):
        for kr in range(3):
            for f in range(4):
                kt = f - t
                here = slice((kr * 4 + f) * wide, (kr * 4 + f + 1) * wide)
                if 0 <= kt < 3:
                    tap = 3 * kt + kr
                    block = weight[:, tap * wide : (tap + 1) * wide]
                else:
                    block = jnp.zeros((channels, wide), BF16)
                out_ref[t * channels : (t + 1) * channels, here] = block


def weight_back_kernel(weight, out_ref):
    channels = weight.shape[0]
    for down in range(3):
        for across in range(3):
            blocks = [
                jnp.transpose(
                    weight[
                        :,
                        (9 * kt + 3 * (2 - down) + 2 - across) * channels : (9 * kt + 3 * (2 - down) + 3 - across)
                        * channels,
                    ]
                )
                for kt in range(3)
            ]
            for t in range(2):
                for f in range(4):
                    kt = t + 2 - f
                    start = ((down * 4 + f) * 3 + across) * channels
                    block = blocks[kt] if 0 <= kt < 3 else jnp.zeros((channels, channels), BF16)
                    out_ref[t * channels : (t + 1) * channels, start : start + channels] = block


def shifted(value, axis, steps):
    count = lax.axis_size(axis)
    initial, last = max(0, -steps), min(count, count - steps)
    return lax.ppermute(value, axis, [(source, source + steps) for source in range(initial, last)])


def rounds(axes):
    for axis in axes:
        count = lax.axis_size(axis)
        step = 1
        while step < count:
            wide = 4 if 4 * step <= count else 2
            yield axis, step, [[(i, i ^ (step * k)) for i in range(count)] for k in range(1, wide)]
            step *= wide


def pairwise(parts, join):
    while len(parts) > 1:
        parts = [join(a, b) for a, b in zip(parts[::2], parts[1::2])]
    return parts[0]


def all_sum(value):
    for axis, _, exchanges in rounds(("tm", "height", "width")):
        parts = [value] + [lax.ppermute(value, axis, pairs) for pairs in exchanges]
        value = pairwise(parts, lambda a, b: a + b)
    return value


def all_stats(value, count):
    for axis, _, exchanges in rounds(("tm", "height", "width")):
        parts = [(value, count)] + [(lax.ppermute(value, axis, pairs), count) for pairs in exchanges]
        value, count = pairwise(parts, joined_stats)
    return value


def joined_stats(first, second):
    (a, count), (b, _) = first, second
    gap = a[:, 0:1] - b[:, 0:1]
    squares = a[:, 1:2] + b[:, 1:2] + gap * gap * (0.5 * count)
    return jnp.concatenate([0.5 * (a[:, 0:1] + b[:, 0:1]), squares], axis=1), 2.0 * count


def swapped(value):
    return lax.ppermute(value, "width", [(0, 1), (1, 0)])


def weight_rounds():
    return list(rounds(("height", "tm")))


def scattered(flags, second, first):
    half, _, channels = second[0].shape
    axis, _, exchanges = weight_rounds()[0]
    parts = len(exchanges) + 1
    rows = half // parts
    terms = [part for mine, theirs in (second, first) for part in (mine, swapped(theirs))]
    part = (2, rows, SLOTS, channels)
    kept, *sent = call(
        functools.partial(first_scatter_kernel, slot=4),
        [shape(part, F32)] + [shape(part, jnp.int16)] * (parts - 1),
        [SMEM] + [VMEM] * 4,
        (flags, *[term.reshape(parts, rows, SLOTS, channels) for term in terms]),
    )
    return [kept] + [lax.ppermute(v, axis, pairs) for v, pairs in zip(sent, exchanges)], sent[0]


def summed(flags, received, after):
    for number, (axis, _, exchanges) in enumerate(weight_rounds()[1:], 5):
        parts = len(exchanges) + 1
        _, rows, _, channels = received[0].shape
        part = (2, rows // parts, SLOTS, channels)
        views = [v.reshape(2, parts, *part[1:]) for v in received]
        kept, *sent = call(
            functools.partial(scatter_kernel, received=len(views), sent=parts, slot=number),
            [shape(part, F32)] + [shape(part, jnp.int16)] * (parts - 1),
            [SMEM] + [VMEM] * (len(views) + len(after)),
            (flags, *views, *after),
        )
        after = ()
        received = [kept] + [lax.ppermute(v, axis, pairs) for v, pairs in zip(sent, exchanges)]
    return received


def gathered(flags, received, after, after_last):
    (total,) = call(
        functools.partial(total_kernel, received=len(received)),
        [shape(received[0].shape, jnp.int16)],
        [VMEM] * (len(received) + len(after)),
        (*received, *after),
    )
    _, rows, _, channels = total.shape
    back = list(enumerate(weight_rounds(), 4))[::-1]
    number, (axis, _, exchanges) = back[0]
    pieces = [total] + [lax.ppermute(total, axis, pairs) for pairs in exchanges]
    values = call(
        functools.partial(split_kernel, received=len(pieces), slot=number),
        [shape((len(pieces), rows, SLOTS, channels), jnp.int16)] * 2,
        [SMEM] + [VMEM] * (len(pieces) + 1),
        (flags, *pieces, after_last),
    )
    results = []
    for value in values:
        for number, (axis, _, exchanges) in back[1:]:
            value = value.reshape(-1, SLOTS, channels)
            pieces = [value] + [lax.ppermute(value, axis, pairs) for pairs in exchanges]
            (value,) = call(
                functools.partial(gather_kernel, slot=number),
                [shape((len(pieces), *value.shape), jnp.int16)],
                [SMEM] + [VMEM] * len(pieces),
                (flags, *pieces),
            )
        results.append(value.reshape(-1, SLOTS, channels))
    return results


def joined(flags, mine, theirs):
    half, _, channels = mine.shape
    total = pl.pallas_call(
        join_kernel,
        grid=(TAPS // 3,),
        out_shape=shape((2 * half, TAPS * channels), F32),
        in_specs=[SMEM, VMEM, VMEM],
        out_specs=pl.BlockSpec((2 * half, 3 * channels), lambda step: (0, step)),
        scratch_shapes=[pltpu.VMEM((half * SLOTS, channels), F32)] * 2,
        compiler_params=pltpu.CompilerParams(vmem_limit_bytes=20 << 20),
        cost_estimate=pl.CostEstimate(flops=0, bytes_accessed=8 << 20, transcendentals=0),
    )(flags, mine, theirs)
    return total


def edges(flags, planes, after):
    channels = planes[0].shape[2]
    args = (*planes, *after)
    (columns,) = call(edges_kernel, [shape((channels, 128), BF16)], [SMEM] + [VMEM] * len(args), (flags, *args))
    return columns


def row_halos(down, up, after=()):
    above, below = shifted(down, "height", 1), shifted(up, "height", -1)
    return call(
        rows_kernel,
        [shape((2, *down.shape[1:]), BF16)] * down.shape[0],
        [VMEM] * (2 + len(after)),
        (above, below, *after),
    )


def with_columns(flags, own, around, after=()):
    edge = swapped(edges(flags, (own, around[0]), after))
    rim = swapped(edges(flags, around[1:], after))
    return *around, edge, rim


def shards(
    latent,
    exponents,
    cotangent,
    conv_first,
    conv_second,
    gain_first,
    shift_first,
    gain_second,
    shift_second,
):
    channels, frames, rows, cols = latent.shape
    groups = exponents.shape[0]
    devices = lax.axis_size("tm") * lax.axis_size("height") * lax.axis_size("width")
    count = float(channels // groups * frames * rows * cols * devices)
    tm, height, width = (lax.axis_index(axis) for axis in ("tm", "height", "width"))
    flags = jnp.stack(
        [
            (tm > 0).astype(jnp.int32),
            (height > 0).astype(jnp.int32),
            (height < lax.axis_size("height") - 1).astype(jnp.int32),
            width.astype(jnp.int32),
        ]
        + [
            (lax.axis_index(axis) // step % (len(exchanges) + 1)).astype(jnp.int32)
            for axis, step, exchanges in weight_rounds()
        ]
    )
    scale = jnp.repeat(jnp.exp2(exponents.astype(F32)), channels // groups)
    zeros = jnp.zeros_like(scale)
    par = jnp.stack([scale, gain_first, shift_first, gain_second, shift_second, zeros, zeros, zeros])
    block = (rows, frames, channels, cols)
    stack = (rows + 2, 4, 3 * channels, cols)
    taps = (2 * channels, 36 * channels)
    halves = [shape((channels // 2 * SLOTS, channels), F32)] * 2
    conv_flops = 3 * 2 * 4 * 256 * 36 * channels * 2 * channels
    small = shape((1, 2, channels), F32)

    message = shape((2, frames, channels, cols), BF16)
    latent, cotangent, down, up, stats_first = call(
        planes_kernel,
        [shape(block, BF16), shape(block, BF16), message, message, small],
        [VMEM] * 3,
        (latent, cotangent, par),
    )
    near, near_c = row_halos(down, up)
    around = with_columns(flags, latent, (shifted(latent, "tm", 1), near, shifted(near, "tm", 1)))
    around_c = (shifted(cotangent, "tm", -1), near_c, shifted(near_c, "tm", -1))
    stats_first = all_stats(stats_first, count / devices)
    (weight_first,) = call(weight_forward_kernel, [shape(taps, BF16)], [VMEM], (conv_first,))
    (weight_second_t,) = call(weight_back_kernel, [shape(taps, BF16)], [VMEM], (conv_second,))
    (weight_first_t,) = call(weight_back_kernel, [shape(taps, BF16)], [VMEM], (conv_first,))

    hidden, stats_second, stack_first = call(
        functools.partial(conv_first_kernel, count=count),
        [shape(block, F32), small, shape(stack, BF16)],
        [SMEM] + [VMEM] * 10,
        (flags, latent, *around, par, stats_first, weight_first, around_c[2]),
        flops=conv_flops,
        transcendentals=3 * latent.size,
    )
    around_c = with_columns(flags, cotangent, around_c, (stats_second,))
    stats_second = all_stats(stats_second, count / devices)
    grad_second, stack_c = call(
        conv_back_kernel,
        [shape(block, F32), shape(stack, BF16)],
        [SMEM] + [VMEM] * 7,
        (flags, cotangent, *around_c, weight_second_t),
        flops=conv_flops,
    )
    act_second, scaled, sums = call(
        functools.partial(norm_second_kernel, count=count),
        [shape(block, BF16), shape(block, F32), small],
        [VMEM] * 4,
        (hidden, grad_second, par, stats_second),
        transcendentals=latent.size,
    )
    sums = all_sum(sums)
    halves_second = call(
        weight_second_kernel,
        halves,
        [SMEM] + [VMEM] * 2,
        (flags, stack_c, act_second),
        scratch=[pltpu.VMEM((rows * cols, frames * channels), BF16)],
        flops=conv_flops,
    )
    message = shape((1, frames, channels, cols), BF16)
    hidden_grad, down, up = call(
        functools.partial(hidden_grad_kernel, count=count),
        [shape(block, BF16), message, message],
        [VMEM] * 5,
        (hidden, scaled, par, stats_second, sums),
    )
    future = shifted(hidden_grad, "tm", -1)
    (near,) = row_halos(down, up, (future,))
    around = (future, near, shifted(near, "tm", -1))
    halves_first = call(
        weight_first_kernel,
        halves,
        [SMEM] + [VMEM] * 2,
        (flags, stack_first, hidden_grad),
        scratch=[pltpu.VMEM((rows * cols, frames * channels), BF16)],
        flops=conv_flops,
    )
    halves_second, halves_first = (
        [v.reshape(channels // 2, SLOTS, channels) for v in halves] for halves in (halves_second, halves_first)
    )
    weights, sent = scattered(flags, halves_second, halves_first)
    around = with_columns(flags, hidden_grad, around, (sent,))
    scaled, sums_first = call(
        functools.partial(first_grad_kernel, count=count),
        [shape(block, F32), small],
        [SMEM] + [VMEM] * 10,
        (flags, hidden_grad, *around, weight_first_t, latent, par, stats_first),
        scratch=[pltpu.VMEM(stack, BF16)],
        flops=conv_flops,
        transcendentals=latent.size,
    )
    weights = summed(flags, weights, around[:2])
    sums_first = all_sum(sums_first)
    decoded_grad, token = call(
        functools.partial(decoded_grad_kernel, count=count),
        [shape((channels, frames, rows, cols), F32), shape((8, 128), F32)],
        [VMEM] * 6,
        (scaled, latent, cotangent, par, stats_first, sums_first),
    )
    second, first = gathered(flags, weights, (sums_first,), token)
    conv_second_grad = joined(flags, second, swapped(second))
    conv_first_grad = joined(flags, first, swapped(first))
    return decoded_grad, conv_first_grad, conv_second_grad


def solution(mesh):
    block = P(None, "tm", "height", "width")
    return jax.shard_map(
        shards,
        mesh=mesh,
        in_specs=(block, P(), block, P(), P(), P(), P(), P(), P()),
        out_specs=(block, P(), P()),
        check_vma=False,
    )
```

```python
import functools

import jax
import jax.numpy as jnp
from jax import lax
from jax.experimental import pallas as pl
from jax.experimental.pallas import tpu as pltpu
from jax.sharding import PartitionSpec as P

epsilon = 1e-05
F32 = jnp.float32
BF16 = jnp.bfloat16
GROUP = 4
TAPS, SLOTS = 27, 32
FULL = 32760.0
LN2 = 0.6931471805599453
VMEM = pl.BlockSpec(memory_space=pltpu.VMEM)
SMEM = pl.BlockSpec(memory_space=pltpu.SMEM)


def call(body, outs, specs, args, scratch=(), flops=0, transcendentals=0, limit=20):
    moved = sum(a.size * a.dtype.itemsize for a in args)
    moved += sum(o.size * o.dtype.itemsize for o in outs)
    return pl.pallas_call(
        body,
        out_shape=tuple(outs),
        in_specs=specs,
        out_specs=tuple(VMEM for _ in outs),
        scratch_shapes=scratch,
        compiler_params=pltpu.CompilerParams(vmem_limit_bytes=limit << 20),
        cost_estimate=pl.CostEstimate(
            flops=flops, bytes_accessed=moved, transcendentals=transcendentals
        ),
    )(*args)


def shape(dims, dtype):
    return jax.ShapeDtypeStruct(dims, dtype)


def group_sums(acc):
    rows = acc.shape[0]
    row = lax.broadcasted_iota(jnp.int32, acc.shape, 0)
    step = 1
    while step < GROUP:
        up = pltpu.roll(acc, rows - step, axis=0)
        down = pltpu.roll(acc, step, axis=0)
        acc = acc + jnp.where((row & step) == 0, up, down)
        step *= 2
    return jnp.sum(acc, axis=1, keepdims=True)


def lanes_of(plane):
    total = plane[:, :128]
    for start in range(128, plane.shape[1], 128):
        total = total + plane[:, start : start + 128]
    return total


def as_rows(first, second):
    channels = first.shape[0]
    lane = lax.broadcasted_iota(jnp.int32, (channels, 128), 1)
    both = jnp.where(lane == 0, first, jnp.where(lane == 1, second, 0.0))
    return jnp.transpose(both)[:2]


def local_stats(planes, count):
    acc = None
    for plane in planes:
        part = lanes_of(plane())
        acc = part if acc is None else acc + part
    mean = group_sums(acc) / count
    acc = None
    for plane in planes:
        off = plane() - mean
        part = lanes_of(off * off)
        acc = part if acc is None else acc + part
    return mean, group_sums(acc)


def put_rows(out_ref, first, second):
    out_ref[0] = as_rows(first, second)


def combined(st_ref, count):
    return st_ref[0, 0:1], st_ref[0, 1:2] / count


def columns_of(*rows):
    rows = list(rows) + [jnp.zeros_like(rows[0])] * (8 - len(rows))
    cols = jnp.transpose(jnp.concatenate(rows, axis=0))
    return [cols[:, i : i + 1] for i in range(8)]


def sigmoid(value):
    return 0.5 + 0.5 * jnp.tanh(0.5 * value)


def planes_kernel(latent_ref, cotangent_ref, par_ref, latent_out, cotangent_out, down_ref, up_ref, st_ref):
    _, frames, rows, cols = latent_ref.shape
    for which, (natural, out) in enumerate(((latent_ref, latent_out), (cotangent_ref, cotangent_out))):
        for row in range(rows):
            for frame in range(frames):
                plane = natural[:, frame, row, :]
                out[row, frame] = plane
                if row == rows - 1:
                    down_ref[which, frame] = plane
                if row == 0:
                    up_ref[which, frame] = plane
    scale = columns_of(par_ref[0:1])[0]
    planes = [
        functools.partial(lambda r, t: latent_out[r, t].astype(F32) * scale, r, t)
        for r in range(rows)
        for t in range(frames)
    ]
    put_rows(st_ref, *local_stats(planes, float(GROUP * rows * frames * cols)))


def rows_kernel(above_ref, below_ref, *refs):
    for which, out in enumerate(refs[-above_ref.shape[0] :]):
        out[0] = above_ref[which]
        out[1] = below_ref[which]


def source(own, other, near, far, other_first):
    def at(row, frame):
        is_other = (frame < 2) == other_first
        if row == 0 or row == own.shape[0] + 1:
            return (far if is_other else near), (0 if row == 0 else 1, frame % 2)
        return (other if is_other else own), (row - 1, frame % 2)

    return at


def edges_kernel(flag_ref, first_ref, second_ref, *refs):
    planes, out_ref = (first_ref, second_ref), refs[-1]
    is_first = flag_ref[3] == 0
    channels = planes[0].shape[2]
    lane = lax.broadcasted_iota(jnp.int32, (channels, 128), 1)
    acc = jnp.zeros((channels, 128), F32)
    number = 0
    for ref in planes:
        for row in range(ref.shape[0]):
            for frame in range(ref.shape[1]):
                last = pltpu.roll(ref[row, frame, :, -128:].astype(F32), 1, axis=1)
                edge = jnp.where(is_first, last, ref[row, frame, :, :128].astype(F32))
                moved = pltpu.roll(edge, number, axis=1) if number else edge
                acc = jnp.where(lane == number, moved, acc)
                number += 1
    out_ref[...] = acc.astype(BF16)


def edge_lane(row, frame, rows, other_first):
    is_other = int((frame < 2) == other_first)
    if row == 0 or row == rows + 1:
        return 1, 4 * is_other + 2 * int(row > 0) + frame % 2
    return 0, 2 * rows * is_other + 2 * (row - 1) + frame % 2


def fill_stack(stack, row, frame, plane, column, on_left, on_right):
    channels, cols = plane.shape
    lane = lax.broadcasted_iota(jnp.int32, (channels, cols), 1)
    column = column.astype(F32)
    left = jnp.where(lane == 0, (column * on_left).astype(BF16), pltpu.roll(plane, 1, axis=1))
    right = jnp.where(lane == cols - 1, (column * on_right).astype(BF16), pltpu.roll(plane, cols - 1, axis=1))
    stack[row, frame, 0:channels] = left
    stack[row, frame, channels : 2 * channels] = plane
    stack[row, frame, 2 * channels : 3 * channels] = right


def sides(flag_ref):
    on_left = (flag_ref[3] != 0).astype(F32)
    on_right = (flag_ref[3] == 0).astype(F32)
    return on_left, on_right


def conv_rows(stack, weight, row):
    three = stack[row : row + 3].reshape(weight.shape[1], stack.shape[3])
    return jnp.dot(weight[...], three, preferred_element_type=F32)


def norm_columns(par_ref, st_ref, count, gain_row):
    par = par_ref[...]
    mean, variance = combined(st_ref, count)
    inverse = 1.0 / jnp.sqrt(variance + epsilon)
    gain = par[gain_row : gain_row + 1]
    shift = par[gain_row + 1 : gain_row + 2]
    return columns_of(mean, inverse, gain, shift, par[0:1])[:5]


def conv_first_kernel(
    flag_ref, own, past, near, far, edge_ref, rim_ref, par_ref, st_ref, weight, after, hidden_ref, st_out, stack_ref,
    *, count
):
    rows, frames, channels, cols = own.shape
    at = source(own, past, near, far, True)
    mean, inverse, gain, shift, scale = norm_columns(par_ref, st_ref, count, 1)

    def act(latent):
        pre = (latent.astype(F32) * scale - mean) * inverse * gain + shift
        return pre * sigmoid(pre)

    has_past = flag_ref[0].astype(F32)
    has_top = flag_ref[1].astype(F32)
    has_bottom = flag_ref[2].astype(F32)
    on_left, on_right = sides(flag_ref)
    edges = (act(edge_ref[...]), act(rim_ref[...]))
    for row in range(rows + 2):
        for frame in range(4):
            ref, index = at(row, frame)
            which, number = edge_lane(row, frame, rows, True)
            plane = act(ref[index])
            column = edges[which][:, number : number + 1]
            factor = None
            if frame < 2:
                factor = has_past
            if row in (0, rows + 1):
                beside = has_top if row == 0 else has_bottom
                factor = beside if factor is None else factor * beside
            if factor is not None:
                plane = plane * factor
                column = column * factor
            fill_stack(stack_ref, row, frame, plane.astype(BF16), column, on_left, on_right)
    for row in range(rows):
        out = conv_rows(stack_ref, weight, row)
        for frame in range(frames):
            hidden_ref[row, frame] = out[frame * channels : (frame + 1) * channels]
    planes = [
        functools.partial(lambda r, t: hidden_ref[r, t], r, t) for r in range(rows) for t in range(frames)
    ]
    put_rows(st_out, *local_stats(planes, float(GROUP * rows * frames * cols)))


def fill_future(stack, flag_ref, own, future, near, far, edge_ref, rim_ref):
    rows = own.shape[0]
    at = source(own, future, near, far, False)
    on_left, on_right = sides(flag_ref)
    edges = (edge_ref[...], rim_ref[...])
    for row in range(rows + 2):
        for frame in range(4):
            ref, index = at(row, frame)
            which, number = edge_lane(row, frame, rows, False)
            fill_stack(stack, row, frame, ref[index], edges[which][:, number : number + 1], on_left, on_right)


def conv_back_kernel(flag_ref, *refs):
    weight, grad_ref, stack_ref = refs[-3:]
    rows, frames, channels, _ = grad_ref.shape
    fill_future(stack_ref, flag_ref, *refs[:-3])
    for row in range(rows):
        out = conv_rows(stack_ref, weight, row)
        for frame in range(frames):
            grad_ref[row, frame] = out[frame * channels : (frame + 1) * channels]


def norm_second_kernel(hidden, grad, par_ref, st_ref, act_ref, scaled_ref, sums_ref, *, count):
    rows, frames, channels, cols = hidden.shape
    mean, inverse, gain, shift, _ = norm_columns(par_ref, st_ref, count, 3)
    first = jnp.zeros((channels, 128), F32)
    second = jnp.zeros((channels, 128), F32)
    for row in range(rows):
        for frame in range(frames):
            normed = (hidden[row, frame] - mean) * inverse
            pre = normed * gain + shift
            sig = sigmoid(pre)
            act = pre * sig
            act_ref[row, frame] = act.astype(BF16)
            scaled = grad[row, frame] * (sig + act * (1.0 - sig)) * gain
            scaled_ref[row, frame] = scaled
            first = first + lanes_of(scaled)
            second = second + lanes_of(scaled * normed)
    put_rows(sums_ref, group_sums(first), group_sums(second))


def hidden_grad_kernel(
    hidden, scaled, par_ref, st_ref, sums_ref, out_ref, down_ref, up_ref, *, count
):
    rows, frames, channels, cols = hidden.shape
    mean, inverse, _, _, _ = norm_columns(par_ref, st_ref, count, 3)
    means = sums_ref[0] / count
    first, second = columns_of(means[0:1], means[1:2])[:2]
    for row in range(rows):
        for frame in range(frames):
            normed = (hidden[row, frame] - mean) * inverse
            plane = (inverse * (scaled[row, frame] - first - normed * second)).astype(BF16)
            out_ref[row, frame] = plane
            if row == rows - 1:
                down_ref[0, frame] = plane
            if row == 0:
                up_ref[0, frame] = plane


def put_halves(flag_ref, mine_ref, theirs_ref, tap, block):
    half = block.shape[0] // 2
    here = pl.ds(tap, half, stride=SLOTS)
    upper, lower = block[:half], block[half:]
    is_first = flag_ref[3] == 0
    mine_ref[here, :] = jnp.where(is_first, upper, lower)
    theirs_ref[here, :] = jnp.where(is_first, lower, upper)


def encoded(value):
    slot = lax.broadcasted_iota(jnp.int32, value.shape, 1)
    value = jnp.where(slot < TAPS, value, 0.0)
    top = jnp.max(jnp.abs(value), axis=1, keepdims=True)
    power = jnp.ceil(jnp.log(jnp.maximum(top, 1e-30)) * (1.0 / LN2))
    number = jnp.round(value * (FULL * jnp.exp(power * -LN2)))
    return jnp.where(slot < TAPS, number, power).astype(jnp.int32).astype(jnp.int16)


def decoded_value(number):
    number = number.astype(jnp.int32).astype(F32)
    return number * (jnp.exp(number[:, SLOTS - 1 : SLOTS] * LN2) * (1.0 / FULL))


def first_scatter_kernel(flag_ref, *refs, slot):
    me = flag_ref[slot]
    for which in range(2):
        mine, other = refs[2 * which], refs[2 * which + 1]
        for k, out in enumerate(refs[4:]):
            total = mine[me ^ k] + other[me ^ k]
            out[which] = total if k == 0 else encoded(total)


def scatter_kernel(flag_ref, *refs, received, sent, slot):
    me = flag_ref[slot]
    for which in range(2):
        for k, out in enumerate(refs[-sent:]):
            total = refs[0][which, me ^ k]
            for ref in refs[1:received]:
                total = total + decoded_value(ref[which, me ^ k])
            out[which] = total if k == 0 else encoded(total)


def total_kernel(*refs, received):
    for which in range(2):
        total = refs[0][which]
        for ref in refs[1:received]:
            total = total + decoded_value(ref[which])
        refs[-1][which] = encoded(total)


def gather_kernel(flag_ref, *refs, received, split, slot):
    me = flag_ref[slot]
    for which in range(2):
        for k, ref in enumerate(refs[:received]):
            if split:
                refs[which - 2][me ^ k] = ref[which]
            else:
                refs[-1][which, me ^ k] = ref[which]


def join_kernel(flag_ref, mine_ref, theirs_ref, out_ref, first_ref, second_ref):
    half, _, channels = mine_ref.shape
    is_first = flag_ref[3] == 0
    first_ref[...] = decoded_value(jnp.where(is_first, mine_ref[...], theirs_ref[...])).reshape(first_ref.shape)
    second_ref[...] = decoded_value(jnp.where(is_first, theirs_ref[...], mine_ref[...])).reshape(second_ref.shape)
    for tap in range(TAPS):
        here = slice(tap * channels, (tap + 1) * channels)
        out_ref[:half, here] = first_ref[pl.ds(tap, half, stride=SLOTS), :]
        out_ref[half:, here] = second_ref[pl.ds(tap, half, stride=SLOTS), :]


def weight_second_kernel(flag_ref, stack_ref, act_ref, mine_ref, theirs_ref, right_ref):
    rows, frames, channels, cols = act_ref.shape
    for row in range(rows):
        right_ref[row * cols : (row + 1) * cols] = jnp.transpose(
            act_ref[row].reshape(frames * channels, cols)
        )
    right = right_ref[...]
    for down in range(3):
        parts = []
        for frame in range(4):
            left = jnp.concatenate([stack_ref[down + row, frame] for row in range(rows)], axis=1)
            parts.append(jnp.dot(left, right, preferred_element_type=F32))
        for kt in range(3):
            term = parts[2 - kt][:, :channels] + parts[3 - kt][:, channels:]
            for across in range(3):
                tap = 9 * kt + 3 * (2 - down) + (2 - across)
                put_halves(flag_ref, mine_ref, theirs_ref, tap, term[across * channels : (across + 1) * channels])


def weight_first_kernel(flag_ref, stack_ref, grad_ref, mine_ref, theirs_ref, right_ref):
    rows, frames, channels, cols = grad_ref.shape
    for row in range(rows):
        right_ref[row * cols : (row + 1) * cols] = jnp.transpose(
            grad_ref[row].reshape(frames * channels, cols)
        )
    right = right_ref[...]
    for down in range(3):
        parts = []
        for frame in range(4):
            left = jnp.concatenate([stack_ref[down + row, frame] for row in range(rows)], axis=1)
            parts.append(jnp.dot(left, right, preferred_element_type=F32))
        for kt in range(3):
            term = parts[kt][:, :channels] + parts[kt + 1][:, channels:]
            for across in range(3):
                tap = 9 * kt + 3 * down + across
                block = jnp.transpose(term[across * channels : (across + 1) * channels])
                put_halves(flag_ref, mine_ref, theirs_ref, tap, block)


def first_grad_kernel(flag_ref, *refs, count):
    weight, latent, par_ref, st_ref, _, scaled_ref, sums_ref, stack_ref = refs[-8:]
    rows, frames, channels, cols = latent.shape
    mean, inverse, gain, shift, scale = norm_columns(par_ref, st_ref, count, 1)
    fill_future(stack_ref, flag_ref, *refs[:-8])
    first = jnp.zeros((channels, 128), F32)
    second = jnp.zeros((channels, 128), F32)
    for row in range(rows):
        out = conv_rows(stack_ref, weight, row)
        for frame in range(frames):
            grad = out[frame * channels : (frame + 1) * channels]
            normed = (latent[row, frame].astype(F32) * scale - mean) * inverse
            pre = normed * gain + shift
            sig = sigmoid(pre)
            scaled = grad * (sig + pre * sig * (1.0 - sig)) * gain
            scaled_ref[row, frame] = scaled
            first = first + lanes_of(scaled)
            second = second + lanes_of(scaled * normed)
    put_rows(sums_ref, group_sums(first), group_sums(second))


def decoded_grad_kernel(scaled, latent, cotangent, par_ref, st_ref, sums_ref, out_ref, token_ref, *, count):
    token_ref[...] = jnp.zeros(token_ref.shape, F32)
    rows, frames, channels, cols = latent.shape
    mean, inverse, _, _, scale = norm_columns(par_ref, st_ref, count, 1)
    means = sums_ref[0] / count
    first, second = columns_of(means[0:1], means[1:2])[:2]
    for row in range(rows):
        for frame in range(frames):
            normed = (latent[row, frame].astype(F32) * scale - mean) * inverse
            out_ref[:, frame, row, :] = cotangent[row, frame].astype(F32) + inverse * (
                scaled[row, frame] - first - normed * second
            )


def weight_forward_kernel(weight, out_ref):
    channels = weight.shape[0]
    wide = 3 * channels
    for t in range(2):
        for kr in range(3):
            for f in range(4):
                kt = f - t
                here = slice((kr * 4 + f) * wide, (kr * 4 + f + 1) * wide)
                if 0 <= kt < 3:
                    tap = 3 * kt + kr
                    block = weight[:, tap * wide : (tap + 1) * wide]
                else:
                    block = jnp.zeros((channels, wide), BF16)
                out_ref[t * channels : (t + 1) * channels, here] = block


def weight_back_kernel(weight, out_ref):
    channels = weight.shape[0]
    for down in range(3):
        for across in range(3):
            blocks = [
                jnp.transpose(
                    weight[
                        :,
                        (9 * kt + 3 * (2 - down) + 2 - across) * channels : (9 * kt + 3 * (2 - down) + 3 - across)
                        * channels,
                    ]
                )
                for kt in range(3)
            ]
            for t in range(2):
                for f in range(4):
                    kt = t + 2 - f
                    start = ((down * 4 + f) * 3 + across) * channels
                    block = blocks[kt] if 0 <= kt < 3 else jnp.zeros((channels, channels), BF16)
                    out_ref[t * channels : (t + 1) * channels, start : start + channels] = block


def shifted(value, axis, steps):
    count = lax.axis_size(axis)
    initial, last = max(0, -steps), min(count, count - steps)
    return lax.ppermute(value, axis, [(source, source + steps) for source in range(initial, last)])


def rounds(axes):
    for axis in axes:
        count = lax.axis_size(axis)
        step = 1
        while step < count:
            wide = 4 if 4 * step <= count else 2
            yield axis, step, [[(i, i ^ (step * k)) for i in range(count)] for k in range(1, wide)]
            step *= wide


def pairwise(parts, join):
    while len(parts) > 1:
        parts = [join(a, b) for a, b in zip(parts[::2], parts[1::2])]
    return parts[0]


def all_sum(value):
    for axis, _, exchanges in rounds(("tm", "height", "width")):
        parts = [value] + [lax.ppermute(value, axis, pairs) for pairs in exchanges]
        value = pairwise(parts, lambda a, b: a + b)
    return value


def all_stats(value, count):
    for axis, _, exchanges in rounds(("tm", "height", "width")):
        parts = [(value, count)] + [(lax.ppermute(value, axis, pairs), count) for pairs in exchanges]
        value, count = pairwise(parts, joined_stats)
    return value


def joined_stats(first, second):
    (a, count), (b, _) = first, second
    gap = a[:, 0:1] - b[:, 0:1]
    squares = a[:, 1:2] + b[:, 1:2] + gap * gap * (0.5 * count)
    return jnp.concatenate([0.5 * (a[:, 0:1] + b[:, 0:1]), squares], axis=1), 2.0 * count


def swapped(value):
    return lax.ppermute(value, "width", [(0, 1), (1, 0)])


def weight_rounds():
    return list(rounds(("height", "tm")))


def scattered(flags, second, first):
    half, _, channels = second[0].shape
    axis, _, exchanges = weight_rounds()[0]
    parts = len(exchanges) + 1
    rows = half // parts
    terms = [part for mine, theirs in (second, first) for part in (mine, swapped(theirs))]
    part = (2, rows, SLOTS, channels)
    kept, *sent = call(
        functools.partial(first_scatter_kernel, slot=4),
        [shape(part, F32)] + [shape(part, jnp.int16)] * (parts - 1),
        [SMEM] + [VMEM] * 4,
        (flags, *[term.reshape(parts, rows, SLOTS, channels) for term in terms]),
    )
    return [kept] + [lax.ppermute(v, axis, pairs) for v, pairs in zip(sent, exchanges)], sent[0]


def summed(flags, received, after):
    for number, (axis, _, exchanges) in enumerate(weight_rounds()[1:], 5):
        parts = len(exchanges) + 1
        _, rows, _, channels = received[0].shape
        part = (2, rows // parts, SLOTS, channels)
        views = [v.reshape(2, parts, *part[1:]) for v in received]
        kept, *sent = call(
            functools.partial(scatter_kernel, received=len(views), sent=parts, slot=number),
            [shape(part, F32)] + [shape(part, jnp.int16)] * (parts - 1),
            [SMEM] + [VMEM] * (len(views) + len(after)),
            (flags, *views, *after),
        )
        after = ()
        received = [kept] + [lax.ppermute(v, axis, pairs) for v, pairs in zip(sent, exchanges)]
        last = sent[0]
    return received, last


def gathered(flags, received, after):
    (total,) = call(
        functools.partial(total_kernel, received=len(received)),
        [shape(received[0].shape, jnp.int16)],
        [VMEM] * len(received),
        tuple(received),
    )
    back = list(enumerate(weight_rounds(), 4))[::-1]
    for number, (axis, _, exchanges) in back:
        _, rows, _, channels = total.shape
        pieces = [total] + [lax.ppermute(total, axis, pairs) for pairs in exchanges]
        parts = len(pieces)
        split = number == 4
        dims = (parts, rows, SLOTS, channels)
        values = call(
            functools.partial(gather_kernel, received=parts, split=split, slot=number),
            [shape(dims, jnp.int16)] * 2 if split else [shape((2, *dims), jnp.int16)],
            [SMEM] + [VMEM] * (parts + len(after)),
            (flags, *pieces, *after),
        )
        after = ()
        total = values[0].reshape(2, -1, SLOTS, channels) if not split else None
    return [value.reshape(-1, SLOTS, channels) for value in values]


def joined(flags, mine, theirs):
    half, _, channels = mine.shape
    (total,) = call(
        join_kernel,
        [shape((2 * half, TAPS * channels), F32)],
        [SMEM] + [VMEM] * 2,
        (flags, mine, theirs),
        scratch=[pltpu.VMEM((half * SLOTS, channels), F32)] * 2,
    )
    return total


def edges(flags, planes, after):
    channels = planes[0].shape[2]
    args = (*planes, *after)
    (columns,) = call(edges_kernel, [shape((channels, 128), BF16)], [SMEM] + [VMEM] * len(args), (flags, *args))
    return columns


def row_halos(down, up, after=()):
    above, below = shifted(down, "height", 1), shifted(up, "height", -1)
    return call(
        rows_kernel,
        [shape((2, *down.shape[1:]), BF16)] * down.shape[0],
        [VMEM] * (2 + len(after)),
        (above, below, *after),
    )


def with_columns(flags, own, around, after=()):
    edge = swapped(edges(flags, (own, around[0]), after))
    rim = swapped(edges(flags, around[1:], after))
    return *around, edge, rim


def shards(
    latent,
    exponents,
    cotangent,
    conv_first,
    conv_second,
    gain_first,
    shift_first,
    gain_second,
    shift_second,
):
    channels, frames, rows, cols = latent.shape
    groups = exponents.shape[0]
    devices = lax.axis_size("tm") * lax.axis_size("height") * lax.axis_size("width")
    count = float(channels // groups * frames * rows * cols * devices)
    tm, height, width = (lax.axis_index(axis) for axis in ("tm", "height", "width"))
    flags = jnp.stack(
        [
            (tm > 0).astype(jnp.int32),
            (height > 0).astype(jnp.int32),
            (height < lax.axis_size("height") - 1).astype(jnp.int32),
            width.astype(jnp.int32),
        ]
        + [
            (lax.axis_index(axis) // step % (len(exchanges) + 1)).astype(jnp.int32)
            for axis, step, exchanges in weight_rounds()
        ]
    )
    scale = jnp.repeat(jnp.exp2(exponents.astype(F32)), channels // groups)
    zeros = jnp.zeros_like(scale)
    par = jnp.stack([scale, gain_first, shift_first, gain_second, shift_second, zeros, zeros, zeros])
    block = (rows, frames, channels, cols)
    stack = (rows + 2, 4, 3 * channels, cols)
    taps = (2 * channels, 36 * channels)
    halves = [shape((channels // 2 * SLOTS, channels), F32)] * 2
    conv_flops = 3 * 2 * 4 * 256 * 36 * channels * 2 * channels
    small = shape((1, 2, channels), F32)

    message = shape((2, frames, channels, cols), BF16)
    latent, cotangent, down, up, stats_first = call(
        planes_kernel,
        [shape(block, BF16), shape(block, BF16), message, message, small],
        [VMEM] * 3,
        (latent, cotangent, par),
    )
    near, near_c = row_halos(down, up)
    around = with_columns(flags, latent, (shifted(latent, "tm", 1), near, shifted(near, "tm", 1)))
    around_c = (shifted(cotangent, "tm", -1), near_c, shifted(near_c, "tm", -1))
    stats_first = all_stats(stats_first, count / devices)
    (weight_first,) = call(weight_forward_kernel, [shape(taps, BF16)], [VMEM], (conv_first,))
    (weight_second_t,) = call(weight_back_kernel, [shape(taps, BF16)], [VMEM], (conv_second,))
    (weight_first_t,) = call(weight_back_kernel, [shape(taps, BF16)], [VMEM], (conv_first,))

    hidden, stats_second, stack_first = call(
        functools.partial(conv_first_kernel, count=count),
        [shape(block, F32), small, shape(stack, BF16)],
        [SMEM] + [VMEM] * 10,
        (flags, latent, *around, par, stats_first, weight_first, around_c[2]),
        flops=conv_flops,
        transcendentals=3 * latent.size,
    )
    around_c = with_columns(flags, cotangent, around_c, (stats_second,))
    stats_second = all_stats(stats_second, count / devices)
    grad_second, stack_c = call(
        conv_back_kernel,
        [shape(block, F32), shape(stack, BF16)],
        [SMEM] + [VMEM] * 7,
        (flags, cotangent, *around_c, weight_second_t),
        flops=conv_flops,
    )
    act_second, scaled, sums = call(
        functools.partial(norm_second_kernel, count=count),
        [shape(block, BF16), shape(block, F32), small],
        [VMEM] * 4,
        (hidden, grad_second, par, stats_second),
        transcendentals=latent.size,
    )
    sums = all_sum(sums)
    halves_second = call(
        weight_second_kernel,
        halves,
        [SMEM] + [VMEM] * 2,
        (flags, stack_c, act_second),
        scratch=[pltpu.VMEM((rows * cols, frames * channels), BF16)],
        flops=conv_flops,
    )
    message = shape((1, frames, channels, cols), BF16)
    hidden_grad, down, up = call(
        functools.partial(hidden_grad_kernel, count=count),
        [shape(block, BF16), message, message],
        [VMEM] * 5,
        (hidden, scaled, par, stats_second, sums),
    )
    future = shifted(hidden_grad, "tm", -1)
    (near,) = row_halos(down, up, (future,))
    around = (future, near, shifted(near, "tm", -1))
    halves_first = call(
        weight_first_kernel,
        halves,
        [SMEM] + [VMEM] * 2,
        (flags, stack_first, hidden_grad),
        scratch=[pltpu.VMEM((rows * cols, frames * channels), BF16)],
        flops=conv_flops,
    )
    halves_second, halves_first = (
        [v.reshape(channels // 2, SLOTS, channels) for v in halves] for halves in (halves_second, halves_first)
    )
    weights, sent = scattered(flags, halves_second, halves_first)
    around = with_columns(flags, hidden_grad, around, (sent,))
    weights, sent = summed(flags, weights, around[:2])
    scaled, sums_first = call(
        functools.partial(first_grad_kernel, count=count),
        [shape(block, F32), small],
        [SMEM] + [VMEM] * 11,
        (flags, hidden_grad, *around, weight_first_t, latent, par, stats_first, sent),
        scratch=[pltpu.VMEM(stack, BF16)],
        flops=conv_flops,
        transcendentals=latent.size,
    )
    sums_first = all_sum(sums_first)
    decoded_grad, token = call(
        functools.partial(decoded_grad_kernel, count=count),
        [shape((channels, frames, rows, cols), F32), shape((8, 128), F32)],
        [VMEM] * 6,
        (scaled, latent, cotangent, par, stats_first, sums_first),
    )
    second, first = gathered(flags, weights, (token,))
    conv_second_grad = joined(flags, second, swapped(second))
    conv_first_grad = joined(flags, first, swapped(first))
    return decoded_grad, conv_first_grad, conv_second_grad


def solution(mesh):
    block = P(None, "tm", "height", "width")
    return jax.shard_map(
        shards,
        mesh=mesh,
        in_specs=(block, P(), block, P(), P(), P(), P(), P(), P()),
        out_specs=(block, P(), P()),
        check_vma=False,
    )
```

```python
import functools

import jax
import jax.numpy as jnp
from jax import lax
from jax.experimental import pallas as pl
from jax.experimental.pallas import tpu as pltpu
from jax.sharding import PartitionSpec as P

epsilon = 1e-05
F32 = jnp.float32
BF16 = jnp.bfloat16
GROUP = 4
TAPS, SLOTS = 27, 32
FULL = 32760.0
LN2 = 0.6931471805599453
VMEM = pl.BlockSpec(memory_space=pltpu.VMEM)
SMEM = pl.BlockSpec(memory_space=pltpu.SMEM)


def call(body, outs, specs, args, scratch=(), flops=0, transcendentals=0, limit=20):
    moved = sum(a.size * a.dtype.itemsize for a in args)
    moved += sum(o.size * o.dtype.itemsize for o in outs)
    return pl.pallas_call(
        body,
        out_shape=tuple(outs),
        in_specs=specs,
        out_specs=tuple(VMEM for _ in outs),
        scratch_shapes=scratch,
        compiler_params=pltpu.CompilerParams(vmem_limit_bytes=limit << 20),
        cost_estimate=pl.CostEstimate(
            flops=flops, bytes_accessed=moved, transcendentals=transcendentals
        ),
    )(*args)


def shape(dims, dtype):
    return jax.ShapeDtypeStruct(dims, dtype)


def group_sums(acc):
    rows = acc.shape[0]
    row = lax.broadcasted_iota(jnp.int32, acc.shape, 0)
    step = 1
    while step < GROUP:
        up = pltpu.roll(acc, rows - step, axis=0)
        down = pltpu.roll(acc, step, axis=0)
        acc = acc + jnp.where((row & step) == 0, up, down)
        step *= 2
    return jnp.sum(acc, axis=1, keepdims=True)


def lanes_of(plane):
    total = plane[:, :128]
    for start in range(128, plane.shape[1], 128):
        total = total + plane[:, start : start + 128]
    return total


def as_rows(first, second):
    channels = first.shape[0]
    lane = lax.broadcasted_iota(jnp.int32, (channels, 128), 1)
    both = jnp.where(lane == 0, first, jnp.where(lane == 1, second, 0.0))
    return jnp.transpose(both)[:2]


def local_stats(planes, count):
    acc = None
    for plane in planes:
        part = lanes_of(plane())
        acc = part if acc is None else acc + part
    mean = group_sums(acc) / count
    acc = None
    for plane in planes:
        off = plane() - mean
        part = lanes_of(off * off)
        acc = part if acc is None else acc + part
    return mean, group_sums(acc)


def put_rows(out_ref, first, second):
    out_ref[0] = as_rows(first, second)


def combined(st_ref, count):
    return st_ref[0, 0:1], st_ref[0, 1:2] / count


def columns_of(*rows):
    rows = list(rows) + [jnp.zeros_like(rows[0])] * (8 - len(rows))
    cols = jnp.transpose(jnp.concatenate(rows, axis=0))
    return [cols[:, i : i + 1] for i in range(8)]


def sigmoid(value):
    return 0.5 + 0.5 * jnp.tanh(0.5 * value)


def planes_kernel(latent_ref, cotangent_ref, par_ref, latent_out, cotangent_out, down_ref, up_ref, st_ref):
    _, frames, rows, cols = latent_ref.shape
    for which, (natural, out) in enumerate(((latent_ref, latent_out), (cotangent_ref, cotangent_out))):
        for row in range(rows):
            for frame in range(frames):
                plane = natural[:, frame, row, :]
                out[row, frame] = plane
                if row == rows - 1:
                    down_ref[which, frame] = plane
                if row == 0:
                    up_ref[which, frame] = plane
    scale = columns_of(par_ref[0:1])[0]
    planes = [
        functools.partial(lambda r, t: latent_out[r, t].astype(F32) * scale, r, t)
        for r in range(rows)
        for t in range(frames)
    ]
    put_rows(st_ref, *local_stats(planes, float(GROUP * rows * frames * cols)))


def rows_kernel(above_ref, below_ref, *refs):
    for which, out in enumerate(refs[-above_ref.shape[0] :]):
        out[0] = above_ref[which]
        out[1] = below_ref[which]


def source(own, other, near, far, other_first):
    def at(row, frame):
        is_other = (frame < 2) == other_first
        if row == 0 or row == own.shape[0] + 1:
            return (far if is_other else near), (0 if row == 0 else 1, frame % 2)
        return (other if is_other else own), (row - 1, frame % 2)

    return at


def edges_kernel(flag_ref, first_ref, second_ref, *refs):
    planes, out_ref = (first_ref, second_ref), refs[-1]
    is_first = flag_ref[3] == 0
    channels = planes[0].shape[2]
    lane = lax.broadcasted_iota(jnp.int32, (channels, 128), 1)
    acc = jnp.zeros((channels, 128), F32)
    number = 0
    for ref in planes:
        for row in range(ref.shape[0]):
            for frame in range(ref.shape[1]):
                last = pltpu.roll(ref[row, frame, :, -128:].astype(F32), 1, axis=1)
                edge = jnp.where(is_first, last, ref[row, frame, :, :128].astype(F32))
                moved = pltpu.roll(edge, number, axis=1) if number else edge
                acc = jnp.where(lane == number, moved, acc)
                number += 1
    out_ref[...] = acc.astype(BF16)


def edge_lane(row, frame, rows, other_first):
    is_other = int((frame < 2) == other_first)
    if row == 0 or row == rows + 1:
        return 1, 4 * is_other + 2 * int(row > 0) + frame % 2
    return 0, 2 * rows * is_other + 2 * (row - 1) + frame % 2


def fill_stack(stack, row, frame, plane, column, on_left, on_right):
    channels, cols = plane.shape
    lane = lax.broadcasted_iota(jnp.int32, (channels, cols), 1)
    column = column.astype(F32)
    left = jnp.where(lane == 0, (column * on_left).astype(BF16), pltpu.roll(plane, 1, axis=1))
    right = jnp.where(lane == cols - 1, (column * on_right).astype(BF16), pltpu.roll(plane, cols - 1, axis=1))
    stack[row, frame, 0:channels] = left
    stack[row, frame, channels : 2 * channels] = plane
    stack[row, frame, 2 * channels : 3 * channels] = right


def sides(flag_ref):
    on_left = (flag_ref[3] != 0).astype(F32)
    on_right = (flag_ref[3] == 0).astype(F32)
    return on_left, on_right


def conv_rows(stack, weight, row):
    three = stack[row : row + 3].reshape(weight.shape[1], stack.shape[3])
    return jnp.dot(weight[...], three, preferred_element_type=F32)


def norm_columns(par_ref, st_ref, count, gain_row):
    par = par_ref[...]
    mean, variance = combined(st_ref, count)
    inverse = 1.0 / jnp.sqrt(variance + epsilon)
    gain = par[gain_row : gain_row + 1]
    shift = par[gain_row + 1 : gain_row + 2]
    return columns_of(mean, inverse, gain, shift, par[0:1])[:5]


def conv_first_kernel(
    flag_ref, own, past, near, far, edge_ref, rim_ref, par_ref, st_ref, weight, after, hidden_ref, st_out, stack_ref,
    *, count
):
    rows, frames, channels, cols = own.shape
    at = source(own, past, near, far, True)
    mean, inverse, gain, shift, scale = norm_columns(par_ref, st_ref, count, 1)

    def act(latent):
        pre = (latent.astype(F32) * scale - mean) * inverse * gain + shift
        return pre * sigmoid(pre)

    has_past = flag_ref[0].astype(F32)
    has_top = flag_ref[1].astype(F32)
    has_bottom = flag_ref[2].astype(F32)
    on_left, on_right = sides(flag_ref)
    edges = (act(edge_ref[...]), act(rim_ref[...]))
    for row in range(rows + 2):
        for frame in range(4):
            ref, index = at(row, frame)
            which, number = edge_lane(row, frame, rows, True)
            plane = act(ref[index])
            column = edges[which][:, number : number + 1]
            factor = None
            if frame < 2:
                factor = has_past
            if row in (0, rows + 1):
                beside = has_top if row == 0 else has_bottom
                factor = beside if factor is None else factor * beside
            if factor is not None:
                plane = plane * factor
                column = column * factor
            fill_stack(stack_ref, row, frame, plane.astype(BF16), column, on_left, on_right)
    for row in range(rows):
        out = conv_rows(stack_ref, weight, row)
        for frame in range(frames):
            hidden_ref[row, frame] = out[frame * channels : (frame + 1) * channels]
    planes = [
        functools.partial(lambda r, t: hidden_ref[r, t], r, t) for r in range(rows) for t in range(frames)
    ]
    put_rows(st_out, *local_stats(planes, float(GROUP * rows * frames * cols)))


def fill_future(stack, flag_ref, own, future, near, far, edge_ref, rim_ref):
    rows = own.shape[0]
    at = source(own, future, near, far, False)
    on_left, on_right = sides(flag_ref)
    edges = (edge_ref[...], rim_ref[...])
    for row in range(rows + 2):
        for frame in range(4):
            ref, index = at(row, frame)
            which, number = edge_lane(row, frame, rows, False)
            fill_stack(stack, row, frame, ref[index], edges[which][:, number : number + 1], on_left, on_right)


def conv_back_kernel(flag_ref, *refs):
    weight, grad_ref, stack_ref = refs[-3:]
    rows, frames, channels, _ = grad_ref.shape
    fill_future(stack_ref, flag_ref, *refs[:-3])
    for row in range(rows):
        out = conv_rows(stack_ref, weight, row)
        for frame in range(frames):
            grad_ref[row, frame] = out[frame * channels : (frame + 1) * channels]


def norm_second_kernel(hidden, grad, par_ref, st_ref, act_ref, scaled_ref, sums_ref, *, count):
    rows, frames, channels, cols = hidden.shape
    mean, inverse, gain, shift, _ = norm_columns(par_ref, st_ref, count, 3)
    first = jnp.zeros((channels, 128), F32)
    second = jnp.zeros((channels, 128), F32)
    for row in range(rows):
        for frame in range(frames):
            normed = (hidden[row, frame] - mean) * inverse
            pre = normed * gain + shift
            sig = sigmoid(pre)
            act = pre * sig
            act_ref[row, frame] = act.astype(BF16)
            scaled = grad[row, frame] * (sig + act * (1.0 - sig)) * gain
            scaled_ref[row, frame] = scaled
            first = first + lanes_of(scaled)
            second = second + lanes_of(scaled * normed)
    put_rows(sums_ref, group_sums(first), group_sums(second))


def hidden_grad_kernel(
    hidden, scaled, par_ref, st_ref, sums_ref, out_ref, down_ref, up_ref, *, count
):
    rows, frames, channels, cols = hidden.shape
    mean, inverse, _, _, _ = norm_columns(par_ref, st_ref, count, 3)
    means = sums_ref[0] / count
    first, second = columns_of(means[0:1], means[1:2])[:2]
    for row in range(rows):
        for frame in range(frames):
            normed = (hidden[row, frame] - mean) * inverse
            plane = (inverse * (scaled[row, frame] - first - normed * second)).astype(BF16)
            out_ref[row, frame] = plane
            if row == rows - 1:
                down_ref[0, frame] = plane
            if row == 0:
                up_ref[0, frame] = plane


def put_halves(flag_ref, mine_ref, theirs_ref, tap, block):
    half = block.shape[0] // 2
    here = pl.ds(tap, half, stride=SLOTS)
    upper, lower = block[:half], block[half:]
    is_first = flag_ref[3] == 0
    mine_ref[here, :] = jnp.where(is_first, upper, lower)
    theirs_ref[here, :] = jnp.where(is_first, lower, upper)


def encoded(value):
    slot = lax.broadcasted_iota(jnp.int32, value.shape, 1)
    value = jnp.where(slot < TAPS, value, 0.0)
    top = jnp.max(jnp.abs(value), axis=1, keepdims=True)
    power = jnp.ceil(jnp.log(jnp.maximum(top, 1e-30)) * (1.0 / LN2))
    number = jnp.round(value * (FULL * jnp.exp(power * -LN2)))
    return jnp.where(slot < TAPS, number, power).astype(jnp.int32).astype(jnp.int16)


def decoded_value(number):
    number = number.astype(jnp.int32).astype(F32)
    return number * (jnp.exp(number[:, SLOTS - 1 : SLOTS] * LN2) * (1.0 / FULL))


def first_scatter_kernel(flag_ref, *refs, slot):
    me = flag_ref[slot]
    for which in range(2):
        mine, other = refs[2 * which], refs[2 * which + 1]
        for k, out in enumerate(refs[4:]):
            total = mine[me ^ k] + other[me ^ k]
            out[which] = total if k == 0 else encoded(total)


def scatter_kernel(flag_ref, *refs, received, sent, slot):
    me = flag_ref[slot]
    for which in range(2):
        for k, out in enumerate(refs[-sent:]):
            total = refs[0][which, me ^ k]
            for ref in refs[1:received]:
                total = total + decoded_value(ref[which, me ^ k])
            out[which] = total if k == 0 else encoded(total)


def total_kernel(*refs, received):
    for which in range(2):
        total = refs[0][which]
        for ref in refs[1:received]:
            total = total + decoded_value(ref[which])
        refs[-1][which] = encoded(total)


def split_kernel(flag_ref, *refs, received, slot):
    me = flag_ref[slot]
    for which in range(2):
        for k, ref in enumerate(refs[:received]):
            refs[which - 2][me ^ k] = ref[which]


def gather_kernel(flag_ref, *refs, slot):
    me = flag_ref[slot]
    for k, ref in enumerate(refs[:-1]):
        refs[-1][me ^ k] = ref[...]


def join_kernel(flag_ref, mine_ref, theirs_ref, out_ref, first_ref, second_ref):
    half, _, channels = mine_ref.shape
    is_first = flag_ref[3] == 0
    first_ref[...] = decoded_value(jnp.where(is_first, mine_ref[...], theirs_ref[...])).reshape(first_ref.shape)
    second_ref[...] = decoded_value(jnp.where(is_first, theirs_ref[...], mine_ref[...])).reshape(second_ref.shape)
    for tap in range(TAPS):
        here = slice(tap * channels, (tap + 1) * channels)
        out_ref[:half, here] = first_ref[pl.ds(tap, half, stride=SLOTS), :]
        out_ref[half:, here] = second_ref[pl.ds(tap, half, stride=SLOTS), :]


def weight_second_kernel(flag_ref, stack_ref, act_ref, mine_ref, theirs_ref, right_ref):
    rows, frames, channels, cols = act_ref.shape
    for row in range(rows):
        right_ref[row * cols : (row + 1) * cols] = jnp.transpose(
            act_ref[row].reshape(frames * channels, cols)
        )
    right = right_ref[...]
    for down in range(3):
        parts = []
        for frame in range(4):
            left = jnp.concatenate([stack_ref[down + row, frame] for row in range(rows)], axis=1)
            parts.append(jnp.dot(left, right, preferred_element_type=F32))
        for kt in range(3):
            term = parts[2 - kt][:, :channels] + parts[3 - kt][:, channels:]
            for across in range(3):
                tap = 9 * kt + 3 * (2 - down) + (2 - across)
                put_halves(flag_ref, mine_ref, theirs_ref, tap, term[across * channels : (across + 1) * channels])


def weight_first_kernel(flag_ref, stack_ref, grad_ref, mine_ref, theirs_ref, right_ref):
    rows, frames, channels, cols = grad_ref.shape
    for row in range(rows):
        right_ref[row * cols : (row + 1) * cols] = jnp.transpose(
            grad_ref[row].reshape(frames * channels, cols)
        )
    right = right_ref[...]
    for down in range(3):
        parts = []
        for frame in range(4):
            left = jnp.concatenate([stack_ref[down + row, frame] for row in range(rows)], axis=1)
            parts.append(jnp.dot(left, right, preferred_element_type=F32))
        for kt in range(3):
            term = parts[kt][:, :channels] + parts[kt + 1][:, channels:]
            for across in range(3):
                tap = 9 * kt + 3 * down + across
                block = jnp.transpose(term[across * channels : (across + 1) * channels])
                put_halves(flag_ref, mine_ref, theirs_ref, tap, block)


def first_grad_kernel(flag_ref, *refs, count):
    weight, latent, par_ref, st_ref, _, scaled_ref, sums_ref, stack_ref = refs[-8:]
    rows, frames, channels, cols = latent.shape
    mean, inverse, gain, shift, scale = norm_columns(par_ref, st_ref, count, 1)
    fill_future(stack_ref, flag_ref, *refs[:-8])
    first = jnp.zeros((channels, 128), F32)
    second = jnp.zeros((channels, 128), F32)
    for row in range(rows):
        out = conv_rows(stack_ref, weight, row)
        for frame in range(frames):
            grad = out[frame * channels : (frame + 1) * channels]
            normed = (latent[row, frame].astype(F32) * scale - mean) * inverse
            pre = normed * gain + shift
            sig = sigmoid(pre)
            scaled = grad * (sig + pre * sig * (1.0 - sig)) * gain
            scaled_ref[row, frame] = scaled
            first = first + lanes_of(scaled)
            second = second + lanes_of(scaled * normed)
    put_rows(sums_ref, group_sums(first), group_sums(second))


def decoded_grad_kernel(scaled, latent, cotangent, par_ref, st_ref, sums_ref, out_ref, token_ref, *, count):
    token_ref[...] = jnp.zeros(token_ref.shape, F32)
    rows, frames, channels, cols = latent.shape
    mean, inverse, _, _, scale = norm_columns(par_ref, st_ref, count, 1)
    means = sums_ref[0] / count
    first, second = columns_of(means[0:1], means[1:2])[:2]
    for row in range(rows):
        for frame in range(frames):
            normed = (latent[row, frame].astype(F32) * scale - mean) * inverse
            out_ref[:, frame, row, :] = cotangent[row, frame].astype(F32) + inverse * (
                scaled[row, frame] - first - normed * second
            )


def weight_forward_kernel(weight, out_ref):
    channels = weight.shape[0]
    wide = 3 * channels
    for t in range(2):
        for kr in range(3):
            for f in range(4):
                kt = f - t
                here = slice((kr * 4 + f) * wide, (kr * 4 + f + 1) * wide)
                if 0 <= kt < 3:
                    tap = 3 * kt + kr
                    block = weight[:, tap * wide : (tap + 1) * wide]
                else:
                    block = jnp.zeros((channels, wide), BF16)
                out_ref[t * channels : (t + 1) * channels, here] = block


def weight_back_kernel(weight, out_ref):
    channels = weight.shape[0]
    for down in range(3):
        for across in range(3):
            blocks = [
                jnp.transpose(
                    weight[
                        :,
                        (9 * kt + 3 * (2 - down) + 2 - across) * channels : (9 * kt + 3 * (2 - down) + 3 - across)
                        * channels,
                    ]
                )
                for kt in range(3)
            ]
            for t in range(2):
                for f in range(4):
                    kt = t + 2 - f
                    start = ((down * 4 + f) * 3 + across) * channels
                    block = blocks[kt] if 0 <= kt < 3 else jnp.zeros((channels, channels), BF16)
                    out_ref[t * channels : (t + 1) * channels, start : start + channels] = block


def shifted(value, axis, steps):
    count = lax.axis_size(axis)
    initial, last = max(0, -steps), min(count, count - steps)
    return lax.ppermute(value, axis, [(source, source + steps) for source in range(initial, last)])


def rounds(axes):
    for axis in axes:
        count = lax.axis_size(axis)
        step = 1
        while step < count:
            wide = 4 if 4 * step <= count else 2
            yield axis, step, [[(i, i ^ (step * k)) for i in range(count)] for k in range(1, wide)]
            step *= wide


def pairwise(parts, join):
    while len(parts) > 1:
        parts = [join(a, b) for a, b in zip(parts[::2], parts[1::2])]
    return parts[0]


def sum_kernel(*refs, parts):
    refs[-1][...] = pairwise([ref[...] for ref in refs[:parts]], lambda a, b: a + b)


def stats_kernel(*refs, parts, count):
    refs[-1][...] = pairwise([(ref[...], count) for ref in refs[:parts]], joined_stats)[0]


def all_sum(value, after=()):
    for axis, _, exchanges in rounds(("tm", "height", "width")):
        parts = [value] + [lax.ppermute(value, axis, pairs) for pairs in exchanges]
        if after:
            value = joined_after(functools.partial(sum_kernel, parts=len(parts)), parts, after)
        else:
            value = pairwise(parts, lambda a, b: a + b)
        after = ()
    return value


def joined_after(body, parts, after):
    (value,) = call(body, [shape(parts[0].shape, F32)], [VMEM] * (len(parts) + len(after)), (*parts, *after))
    return value


def all_stats(value, count, after=()):
    for axis, _, exchanges in rounds(("tm", "height", "width")):
        parts = [value] + [lax.ppermute(value, axis, pairs) for pairs in exchanges]
        if after:
            value = joined_after(functools.partial(stats_kernel, parts=len(parts), count=count), parts, after)
        else:
            value, _ = pairwise([(part, count) for part in parts], joined_stats)
        count, after = count * len(parts), ()
    return value


def joined_stats(first, second):
    (a, count), (b, _) = first, second
    gap = a[:, 0:1] - b[:, 0:1]
    squares = a[:, 1:2] + b[:, 1:2] + gap * gap * (0.5 * count)
    return jnp.concatenate([0.5 * (a[:, 0:1] + b[:, 0:1]), squares], axis=1), 2.0 * count


def swapped(value):
    return lax.ppermute(value, "width", [(0, 1), (1, 0)])


def weight_rounds():
    return list(rounds(("height", "tm")))


def scattered(flags, second, first):
    half, _, channels = second[0].shape
    axis, _, exchanges = weight_rounds()[0]
    parts = len(exchanges) + 1
    rows = half // parts
    terms = [part for mine, theirs in (second, first) for part in (mine, swapped(theirs))]
    part = (2, rows, SLOTS, channels)
    kept, *sent = call(
        functools.partial(first_scatter_kernel, slot=4),
        [shape(part, F32)] + [shape(part, jnp.int16)] * (parts - 1),
        [SMEM] + [VMEM] * 4,
        (flags, *[term.reshape(parts, rows, SLOTS, channels) for term in terms]),
    )
    return [kept] + [lax.ppermute(v, axis, pairs) for v, pairs in zip(sent, exchanges)], sent[0]


def summed(flags, received, after):
    for number, (axis, _, exchanges) in enumerate(weight_rounds()[1:], 5):
        parts = len(exchanges) + 1
        _, rows, _, channels = received[0].shape
        part = (2, rows // parts, SLOTS, channels)
        views = [v.reshape(2, parts, *part[1:]) for v in received]
        kept, *sent = call(
            functools.partial(scatter_kernel, received=len(views), sent=parts, slot=number),
            [shape(part, F32)] + [shape(part, jnp.int16)] * (parts - 1),
            [SMEM] + [VMEM] * (len(views) + len(after)),
            (flags, *views, *after),
        )
        after = ()
        received = [kept] + [lax.ppermute(v, axis, pairs) for v, pairs in zip(sent, exchanges)]
        last = sent[0]
    return received, last


def gathered(flags, received, after, after_last):
    (total,) = call(
        functools.partial(total_kernel, received=len(received)),
        [shape(received[0].shape, jnp.int16)],
        [VMEM] * (len(received) + len(after)),
        (*received, *after),
    )
    _, rows, _, channels = total.shape
    back = list(enumerate(weight_rounds(), 4))[::-1]
    number, (axis, _, exchanges) = back[0]
    pieces = [total] + [lax.ppermute(total, axis, pairs) for pairs in exchanges]
    values = call(
        functools.partial(split_kernel, received=len(pieces), slot=number),
        [shape((len(pieces), rows, SLOTS, channels), jnp.int16)] * 2,
        [SMEM] + [VMEM] * (len(pieces) + 1),
        (flags, *pieces, after_last),
    )
    results = []
    for value in values:
        for number, (axis, _, exchanges) in back[1:]:
            value = value.reshape(-1, SLOTS, channels)
            pieces = [value] + [lax.ppermute(value, axis, pairs) for pairs in exchanges]
            (value,) = call(
                functools.partial(gather_kernel, slot=number),
                [shape((len(pieces), *value.shape), jnp.int16)],
                [SMEM] + [VMEM] * len(pieces),
                (flags, *pieces),
            )
        results.append(value.reshape(-1, SLOTS, channels))
    return results


def joined(flags, mine, theirs):
    half, _, channels = mine.shape
    (total,) = call(
        join_kernel,
        [shape((2 * half, TAPS * channels), F32)],
        [SMEM] + [VMEM] * 2,
        (flags, mine, theirs),
        scratch=[pltpu.VMEM((half * SLOTS, channels), F32)] * 2,
    )
    return total


def edges(flags, planes, after):
    channels = planes[0].shape[2]
    args = (*planes, *after)
    (columns,) = call(edges_kernel, [shape((channels, 128), BF16)], [SMEM] + [VMEM] * len(args), (flags, *args))
    return columns


def row_halos(down, up, after=()):
    above, below = shifted(down, "height", 1), shifted(up, "height", -1)
    return call(
        rows_kernel,
        [shape((2, *down.shape[1:]), BF16)] * down.shape[0],
        [VMEM] * (2 + len(after)),
        (above, below, *after),
    )


def with_columns(flags, own, around, after=()):
    edge = swapped(edges(flags, (own, around[0]), after))
    rim = swapped(edges(flags, around[1:], after))
    return *around, edge, rim


def shards(
    latent,
    exponents,
    cotangent,
    conv_first,
    conv_second,
    gain_first,
    shift_first,
    gain_second,
    shift_second,
):
    channels, frames, rows, cols = latent.shape
    groups = exponents.shape[0]
    devices = lax.axis_size("tm") * lax.axis_size("height") * lax.axis_size("width")
    count = float(channels // groups * frames * rows * cols * devices)
    tm, height, width = (lax.axis_index(axis) for axis in ("tm", "height", "width"))
    flags = jnp.stack(
        [
            (tm > 0).astype(jnp.int32),
            (height > 0).astype(jnp.int32),
            (height < lax.axis_size("height") - 1).astype(jnp.int32),
            width.astype(jnp.int32),
        ]
        + [
            (lax.axis_index(axis) // step % (len(exchanges) + 1)).astype(jnp.int32)
            for axis, step, exchanges in weight_rounds()
        ]
    )
    scale = jnp.repeat(jnp.exp2(exponents.astype(F32)), channels // groups)
    zeros = jnp.zeros_like(scale)
    par = jnp.stack([scale, gain_first, shift_first, gain_second, shift_second, zeros, zeros, zeros])
    block = (rows, frames, channels, cols)
    stack = (rows + 2, 4, 3 * channels, cols)
    taps = (2 * channels, 36 * channels)
    halves = [shape((channels // 2 * SLOTS, channels), F32)] * 2
    conv_flops = 3 * 2 * 4 * 256 * 36 * channels * 2 * channels
    small = shape((1, 2, channels), F32)

    message = shape((2, frames, channels, cols), BF16)
    latent, cotangent, down, up, stats_first = call(
        planes_kernel,
        [shape(block, BF16), shape(block, BF16), message, message, small],
        [VMEM] * 3,
        (latent, cotangent, par),
    )
    near, near_c = row_halos(down, up)
    around = with_columns(flags, latent, (shifted(latent, "tm", 1), near, shifted(near, "tm", 1)))
    around_c = (shifted(cotangent, "tm", -1), near_c, shifted(near_c, "tm", -1))
    stats_first = all_stats(stats_first, count / devices)
    (weight_first,) = call(weight_forward_kernel, [shape(taps, BF16)], [VMEM], (conv_first,))
    (weight_second_t,) = call(weight_back_kernel, [shape(taps, BF16)], [VMEM], (conv_second,))
    (weight_first_t,) = call(weight_back_kernel, [shape(taps, BF16)], [VMEM], (conv_first,))

    hidden, stats_second, stack_first = call(
        functools.partial(conv_first_kernel, count=count),
        [shape(block, F32), small, shape(stack, BF16)],
        [SMEM] + [VMEM] * 10,
        (flags, latent, *around, par, stats_first, weight_first, around_c[2]),
        flops=conv_flops,
        transcendentals=3 * latent.size,
    )
    around_c = with_columns(flags, cotangent, around_c, (stats_second,))
    grad_second, stack_c = call(
        conv_back_kernel,
        [shape(block, F32), shape(stack, BF16)],
        [SMEM] + [VMEM] * 7,
        (flags, cotangent, *around_c, weight_second_t),
        flops=conv_flops,
    )
    stats_second = all_stats(stats_second, count / devices, (grad_second,))
    act_second, scaled, sums = call(
        functools.partial(norm_second_kernel, count=count),
        [shape(block, BF16), shape(block, F32), small],
        [VMEM] * 4,
        (hidden, grad_second, par, stats_second),
        transcendentals=latent.size,
    )
    halves_second = call(
        weight_second_kernel,
        halves,
        [SMEM] + [VMEM] * 2,
        (flags, stack_c, act_second),
        scratch=[pltpu.VMEM((rows * cols, frames * channels), BF16)],
        flops=conv_flops,
    )
    sums = all_sum(sums, (halves_second[0],))
    message = shape((1, frames, channels, cols), BF16)
    hidden_grad, down, up = call(
        functools.partial(hidden_grad_kernel, count=count),
        [shape(block, BF16), message, message],
        [VMEM] * 5,
        (hidden, scaled, par, stats_second, sums),
    )
    future = shifted(hidden_grad, "tm", -1)
    (near,) = row_halos(down, up, (future,))
    around = (future, near, shifted(near, "tm", -1))
    halves_first = call(
        weight_first_kernel,
        halves,
        [SMEM] + [VMEM] * 2,
        (flags, stack_first, hidden_grad),
        scratch=[pltpu.VMEM((rows * cols, frames * channels), BF16)],
        flops=conv_flops,
    )
    halves_second, halves_first = (
        [v.reshape(channels // 2, SLOTS, channels) for v in halves] for halves in (halves_second, halves_first)
    )
    weights, sent = scattered(flags, halves_second, halves_first)
    around = with_columns(flags, hidden_grad, around, (sent,))
    weights, sent = summed(flags, weights, around[:2])
    scaled, sums_first = call(
        functools.partial(first_grad_kernel, count=count),
        [shape(block, F32), small],
        [SMEM] + [VMEM] * 11,
        (flags, hidden_grad, *around, weight_first_t, latent, par, stats_first, sent),
        scratch=[pltpu.VMEM(stack, BF16)],
        flops=conv_flops,
        transcendentals=latent.size,
    )
    sums_first = all_sum(sums_first)
    decoded_grad, token = call(
        functools.partial(decoded_grad_kernel, count=count),
        [shape((channels, frames, rows, cols), F32), shape((8, 128), F32)],
        [VMEM] * 6,
        (scaled, latent, cotangent, par, stats_first, sums_first),
    )
    second, first = gathered(flags, weights, (), token)
    conv_second_grad = joined(flags, second, swapped(second))
    conv_first_grad = joined(flags, first, swapped(first))
    return decoded_grad, conv_first_grad, conv_second_grad


def solution(mesh):
    block = P(None, "tm", "height", "width")
    return jax.shard_map(
        shards,
        mesh=mesh,
        in_specs=(block, P(), block, P(), P(), P(), P(), P(), P()),
        out_specs=(block, P(), P()),
        check_vma=False,
    )
```

```python
import functools

import jax
import jax.numpy as jnp
from jax import lax
from jax.experimental import pallas as pl
from jax.experimental.pallas import tpu as pltpu
from jax.sharding import PartitionSpec as P

epsilon = 1e-05
F32 = jnp.float32
BF16 = jnp.bfloat16
GROUP = 4
TAPS, SLOTS = 27, 32
FULL, LOW = 32760.0, 65000.0
LN2 = 0.6931471805599453
VMEM = pl.BlockSpec(memory_space=pltpu.VMEM)
SMEM = pl.BlockSpec(memory_space=pltpu.SMEM)


def call(body, outs, specs, args, scratch=(), flops=0, transcendentals=0, limit=20):
    moved = sum(a.size * a.dtype.itemsize for a in args)
    moved += sum(o.size * o.dtype.itemsize for o in outs)
    return pl.pallas_call(
        body,
        out_shape=tuple(outs),
        in_specs=specs,
        out_specs=tuple(VMEM for _ in outs),
        scratch_shapes=scratch,
        compiler_params=pltpu.CompilerParams(vmem_limit_bytes=limit << 20),
        cost_estimate=pl.CostEstimate(
            flops=flops, bytes_accessed=moved, transcendentals=transcendentals
        ),
    )(*args)


def shape(dims, dtype):
    return jax.ShapeDtypeStruct(dims, dtype)


def group_sums(acc):
    rows = acc.shape[0]
    row = lax.broadcasted_iota(jnp.int32, acc.shape, 0)
    step = 1
    while step < GROUP:
        up = pltpu.roll(acc, rows - step, axis=0)
        down = pltpu.roll(acc, step, axis=0)
        acc = acc + jnp.where((row & step) == 0, up, down)
        step *= 2
    return jnp.sum(acc, axis=1, keepdims=True)


def lanes_of(plane):
    total = plane[:, :128]
    for start in range(128, plane.shape[1], 128):
        total = total + plane[:, start : start + 128]
    return total


def as_rows(first, second):
    channels = first.shape[0]
    lane = lax.broadcasted_iota(jnp.int32, (channels, 128), 1)
    both = jnp.where(lane == 0, first, jnp.where(lane == 1, second, 0.0))
    return jnp.transpose(both)[:2]


def local_stats(planes, count):
    acc = None
    for plane in planes:
        part = lanes_of(plane())
        acc = part if acc is None else acc + part
    mean = group_sums(acc) / count
    acc = None
    for plane in planes:
        off = plane() - mean
        part = lanes_of(off * off)
        acc = part if acc is None else acc + part
    return mean, group_sums(acc)


def put_rows(out_ref, first, second):
    out_ref[0] = as_rows(first, second)


def combined(st_ref, count):
    return st_ref[0, 0:1], st_ref[0, 1:2] / count


def columns_of(*rows):
    rows = list(rows) + [jnp.zeros_like(rows[0])] * (8 - len(rows))
    cols = jnp.transpose(jnp.concatenate(rows, axis=0))
    return [cols[:, i : i + 1] for i in range(8)]


def sigmoid(value):
    return 0.5 + 0.5 * jnp.tanh(0.5 * value)


def planes_kernel(latent_ref, cotangent_ref, par_ref, latent_out, cotangent_out, down_ref, up_ref, st_ref):
    _, frames, rows, cols = latent_ref.shape
    for which, (natural, out) in enumerate(((latent_ref, latent_out), (cotangent_ref, cotangent_out))):
        for row in range(rows):
            for frame in range(frames):
                plane = natural[:, frame, row, :]
                out[row, frame] = plane
                if row == rows - 1:
                    down_ref[which, frame] = plane
                if row == 0:
                    up_ref[which, frame] = plane
    scale = columns_of(par_ref[0:1])[0]
    planes = [
        functools.partial(lambda r, t: latent_out[r, t].astype(F32) * scale, r, t)
        for r in range(rows)
        for t in range(frames)
    ]
    put_rows(st_ref, *local_stats(planes, float(GROUP * rows * frames * cols)))


def rows_kernel(above_ref, below_ref, *refs):
    for which, out in enumerate(refs[-above_ref.shape[0] :]):
        out[0] = above_ref[which]
        out[1] = below_ref[which]


def source(own, other, near, far, other_first):
    def at(row, frame):
        is_other = (frame < 2) == other_first
        if row == 0 or row == own.shape[0] + 1:
            return (far if is_other else near), (0 if row == 0 else 1, frame % 2)
        return (other if is_other else own), (row - 1, frame % 2)

    return at


def edges_kernel(flag_ref, first_ref, second_ref, *refs):
    planes, out_ref = (first_ref, second_ref), refs[-1]
    is_first = flag_ref[3] == 0
    channels = planes[0].shape[2]
    lane = lax.broadcasted_iota(jnp.int32, (channels, 128), 1)
    acc = jnp.zeros((channels, 128), F32)
    number = 0
    for ref in planes:
        for row in range(ref.shape[0]):
            for frame in range(ref.shape[1]):
                last = pltpu.roll(ref[row, frame, :, -128:].astype(F32), 1, axis=1)
                edge = jnp.where(is_first, last, ref[row, frame, :, :128].astype(F32))
                moved = pltpu.roll(edge, number, axis=1) if number else edge
                acc = jnp.where(lane == number, moved, acc)
                number += 1
    out_ref[...] = acc.astype(BF16)


def edge_lane(row, frame, rows, other_first):
    is_other = int((frame < 2) == other_first)
    if row == 0 or row == rows + 1:
        return 1, 4 * is_other + 2 * int(row > 0) + frame % 2
    return 0, 2 * rows * is_other + 2 * (row - 1) + frame % 2


def fill_stack(stack, row, frame, plane, column, on_left, on_right):
    channels, cols = plane.shape
    lane = lax.broadcasted_iota(jnp.int32, (channels, cols), 1)
    column = column.astype(F32)
    left = jnp.where(lane == 0, (column * on_left).astype(BF16), pltpu.roll(plane, 1, axis=1))
    right = jnp.where(lane == cols - 1, (column * on_right).astype(BF16), pltpu.roll(plane, cols - 1, axis=1))
    stack[row, frame, 0:channels] = left
    stack[row, frame, channels : 2 * channels] = plane
    stack[row, frame, 2 * channels : 3 * channels] = right


def sides(flag_ref):
    on_left = (flag_ref[3] != 0).astype(F32)
    on_right = (flag_ref[3] == 0).astype(F32)
    return on_left, on_right


def conv_rows(stack, weight, row):
    three = stack[row : row + 3].reshape(weight.shape[1], stack.shape[3])
    return jnp.dot(weight[...], three, preferred_element_type=F32)


def norm_columns(par_ref, st_ref, count, gain_row):
    par = par_ref[...]
    mean, variance = combined(st_ref, count)
    inverse = 1.0 / jnp.sqrt(variance + epsilon)
    gain = par[gain_row : gain_row + 1]
    shift = par[gain_row + 1 : gain_row + 2]
    return columns_of(mean, inverse, gain, shift, par[0:1])[:5]


def conv_first_kernel(
    flag_ref, own, past, near, far, edge_ref, rim_ref, par_ref, st_ref, weight, after, hidden_ref, st_out, stack_ref,
    *, count
):
    rows, frames, channels, cols = own.shape
    at = source(own, past, near, far, True)
    mean, inverse, gain, shift, scale = norm_columns(par_ref, st_ref, count, 1)

    def act(latent):
        pre = (latent.astype(F32) * scale - mean) * inverse * gain + shift
        return pre * sigmoid(pre)

    has_past = flag_ref[0].astype(F32)
    has_top = flag_ref[1].astype(F32)
    has_bottom = flag_ref[2].astype(F32)
    on_left, on_right = sides(flag_ref)
    edges = (act(edge_ref[...]), act(rim_ref[...]))
    for row in range(rows + 2):
        for frame in range(4):
            ref, index = at(row, frame)
            which, number = edge_lane(row, frame, rows, True)
            plane = act(ref[index])
            column = edges[which][:, number : number + 1]
            factor = None
            if frame < 2:
                factor = has_past
            if row in (0, rows + 1):
                beside = has_top if row == 0 else has_bottom
                factor = beside if factor is None else factor * beside
            if factor is not None:
                plane = plane * factor
                column = column * factor
            fill_stack(stack_ref, row, frame, plane.astype(BF16), column, on_left, on_right)
    for row in range(rows):
        out = conv_rows(stack_ref, weight, row)
        for frame in range(frames):
            hidden_ref[row, frame] = out[frame * channels : (frame + 1) * channels]
    planes = [
        functools.partial(lambda r, t: hidden_ref[r, t], r, t) for r in range(rows) for t in range(frames)
    ]
    put_rows(st_out, *local_stats(planes, float(GROUP * rows * frames * cols)))


def fill_future(stack, flag_ref, own, future, near, far, edge_ref, rim_ref):
    rows = own.shape[0]
    at = source(own, future, near, far, False)
    on_left, on_right = sides(flag_ref)
    edges = (edge_ref[...], rim_ref[...])
    for row in range(rows + 2):
        for frame in range(4):
            ref, index = at(row, frame)
            which, number = edge_lane(row, frame, rows, False)
            fill_stack(stack, row, frame, ref[index], edges[which][:, number : number + 1], on_left, on_right)


def conv_back_kernel(flag_ref, *refs):
    weight, grad_ref, stack_ref = refs[-3:]
    rows, frames, channels, _ = grad_ref.shape
    fill_future(stack_ref, flag_ref, *refs[:-3])
    for row in range(rows):
        out = conv_rows(stack_ref, weight, row)
        for frame in range(frames):
            grad_ref[row, frame] = out[frame * channels : (frame + 1) * channels]


def norm_second_kernel(hidden, grad, par_ref, st_ref, act_ref, scaled_ref, sums_ref, *, count):
    rows, frames, channels, cols = hidden.shape
    mean, inverse, gain, shift, _ = norm_columns(par_ref, st_ref, count, 3)
    first = jnp.zeros((channels, 128), F32)
    second = jnp.zeros((channels, 128), F32)
    for row in range(rows):
        for frame in range(frames):
            normed = (hidden[row, frame] - mean) * inverse
            pre = normed * gain + shift
            sig = sigmoid(pre)
            act = pre * sig
            act_ref[row, frame] = act.astype(BF16)
            scaled = grad[row, frame] * (sig + act * (1.0 - sig)) * gain
            scaled_ref[row, frame] = scaled
            first = first + lanes_of(scaled)
            second = second + lanes_of(scaled * normed)
    put_rows(sums_ref, group_sums(first), group_sums(second))


def hidden_grad_kernel(
    hidden, scaled, par_ref, st_ref, sums_ref, out_ref, down_ref, up_ref, *, count
):
    rows, frames, channels, cols = hidden.shape
    mean, inverse, _, _, _ = norm_columns(par_ref, st_ref, count, 3)
    means = sums_ref[0] / count
    first, second = columns_of(means[0:1], means[1:2])[:2]
    for row in range(rows):
        for frame in range(frames):
            normed = (hidden[row, frame] - mean) * inverse
            plane = (inverse * (scaled[row, frame] - first - normed * second)).astype(BF16)
            out_ref[row, frame] = plane
            if row == rows - 1:
                down_ref[0, frame] = plane
            if row == 0:
                up_ref[0, frame] = plane


def put_halves(flag_ref, mine_ref, theirs_ref, tap, block):
    half = block.shape[0] // 2
    here = pl.ds(tap, half, stride=SLOTS)
    upper, lower = block[:half], block[half:]
    is_first = flag_ref[3] == 0
    mine_ref[here, :] = jnp.where(is_first, upper, lower)
    theirs_ref[here, :] = jnp.where(is_first, lower, upper)


def encoded(value, digits=None):
    slot = lax.broadcasted_iota(jnp.int32, value.shape, 1)
    value = jnp.where(slot < TAPS, value, 0.0)
    top = jnp.max(jnp.abs(value), axis=1, keepdims=True)
    power = jnp.ceil(jnp.log(jnp.maximum(top, 1e-30)) * (1.0 / LN2))
    number = jnp.round(value * (FULL * jnp.exp(power * -LN2)))
    number = jnp.where(slot < TAPS, number, power)
    if digits is not None:
        first_row = lax.broadcasted_iota(jnp.int32, value.shape, 0) == 0
        for place, digit in enumerate(digits):
            number = jnp.where(first_row & (slot == TAPS + place), digit[None], number)
    return number.astype(jnp.int32).astype(jnp.int16)


def digits_of(value):
    power = jnp.ceil(jnp.log(jnp.maximum(jnp.abs(value), 1e-30)) * (1.0 / LN2))
    scaled = value * (FULL * jnp.exp(power * -LN2))
    high = jnp.round(scaled)
    return high, jnp.round((scaled - high) * LOW), power


def value_of(number):
    number = number.astype(jnp.int32).astype(F32)
    high, low, power = (number[TAPS + place : TAPS + place + 1] for place in range(3))
    return (high + low * (1.0 / LOW)) * (jnp.exp(power * LN2) * (1.0 / FULL))


def decoded_value(number):
    number = number.astype(jnp.int32).astype(F32)
    return number * (jnp.exp(number[:, SLOTS - 1 : SLOTS] * LN2) * (1.0 / FULL))


def first_scatter_kernel(flag_ref, *refs, slot):
    me = flag_ref[slot]
    for which in range(2):
        mine, other = refs[2 * which], refs[2 * which + 1]
        for k, out in enumerate(refs[4:]):
            total = mine[me ^ k] + other[me ^ k]
            out[which] = total if k == 0 else encoded(total)


def scatter_kernel(flag_ref, sums_ref, *refs, received, sent, slot, last):
    me = flag_ref[slot]
    for which in range(2):
        digits = digits_of(sums_ref[0, which : which + 1]) if last else None
        for k, out in enumerate(refs[-sent:]):
            total = refs[0][which, me ^ k]
            for ref in refs[1:received]:
                total = total + decoded_value(ref[which, me ^ k])
            out[which] = total if k == 0 else encoded(total, digits)


def total_kernel(sums_ref, *refs, received):
    out_ref, sums_out = refs[-2:]
    for which in range(2):
        total = refs[0][which]
        terms = sums_ref[0, which : which + 1]
        for ref in refs[1:received]:
            total = total + decoded_value(ref[which])
            terms = terms + value_of(ref[which, 0])
        out_ref[which] = encoded(total)
        sums_out[0, which : which + 1] = terms


def split_kernel(flag_ref, *refs, received, slot):
    me = flag_ref[slot]
    for which in range(2):
        for k, ref in enumerate(refs[:received]):
            refs[which - 2][me ^ k] = ref[which]


def gather_kernel(flag_ref, *refs, slot):
    me = flag_ref[slot]
    for k, ref in enumerate(refs[:-1]):
        refs[-1][me ^ k] = ref[...]


def join_kernel(flag_ref, mine_ref, theirs_ref, out_ref, first_ref, second_ref):
    half, _, channels = mine_ref.shape
    is_first = flag_ref[3] == 0
    first_ref[...] = decoded_value(jnp.where(is_first, mine_ref[...], theirs_ref[...])).reshape(first_ref.shape)
    second_ref[...] = decoded_value(jnp.where(is_first, theirs_ref[...], mine_ref[...])).reshape(second_ref.shape)
    for tap in range(TAPS):
        here = slice(tap * channels, (tap + 1) * channels)
        out_ref[:half, here] = first_ref[pl.ds(tap, half, stride=SLOTS), :]
        out_ref[half:, here] = second_ref[pl.ds(tap, half, stride=SLOTS), :]


def weight_second_kernel(flag_ref, stack_ref, act_ref, mine_ref, theirs_ref, right_ref):
    rows, frames, channels, cols = act_ref.shape
    for row in range(rows):
        right_ref[row * cols : (row + 1) * cols] = jnp.transpose(
            act_ref[row].reshape(frames * channels, cols)
        )
    right = right_ref[...]
    for down in range(3):
        parts = []
        for frame in range(4):
            left = jnp.concatenate([stack_ref[down + row, frame] for row in range(rows)], axis=1)
            parts.append(jnp.dot(left, right, preferred_element_type=F32))
        for kt in range(3):
            term = parts[2 - kt][:, :channels] + parts[3 - kt][:, channels:]
            for across in range(3):
                tap = 9 * kt + 3 * (2 - down) + (2 - across)
                put_halves(flag_ref, mine_ref, theirs_ref, tap, term[across * channels : (across + 1) * channels])


def weight_first_kernel(flag_ref, stack_ref, grad_ref, mine_ref, theirs_ref, right_ref):
    rows, frames, channels, cols = grad_ref.shape
    for row in range(rows):
        right_ref[row * cols : (row + 1) * cols] = jnp.transpose(
            grad_ref[row].reshape(frames * channels, cols)
        )
    right = right_ref[...]
    for down in range(3):
        parts = []
        for frame in range(4):
            left = jnp.concatenate([stack_ref[down + row, frame] for row in range(rows)], axis=1)
            parts.append(jnp.dot(left, right, preferred_element_type=F32))
        for kt in range(3):
            term = parts[kt][:, :channels] + parts[kt + 1][:, channels:]
            for across in range(3):
                tap = 9 * kt + 3 * down + across
                block = jnp.transpose(term[across * channels : (across + 1) * channels])
                put_halves(flag_ref, mine_ref, theirs_ref, tap, block)


def first_grad_kernel(flag_ref, *refs, count):
    weight, latent, par_ref, st_ref = refs[6:10]
    scaled_ref, sums_ref, stack_ref = refs[-3:]
    rows, frames, channels, cols = latent.shape
    mean, inverse, gain, shift, scale = norm_columns(par_ref, st_ref, count, 1)
    fill_future(stack_ref, flag_ref, *refs[:6])
    first = jnp.zeros((channels, 128), F32)
    second = jnp.zeros((channels, 128), F32)
    for row in range(rows):
        out = conv_rows(stack_ref, weight, row)
        for frame in range(frames):
            grad = out[frame * channels : (frame + 1) * channels]
            normed = (latent[row, frame].astype(F32) * scale - mean) * inverse
            pre = normed * gain + shift
            sig = sigmoid(pre)
            scaled = grad * (sig + pre * sig * (1.0 - sig)) * gain
            scaled_ref[row, frame] = scaled
            first = first + lanes_of(scaled)
            second = second + lanes_of(scaled * normed)
    put_rows(sums_ref, group_sums(first), group_sums(second))


def decoded_grad_kernel(scaled, latent, cotangent, par_ref, st_ref, sums_ref, out_ref, token_ref, *, count):
    token_ref[...] = jnp.zeros(token_ref.shape, F32)
    rows, frames, channels, cols = latent.shape
    mean, inverse, _, _, scale = norm_columns(par_ref, st_ref, count, 1)
    means = sums_ref[0] / count
    first, second = columns_of(means[0:1], means[1:2])[:2]
    for row in range(rows):
        for frame in range(frames):
            normed = (latent[row, frame].astype(F32) * scale - mean) * inverse
            out_ref[:, frame, row, :] = cotangent[row, frame].astype(F32) + inverse * (
                scaled[row, frame] - first - normed * second
            )


def weight_forward_kernel(weight, out_ref):
    channels = weight.shape[0]
    wide = 3 * channels
    for t in range(2):
        for kr in range(3):
            for f in range(4):
                kt = f - t
                here = slice((kr * 4 + f) * wide, (kr * 4 + f + 1) * wide)
                if 0 <= kt < 3:
                    tap = 3 * kt + kr
                    block = weight[:, tap * wide : (tap + 1) * wide]
                else:
                    block = jnp.zeros((channels, wide), BF16)
                out_ref[t * channels : (t + 1) * channels, here] = block


def weight_back_kernel(weight, out_ref):
    channels = weight.shape[0]
    for down in range(3):
        for across in range(3):
            blocks = [
                jnp.transpose(
                    weight[
                        :,
                        (9 * kt + 3 * (2 - down) + 2 - across) * channels : (9 * kt + 3 * (2 - down) + 3 - across)
                        * channels,
                    ]
                )
                for kt in range(3)
            ]
            for t in range(2):
                for f in range(4):
                    kt = t + 2 - f
                    start = ((down * 4 + f) * 3 + across) * channels
                    block = blocks[kt] if 0 <= kt < 3 else jnp.zeros((channels, channels), BF16)
                    out_ref[t * channels : (t + 1) * channels, start : start + channels] = block


def shifted(value, axis, steps):
    count = lax.axis_size(axis)
    initial, last = max(0, -steps), min(count, count - steps)
    return lax.ppermute(value, axis, [(source, source + steps) for source in range(initial, last)])


def rounds(axes):
    for axis in axes:
        count = lax.axis_size(axis)
        step = 1
        while step < count:
            wide = 4 if 4 * step <= count else 2
            yield axis, step, [[(i, i ^ (step * k)) for i in range(count)] for k in range(1, wide)]
            step *= wide


def pairwise(parts, join):
    while len(parts) > 1:
        parts = [join(a, b) for a, b in zip(parts[::2], parts[1::2])]
    return parts[0]


def sum_kernel(*refs, parts):
    refs[-1][...] = pairwise([ref[...] for ref in refs[:parts]], lambda a, b: a + b)


def stats_kernel(*refs, parts, count):
    refs[-1][...] = pairwise([(ref[...], count) for ref in refs[:parts]], joined_stats)[0]


def all_sum(value, after=(), axes=("tm", "height", "width")):
    for axis, _, exchanges in rounds(axes):
        parts = [value] + [lax.ppermute(value, axis, pairs) for pairs in exchanges]
        if after:
            value = joined_after(functools.partial(sum_kernel, parts=len(parts)), parts, after)
        else:
            value = pairwise(parts, lambda a, b: a + b)
        after = ()
    return value


def joined_after(body, parts, after):
    (value,) = call(body, [shape(parts[0].shape, F32)], [VMEM] * (len(parts) + len(after)), (*parts, *after))
    return value


def all_stats(value, count, after=()):
    for axis, _, exchanges in rounds(("tm", "height", "width")):
        parts = [value] + [lax.ppermute(value, axis, pairs) for pairs in exchanges]
        if after:
            value = joined_after(functools.partial(stats_kernel, parts=len(parts), count=count), parts, after)
        else:
            value, _ = pairwise([(part, count) for part in parts], joined_stats)
        count, after = count * len(parts), ()
    return value


def joined_stats(first, second):
    (a, count), (b, _) = first, second
    gap = a[:, 0:1] - b[:, 0:1]
    squares = a[:, 1:2] + b[:, 1:2] + gap * gap * (0.5 * count)
    return jnp.concatenate([0.5 * (a[:, 0:1] + b[:, 0:1]), squares], axis=1), 2.0 * count


def swapped(value):
    return lax.ppermute(value, "width", [(0, 1), (1, 0)])


def weight_rounds():
    return list(rounds(("height", "tm")))


def scattered(flags, second, first):
    half, _, channels = second[0].shape
    axis, _, exchanges = weight_rounds()[0]
    parts = len(exchanges) + 1
    rows = half // parts
    terms = [part for mine, theirs in (second, first) for part in (mine, swapped(theirs))]
    part = (2, rows, SLOTS, channels)
    kept, *sent = call(
        functools.partial(first_scatter_kernel, slot=4),
        [shape(part, F32)] + [shape(part, jnp.int16)] * (parts - 1),
        [SMEM] + [VMEM] * 4,
        (flags, *[term.reshape(parts, rows, SLOTS, channels) for term in terms]),
    )
    return [kept] + [lax.ppermute(v, axis, pairs) for v, pairs in zip(sent, exchanges)], sent[0]


def summed(flags, received, sums, after):
    others = weight_rounds()[1:]
    for number, (axis, _, exchanges) in enumerate(others, 5):
        parts = len(exchanges) + 1
        _, rows, _, channels = received[0].shape
        part = (2, rows // parts, SLOTS, channels)
        views = [v.reshape(2, parts, *part[1:]) for v in received]
        last = number == len(others) + 4
        kept, *sent = call(
            functools.partial(scatter_kernel, received=len(views), sent=parts, slot=number, last=last),
            [shape(part, F32)] + [shape(part, jnp.int16)] * (parts - 1),
            [SMEM] + [VMEM] * (1 + len(views) + len(after)),
            (flags, sums, *views, *after),
        )
        after = ()
        received = [kept] + [lax.ppermute(v, axis, pairs) for v, pairs in zip(sent, exchanges)]
    return call(
        functools.partial(total_kernel, received=len(received)),
        [shape(received[0].shape, jnp.int16), shape(sums.shape, F32)],
        [VMEM] * (1 + len(received)),
        (sums, *received),
    )


def gathered(flags, total, after_last):
    _, rows, _, channels = total.shape
    back = list(enumerate(weight_rounds(), 4))[::-1]
    number, (axis, _, exchanges) = back[0]
    pieces = [total] + [lax.ppermute(total, axis, pairs) for pairs in exchanges]
    values = call(
        functools.partial(split_kernel, received=len(pieces), slot=number),
        [shape((len(pieces), rows, SLOTS, channels), jnp.int16)] * 2,
        [SMEM] + [VMEM] * (len(pieces) + 1),
        (flags, *pieces, after_last),
    )
    results = []
    for value in values:
        for number, (axis, _, exchanges) in back[1:]:
            value = value.reshape(-1, SLOTS, channels)
            pieces = [value] + [lax.ppermute(value, axis, pairs) for pairs in exchanges]
            (value,) = call(
                functools.partial(gather_kernel, slot=number),
                [shape((len(pieces), *value.shape), jnp.int16)],
                [SMEM] + [VMEM] * len(pieces),
                (flags, *pieces),
            )
        results.append(value.reshape(-1, SLOTS, channels))
    return results


def joined(flags, mine, theirs):
    half, _, channels = mine.shape
    (total,) = call(
        join_kernel,
        [shape((2 * half, TAPS * channels), F32)],
        [SMEM] + [VMEM] * 2,
        (flags, mine, theirs),
        scratch=[pltpu.VMEM((half * SLOTS, channels), F32)] * 2,
    )
    return total


def edges(flags, planes, after):
    channels = planes[0].shape[2]
    args = (*planes, *after)
    (columns,) = call(edges_kernel, [shape((channels, 128), BF16)], [SMEM] + [VMEM] * len(args), (flags, *args))
    return columns


def row_halos(down, up, after=()):
    above, below = shifted(down, "height", 1), shifted(up, "height", -1)
    return call(
        rows_kernel,
        [shape((2, *down.shape[1:]), BF16)] * down.shape[0],
        [VMEM] * (2 + len(after)),
        (above, below, *after),
    )


def with_columns(flags, own, around, after=()):
    edge = swapped(edges(flags, (own, around[0]), after))
    rim = swapped(edges(flags, around[1:], after))
    return *around, edge, rim


def shards(
    latent,
    exponents,
    cotangent,
    conv_first,
    conv_second,
    gain_first,
    shift_first,
    gain_second,
    shift_second,
):
    channels, frames, rows, cols = latent.shape
    groups = exponents.shape[0]
    devices = lax.axis_size("tm") * lax.axis_size("height") * lax.axis_size("width")
    count = float(channels // groups * frames * rows * cols * devices)
    tm, height, width = (lax.axis_index(axis) for axis in ("tm", "height", "width"))
    flags = jnp.stack(
        [
            (tm > 0).astype(jnp.int32),
            (height > 0).astype(jnp.int32),
            (height < lax.axis_size("height") - 1).astype(jnp.int32),
            width.astype(jnp.int32),
        ]
        + [
            (lax.axis_index(axis) // step % (len(exchanges) + 1)).astype(jnp.int32)
            for axis, step, exchanges in weight_rounds()
        ]
    )
    scale = jnp.repeat(jnp.exp2(exponents.astype(F32)), channels // groups)
    zeros = jnp.zeros_like(scale)
    par = jnp.stack([scale, gain_first, shift_first, gain_second, shift_second, zeros, zeros, zeros])
    block = (rows, frames, channels, cols)
    stack = (rows + 2, 4, 3 * channels, cols)
    taps = (2 * channels, 36 * channels)
    halves = [shape((channels // 2 * SLOTS, channels), F32)] * 2
    conv_flops = 3 * 2 * 4 * 256 * 36 * channels * 2 * channels
    small = shape((1, 2, channels), F32)

    message = shape((2, frames, channels, cols), BF16)
    latent, cotangent, down, up, stats_first = call(
        planes_kernel,
        [shape(block, BF16), shape(block, BF16), message, message, small],
        [VMEM] * 3,
        (latent, cotangent, par),
    )
    near, near_c = row_halos(down, up)
    around = with_columns(flags, latent, (shifted(latent, "tm", 1), near, shifted(near, "tm", 1)))
    around_c = (shifted(cotangent, "tm", -1), near_c, shifted(near_c, "tm", -1))
    stats_first = all_stats(stats_first, count / devices)
    (weight_first,) = call(weight_forward_kernel, [shape(taps, BF16)], [VMEM], (conv_first,))
    (weight_second_t,) = call(weight_back_kernel, [shape(taps, BF16)], [VMEM], (conv_second,))
    (weight_first_t,) = call(weight_back_kernel, [shape(taps, BF16)], [VMEM], (conv_first,))

    hidden, stats_second, stack_first = call(
        functools.partial(conv_first_kernel, count=count),
        [shape(block, F32), small, shape(stack, BF16)],
        [SMEM] + [VMEM] * 10,
        (flags, latent, *around, par, stats_first, weight_first, around_c[2]),
        flops=conv_flops,
        transcendentals=3 * latent.size,
    )
    around_c = with_columns(flags, cotangent, around_c, (stats_second,))
    grad_second, stack_c = call(
        conv_back_kernel,
        [shape(block, F32), shape(stack, BF16)],
        [SMEM] + [VMEM] * 7,
        (flags, cotangent, *around_c, weight_second_t),
        flops=conv_flops,
    )
    stats_second = all_stats(stats_second, count / devices, (grad_second,))
    act_second, scaled, sums = call(
        functools.partial(norm_second_kernel, count=count),
        [shape(block, BF16), shape(block, F32), small],
        [VMEM] * 4,
        (hidden, grad_second, par, stats_second),
        transcendentals=latent.size,
    )
    halves_second = call(
        weight_second_kernel,
        halves,
        [SMEM] + [VMEM] * 2,
        (flags, stack_c, act_second),
        scratch=[pltpu.VMEM((rows * cols, frames * channels), BF16)],
        flops=conv_flops,
    )
    sums = all_sum(sums, (halves_second[0],))
    message = shape((1, frames, channels, cols), BF16)
    hidden_grad, down, up = call(
        functools.partial(hidden_grad_kernel, count=count),
        [shape(block, BF16), message, message],
        [VMEM] * 5,
        (hidden, scaled, par, stats_second, sums),
    )
    future = shifted(hidden_grad, "tm", -1)
    halves_first = call(
        weight_first_kernel,
        halves,
        [SMEM] + [VMEM] * 2,
        (flags, stack_first, hidden_grad),
        scratch=[pltpu.VMEM((rows * cols, frames * channels), BF16)],
        flops=conv_flops,
    )
    (near,) = row_halos(down, up, (future, halves_first[0]))
    around = (future, near, shifted(near, "tm", -1))
    halves_second, halves_first = (
        [v.reshape(channels // 2, SLOTS, channels) for v in halves] for halves in (halves_second, halves_first)
    )
    weights, sent = scattered(flags, halves_second, halves_first)
    around = with_columns(flags, hidden_grad, around, (sent,))
    scaled, sums_first = call(
        functools.partial(first_grad_kernel, count=count),
        [shape(block, F32), small],
        [SMEM] + [VMEM] * (9 + len(weights)),
        (flags, hidden_grad, *around, weight_first_t, latent, par, stats_first, *weights[1:]),
        scratch=[pltpu.VMEM(stack, BF16)],
        flops=conv_flops,
        transcendentals=latent.size,
    )
    total, sums_first = summed(flags, weights, sums_first, around[:2])
    sums_first = all_sum(sums_first, axes=("height", "width"))
    decoded_grad, token = call(
        functools.partial(decoded_grad_kernel, count=count),
        [shape((channels, frames, rows, cols), F32), shape((8, 128), F32)],
        [VMEM] * 6,
        (scaled, latent, cotangent, par, stats_first, sums_first),
    )
    second, first = gathered(flags, total, token)
    conv_second_grad = joined(flags, second, swapped(second))
    conv_first_grad = joined(flags, first, swapped(first))
    return decoded_grad, conv_first_grad, conv_second_grad


def solution(mesh):
    block = P(None, "tm", "height", "width")
    return jax.shard_map(
        shards,
        mesh=mesh,
        in_specs=(block, P(), block, P(), P(), P(), P(), P(), P()),
        out_specs=(block, P(), P()),
        check_vma=False,
    )
```

```python
import functools

import jax
import jax.numpy as jnp
from jax import lax
from jax.experimental import pallas as pl
from jax.experimental.pallas import tpu as pltpu
from jax.sharding import PartitionSpec as P

epsilon = 1e-05
F32 = jnp.float32
BF16 = jnp.bfloat16
GROUP = 4
TAPS, SLOTS = 27, 32
FULL, LOW = 32760.0, 65000.0
LN2 = 0.6931471805599453
VMEM = pl.BlockSpec(memory_space=pltpu.VMEM)
SMEM = pl.BlockSpec(memory_space=pltpu.SMEM)


def call(body, outs, specs, args, scratch=(), flops=0, transcendentals=0, limit=20):
    moved = sum(a.size * a.dtype.itemsize for a in args)
    moved += sum(o.size * o.dtype.itemsize for o in outs)
    return pl.pallas_call(
        body,
        out_shape=tuple(outs),
        in_specs=specs,
        out_specs=tuple(VMEM for _ in outs),
        scratch_shapes=scratch,
        compiler_params=pltpu.CompilerParams(vmem_limit_bytes=limit << 20),
        cost_estimate=pl.CostEstimate(
            flops=flops, bytes_accessed=moved, transcendentals=transcendentals
        ),
    )(*args)


def shape(dims, dtype):
    return jax.ShapeDtypeStruct(dims, dtype)


def group_sums(acc):
    rows = acc.shape[0]
    row = lax.broadcasted_iota(jnp.int32, acc.shape, 0)
    step = 1
    while step < GROUP:
        up = pltpu.roll(acc, rows - step, axis=0)
        down = pltpu.roll(acc, step, axis=0)
        acc = acc + jnp.where((row & step) == 0, up, down)
        step *= 2
    return jnp.sum(acc, axis=1, keepdims=True)


def lanes_of(plane):
    total = plane[:, :128]
    for start in range(128, plane.shape[1], 128):
        total = total + plane[:, start : start + 128]
    return total


def as_rows(first, second):
    channels = first.shape[0]
    lane = lax.broadcasted_iota(jnp.int32, (channels, 128), 1)
    both = jnp.where(lane == 0, first, jnp.where(lane == 1, second, 0.0))
    return jnp.transpose(both)[:2]


def local_stats(planes, count):
    acc = None
    for plane in planes:
        part = lanes_of(plane())
        acc = part if acc is None else acc + part
    mean = group_sums(acc) / count
    acc = None
    for plane in planes:
        off = plane() - mean
        part = lanes_of(off * off)
        acc = part if acc is None else acc + part
    return mean, group_sums(acc)


def put_rows(out_ref, first, second):
    out_ref[0] = as_rows(first, second)


def combined(st_ref, count):
    return st_ref[0, 0:1], st_ref[0, 1:2] / count


def columns_of(*rows):
    rows = list(rows) + [jnp.zeros_like(rows[0])] * (8 - len(rows))
    cols = jnp.transpose(jnp.concatenate(rows, axis=0))
    return [cols[:, i : i + 1] for i in range(8)]


def sigmoid(value):
    return 0.5 + 0.5 * jnp.tanh(0.5 * value)


def planes_kernel(latent_ref, cotangent_ref, par_ref, latent_out, cotangent_out, down_ref, up_ref, st_ref):
    _, frames, rows, cols = latent_ref.shape
    for which, (natural, out) in enumerate(((latent_ref, latent_out), (cotangent_ref, cotangent_out))):
        for row in range(rows):
            for frame in range(frames):
                plane = natural[:, frame, row, :]
                out[row, frame] = plane
                if row == rows - 1:
                    down_ref[which, frame] = plane
                if row == 0:
                    up_ref[which, frame] = plane
    scale = columns_of(par_ref[0:1])[0]
    planes = [
        functools.partial(lambda r, t: latent_out[r, t].astype(F32) * scale, r, t)
        for r in range(rows)
        for t in range(frames)
    ]
    put_rows(st_ref, *local_stats(planes, float(GROUP * rows * frames * cols)))


def rows_kernel(above_ref, below_ref, *refs):
    for which, out in enumerate(refs[-above_ref.shape[0] :]):
        out[0] = above_ref[which]
        out[1] = below_ref[which]


def rows_and_term_kernel(above_ref, below_ref, after, theirs_ref, near_ref, term_ref):
    near_ref[0] = above_ref[0]
    near_ref[1] = below_ref[0]
    term_ref[...] = encoded(theirs_ref[...])


def source(own, other, near, far, other_first):
    def at(row, frame):
        is_other = (frame < 2) == other_first
        if row == 0 or row == own.shape[0] + 1:
            return (far if is_other else near), (0 if row == 0 else 1, frame % 2)
        return (other if is_other else own), (row - 1, frame % 2)

    return at


def edges_kernel(flag_ref, first_ref, second_ref, *refs):
    planes, out_ref = (first_ref, second_ref), refs[-1]
    is_first = flag_ref[3] == 0
    channels = planes[0].shape[2]
    lane = lax.broadcasted_iota(jnp.int32, (channels, 128), 1)
    acc = jnp.zeros((channels, 128), F32)
    number = 0
    for ref in planes:
        for row in range(ref.shape[0]):
            for frame in range(ref.shape[1]):
                last = pltpu.roll(ref[row, frame, :, -128:].astype(F32), 1, axis=1)
                edge = jnp.where(is_first, last, ref[row, frame, :, :128].astype(F32))
                moved = pltpu.roll(edge, number, axis=1) if number else edge
                acc = jnp.where(lane == number, moved, acc)
                number += 1
    out_ref[...] = acc.astype(BF16)


def edge_lane(row, frame, rows, other_first):
    is_other = int((frame < 2) == other_first)
    if row == 0 or row == rows + 1:
        return 1, 4 * is_other + 2 * int(row > 0) + frame % 2
    return 0, 2 * rows * is_other + 2 * (row - 1) + frame % 2


def fill_stack(stack, row, frame, plane, column, on_left, on_right):
    channels, cols = plane.shape
    lane = lax.broadcasted_iota(jnp.int32, (channels, cols), 1)
    column = column.astype(F32)
    left = jnp.where(lane == 0, (column * on_left).astype(BF16), pltpu.roll(plane, 1, axis=1))
    right = jnp.where(lane == cols - 1, (column * on_right).astype(BF16), pltpu.roll(plane, cols - 1, axis=1))
    stack[row, frame, 0:channels] = left
    stack[row, frame, channels : 2 * channels] = plane
    stack[row, frame, 2 * channels : 3 * channels] = right


def sides(flag_ref):
    on_left = (flag_ref[3] != 0).astype(F32)
    on_right = (flag_ref[3] == 0).astype(F32)
    return on_left, on_right


def conv_rows(stack, weight, row):
    three = stack[row : row + 3].reshape(weight.shape[1], stack.shape[3])
    return jnp.dot(weight[...], three, preferred_element_type=F32)


def norm_columns(par_ref, st_ref, count, gain_row):
    par = par_ref[...]
    mean, variance = combined(st_ref, count)
    inverse = 1.0 / jnp.sqrt(variance + epsilon)
    gain = par[gain_row : gain_row + 1]
    shift = par[gain_row + 1 : gain_row + 2]
    return columns_of(mean, inverse, gain, shift, par[0:1])[:5]


def conv_first_kernel(
    flag_ref, own, past, near, far, edge_ref, rim_ref, par_ref, st_ref, weight, after, hidden_ref, st_out, stack_ref,
    *, count
):
    rows, frames, channels, cols = own.shape
    at = source(own, past, near, far, True)
    mean, inverse, gain, shift, scale = norm_columns(par_ref, st_ref, count, 1)

    def act(latent):
        pre = (latent.astype(F32) * scale - mean) * inverse * gain + shift
        return pre * sigmoid(pre)

    has_past = flag_ref[0].astype(F32)
    has_top = flag_ref[1].astype(F32)
    has_bottom = flag_ref[2].astype(F32)
    on_left, on_right = sides(flag_ref)
    edges = (act(edge_ref[...]), act(rim_ref[...]))
    for row in range(rows + 2):
        for frame in range(4):
            ref, index = at(row, frame)
            which, number = edge_lane(row, frame, rows, True)
            plane = act(ref[index])
            column = edges[which][:, number : number + 1]
            factor = None
            if frame < 2:
                factor = has_past
            if row in (0, rows + 1):
                beside = has_top if row == 0 else has_bottom
                factor = beside if factor is None else factor * beside
            if factor is not None:
                plane = plane * factor
                column = column * factor
            fill_stack(stack_ref, row, frame, plane.astype(BF16), column, on_left, on_right)
    for row in range(rows):
        out = conv_rows(stack_ref, weight, row)
        for frame in range(frames):
            hidden_ref[row, frame] = out[frame * channels : (frame + 1) * channels]
    planes = [
        functools.partial(lambda r, t: hidden_ref[r, t], r, t) for r in range(rows) for t in range(frames)
    ]
    put_rows(st_out, *local_stats(planes, float(GROUP * rows * frames * cols)))


def fill_future(stack, flag_ref, own, future, near, far, edge_ref, rim_ref):
    rows = own.shape[0]
    at = source(own, future, near, far, False)
    on_left, on_right = sides(flag_ref)
    edges = (edge_ref[...], rim_ref[...])
    for row in range(rows + 2):
        for frame in range(4):
            ref, index = at(row, frame)
            which, number = edge_lane(row, frame, rows, False)
            fill_stack(stack, row, frame, ref[index], edges[which][:, number : number + 1], on_left, on_right)


def conv_back_kernel(flag_ref, *refs):
    weight, grad_ref, stack_ref = refs[-3:]
    rows, frames, channels, _ = grad_ref.shape
    fill_future(stack_ref, flag_ref, *refs[:-3])
    for row in range(rows):
        out = conv_rows(stack_ref, weight, row)
        for frame in range(frames):
            grad_ref[row, frame] = out[frame * channels : (frame + 1) * channels]


def norm_second_kernel(hidden, grad, par_ref, st_ref, act_ref, scaled_ref, sums_ref, *, count):
    rows, frames, channels, cols = hidden.shape
    mean, inverse, gain, shift, _ = norm_columns(par_ref, st_ref, count, 3)
    first = jnp.zeros((channels, 128), F32)
    second = jnp.zeros((channels, 128), F32)
    for row in range(rows):
        for frame in range(frames):
            normed = (hidden[row, frame] - mean) * inverse
            pre = normed * gain + shift
            sig = sigmoid(pre)
            act = pre * sig
            act_ref[row, frame] = act.astype(BF16)
            scaled = grad[row, frame] * (sig + act * (1.0 - sig)) * gain
            scaled_ref[row, frame] = scaled
            first = first + lanes_of(scaled)
            second = second + lanes_of(scaled * normed)
    put_rows(sums_ref, group_sums(first), group_sums(second))


def hidden_grad_kernel(
    hidden, scaled, par_ref, st_ref, sums_ref, out_ref, down_ref, up_ref, *, count
):
    rows, frames, channels, cols = hidden.shape
    mean, inverse, _, _, _ = norm_columns(par_ref, st_ref, count, 3)
    means = sums_ref[0] / count
    first, second = columns_of(means[0:1], means[1:2])[:2]
    for row in range(rows):
        for frame in range(frames):
            normed = (hidden[row, frame] - mean) * inverse
            plane = (inverse * (scaled[row, frame] - first - normed * second)).astype(BF16)
            out_ref[row, frame] = plane
            if row == rows - 1:
                down_ref[0, frame] = plane
            if row == 0:
                up_ref[0, frame] = plane


def put_halves(flag_ref, mine_ref, theirs_ref, tap, block):
    half = block.shape[0] // 2
    here = pl.ds(tap, half, stride=SLOTS)
    upper, lower = block[:half], block[half:]
    is_first = flag_ref[3] == 0
    mine_ref[here, :] = jnp.where(is_first, upper, lower)
    theirs_ref[here, :] = jnp.where(is_first, lower, upper)


def encoded(value, digits=None):
    slot = lax.broadcasted_iota(jnp.int32, value.shape, 1)
    value = jnp.where(slot < TAPS, value, 0.0)
    top = jnp.max(jnp.abs(value), axis=1, keepdims=True)
    power = jnp.ceil(jnp.log(jnp.maximum(top, 1e-30)) * (1.0 / LN2))
    number = jnp.round(value * (FULL * jnp.exp(power * -LN2)))
    number = jnp.where(slot < TAPS, number, power)
    if digits is not None:
        first_row = lax.broadcasted_iota(jnp.int32, value.shape, 0) == 0
        for place, digit in enumerate(digits):
            number = jnp.where(first_row & (slot == TAPS + place), digit[None], number)
    return number.astype(jnp.int32).astype(jnp.int16)


def digits_of(value):
    power = jnp.ceil(jnp.log(jnp.maximum(jnp.abs(value), 1e-30)) * (1.0 / LN2))
    scaled = value * (FULL * jnp.exp(power * -LN2))
    high = jnp.round(scaled)
    return high, jnp.round((scaled - high) * LOW), power


def value_of(number):
    number = number.astype(jnp.int32).astype(F32)
    high, low, power = (number[TAPS + place : TAPS + place + 1] for place in range(3))
    return (high + low * (1.0 / LOW)) * (jnp.exp(power * LN2) * (1.0 / FULL))


def decoded_value(number):
    number = number.astype(jnp.int32).astype(F32)
    return number * (jnp.exp(number[:, SLOTS - 1 : SLOTS] * LN2) * (1.0 / FULL))


def first_scatter_kernel(flag_ref, *refs, slot):
    me = flag_ref[slot]
    for which in range(2):
        mine, other = refs[2 * which], refs[2 * which + 1]
        for k, out in enumerate(refs[4:]):
            total = other[me ^ k]
            total = mine[me ^ k] + (total if total.dtype == F32 else decoded_value(total))
            out[which] = total if k == 0 else encoded(total)


def scatter_kernel(flag_ref, sums_ref, *refs, received, sent, slot, last):
    me = flag_ref[slot]
    for which in range(2):
        digits = digits_of(sums_ref[0, which : which + 1]) if last else None
        for k, out in enumerate(refs[-sent:]):
            total = refs[0][which, me ^ k]
            for ref in refs[1:received]:
                total = total + decoded_value(ref[which, me ^ k])
            out[which] = total if k == 0 else encoded(total, digits)


def total_kernel(sums_ref, *refs, received):
    out_ref, sums_out = refs[-2:]
    for which in range(2):
        total = refs[0][which]
        terms = sums_ref[0, which : which + 1]
        for ref in refs[1:received]:
            total = total + decoded_value(ref[which])
            terms = terms + value_of(ref[which, 0])
        out_ref[which] = encoded(total)
        sums_out[0, which : which + 1] = terms


def split_kernel(flag_ref, *refs, received, slot):
    me = flag_ref[slot]
    for which in range(2):
        for k, ref in enumerate(refs[:received]):
            refs[which - 2][me ^ k] = ref[which]


def gather_kernel(flag_ref, *refs, slot):
    me = flag_ref[slot]
    for k, ref in enumerate(refs[:-1]):
        refs[-1][me ^ k] = ref[...]


def join_kernel(flag_ref, mine_ref, theirs_ref, out_ref, first_ref, second_ref):
    half, _, channels = mine_ref.shape
    is_first = flag_ref[3] == 0
    first_ref[...] = decoded_value(jnp.where(is_first, mine_ref[...], theirs_ref[...])).reshape(first_ref.shape)
    second_ref[...] = decoded_value(jnp.where(is_first, theirs_ref[...], mine_ref[...])).reshape(second_ref.shape)
    for tap in range(TAPS):
        here = slice(tap * channels, (tap + 1) * channels)
        out_ref[:half, here] = first_ref[pl.ds(tap, half, stride=SLOTS), :]
        out_ref[half:, here] = second_ref[pl.ds(tap, half, stride=SLOTS), :]


def weight_second_kernel(flag_ref, stack_ref, act_ref, mine_ref, theirs_ref, right_ref):
    rows, frames, channels, cols = act_ref.shape
    for row in range(rows):
        right_ref[row * cols : (row + 1) * cols] = jnp.transpose(
            act_ref[row].reshape(frames * channels, cols)
        )
    right = right_ref[...]
    for down in range(3):
        parts = []
        for frame in range(4):
            left = jnp.concatenate([stack_ref[down + row, frame] for row in range(rows)], axis=1)
            parts.append(jnp.dot(left, right, preferred_element_type=F32))
        for kt in range(3):
            term = parts[2 - kt][:, :channels] + parts[3 - kt][:, channels:]
            for across in range(3):
                tap = 9 * kt + 3 * (2 - down) + (2 - across)
                put_halves(flag_ref, mine_ref, theirs_ref, tap, term[across * channels : (across + 1) * channels])


def weight_first_kernel(flag_ref, stack_ref, grad_ref, mine_ref, theirs_ref, right_ref):
    rows, frames, channels, cols = grad_ref.shape
    for row in range(rows):
        right_ref[row * cols : (row + 1) * cols] = jnp.transpose(
            grad_ref[row].reshape(frames * channels, cols)
        )
    right = right_ref[...]
    for down in range(3):
        parts = []
        for frame in range(4):
            left = jnp.concatenate([stack_ref[down + row, frame] for row in range(rows)], axis=1)
            parts.append(jnp.dot(left, right, preferred_element_type=F32))
        for kt in range(3):
            term = parts[kt][:, :channels] + parts[kt + 1][:, channels:]
            for across in range(3):
                tap = 9 * kt + 3 * down + across
                block = jnp.transpose(term[across * channels : (across + 1) * channels])
                put_halves(flag_ref, mine_ref, theirs_ref, tap, block)


def first_grad_kernel(flag_ref, *refs, count):
    weight, latent, par_ref, st_ref = refs[6:10]
    scaled_ref, sums_ref, stack_ref = refs[-3:]
    rows, frames, channels, cols = latent.shape
    mean, inverse, gain, shift, scale = norm_columns(par_ref, st_ref, count, 1)
    fill_future(stack_ref, flag_ref, *refs[:6])
    first = jnp.zeros((channels, 128), F32)
    second = jnp.zeros((channels, 128), F32)
    for row in range(rows):
        out = conv_rows(stack_ref, weight, row)
        for frame in range(frames):
            grad = out[frame * channels : (frame + 1) * channels]
            normed = (latent[row, frame].astype(F32) * scale - mean) * inverse
            pre = normed * gain + shift
            sig = sigmoid(pre)
            scaled = grad * (sig + pre * sig * (1.0 - sig)) * gain
            scaled_ref[row, frame] = scaled
            first = first + lanes_of(scaled)
            second = second + lanes_of(scaled * normed)
    put_rows(sums_ref, group_sums(first), group_sums(second))


def decoded_grad_kernel(scaled, latent, cotangent, par_ref, st_ref, sums_ref, out_ref, token_ref, *, count):
    token_ref[...] = jnp.zeros(token_ref.shape, F32)
    rows, frames, channels, cols = latent.shape
    mean, inverse, _, _, scale = norm_columns(par_ref, st_ref, count, 1)
    means = sums_ref[0] / count
    first, second = columns_of(means[0:1], means[1:2])[:2]
    for row in range(rows):
        for frame in range(frames):
            normed = (latent[row, frame].astype(F32) * scale - mean) * inverse
            out_ref[:, frame, row, :] = cotangent[row, frame].astype(F32) + inverse * (
                scaled[row, frame] - first - normed * second
            )


def weight_forward_kernel(weight, out_ref):
    channels = weight.shape[0]
    wide = 3 * channels
    for t in range(2):
        for kr in range(3):
            for f in range(4):
                kt = f - t
                here = slice((kr * 4 + f) * wide, (kr * 4 + f + 1) * wide)
                if 0 <= kt < 3:
                    tap = 3 * kt + kr
                    block = weight[:, tap * wide : (tap + 1) * wide]
                else:
                    block = jnp.zeros((channels, wide), BF16)
                out_ref[t * channels : (t + 1) * channels, here] = block


def weight_back_kernel(weight, out_ref):
    channels = weight.shape[0]
    for down in range(3):
        for across in range(3):
            blocks = [
                jnp.transpose(
                    weight[
                        :,
                        (9 * kt + 3 * (2 - down) + 2 - across) * channels : (9 * kt + 3 * (2 - down) + 3 - across)
                        * channels,
                    ]
                )
                for kt in range(3)
            ]
            for t in range(2):
                for f in range(4):
                    kt = t + 2 - f
                    start = ((down * 4 + f) * 3 + across) * channels
                    block = blocks[kt] if 0 <= kt < 3 else jnp.zeros((channels, channels), BF16)
                    out_ref[t * channels : (t + 1) * channels, start : start + channels] = block


def shifted(value, axis, steps):
    count = lax.axis_size(axis)
    initial, last = max(0, -steps), min(count, count - steps)
    return lax.ppermute(value, axis, [(source, source + steps) for source in range(initial, last)])


def rounds(axes):
    for axis in axes:
        count = lax.axis_size(axis)
        step = 1
        while step < count:
            wide = 4 if 4 * step <= count else 2
            yield axis, step, [[(i, i ^ (step * k)) for i in range(count)] for k in range(1, wide)]
            step *= wide


def pairwise(parts, join):
    while len(parts) > 1:
        parts = [join(a, b) for a, b in zip(parts[::2], parts[1::2])]
    return parts[0]


def sum_kernel(*refs, parts):
    refs[-1][...] = pairwise([ref[...] for ref in refs[:parts]], lambda a, b: a + b)


def stats_kernel(*refs, parts, count):
    refs[-1][...] = pairwise([(ref[...], count) for ref in refs[:parts]], joined_stats)[0]


def all_sum(value, after=(), axes=("tm", "height", "width")):
    for axis, _, exchanges in rounds(axes):
        parts = [value] + [lax.ppermute(value, axis, pairs) for pairs in exchanges]
        if after:
            value = joined_after(functools.partial(sum_kernel, parts=len(parts)), parts, after)
        else:
            value = pairwise(parts, lambda a, b: a + b)
        after = ()
    return value


def joined_after(body, parts, after):
    (value,) = call(body, [shape(parts[0].shape, F32)], [VMEM] * (len(parts) + len(after)), (*parts, *after))
    return value


def all_stats(value, count, after=()):
    for axis, _, exchanges in rounds(("tm", "height", "width")):
        parts = [value] + [lax.ppermute(value, axis, pairs) for pairs in exchanges]
        if after:
            value = joined_after(functools.partial(stats_kernel, parts=len(parts), count=count), parts, after)
        else:
            value, _ = pairwise([(part, count) for part in parts], joined_stats)
        count, after = count * len(parts), ()
    return value


def joined_stats(first, second):
    (a, count), (b, _) = first, second
    gap = a[:, 0:1] - b[:, 0:1]
    squares = a[:, 1:2] + b[:, 1:2] + gap * gap * (0.5 * count)
    return jnp.concatenate([0.5 * (a[:, 0:1] + b[:, 0:1]), squares], axis=1), 2.0 * count


def swapped(value):
    return lax.ppermute(value, "width", [(0, 1), (1, 0)])


def weight_rounds():
    return list(rounds(("height", "tm")))


def scattered(flags, second, first):
    half, _, channels = second[0].shape
    axis, _, exchanges = weight_rounds()[0]
    parts = len(exchanges) + 1
    rows = half // parts
    terms = [part for mine, theirs in (second, first) for part in (mine, theirs)]
    part = (2, rows, SLOTS, channels)
    kept, *sent = call(
        functools.partial(first_scatter_kernel, slot=4),
        [shape(part, F32)] + [shape(part, jnp.int16)] * (parts - 1),
        [SMEM] + [VMEM] * 4,
        (flags, *[term.reshape(parts, rows, SLOTS, channels) for term in terms]),
    )
    return [kept] + [lax.ppermute(v, axis, pairs) for v, pairs in zip(sent, exchanges)], sent[0]


def summed(flags, received, sums, after):
    others = weight_rounds()[1:]
    for number, (axis, _, exchanges) in enumerate(others, 5):
        parts = len(exchanges) + 1
        _, rows, _, channels = received[0].shape
        part = (2, rows // parts, SLOTS, channels)
        views = [v.reshape(2, parts, *part[1:]) for v in received]
        last = number == len(others) + 4
        kept, *sent = call(
            functools.partial(scatter_kernel, received=len(views), sent=parts, slot=number, last=last),
            [shape(part, F32)] + [shape(part, jnp.int16)] * (parts - 1),
            [SMEM] + [VMEM] * (1 + len(views) + len(after)),
            (flags, sums, *views, *after),
        )
        after = ()
        received = [kept] + [lax.ppermute(v, axis, pairs) for v, pairs in zip(sent, exchanges)]
    return call(
        functools.partial(total_kernel, received=len(received)),
        [shape(received[0].shape, jnp.int16), shape(sums.shape, F32)],
        [VMEM] * (1 + len(received)),
        (sums, *received),
    )


def gathered(flags, total, after_last):
    _, rows, _, channels = total.shape
    back = list(enumerate(weight_rounds(), 4))[::-1]
    number, (axis, _, exchanges) = back[0]
    pieces = [total] + [lax.ppermute(total, axis, pairs) for pairs in exchanges]
    values = call(
        functools.partial(split_kernel, received=len(pieces), slot=number),
        [shape((len(pieces), rows, SLOTS, channels), jnp.int16)] * 2,
        [SMEM] + [VMEM] * (len(pieces) + 1),
        (flags, *pieces, after_last),
    )
    results = []
    for value in values:
        for number, (axis, _, exchanges) in back[1:]:
            value = value.reshape(-1, SLOTS, channels)
            pieces = [value] + [lax.ppermute(value, axis, pairs) for pairs in exchanges]
            (value,) = call(
                functools.partial(gather_kernel, slot=number),
                [shape((len(pieces), *value.shape), jnp.int16)],
                [SMEM] + [VMEM] * len(pieces),
                (flags, *pieces),
            )
        results.append(value.reshape(-1, SLOTS, channels))
    return results


def joined(flags, mine, theirs):
    half, _, channels = mine.shape
    (total,) = call(
        join_kernel,
        [shape((2 * half, TAPS * channels), F32)],
        [SMEM] + [VMEM] * 2,
        (flags, mine, theirs),
        scratch=[pltpu.VMEM((half * SLOTS, channels), F32)] * 2,
    )
    return total


def edges(flags, planes, after):
    channels = planes[0].shape[2]
    args = (*planes, *after)
    (columns,) = call(edges_kernel, [shape((channels, 128), BF16)], [SMEM] + [VMEM] * len(args), (flags, *args))
    return columns


def row_halos(down, up, after=()):
    above, below = shifted(down, "height", 1), shifted(up, "height", -1)
    return call(
        rows_kernel,
        [shape((2, *down.shape[1:]), BF16)] * down.shape[0],
        [VMEM] * (2 + len(after)),
        (above, below, *after),
    )


def with_columns(flags, own, around, after=()):
    edge = swapped(edges(flags, (own, around[0]), after))
    rim = swapped(edges(flags, around[1:], after))
    return *around, edge, rim


def shards(
    latent,
    exponents,
    cotangent,
    conv_first,
    conv_second,
    gain_first,
    shift_first,
    gain_second,
    shift_second,
):
    channels, frames, rows, cols = latent.shape
    groups = exponents.shape[0]
    devices = lax.axis_size("tm") * lax.axis_size("height") * lax.axis_size("width")
    count = float(channels // groups * frames * rows * cols * devices)
    tm, height, width = (lax.axis_index(axis) for axis in ("tm", "height", "width"))
    flags = jnp.stack(
        [
            (tm > 0).astype(jnp.int32),
            (height > 0).astype(jnp.int32),
            (height < lax.axis_size("height") - 1).astype(jnp.int32),
            width.astype(jnp.int32),
        ]
        + [
            (lax.axis_index(axis) // step % (len(exchanges) + 1)).astype(jnp.int32)
            for axis, step, exchanges in weight_rounds()
        ]
    )
    scale = jnp.repeat(jnp.exp2(exponents.astype(F32)), channels // groups)
    zeros = jnp.zeros_like(scale)
    par = jnp.stack([scale, gain_first, shift_first, gain_second, shift_second, zeros, zeros, zeros])
    block = (rows, frames, channels, cols)
    stack = (rows + 2, 4, 3 * channels, cols)
    taps = (2 * channels, 36 * channels)
    halves = [shape((channels // 2 * SLOTS, channels), F32)] * 2
    conv_flops = 3 * 2 * 4 * 256 * 36 * channels * 2 * channels
    small = shape((1, 2, channels), F32)

    message = shape((2, frames, channels, cols), BF16)
    latent, cotangent, down, up, stats_first = call(
        planes_kernel,
        [shape(block, BF16), shape(block, BF16), message, message, small],
        [VMEM] * 3,
        (latent, cotangent, par),
    )
    near, near_c = row_halos(down, up)
    around = with_columns(flags, latent, (shifted(latent, "tm", 1), near, shifted(near, "tm", 1)))
    around_c = (shifted(cotangent, "tm", -1), near_c, shifted(near_c, "tm", -1))
    stats_first = all_stats(stats_first, count / devices)
    (weight_first,) = call(weight_forward_kernel, [shape(taps, BF16)], [VMEM], (conv_first,))
    (weight_second_t,) = call(weight_back_kernel, [shape(taps, BF16)], [VMEM], (conv_second,))
    (weight_first_t,) = call(weight_back_kernel, [shape(taps, BF16)], [VMEM], (conv_first,))

    hidden, stats_second, stack_first = call(
        functools.partial(conv_first_kernel, count=count),
        [shape(block, F32), small, shape(stack, BF16)],
        [SMEM] + [VMEM] * 10,
        (flags, latent, *around, par, stats_first, weight_first, around_c[2]),
        flops=conv_flops,
        transcendentals=3 * latent.size,
    )
    around_c = with_columns(flags, cotangent, around_c, (stats_second,))
    grad_second, stack_c = call(
        conv_back_kernel,
        [shape(block, F32), shape(stack, BF16)],
        [SMEM] + [VMEM] * 7,
        (flags, cotangent, *around_c, weight_second_t),
        flops=conv_flops,
    )
    stats_second = all_stats(stats_second, count / devices, (grad_second,))
    act_second, scaled, sums = call(
        functools.partial(norm_second_kernel, count=count),
        [shape(block, BF16), shape(block, F32), small],
        [VMEM] * 4,
        (hidden, grad_second, par, stats_second),
        transcendentals=latent.size,
    )
    halves_second = call(
        weight_second_kernel,
        halves,
        [SMEM] + [VMEM] * 2,
        (flags, stack_c, act_second),
        scratch=[pltpu.VMEM((rows * cols, frames * channels), BF16)],
        flops=conv_flops,
    )
    sums = all_sum(sums, (halves_second[0],))
    message = shape((1, frames, channels, cols), BF16)
    hidden_grad, down, up = call(
        functools.partial(hidden_grad_kernel, count=count),
        [shape(block, BF16), message, message],
        [VMEM] * 5,
        (hidden, scaled, par, stats_second, sums),
    )
    future = shifted(hidden_grad, "tm", -1)
    halves_first = call(
        weight_first_kernel,
        halves,
        [SMEM] + [VMEM] * 2,
        (flags, stack_first, hidden_grad),
        scratch=[pltpu.VMEM((rows * cols, frames * channels), BF16)],
        flops=conv_flops,
    )
    halves_second, halves_first = (
        [v.reshape(channels // 2, SLOTS, channels) for v in halves] for halves in (halves_second, halves_first)
    )
    near, term = call(
        rows_and_term_kernel,
        [shape((2, frames, channels, cols), BF16), shape(halves_first[1].shape, jnp.int16)],
        [VMEM] * 4,
        (shifted(down, "height", 1), shifted(up, "height", -1), future, halves_first[1]),
    )
    around = (future, near, shifted(near, "tm", -1))
    halves_second = halves_second[0], swapped(halves_second[1])
    halves_first = halves_first[0], swapped(term)
    weights, sent = scattered(flags, halves_second, halves_first)
    around = with_columns(flags, hidden_grad, around, (sent,))
    scaled, sums_first = call(
        functools.partial(first_grad_kernel, count=count),
        [shape(block, F32), small],
        [SMEM] + [VMEM] * (9 + len(weights)),
        (flags, hidden_grad, *around, weight_first_t, latent, par, stats_first, *weights[1:]),
        scratch=[pltpu.VMEM(stack, BF16)],
        flops=conv_flops,
        transcendentals=latent.size,
    )
    total, sums_first = summed(flags, weights, sums_first, around[:2])
    sums_first = all_sum(sums_first, axes=("height", "width"))
    decoded_grad, token = call(
        functools.partial(decoded_grad_kernel, count=count),
        [shape((channels, frames, rows, cols), F32), shape((8, 128), F32)],
        [VMEM] * 6,
        (scaled, latent, cotangent, par, stats_first, sums_first),
    )
    second, first = gathered(flags, total, token)
    conv_second_grad = joined(flags, second, swapped(second))
    conv_first_grad = joined(flags, first, swapped(first))
    return decoded_grad, conv_first_grad, conv_second_grad


def solution(mesh):
    block = P(None, "tm", "height", "width")
    return jax.shard_map(
        shards,
        mesh=mesh,
        in_specs=(block, P(), block, P(), P(), P(), P(), P(), P()),
        out_specs=(block, P(), P()),
        check_vma=False,
    )
```

```python
import functools

import jax
import jax.numpy as jnp
from jax import lax
from jax.experimental import pallas as pl
from jax.experimental.pallas import tpu as pltpu
from jax.sharding import PartitionSpec as P

epsilon = 1e-05
F32 = jnp.float32
BF16 = jnp.bfloat16
GROUP = 4
TAPS, SLOTS = 27, 32
FULL, LOW = 32760.0, 65000.0
LN2 = 0.6931471805599453
VMEM = pl.BlockSpec(memory_space=pltpu.VMEM)
SMEM = pl.BlockSpec(memory_space=pltpu.SMEM)


def call(body, outs, specs, args, scratch=(), flops=0, transcendentals=0, limit=20):
    moved = sum(a.size * a.dtype.itemsize for a in args)
    moved += sum(o.size * o.dtype.itemsize for o in outs)
    return pl.pallas_call(
        body,
        out_shape=tuple(outs),
        in_specs=specs,
        out_specs=tuple(VMEM for _ in outs),
        scratch_shapes=scratch,
        compiler_params=pltpu.CompilerParams(vmem_limit_bytes=limit << 20),
        cost_estimate=pl.CostEstimate(
            flops=flops, bytes_accessed=moved, transcendentals=transcendentals
        ),
    )(*args)


def shape(dims, dtype):
    return jax.ShapeDtypeStruct(dims, dtype)


def group_sums(acc):
    rows = acc.shape[0]
    row = lax.broadcasted_iota(jnp.int32, acc.shape, 0)
    step = 1
    while step < GROUP:
        up = pltpu.roll(acc, rows - step, axis=0)
        down = pltpu.roll(acc, step, axis=0)
        acc = acc + jnp.where((row & step) == 0, up, down)
        step *= 2
    return jnp.sum(acc, axis=1, keepdims=True)


def lanes_of(plane):
    total = plane[:, :128]
    for start in range(128, plane.shape[1], 128):
        total = total + plane[:, start : start + 128]
    return total


def as_rows(first, second):
    channels = first.shape[0]
    lane = lax.broadcasted_iota(jnp.int32, (channels, 128), 1)
    both = jnp.where(lane == 0, first, jnp.where(lane == 1, second, 0.0))
    return jnp.transpose(both)[:2]


def local_stats(planes, count):
    acc = None
    for plane in planes:
        part = lanes_of(plane())
        acc = part if acc is None else acc + part
    mean = group_sums(acc) / count
    acc = None
    for plane in planes:
        off = plane() - mean
        part = lanes_of(off * off)
        acc = part if acc is None else acc + part
    return mean, group_sums(acc)


def put_rows(out_ref, first, second):
    out_ref[0] = as_rows(first, second)


def combined(st_ref, count):
    return st_ref[0, 0:1], st_ref[0, 1:2] / count


def columns_of(*rows):
    rows = list(rows) + [jnp.zeros_like(rows[0])] * (8 - len(rows))
    cols = jnp.transpose(jnp.concatenate(rows, axis=0))
    return [cols[:, i : i + 1] for i in range(8)]


def sigmoid(value):
    return 0.5 + 0.5 * jnp.tanh(0.5 * value)


def planes_kernel(latent_ref, cotangent_ref, par_ref, latent_out, cotangent_out, down_ref, up_ref, st_ref):
    _, frames, rows, cols = latent_ref.shape
    for which, (natural, out) in enumerate(((latent_ref, latent_out), (cotangent_ref, cotangent_out))):
        for row in range(rows):
            for frame in range(frames):
                plane = natural[:, frame, row, :]
                out[row, frame] = plane
                if row == rows - 1:
                    down_ref[which, frame] = plane
                if row == 0:
                    up_ref[which, frame] = plane
    scale = columns_of(par_ref[0:1])[0]
    planes = [
        functools.partial(lambda r, t: latent_out[r, t].astype(F32) * scale, r, t)
        for r in range(rows)
        for t in range(frames)
    ]
    put_rows(st_ref, *local_stats(planes, float(GROUP * rows * frames * cols)))


def rows_kernel(above_ref, below_ref, *refs):
    for which, out in enumerate(refs[-above_ref.shape[0] :]):
        out[0] = above_ref[which]
        out[1] = below_ref[which]


def rows_and_term_kernel(above_ref, below_ref, after, theirs_ref, near_ref, term_ref):
    near_ref[0] = above_ref[0]
    near_ref[1] = below_ref[0]
    term_ref[...] = encoded(theirs_ref[...])


def source(own, other, near, far, other_first):
    def at(row, frame):
        is_other = (frame < 2) == other_first
        if row == 0 or row == own.shape[0] + 1:
            return (far if is_other else near), (0 if row == 0 else 1, frame % 2)
        return (other if is_other else own), (row - 1, frame % 2)

    return at


def edges_kernel(flag_ref, first_ref, second_ref, *refs):
    planes, out_ref = (first_ref, second_ref), refs[-1]
    is_first = flag_ref[3] == 0
    channels = planes[0].shape[2]
    lane = lax.broadcasted_iota(jnp.int32, (channels, 128), 1)
    start = pl.multiple_of(jnp.where(is_first, first_ref.shape[3] - 128, 0), 128)
    acc = jnp.zeros((channels, 128), F32)
    number = 0
    for ref in planes:
        for row in range(ref.shape[0]):
            for frame in range(ref.shape[1]):
                half = ref[row, frame, :, pl.ds(start, 128)].astype(F32)
                moved = pltpu.roll(half, number + is_first.astype(jnp.int32), axis=1)
                acc = jnp.where(lane == number, moved, acc)
                number += 1
    out_ref[...] = acc.astype(BF16)


def edge_lane(row, frame, rows, other_first):
    is_other = int((frame < 2) == other_first)
    if row == 0 or row == rows + 1:
        return 1, 4 * is_other + 2 * int(row > 0) + frame % 2
    return 0, 2 * rows * is_other + 2 * (row - 1) + frame % 2


def fill_stack(stack, row, frame, plane, column, on_left, on_right):
    channels, cols = plane.shape
    lane = lax.broadcasted_iota(jnp.int32, (channels, cols), 1)
    column = column.astype(F32)
    left = jnp.where(lane == 0, (column * on_left).astype(BF16), pltpu.roll(plane, 1, axis=1))
    right = jnp.where(lane == cols - 1, (column * on_right).astype(BF16), pltpu.roll(plane, cols - 1, axis=1))
    stack[row, frame, 0:channels] = left
    stack[row, frame, channels : 2 * channels] = plane
    stack[row, frame, 2 * channels : 3 * channels] = right


def sides(flag_ref):
    on_left = (flag_ref[3] != 0).astype(F32)
    on_right = (flag_ref[3] == 0).astype(F32)
    return on_left, on_right


def conv_rows(stack, weight, row):
    three = stack[row : row + 3].reshape(weight.shape[1], stack.shape[3])
    return jnp.dot(weight[...], three, preferred_element_type=F32)


def norm_columns(par_ref, st_ref, count, gain_row):
    par = par_ref[...]
    mean, variance = combined(st_ref, count)
    inverse = 1.0 / jnp.sqrt(variance + epsilon)
    gain = par[gain_row : gain_row + 1]
    shift = par[gain_row + 1 : gain_row + 2]
    return columns_of(mean, inverse, gain, shift, par[0:1])[:5]


def conv_first_kernel(
    flag_ref, own, past, near, far, edge_ref, rim_ref, par_ref, st_ref, weight, after, hidden_ref, st_out, stack_ref,
    *, count
):
    rows, frames, channels, cols = own.shape
    at = source(own, past, near, far, True)
    mean, inverse, gain, shift, scale = norm_columns(par_ref, st_ref, count, 1)

    def act(latent):
        pre = (latent.astype(F32) * scale - mean) * inverse * gain + shift
        return pre * sigmoid(pre)

    has_past = flag_ref[0].astype(F32)
    has_top = flag_ref[1].astype(F32)
    has_bottom = flag_ref[2].astype(F32)
    on_left, on_right = sides(flag_ref)
    edges = (act(edge_ref[...]), act(rim_ref[...]))
    for row in range(rows + 2):
        for frame in range(4):
            ref, index = at(row, frame)
            which, number = edge_lane(row, frame, rows, True)
            plane = act(ref[index])
            column = edges[which][:, number : number + 1]
            factor = None
            if frame < 2:
                factor = has_past
            if row in (0, rows + 1):
                beside = has_top if row == 0 else has_bottom
                factor = beside if factor is None else factor * beside
            if factor is not None:
                plane = plane * factor
                column = column * factor
            fill_stack(stack_ref, row, frame, plane.astype(BF16), column, on_left, on_right)
    for row in range(rows):
        out = conv_rows(stack_ref, weight, row)
        for frame in range(frames):
            hidden_ref[row, frame] = out[frame * channels : (frame + 1) * channels]
    planes = [
        functools.partial(lambda r, t: hidden_ref[r, t], r, t) for r in range(rows) for t in range(frames)
    ]
    put_rows(st_out, *local_stats(planes, float(GROUP * rows * frames * cols)))


def fill_future(stack, flag_ref, own, future, near, far, edge_ref, rim_ref):
    rows = own.shape[0]
    at = source(own, future, near, far, False)
    on_left, on_right = sides(flag_ref)
    edges = (edge_ref[...], rim_ref[...])
    for row in range(rows + 2):
        for frame in range(4):
            ref, index = at(row, frame)
            which, number = edge_lane(row, frame, rows, False)
            fill_stack(stack, row, frame, ref[index], edges[which][:, number : number + 1], on_left, on_right)


def conv_back_kernel(flag_ref, *refs):
    weight, grad_ref, stack_ref = refs[-3:]
    rows, frames, channels, _ = grad_ref.shape
    fill_future(stack_ref, flag_ref, *refs[:-3])
    for row in range(rows):
        out = conv_rows(stack_ref, weight, row)
        for frame in range(frames):
            grad_ref[row, frame] = out[frame * channels : (frame + 1) * channels]


def norm_second_kernel(hidden, grad, par_ref, st_ref, act_ref, scaled_ref, sums_ref, *, count):
    rows, frames, channels, cols = hidden.shape
    mean, inverse, gain, shift, _ = norm_columns(par_ref, st_ref, count, 3)
    first = jnp.zeros((channels, 128), F32)
    second = jnp.zeros((channels, 128), F32)
    for row in range(rows):
        for frame in range(frames):
            normed = (hidden[row, frame] - mean) * inverse
            pre = normed * gain + shift
            sig = sigmoid(pre)
            act = pre * sig
            act_ref[row, frame] = act.astype(BF16)
            scaled = grad[row, frame] * (sig + act * (1.0 - sig)) * gain
            scaled_ref[row, frame] = scaled
            first = first + lanes_of(scaled)
            second = second + lanes_of(scaled * normed)
    put_rows(sums_ref, group_sums(first), group_sums(second))


def hidden_grad_kernel(
    hidden, scaled, par_ref, st_ref, sums_ref, out_ref, down_ref, up_ref, *, count
):
    rows, frames, channels, cols = hidden.shape
    mean, inverse, _, _, _ = norm_columns(par_ref, st_ref, count, 3)
    means = sums_ref[0] / count
    first, second = columns_of(means[0:1], means[1:2])[:2]
    for row in range(rows):
        for frame in range(frames):
            normed = (hidden[row, frame] - mean) * inverse
            plane = (inverse * (scaled[row, frame] - first - normed * second)).astype(BF16)
            out_ref[row, frame] = plane
            if row == rows - 1:
                down_ref[0, frame] = plane
            if row == 0:
                up_ref[0, frame] = plane


def put_halves(flag_ref, mine_ref, theirs_ref, tap, block):
    half = block.shape[0] // 2
    here = pl.ds(tap, half, stride=SLOTS)
    upper, lower = block[:half], block[half:]
    is_first = flag_ref[3] == 0
    mine_ref[here, :] = jnp.where(is_first, upper, lower)
    theirs_ref[here, :] = jnp.where(is_first, lower, upper)


def encoded(value, digits=None):
    slot = lax.broadcasted_iota(jnp.int32, value.shape, 1)
    value = jnp.where(slot < TAPS, value, 0.0)
    top = jnp.max(jnp.abs(value), axis=1, keepdims=True)
    power = jnp.ceil(jnp.log(jnp.maximum(top, 1e-30)) * (1.0 / LN2))
    number = jnp.round(value * (FULL * jnp.exp(power * -LN2)))
    number = jnp.where(slot < TAPS, number, power)
    if digits is not None:
        first_row = lax.broadcasted_iota(jnp.int32, value.shape, 0) == 0
        for place, digit in enumerate(digits):
            number = jnp.where(first_row & (slot == TAPS + place), digit[None], number)
    return number.astype(jnp.int32).astype(jnp.int16)


def digits_of(value):
    power = jnp.ceil(jnp.log(jnp.maximum(jnp.abs(value), 1e-30)) * (1.0 / LN2))
    scaled = value * (FULL * jnp.exp(power * -LN2))
    high = jnp.round(scaled)
    return high, jnp.round((scaled - high) * LOW), power


def value_of(number):
    number = number.astype(jnp.int32).astype(F32)
    high, low, power = (number[TAPS + place : TAPS + place + 1] for place in range(3))
    return (high + low * (1.0 / LOW)) * (jnp.exp(power * LN2) * (1.0 / FULL))


def decoded_value(number):
    number = number.astype(jnp.int32).astype(F32)
    return number * (jnp.exp(number[:, SLOTS - 1 : SLOTS] * LN2) * (1.0 / FULL))


def first_scatter_kernel(flag_ref, *refs, slot):
    me = flag_ref[slot]
    for which in range(2):
        mine, other = refs[2 * which], refs[2 * which + 1]
        for k, out in enumerate(refs[4:]):
            total = other[me ^ k]
            total = mine[me ^ k] + (total if total.dtype == F32 else decoded_value(total))
            out[which] = total if k == 0 else encoded(total)


def scatter_kernel(flag_ref, sums_ref, *refs, received, sent, slot, last):
    me = flag_ref[slot]
    for which in range(2):
        digits = digits_of(sums_ref[0, which : which + 1]) if last else None
        for k, out in enumerate(refs[-sent:]):
            total = refs[0][which, me ^ k]
            for ref in refs[1:received]:
                total = total + decoded_value(ref[which, me ^ k])
            out[which] = total if k == 0 else encoded(total, digits)


def total_kernel(sums_ref, *refs, received):
    out_ref, sums_out = refs[-2:]
    for which in range(2):
        total = refs[0][which]
        terms = sums_ref[0, which : which + 1]
        for ref in refs[1:received]:
            total = total + decoded_value(ref[which])
            terms = terms + value_of(ref[which, 0])
        out_ref[which] = encoded(total)
        sums_out[0, which : which + 1] = terms


def split_kernel(flag_ref, *refs, received, slot):
    me = flag_ref[slot]
    for which in range(2):
        for k, ref in enumerate(refs[:received]):
            refs[which - 2][me ^ k] = ref[which]


def gather_kernel(flag_ref, *refs, slot):
    me = flag_ref[slot]
    for k, ref in enumerate(refs[:-1]):
        refs[-1][me ^ k] = ref[...]


def join_kernel(flag_ref, mine_ref, theirs_ref, out_ref, first_ref, second_ref):
    half, _, channels = mine_ref.shape
    is_first = flag_ref[3] == 0
    first_ref[...] = decoded_value(jnp.where(is_first, mine_ref[...], theirs_ref[...])).reshape(first_ref.shape)
    second_ref[...] = decoded_value(jnp.where(is_first, theirs_ref[...], mine_ref[...])).reshape(second_ref.shape)
    for tap in range(TAPS):
        here = slice(tap * channels, (tap + 1) * channels)
        out_ref[:half, here] = first_ref[pl.ds(tap, half, stride=SLOTS), :]
        out_ref[half:, here] = second_ref[pl.ds(tap, half, stride=SLOTS), :]


def weight_second_kernel(flag_ref, stack_ref, act_ref, mine_ref, theirs_ref, right_ref):
    rows, frames, channels, cols = act_ref.shape
    for row in range(rows):
        right_ref[row * cols : (row + 1) * cols] = jnp.transpose(
            act_ref[row].reshape(frames * channels, cols)
        )
    right = right_ref[...]
    for down in range(3):
        parts = []
        for frame in range(4):
            left = jnp.concatenate([stack_ref[down + row, frame] for row in range(rows)], axis=1)
            parts.append(jnp.dot(left, right, preferred_element_type=F32))
        for kt in range(3):
            term = parts[2 - kt][:, :channels] + parts[3 - kt][:, channels:]
            for across in range(3):
                tap = 9 * kt + 3 * (2 - down) + (2 - across)
                put_halves(flag_ref, mine_ref, theirs_ref, tap, term[across * channels : (across + 1) * channels])


def weight_first_kernel(flag_ref, stack_ref, grad_ref, mine_ref, theirs_ref, right_ref):
    rows, frames, channels, cols = grad_ref.shape
    for row in range(rows):
        right_ref[row * cols : (row + 1) * cols] = jnp.transpose(
            grad_ref[row].reshape(frames * channels, cols)
        )
    right = right_ref[...]
    for down in range(3):
        parts = []
        for frame in range(4):
            left = jnp.concatenate([stack_ref[down + row, frame] for row in range(rows)], axis=1)
            parts.append(jnp.dot(left, right, preferred_element_type=F32))
        for kt in range(3):
            term = parts[kt][:, :channels] + parts[kt + 1][:, channels:]
            for across in range(3):
                tap = 9 * kt + 3 * down + across
                block = jnp.transpose(term[across * channels : (across + 1) * channels])
                put_halves(flag_ref, mine_ref, theirs_ref, tap, block)


def first_grad_kernel(flag_ref, *refs, count):
    weight, latent, par_ref, st_ref = refs[6:10]
    scaled_ref, sums_ref, stack_ref = refs[-3:]
    rows, frames, channels, cols = latent.shape
    mean, inverse, gain, shift, scale = norm_columns(par_ref, st_ref, count, 1)
    fill_future(stack_ref, flag_ref, *refs[:6])
    first = jnp.zeros((channels, 128), F32)
    second = jnp.zeros((channels, 128), F32)
    for row in range(rows):
        out = conv_rows(stack_ref, weight, row)
        for frame in range(frames):
            grad = out[frame * channels : (frame + 1) * channels]
            normed = (latent[row, frame].astype(F32) * scale - mean) * inverse
            pre = normed * gain + shift
            sig = sigmoid(pre)
            scaled = grad * (sig + pre * sig * (1.0 - sig)) * gain
            scaled_ref[row, frame] = scaled
            first = first + lanes_of(scaled)
            second = second + lanes_of(scaled * normed)
    put_rows(sums_ref, group_sums(first), group_sums(second))


def decoded_grad_kernel(scaled, latent, cotangent, par_ref, st_ref, sums_ref, out_ref, token_ref, *, count):
    token_ref[...] = jnp.zeros(token_ref.shape, F32)
    rows, frames, channels, cols = latent.shape
    mean, inverse, _, _, scale = norm_columns(par_ref, st_ref, count, 1)
    means = sums_ref[0] / count
    first, second = columns_of(means[0:1], means[1:2])[:2]
    for row in range(rows):
        for frame in range(frames):
            normed = (latent[row, frame].astype(F32) * scale - mean) * inverse
            out_ref[:, frame, row, :] = cotangent[row, frame].astype(F32) + inverse * (
                scaled[row, frame] - first - normed * second
            )


def weight_forward_kernel(weight, out_ref):
    channels = weight.shape[0]
    wide = 3 * channels
    for t in range(2):
        for kr in range(3):
            for f in range(4):
                kt = f - t
                here = slice((kr * 4 + f) * wide, (kr * 4 + f + 1) * wide)
                if 0 <= kt < 3:
                    tap = 3 * kt + kr
                    block = weight[:, tap * wide : (tap + 1) * wide]
                else:
                    block = jnp.zeros((channels, wide), BF16)
                out_ref[t * channels : (t + 1) * channels, here] = block


def weight_back_kernel(weight, out_ref):
    channels = weight.shape[0]
    for down in range(3):
        for across in range(3):
            blocks = [
                jnp.transpose(
                    weight[
                        :,
                        (9 * kt + 3 * (2 - down) + 2 - across) * channels : (9 * kt + 3 * (2 - down) + 3 - across)
                        * channels,
                    ]
                )
                for kt in range(3)
            ]
            for t in range(2):
                for f in range(4):
                    kt = t + 2 - f
                    start = ((down * 4 + f) * 3 + across) * channels
                    block = blocks[kt] if 0 <= kt < 3 else jnp.zeros((channels, channels), BF16)
                    out_ref[t * channels : (t + 1) * channels, start : start + channels] = block


def shifted(value, axis, steps):
    count = lax.axis_size(axis)
    initial, last = max(0, -steps), min(count, count - steps)
    return lax.ppermute(value, axis, [(source, source + steps) for source in range(initial, last)])


def rounds(axes):
    for axis in axes:
        count = lax.axis_size(axis)
        step = 1
        while step < count:
            wide = 4 if 4 * step <= count else 2
            yield axis, step, [[(i, i ^ (step * k)) for i in range(count)] for k in range(1, wide)]
            step *= wide


def pairwise(parts, join):
    while len(parts) > 1:
        parts = [join(a, b) for a, b in zip(parts[::2], parts[1::2])]
    return parts[0]


def sum_kernel(*refs, parts):
    refs[-1][...] = pairwise([ref[...] for ref in refs[:parts]], lambda a, b: a + b)


def stats_kernel(*refs, parts, count):
    refs[-1][...] = pairwise([(ref[...], count) for ref in refs[:parts]], joined_stats)[0]


def all_sum(value, after=(), axes=("tm", "height", "width")):
    for axis, _, exchanges in rounds(axes):
        parts = [value] + [lax.ppermute(value, axis, pairs) for pairs in exchanges]
        if after:
            value = joined_after(functools.partial(sum_kernel, parts=len(parts)), parts, after)
        else:
            value = pairwise(parts, lambda a, b: a + b)
        after = ()
    return value


def joined_after(body, parts, after):
    (value,) = call(body, [shape(parts[0].shape, F32)], [VMEM] * (len(parts) + len(after)), (*parts, *after))
    return value


def all_stats(value, count, after=()):
    for axis, _, exchanges in rounds(("tm", "height", "width")):
        parts = [value] + [lax.ppermute(value, axis, pairs) for pairs in exchanges]
        if after:
            value = joined_after(functools.partial(stats_kernel, parts=len(parts), count=count), parts, after)
        else:
            value, _ = pairwise([(part, count) for part in parts], joined_stats)
        count, after = count * len(parts), ()
    return value


def joined_stats(first, second):
    (a, count), (b, _) = first, second
    gap = a[:, 0:1] - b[:, 0:1]
    squares = a[:, 1:2] + b[:, 1:2] + gap * gap * (0.5 * count)
    return jnp.concatenate([0.5 * (a[:, 0:1] + b[:, 0:1]), squares], axis=1), 2.0 * count


def swapped(value):
    return lax.ppermute(value, "width", [(0, 1), (1, 0)])


def weight_rounds():
    return list(rounds(("height", "tm")))


def scattered(flags, second, first):
    half, _, channels = second[0].shape
    axis, _, exchanges = weight_rounds()[0]
    parts = len(exchanges) + 1
    rows = half // parts
    terms = [part for mine, theirs in (second, first) for part in (mine, theirs)]
    part = (2, rows, SLOTS, channels)
    kept, *sent = call(
        functools.partial(first_scatter_kernel, slot=4),
        [shape(part, F32)] + [shape(part, jnp.int16)] * (parts - 1),
        [SMEM] + [VMEM] * 4,
        (flags, *[term.reshape(parts, rows, SLOTS, channels) for term in terms]),
    )
    return [kept] + [lax.ppermute(v, axis, pairs) for v, pairs in zip(sent, exchanges)], sent[0]


def summed(flags, received, sums, after):
    others = weight_rounds()[1:]
    for number, (axis, _, exchanges) in enumerate(others, 5):
        parts = len(exchanges) + 1
        _, rows, _, channels = received[0].shape
        part = (2, rows // parts, SLOTS, channels)
        views = [v.reshape(2, parts, *part[1:]) for v in received]
        last = number == len(others) + 4
        kept, *sent = call(
            functools.partial(scatter_kernel, received=len(views), sent=parts, slot=number, last=last),
            [shape(part, F32)] + [shape(part, jnp.int16)] * (parts - 1),
            [SMEM] + [VMEM] * (1 + len(views) + len(after)),
            (flags, sums, *views, *after),
        )
        after = ()
        received = [kept] + [lax.ppermute(v, axis, pairs) for v, pairs in zip(sent, exchanges)]
    return call(
        functools.partial(total_kernel, received=len(received)),
        [shape(received[0].shape, jnp.int16), shape(sums.shape, F32)],
        [VMEM] * (1 + len(received)),
        (sums, *received),
    )


def gathered(flags, total, after_last):
    _, rows, _, channels = total.shape
    back = list(enumerate(weight_rounds(), 4))[::-1]
    number, (axis, _, exchanges) = back[0]
    pieces = [total] + [lax.ppermute(total, axis, pairs) for pairs in exchanges]
    values = call(
        functools.partial(split_kernel, received=len(pieces), slot=number),
        [shape((len(pieces), rows, SLOTS, channels), jnp.int16)] * 2,
        [SMEM] + [VMEM] * (len(pieces) + 1),
        (flags, *pieces, after_last),
    )
    results = []
    for value in values:
        for number, (axis, _, exchanges) in back[1:]:
            value = value.reshape(-1, SLOTS, channels)
            pieces = [value] + [lax.ppermute(value, axis, pairs) for pairs in exchanges]
            (value,) = call(
                functools.partial(gather_kernel, slot=number),
                [shape((len(pieces), *value.shape), jnp.int16)],
                [SMEM] + [VMEM] * len(pieces),
                (flags, *pieces),
            )
        results.append(value.reshape(-1, SLOTS, channels))
    return results


def joined(flags, mine, theirs):
    half, _, channels = mine.shape
    (total,) = call(
        join_kernel,
        [shape((2 * half, TAPS * channels), F32)],
        [SMEM] + [VMEM] * 2,
        (flags, mine, theirs),
        scratch=[pltpu.VMEM((half * SLOTS, channels), F32)] * 2,
    )
    return total


def edges(flags, planes, after):
    channels = planes[0].shape[2]
    args = (*planes, *after)
    (columns,) = call(edges_kernel, [shape((channels, 128), BF16)], [SMEM] + [VMEM] * len(args), (flags, *args))
    return columns


def row_halos(down, up, after=()):
    above, below = shifted(down, "height", 1), shifted(up, "height", -1)
    return call(
        rows_kernel,
        [shape((2, *down.shape[1:]), BF16)] * down.shape[0],
        [VMEM] * (2 + len(after)),
        (above, below, *after),
    )


def with_columns(flags, own, around, after=()):
    edge = swapped(edges(flags, (own, around[0]), after))
    rim = swapped(edges(flags, around[1:], after))
    return *around, edge, rim


def shards(
    latent,
    exponents,
    cotangent,
    conv_first,
    conv_second,
    gain_first,
    shift_first,
    gain_second,
    shift_second,
):
    channels, frames, rows, cols = latent.shape
    groups = exponents.shape[0]
    devices = lax.axis_size("tm") * lax.axis_size("height") * lax.axis_size("width")
    count = float(channels // groups * frames * rows * cols * devices)
    tm, height, width = (lax.axis_index(axis) for axis in ("tm", "height", "width"))
    flags = jnp.stack(
        [
            (tm > 0).astype(jnp.int32),
            (height > 0).astype(jnp.int32),
            (height < lax.axis_size("height") - 1).astype(jnp.int32),
            width.astype(jnp.int32),
        ]
        + [
            (lax.axis_index(axis) // step % (len(exchanges) + 1)).astype(jnp.int32)
            for axis, step, exchanges in weight_rounds()
        ]
    )
    scale = jnp.repeat(jnp.exp2(exponents.astype(F32)), channels // groups)
    zeros = jnp.zeros_like(scale)
    par = jnp.stack([scale, gain_first, shift_first, gain_second, shift_second, zeros, zeros, zeros])
    block = (rows, frames, channels, cols)
    stack = (rows + 2, 4, 3 * channels, cols)
    taps = (2 * channels, 36 * channels)
    halves = [shape((channels // 2 * SLOTS, channels), F32)] * 2
    conv_flops = 3 * 2 * 4 * 256 * 36 * channels * 2 * channels
    small = shape((1, 2, channels), F32)

    message = shape((2, frames, channels, cols), BF16)
    latent, cotangent, down, up, stats_first = call(
        planes_kernel,
        [shape(block, BF16), shape(block, BF16), message, message, small],
        [VMEM] * 3,
        (latent, cotangent, par),
    )
    near, near_c = row_halos(down, up)
    around = with_columns(flags, latent, (shifted(latent, "tm", 1), near, shifted(near, "tm", 1)))
    around_c = (shifted(cotangent, "tm", -1), near_c, shifted(near_c, "tm", -1))
    stats_first = all_stats(stats_first, count / devices)
    (weight_first,) = call(weight_forward_kernel, [shape(taps, BF16)], [VMEM], (conv_first,))
    (weight_second_t,) = call(weight_back_kernel, [shape(taps, BF16)], [VMEM], (conv_second,))
    (weight_first_t,) = call(weight_back_kernel, [shape(taps, BF16)], [VMEM], (conv_first,))

    hidden, stats_second, stack_first = call(
        functools.partial(conv_first_kernel, count=count),
        [shape(block, F32), small, shape(stack, BF16)],
        [SMEM] + [VMEM] * 10,
        (flags, latent, *around, par, stats_first, weight_first, around_c[2]),
        flops=conv_flops,
        transcendentals=3 * latent.size,
    )
    around_c = with_columns(flags, cotangent, around_c, (stats_second,))
    grad_second, stack_c = call(
        conv_back_kernel,
        [shape(block, F32), shape(stack, BF16)],
        [SMEM] + [VMEM] * 7,
        (flags, cotangent, *around_c, weight_second_t),
        flops=conv_flops,
    )
    stats_second = all_stats(stats_second, count / devices, (grad_second,))
    act_second, scaled, sums = call(
        functools.partial(norm_second_kernel, count=count),
        [shape(block, BF16), shape(block, F32), small],
        [VMEM] * 4,
        (hidden, grad_second, par, stats_second),
        transcendentals=latent.size,
    )
    halves_second = call(
        weight_second_kernel,
        halves,
        [SMEM] + [VMEM] * 2,
        (flags, stack_c, act_second),
        scratch=[pltpu.VMEM((rows * cols, frames * channels), BF16)],
        flops=conv_flops,
    )
    sums = all_sum(sums, (halves_second[0],))
    message = shape((1, frames, channels, cols), BF16)
    hidden_grad, down, up = call(
        functools.partial(hidden_grad_kernel, count=count),
        [shape(block, BF16), message, message],
        [VMEM] * 5,
        (hidden, scaled, par, stats_second, sums),
    )
    future = shifted(hidden_grad, "tm", -1)
    halves_first = call(
        weight_first_kernel,
        halves,
        [SMEM] + [VMEM] * 2,
        (flags, stack_first, hidden_grad),
        scratch=[pltpu.VMEM((rows * cols, frames * channels), BF16)],
        flops=conv_flops,
    )
    halves_second, halves_first = (
        [v.reshape(channels // 2, SLOTS, channels) for v in halves] for halves in (halves_second, halves_first)
    )
    near, term = call(
        rows_and_term_kernel,
        [shape((2, frames, channels, cols), BF16), shape(halves_first[1].shape, jnp.int16)],
        [VMEM] * 4,
        (shifted(down, "height", 1), shifted(up, "height", -1), future, halves_first[1]),
    )
    around = (future, near, shifted(near, "tm", -1))
    halves_second = halves_second[0], swapped(halves_second[1])
    halves_first = halves_first[0], swapped(term)
    weights, sent = scattered(flags, halves_second, halves_first)
    around = with_columns(flags, hidden_grad, around, (sent,))
    scaled, sums_first = call(
        functools.partial(first_grad_kernel, count=count),
        [shape(block, F32), small],
        [SMEM] + [VMEM] * (9 + len(weights)),
        (flags, hidden_grad, *around, weight_first_t, latent, par, stats_first, *weights[1:]),
        scratch=[pltpu.VMEM(stack, BF16)],
        flops=conv_flops,
        transcendentals=latent.size,
    )
    total, sums_first = summed(flags, weights, sums_first, around[:2])
    sums_first = all_sum(sums_first, axes=("height", "width"))
    decoded_grad, token = call(
        functools.partial(decoded_grad_kernel, count=count),
        [shape((channels, frames, rows, cols), F32), shape((8, 128), F32)],
        [VMEM] * 6,
        (scaled, latent, cotangent, par, stats_first, sums_first),
    )
    second, first = gathered(flags, total, token)
    conv_second_grad = joined(flags, second, swapped(second))
    conv_first_grad = joined(flags, first, swapped(first))
    return decoded_grad, conv_first_grad, conv_second_grad


def solution(mesh):
    block = P(None, "tm", "height", "width")
    return jax.shard_map(
        shards,
        mesh=mesh,
        in_specs=(block, P(), block, P(), P(), P(), P(), P(), P()),
        out_specs=(block, P(), P()),
        check_vma=False,
    )
```

```python
import functools

import jax
import jax.numpy as jnp
from jax import lax
from jax.experimental import pallas as pl
from jax.experimental.pallas import tpu as pltpu
from jax.sharding import PartitionSpec as P

epsilon = 1e-05
F32 = jnp.float32
BF16 = jnp.bfloat16
GROUP = 4
TAPS, SLOTS = 27, 32
FULL, LOW = 32760.0, 65000.0
LN2 = 0.6931471805599453
VMEM = pl.BlockSpec(memory_space=pltpu.VMEM)
SMEM = pl.BlockSpec(memory_space=pltpu.SMEM)


def call(body, outs, specs, args, scratch=(), flops=0, transcendentals=0, limit=20):
    moved = sum(a.size * a.dtype.itemsize for a in args)
    moved += sum(o.size * o.dtype.itemsize for o in outs)
    return pl.pallas_call(
        body,
        out_shape=tuple(outs),
        in_specs=specs,
        out_specs=tuple(VMEM for _ in outs),
        scratch_shapes=scratch,
        compiler_params=pltpu.CompilerParams(vmem_limit_bytes=limit << 20),
        cost_estimate=pl.CostEstimate(
            flops=flops, bytes_accessed=moved, transcendentals=transcendentals
        ),
    )(*args)


def shape(dims, dtype):
    return jax.ShapeDtypeStruct(dims, dtype)


def group_sums(acc):
    rows = acc.shape[0]
    row = lax.broadcasted_iota(jnp.int32, acc.shape, 0)
    step = 1
    while step < GROUP:
        up = pltpu.roll(acc, rows - step, axis=0)
        down = pltpu.roll(acc, step, axis=0)
        acc = acc + jnp.where((row & step) == 0, up, down)
        step *= 2
    return jnp.sum(acc, axis=1, keepdims=True)


def lanes_of(plane):
    total = plane[:, :128]
    for start in range(128, plane.shape[1], 128):
        total = total + plane[:, start : start + 128]
    return total


def as_rows(first, second):
    channels = first.shape[0]
    lane = lax.broadcasted_iota(jnp.int32, (channels, 128), 1)
    both = jnp.where(lane == 0, first, jnp.where(lane == 1, second, 0.0))
    return jnp.transpose(both)[:2]


def local_stats(planes, count):
    acc = None
    for plane in planes:
        part = lanes_of(plane())
        acc = part if acc is None else acc + part
    mean = group_sums(acc) / count
    acc = None
    for plane in planes:
        off = plane() - mean
        part = lanes_of(off * off)
        acc = part if acc is None else acc + part
    return mean, group_sums(acc)


def put_rows(out_ref, first, second):
    out_ref[0] = as_rows(first, second)


def combined(st_ref, count):
    return st_ref[0, 0:1], st_ref[0, 1:2] / count


def columns_of(*rows):
    rows = list(rows) + [jnp.zeros_like(rows[0])] * (8 - len(rows))
    cols = jnp.transpose(jnp.concatenate(rows, axis=0))
    return [cols[:, i : i + 1] for i in range(8)]


def sigmoid(value):
    return 0.5 + 0.5 * jnp.tanh(0.5 * value)


def planes_kernel(latent_ref, cotangent_ref, par_ref, latent_out, cotangent_out, down_ref, up_ref, st_ref):
    _, frames, rows, cols = latent_ref.shape
    for which, (natural, out) in enumerate(((latent_ref, latent_out), (cotangent_ref, cotangent_out))):
        for row in range(rows):
            for frame in range(frames):
                plane = natural[:, frame, row, :]
                out[row, frame] = plane
                if row == rows - 1:
                    down_ref[which, frame] = plane
                if row == 0:
                    up_ref[which, frame] = plane
    scale = columns_of(par_ref[0:1])[0]
    planes = [
        functools.partial(lambda r, t: latent_out[r, t].astype(F32) * scale, r, t)
        for r in range(rows)
        for t in range(frames)
    ]
    put_rows(st_ref, *local_stats(planes, float(GROUP * rows * frames * cols)))


def rows_kernel(above_ref, below_ref, *refs):
    for which, out in enumerate(refs[-above_ref.shape[0] :]):
        out[0] = above_ref[which]
        out[1] = below_ref[which]


def rows_and_term_kernel(above_ref, below_ref, after, theirs_ref, near_ref, term_ref):
    near_ref[0] = above_ref[0]
    near_ref[1] = below_ref[0]
    term_ref[...] = encoded(theirs_ref[...])


def source(own, other, near, far, other_first):
    def at(row, frame):
        is_other = (frame < 2) == other_first
        if row == 0 or row == own.shape[0] + 1:
            return (far if is_other else near), (0 if row == 0 else 1, frame % 2)
        return (other if is_other else own), (row - 1, frame % 2)

    return at


def edges_kernel(flag_ref, first_ref, second_ref, *refs):
    planes, out_ref = (first_ref, second_ref), refs[-1]
    is_first = flag_ref[3] == 0
    channels = planes[0].shape[2]
    lane = lax.broadcasted_iota(jnp.int32, (channels, 128), 1)
    start = pl.multiple_of(jnp.where(is_first, first_ref.shape[3] - 128, 0), 128)
    acc = jnp.zeros((channels, 128), F32)
    number = 0
    for ref in planes:
        for row in range(ref.shape[0]):
            for frame in range(ref.shape[1]):
                half = ref[row, frame, :, pl.ds(start, 128)].astype(F32)
                moved = pltpu.roll(half, number + is_first.astype(jnp.int32), axis=1)
                acc = jnp.where(lane == number, moved, acc)
                number += 1
    out_ref[...] = acc.astype(BF16)


def edge_lane(row, frame, rows, other_first):
    is_other = int((frame < 2) == other_first)
    if row == 0 or row == rows + 1:
        return 1, 4 * is_other + 2 * int(row > 0) + frame % 2
    return 0, 2 * rows * is_other + 2 * (row - 1) + frame % 2


def fill_stack(stack, row, frame, plane, column, on_left, on_right):
    channels, cols = plane.shape
    lane = lax.broadcasted_iota(jnp.int32, (channels, cols), 1)
    column = column.astype(F32)
    left = jnp.where(lane == 0, (column * on_left).astype(BF16), pltpu.roll(plane, 1, axis=1))
    right = jnp.where(lane == cols - 1, (column * on_right).astype(BF16), pltpu.roll(plane, cols - 1, axis=1))
    stack[row, frame, 0:channels] = left
    stack[row, frame, channels : 2 * channels] = plane
    stack[row, frame, 2 * channels : 3 * channels] = right


def sides(flag_ref):
    on_left = (flag_ref[3] != 0).astype(F32)
    on_right = (flag_ref[3] == 0).astype(F32)
    return on_left, on_right


def conv_rows(stack, weight, row):
    three = stack[row : row + 3].reshape(weight.shape[1], stack.shape[3])
    return jnp.dot(weight[...], three, preferred_element_type=F32)


def norm_columns(par_ref, st_ref, count, gain_row):
    par = par_ref[...]
    mean, variance = combined(st_ref, count)
    inverse = 1.0 / jnp.sqrt(variance + epsilon)
    gain = par[gain_row : gain_row + 1]
    shift = par[gain_row + 1 : gain_row + 2]
    return columns_of(mean, inverse, gain, shift, par[0:1])[:5]


def conv_first_kernel(
    flag_ref, own, past, near, far, edge_ref, rim_ref, par_ref, st_ref, weight, after, hidden_ref, st_out, stack_ref,
    *, count
):
    rows, frames, channels, cols = own.shape
    at = source(own, past, near, far, True)
    mean, inverse, gain, shift, scale = norm_columns(par_ref, st_ref, count, 1)

    def act(latent):
        pre = (latent.astype(F32) * scale - mean) * inverse * gain + shift
        return pre * sigmoid(pre)

    has_past = flag_ref[0].astype(F32)
    has_top = flag_ref[1].astype(F32)
    has_bottom = flag_ref[2].astype(F32)
    on_left, on_right = sides(flag_ref)
    edges = (act(edge_ref[...]), act(rim_ref[...]))
    for row in range(rows + 2):
        for frame in range(4):
            ref, index = at(row, frame)
            which, number = edge_lane(row, frame, rows, True)
            plane = act(ref[index])
            column = edges[which][:, number : number + 1]
            factor = None
            if frame < 2:
                factor = has_past
            if row in (0, rows + 1):
                beside = has_top if row == 0 else has_bottom
                factor = beside if factor is None else factor * beside
            if factor is not None:
                plane = plane * factor
                column = column * factor
            fill_stack(stack_ref, row, frame, plane.astype(BF16), column, on_left, on_right)
    for row in range(rows):
        out = conv_rows(stack_ref, weight, row)
        for frame in range(frames):
            hidden_ref[row, frame] = out[frame * channels : (frame + 1) * channels]
    planes = [
        functools.partial(lambda r, t: hidden_ref[r, t], r, t) for r in range(rows) for t in range(frames)
    ]
    put_rows(st_out, *local_stats(planes, float(GROUP * rows * frames * cols)))


def fill_future(stack, flag_ref, own, future, near, far, edge_ref, rim_ref):
    rows = own.shape[0]
    at = source(own, future, near, far, False)
    on_left, on_right = sides(flag_ref)
    edges = (edge_ref[...], rim_ref[...])
    for row in range(rows + 2):
        for frame in range(4):
            ref, index = at(row, frame)
            which, number = edge_lane(row, frame, rows, False)
            fill_stack(stack, row, frame, ref[index], edges[which][:, number : number + 1], on_left, on_right)


def conv_back_kernel(flag_ref, *refs):
    weight, grad_ref, stack_ref = refs[-3:]
    rows, frames, channels, _ = grad_ref.shape
    fill_future(stack_ref, flag_ref, *refs[:-3])
    for row in range(rows):
        out = conv_rows(stack_ref, weight, row)
        for frame in range(frames):
            grad_ref[row, frame] = out[frame * channels : (frame + 1) * channels]


def norm_second_kernel(hidden, grad, par_ref, st_ref, act_ref, scaled_ref, sums_ref, *, count):
    rows, frames, channels, cols = hidden.shape
    mean, inverse, gain, shift, _ = norm_columns(par_ref, st_ref, count, 3)
    first = jnp.zeros((channels, 128), F32)
    second = jnp.zeros((channels, 128), F32)
    for row in range(rows):
        for frame in range(frames):
            normed = (hidden[row, frame] - mean) * inverse
            pre = normed * gain + shift
            sig = sigmoid(pre)
            act = pre * sig
            act_ref[row, frame] = act.astype(BF16)
            scaled = grad[row, frame] * (sig + act * (1.0 - sig)) * gain
            scaled_ref[row, frame] = scaled
            first = first + lanes_of(scaled)
            second = second + lanes_of(scaled * normed)
    put_rows(sums_ref, group_sums(first), group_sums(second))


def hidden_grad_kernel(
    hidden, scaled, par_ref, st_ref, sums_ref, out_ref, down_ref, up_ref, *, count
):
    rows, frames, channels, cols = hidden.shape
    mean, inverse, _, _, _ = norm_columns(par_ref, st_ref, count, 3)
    means = sums_ref[0] / count
    first, second = columns_of(means[0:1], means[1:2])[:2]
    for row in range(rows):
        for frame in range(frames):
            normed = (hidden[row, frame] - mean) * inverse
            plane = (inverse * (scaled[row, frame] - first - normed * second)).astype(BF16)
            out_ref[row, frame] = plane
            if row == rows - 1:
                down_ref[0, frame] = plane
            if row == 0:
                up_ref[0, frame] = plane


def put_halves(flag_ref, mine_ref, theirs_ref, tap, block):
    half = block.shape[0] // 2
    here = pl.ds(tap, half, stride=SLOTS)
    upper, lower = block[:half], block[half:]
    is_first = flag_ref[3] == 0
    mine_ref[here, :] = jnp.where(is_first, upper, lower)
    theirs_ref[here, :] = jnp.where(is_first, lower, upper)


def encoded(value, digits=None):
    slot = lax.broadcasted_iota(jnp.int32, value.shape, 1)
    value = jnp.where(slot < TAPS, value, 0.0)
    top = jnp.max(jnp.abs(value), axis=1, keepdims=True)
    power = jnp.ceil(jnp.log(jnp.maximum(top, 1e-30)) * (1.0 / LN2))
    number = jnp.round(value * (FULL * jnp.exp(power * -LN2)))
    number = jnp.where(slot < TAPS, number, power)
    if digits is not None:
        first_row = lax.broadcasted_iota(jnp.int32, value.shape, 0) == 0
        for place, digit in enumerate(digits):
            number = jnp.where(first_row & (slot == TAPS + place), digit[None], number)
    return number.astype(jnp.int32).astype(jnp.int16)


def digits_of(value):
    power = jnp.ceil(jnp.log(jnp.maximum(jnp.abs(value), 1e-30)) * (1.0 / LN2))
    scaled = value * (FULL * jnp.exp(power * -LN2))
    high = jnp.round(scaled)
    return high, jnp.round((scaled - high) * LOW), power


def value_of(number):
    number = number.astype(jnp.int32).astype(F32)
    high, low, power = (number[TAPS + place : TAPS + place + 1] for place in range(3))
    return (high + low * (1.0 / LOW)) * (jnp.exp(power * LN2) * (1.0 / FULL))


def decoded_value(number):
    number = number.astype(jnp.int32).astype(F32)
    return number * (jnp.exp(number[:, SLOTS - 1 : SLOTS] * LN2) * (1.0 / FULL))


def first_scatter_kernel(flag_ref, *refs, slot):
    me = flag_ref[slot]
    for which in range(2):
        mine, other = refs[2 * which], refs[2 * which + 1]
        for k, out in enumerate(refs[4:]):
            total = other[me ^ k]
            total = mine[me ^ k] + (total if total.dtype == F32 else decoded_value(total))
            out[which] = total if k == 0 else encoded(total)


def scatter_kernel(flag_ref, sums_ref, *refs, received, sent, slot, last):
    me = flag_ref[slot]
    for which in range(2):
        digits = digits_of(sums_ref[0, which : which + 1]) if last else None
        for k, out in enumerate(refs[-sent:]):
            total = refs[0][which, me ^ k]
            for ref in refs[1:received]:
                total = total + decoded_value(ref[which, me ^ k])
            out[which] = total if k == 0 else encoded(total, digits)


def total_kernel(sums_ref, *refs, received):
    out_ref, sums_out = refs[-2:]
    for which in range(2):
        total = refs[0][which]
        terms = sums_ref[0, which : which + 1]
        for ref in refs[1:received]:
            total = total + decoded_value(ref[which])
            terms = terms + value_of(ref[which, 0])
        out_ref[which] = encoded(total)
        sums_out[0, which : which + 1] = terms


def split_kernel(flag_ref, *refs, received, slot):
    me = flag_ref[slot]
    for which in range(2):
        for k, ref in enumerate(refs[:received]):
            refs[which - 2][me ^ k] = ref[which]


def gather_kernel(flag_ref, *refs, received, slot):
    me = flag_ref[slot]
    for k, ref in enumerate(refs[:received]):
        refs[-1][me ^ k] = ref[...]


def join_kernel(flag_ref, mine_ref, theirs_ref, out_ref, first_ref, second_ref):
    half, _, channels = mine_ref.shape
    is_first = flag_ref[3] == 0
    first_ref[...] = decoded_value(jnp.where(is_first, mine_ref[...], theirs_ref[...])).reshape(first_ref.shape)
    second_ref[...] = decoded_value(jnp.where(is_first, theirs_ref[...], mine_ref[...])).reshape(second_ref.shape)
    for tap in range(TAPS):
        here = slice(tap * channels, (tap + 1) * channels)
        out_ref[:half, here] = first_ref[pl.ds(tap, half, stride=SLOTS), :]
        out_ref[half:, here] = second_ref[pl.ds(tap, half, stride=SLOTS), :]


def weight_second_kernel(flag_ref, stack_ref, act_ref, mine_ref, theirs_ref, right_ref):
    rows, frames, channels, cols = act_ref.shape
    for row in range(rows):
        right_ref[row * cols : (row + 1) * cols] = jnp.transpose(
            act_ref[row].reshape(frames * channels, cols)
        )
    right = right_ref[...]
    for down in range(3):
        parts = []
        for frame in range(4):
            left = jnp.concatenate([stack_ref[down + row, frame] for row in range(rows)], axis=1)
            parts.append(jnp.dot(left, right, preferred_element_type=F32))
        for kt in range(3):
            term = parts[2 - kt][:, :channels] + parts[3 - kt][:, channels:]
            for across in range(3):
                tap = 9 * kt + 3 * (2 - down) + (2 - across)
                put_halves(flag_ref, mine_ref, theirs_ref, tap, term[across * channels : (across + 1) * channels])


def weight_first_kernel(flag_ref, stack_ref, grad_ref, mine_ref, theirs_ref, right_ref):
    rows, frames, channels, cols = grad_ref.shape
    for row in range(rows):
        right_ref[row * cols : (row + 1) * cols] = jnp.transpose(
            grad_ref[row].reshape(frames * channels, cols)
        )
    right = right_ref[...]
    for down in range(3):
        parts = []
        for frame in range(4):
            left = jnp.concatenate([stack_ref[down + row, frame] for row in range(rows)], axis=1)
            parts.append(jnp.dot(left, right, preferred_element_type=F32))
        for kt in range(3):
            term = parts[kt][:, :channels] + parts[kt + 1][:, channels:]
            for across in range(3):
                tap = 9 * kt + 3 * down + across
                block = jnp.transpose(term[across * channels : (across + 1) * channels])
                put_halves(flag_ref, mine_ref, theirs_ref, tap, block)


def first_grad_kernel(flag_ref, *refs, count):
    weight, latent, par_ref, st_ref = refs[6:10]
    scaled_ref, sums_ref, stack_ref = refs[-3:]
    rows, frames, channels, cols = latent.shape
    mean, inverse, gain, shift, scale = norm_columns(par_ref, st_ref, count, 1)
    fill_future(stack_ref, flag_ref, *refs[:6])
    first = jnp.zeros((channels, 128), F32)
    second = jnp.zeros((channels, 128), F32)
    for row in range(rows):
        out = conv_rows(stack_ref, weight, row)
        for frame in range(frames):
            grad = out[frame * channels : (frame + 1) * channels]
            normed = (latent[row, frame].astype(F32) * scale - mean) * inverse
            pre = normed * gain + shift
            sig = sigmoid(pre)
            scaled = grad * (sig + pre * sig * (1.0 - sig)) * gain
            scaled_ref[row, frame] = scaled
            first = first + lanes_of(scaled)
            second = second + lanes_of(scaled * normed)
    put_rows(sums_ref, group_sums(first), group_sums(second))


def decoded_grad_kernel(scaled, latent, cotangent, par_ref, st_ref, sums_ref, out_ref, *, count):
    rows, frames, channels, cols = latent.shape
    mean, inverse, _, _, scale = norm_columns(par_ref, st_ref, count, 1)
    means = sums_ref[0] / count
    first, second = columns_of(means[0:1], means[1:2])[:2]
    for row in range(rows):
        for frame in range(frames):
            normed = (latent[row, frame].astype(F32) * scale - mean) * inverse
            out_ref[:, frame, row, :] = cotangent[row, frame].astype(F32) + inverse * (
                scaled[row, frame] - first - normed * second
            )


def weight_forward_kernel(weight, out_ref):
    channels = weight.shape[0]
    wide = 3 * channels
    for t in range(2):
        for kr in range(3):
            for f in range(4):
                kt = f - t
                here = slice((kr * 4 + f) * wide, (kr * 4 + f + 1) * wide)
                if 0 <= kt < 3:
                    tap = 3 * kt + kr
                    block = weight[:, tap * wide : (tap + 1) * wide]
                else:
                    block = jnp.zeros((channels, wide), BF16)
                out_ref[t * channels : (t + 1) * channels, here] = block


def weight_back_kernel(weight, out_ref):
    channels = weight.shape[0]
    for down in range(3):
        for across in range(3):
            blocks = [
                jnp.transpose(
                    weight[
                        :,
                        (9 * kt + 3 * (2 - down) + 2 - across) * channels : (9 * kt + 3 * (2 - down) + 3 - across)
                        * channels,
                    ]
                )
                for kt in range(3)
            ]
            for t in range(2):
                for f in range(4):
                    kt = t + 2 - f
                    start = ((down * 4 + f) * 3 + across) * channels
                    block = blocks[kt] if 0 <= kt < 3 else jnp.zeros((channels, channels), BF16)
                    out_ref[t * channels : (t + 1) * channels, start : start + channels] = block


def shifted(value, axis, steps):
    count = lax.axis_size(axis)
    initial, last = max(0, -steps), min(count, count - steps)
    return lax.ppermute(value, axis, [(source, source + steps) for source in range(initial, last)])


def rounds(axes):
    for axis in axes:
        count = lax.axis_size(axis)
        step = 1
        while step < count:
            wide = 4 if 4 * step <= count else 2
            yield axis, step, [[(i, i ^ (step * k)) for i in range(count)] for k in range(1, wide)]
            step *= wide


def pairwise(parts, join):
    while len(parts) > 1:
        parts = [join(a, b) for a, b in zip(parts[::2], parts[1::2])]
    return parts[0]


def sum_kernel(*refs, parts):
    refs[-1][...] = pairwise([ref[...] for ref in refs[:parts]], lambda a, b: a + b)


def stats_kernel(*refs, parts, count):
    refs[-1][...] = pairwise([(ref[...], count) for ref in refs[:parts]], joined_stats)[0]


def all_sum(value, after=(), axes=("tm", "height", "width")):
    for axis, _, exchanges in rounds(axes):
        parts = [value] + [lax.ppermute(value, axis, pairs) for pairs in exchanges]
        if after:
            value = joined_after(functools.partial(sum_kernel, parts=len(parts)), parts, after)
        else:
            value = pairwise(parts, lambda a, b: a + b)
        after = ()
    return value


def joined_after(body, parts, after):
    (value,) = call(body, [shape(parts[0].shape, F32)], [VMEM] * (len(parts) + len(after)), (*parts, *after))
    return value


def all_stats(value, count, after=()):
    for axis, _, exchanges in rounds(("tm", "height", "width")):
        parts = [value] + [lax.ppermute(value, axis, pairs) for pairs in exchanges]
        if after:
            value = joined_after(functools.partial(stats_kernel, parts=len(parts), count=count), parts, after)
        else:
            value, _ = pairwise([(part, count) for part in parts], joined_stats)
        count, after = count * len(parts), ()
    return value


def joined_stats(first, second):
    (a, count), (b, _) = first, second
    gap = a[:, 0:1] - b[:, 0:1]
    squares = a[:, 1:2] + b[:, 1:2] + gap * gap * (0.5 * count)
    return jnp.concatenate([0.5 * (a[:, 0:1] + b[:, 0:1]), squares], axis=1), 2.0 * count


def swapped(value):
    return lax.ppermute(value, "width", [(0, 1), (1, 0)])


def weight_rounds():
    return list(rounds(("height", "tm")))


def scattered(flags, second, first):
    half, _, channels = second[0].shape
    axis, _, exchanges = weight_rounds()[0]
    parts = len(exchanges) + 1
    rows = half // parts
    terms = [part for mine, theirs in (second, first) for part in (mine, theirs)]
    part = (2, rows, SLOTS, channels)
    kept, *sent = call(
        functools.partial(first_scatter_kernel, slot=4),
        [shape(part, F32)] + [shape(part, jnp.int16)] * (parts - 1),
        [SMEM] + [VMEM] * 4,
        (flags, *[term.reshape(parts, rows, SLOTS, channels) for term in terms]),
    )
    return [kept] + [lax.ppermute(v, axis, pairs) for v, pairs in zip(sent, exchanges)], sent[0]


def summed(flags, received, sums, after):
    others = weight_rounds()[1:]
    for number, (axis, _, exchanges) in enumerate(others, 5):
        parts = len(exchanges) + 1
        _, rows, _, channels = received[0].shape
        part = (2, rows // parts, SLOTS, channels)
        views = [v.reshape(2, parts, *part[1:]) for v in received]
        last = number == len(others) + 4
        kept, *sent = call(
            functools.partial(scatter_kernel, received=len(views), sent=parts, slot=number, last=last),
            [shape(part, F32)] + [shape(part, jnp.int16)] * (parts - 1),
            [SMEM] + [VMEM] * (1 + len(views) + len(after)),
            (flags, sums, *views, *after),
        )
        after = ()
        received = [kept] + [lax.ppermute(v, axis, pairs) for v, pairs in zip(sent, exchanges)]
    return call(
        functools.partial(total_kernel, received=len(received)),
        [shape(received[0].shape, jnp.int16), shape(sums.shape, F32)],
        [VMEM] * (1 + len(received)),
        (sums, *received),
    )


def gathered(flags, total, after_last):
    _, rows, _, channels = total.shape
    back = list(enumerate(weight_rounds(), 4))[::-1]
    number, (axis, _, exchanges) = back[0]
    pieces = [total] + [lax.ppermute(total, axis, pairs) for pairs in exchanges]
    values = call(
        functools.partial(split_kernel, received=len(pieces), slot=number),
        [shape((len(pieces), rows, SLOTS, channels), jnp.int16)] * 2,
        [SMEM] + [VMEM] * len(pieces),
        (flags, *pieces),
    )
    results = []
    for which, value in enumerate(values):
        after = (after_last,) if which else ()
        for number, (axis, _, exchanges) in back[1:]:
            value = value.reshape(-1, SLOTS, channels)
            pieces = [value] + [lax.ppermute(value, axis, pairs) for pairs in exchanges]
            (value,) = call(
                functools.partial(gather_kernel, received=len(pieces), slot=number),
                [shape((len(pieces), *value.shape), jnp.int16)],
                [SMEM] + [VMEM] * (len(pieces) + len(after)),
                (flags, *pieces, *after),
            )
        results.append(value.reshape(-1, SLOTS, channels))
    return results


def joined(flags, mine, theirs):
    half, _, channels = mine.shape
    (total,) = call(
        join_kernel,
        [shape((2 * half, TAPS * channels), F32)],
        [SMEM] + [VMEM] * 2,
        (flags, mine, theirs),
        scratch=[pltpu.VMEM((half * SLOTS, channels), F32)] * 2,
    )
    return total


def edges(flags, planes, after):
    channels = planes[0].shape[2]
    args = (*planes, *after)
    (columns,) = call(edges_kernel, [shape((channels, 128), BF16)], [SMEM] + [VMEM] * len(args), (flags, *args))
    return columns


def row_halos(down, up, after=()):
    above, below = shifted(down, "height", 1), shifted(up, "height", -1)
    return call(
        rows_kernel,
        [shape((2, *down.shape[1:]), BF16)] * down.shape[0],
        [VMEM] * (2 + len(after)),
        (above, below, *after),
    )


def with_columns(flags, own, around, after=()):
    edge = swapped(edges(flags, (own, around[0]), after))
    rim = swapped(edges(flags, around[1:], after))
    return *around, edge, rim


def shards(
    latent,
    exponents,
    cotangent,
    conv_first,
    conv_second,
    gain_first,
    shift_first,
    gain_second,
    shift_second,
):
    channels, frames, rows, cols = latent.shape
    groups = exponents.shape[0]
    devices = lax.axis_size("tm") * lax.axis_size("height") * lax.axis_size("width")
    count = float(channels // groups * frames * rows * cols * devices)
    tm, height, width = (lax.axis_index(axis) for axis in ("tm", "height", "width"))
    flags = jnp.stack(
        [
            (tm > 0).astype(jnp.int32),
            (height > 0).astype(jnp.int32),
            (height < lax.axis_size("height") - 1).astype(jnp.int32),
            width.astype(jnp.int32),
        ]
        + [
            (lax.axis_index(axis) // step % (len(exchanges) + 1)).astype(jnp.int32)
            for axis, step, exchanges in weight_rounds()
        ]
    )
    scale = jnp.repeat(jnp.exp2(exponents.astype(F32)), channels // groups)
    zeros = jnp.zeros_like(scale)
    par = jnp.stack([scale, gain_first, shift_first, gain_second, shift_second, zeros, zeros, zeros])
    block = (rows, frames, channels, cols)
    stack = (rows + 2, 4, 3 * channels, cols)
    taps = (2 * channels, 36 * channels)
    halves = [shape((channels // 2 * SLOTS, channels), F32)] * 2
    conv_flops = 3 * 2 * 4 * 256 * 36 * channels * 2 * channels
    small = shape((1, 2, channels), F32)

    message = shape((2, frames, channels, cols), BF16)
    latent, cotangent, down, up, stats_first = call(
        planes_kernel,
        [shape(block, BF16), shape(block, BF16), message, message, small],
        [VMEM] * 3,
        (latent, cotangent, par),
    )
    near, near_c = row_halos(down, up)
    around = with_columns(flags, latent, (shifted(latent, "tm", 1), near, shifted(near, "tm", 1)))
    around_c = (shifted(cotangent, "tm", -1), near_c, shifted(near_c, "tm", -1))
    stats_first = all_stats(stats_first, count / devices)
    (weight_first,) = call(weight_forward_kernel, [shape(taps, BF16)], [VMEM], (conv_first,))
    (weight_second_t,) = call(weight_back_kernel, [shape(taps, BF16)], [VMEM], (conv_second,))
    (weight_first_t,) = call(weight_back_kernel, [shape(taps, BF16)], [VMEM], (conv_first,))

    hidden, stats_second, stack_first = call(
        functools.partial(conv_first_kernel, count=count),
        [shape(block, F32), small, shape(stack, BF16)],
        [SMEM] + [VMEM] * 10,
        (flags, latent, *around, par, stats_first, weight_first, around_c[2]),
        flops=conv_flops,
        transcendentals=3 * latent.size,
    )
    around_c = with_columns(flags, cotangent, around_c, (stats_second,))
    grad_second, stack_c = call(
        conv_back_kernel,
        [shape(block, F32), shape(stack, BF16)],
        [SMEM] + [VMEM] * 7,
        (flags, cotangent, *around_c, weight_second_t),
        flops=conv_flops,
    )
    stats_second = all_stats(stats_second, count / devices, (grad_second,))
    act_second, scaled, sums = call(
        functools.partial(norm_second_kernel, count=count),
        [shape(block, BF16), shape(block, F32), small],
        [VMEM] * 4,
        (hidden, grad_second, par, stats_second),
        transcendentals=latent.size,
    )
    halves_second = call(
        weight_second_kernel,
        halves,
        [SMEM] + [VMEM] * 2,
        (flags, stack_c, act_second),
        scratch=[pltpu.VMEM((rows * cols, frames * channels), BF16)],
        flops=conv_flops,
    )
    sums = all_sum(sums, (halves_second[0],))
    message = shape((1, frames, channels, cols), BF16)
    hidden_grad, down, up = call(
        functools.partial(hidden_grad_kernel, count=count),
        [shape(block, BF16), message, message],
        [VMEM] * 5,
        (hidden, scaled, par, stats_second, sums),
    )
    future = shifted(hidden_grad, "tm", -1)
    halves_first = call(
        weight_first_kernel,
        halves,
        [SMEM] + [VMEM] * 2,
        (flags, stack_first, hidden_grad),
        scratch=[pltpu.VMEM((rows * cols, frames * channels), BF16)],
        flops=conv_flops,
    )
    halves_second, halves_first = (
        [v.reshape(channels // 2, SLOTS, channels) for v in halves] for halves in (halves_second, halves_first)
    )
    near, term = call(
        rows_and_term_kernel,
        [shape((2, frames, channels, cols), BF16), shape(halves_first[1].shape, jnp.int16)],
        [VMEM] * 4,
        (shifted(down, "height", 1), shifted(up, "height", -1), future, halves_first[1]),
    )
    around = (future, near, shifted(near, "tm", -1))
    halves_second = halves_second[0], swapped(halves_second[1])
    halves_first = halves_first[0], swapped(term)
    weights, sent = scattered(flags, halves_second, halves_first)
    around = with_columns(flags, hidden_grad, around, (sent,))
    scaled, sums_first = call(
        functools.partial(first_grad_kernel, count=count),
        [shape(block, F32), small],
        [SMEM] + [VMEM] * (9 + len(weights)),
        (flags, hidden_grad, *around, weight_first_t, latent, par, stats_first, *weights[1:]),
        scratch=[pltpu.VMEM(stack, BF16)],
        flops=conv_flops,
        transcendentals=latent.size,
    )
    total, sums_first = summed(flags, weights, sums_first, around[:2])
    sums_first = all_sum(sums_first, axes=("height", "width"))
    (decoded_grad,) = call(
        functools.partial(decoded_grad_kernel, count=count),
        [shape((channels, frames, rows, cols), F32)],
        [VMEM] * 6,
        (scaled, latent, cotangent, par, stats_first, sums_first),
    )
    second, first = gathered(flags, total, sums_first)
    conv_second_grad = joined(flags, second, swapped(second))
    conv_first_grad = joined(flags, first, swapped(first))
    return decoded_grad, conv_first_grad, conv_second_grad


def solution(mesh):
    block = P(None, "tm", "height", "width")
    return jax.shard_map(
        shards,
        mesh=mesh,
        in_specs=(block, P(), block, P(), P(), P(), P(), P(), P()),
        out_specs=(block, P(), P()),
        check_vma=False,
    )
```
